256 devices in a mesh: kgrp: 4 (over x_hi, core), band: 64 (over y, x_lo, z).
Axes of the slice: x: 4 (x_hi: 2, x_lo: 2; x = x_hi * 2 + x_lo), y: 4, z: 8, core: 2. Of those that a mesh axis runs over, the one named last changes fastest.
Arguments:
- orbitals: bfloat16 [4, 2, 4096, 432], P('kgrp', None, 'band'), may hold values from -1.75 to 1.75
- kernels: bfloat16 [4, 2, 4096, 4096], P(None, None, 'band'), may hold values from -0.0014648438 to 0.0014648438
- pair_kdiff: int32 [4], P('kgrp'), may hold values from 0 to 7
- stored_kernel_index: int32 [8], replicated, may hold values from 0 to 3
Outputs:
- exchange: float32 [4, 2, 186624], P('kgrp', None, 'band')
The draws below stay inside these ranges and needn't reach their ends.
All inputs are finite; a program needn't handle non-finite values.
Results may differ from the reference program's by a relative error of at most 0.0041.
Values may be sent and summed in bfloat16 or wider, within the bound.
No kernel may reach another device: no remote copies, remote signals or barrier semaphores. Data moves between devices by JAX's collectives and lax.ppermute only.
A program may use at most 128 MiB of HBM per device.

```python
import jax
import jax.numpy as jnp
from jax import lax

NB = 432
INTERP_POINTS = 4096
KERNEL_SLOTS = 4
KPOINT_DIFFS = 8
NK = 4


def place_ends(entries, rng, smallest, top_value):
    spot = [jax.random.randint(jax.random.fold_in(rng, axis), (), 0, length) for axis, length in enumerate(entries.shape)]
    main_axis = entries.shape.index(max(entries.shape))
    next_to = spot[:main_axis] + [(spot[main_axis] + 1) % entries.shape[main_axis]] + spot[main_axis + 1:]
    return entries.at[tuple(spot)].set(smallest).at[tuple(next_to)].set(top_value)


def levels(key, extent, pieces, smallest, largest):
    gain, own = 1.0, jax.random.fold_in(key, 6)
    for axis_at, shards_of in pieces:
        steps = jnp.exp(jax.random.uniform(jax.random.fold_in(own, axis_at), (shards_of,), jnp.float32, smallest / len(pieces), largest / len(pieces)))
        gain = gain * jnp.repeat(steps, extent[axis_at] // shards_of).reshape([-1 if axis == axis_at else 1 for axis in range(len(extent))])
    return gain


def gaussian(stream_key, extent, spread, limit, pieces=(), dtype=jnp.bfloat16):
    entries = spread * jax.random.normal(stream_key, extent, jnp.float32)
    if pieces:
        entries = entries * levels(stream_key, extent, pieces, -0.22, 0.18)
    return jnp.clip(entries, -limit, limit).astype(dtype)


def setup_inputs(seed: int = 0) -> dict:
    seeds = jax.random.split(jax.random.key(seed), 5)
    orbitals = gaussian(seeds[0], (NK, 2, INTERP_POINTS, NB), ((32 * NB) ** -0.125), 1.75, ((0, 4), (2, 64)))
    kernels = gaussian(seeds[1], (KERNEL_SLOTS, 2, INTERP_POINTS, INTERP_POINTS), (1.0 / INTERP_POINTS), 0.0014648438, ((2, 64),))
    pair_kdiff = place_ends(jax.random.randint(seeds[2], (NK,), 0, KPOINT_DIFFS), jax.random.fold_in(seeds[2], 1), 0, KPOINT_DIFFS - 1).astype(jnp.int32)
    stored_kernel_index = place_ends(jax.random.randint(seeds[3], (KPOINT_DIFFS,), 0, KERNEL_SLOTS), jax.random.fold_in(seeds[3], 1), 0, KERNEL_SLOTS - 1).astype(jnp.int32)
    return dict(orbitals=orbitals, kernels=kernels, pair_kdiff=pair_kdiff, stored_kernel_index=stored_kernel_index)


def contract_last(leading, trailing):
    return lax.dot_general(leading, trailing, (((1,), (1,)), ((), ())), preferred_element_type=jnp.float32)


def contract_first(leading, trailing):
    return lax.dot_general(leading, trailing, (((0,), (0,)), ((), ())), preferred_element_type=jnp.float32)


def product(leading, trailing):
    return jnp.dot(leading, trailing, preferred_element_type=jnp.float32)


def density(first_rows, second_rows):
    real_part = contract_last(first_rows[0], second_rows[0]) + contract_last(first_rows[1], second_rows[1])
    imag_part = contract_last(first_rows[1], second_rows[0]) - contract_last(first_rows[0], second_rows[1])
    return real_part, imag_part


def project(orbit_rows, real_part, imag_part):
    real_half = real_part.astype(jnp.bfloat16)
    imag_half = imag_part.astype(jnp.bfloat16)
    matrix_real = -(contract_first(orbit_rows[0], real_half) + contract_first(orbit_rows[1], imag_half))
    matrix_imag = -(contract_first(orbit_rows[0], imag_half) - contract_first(orbit_rows[1], real_half))
    return jnp.stack([matrix_real, matrix_imag]).reshape(2, -1)


def pair_terms(local_orbital_rows, partner_orbit, kernel):
    kern_real = kernel[0].astype(jnp.float32)
    kern_imag = kernel[1].astype(jnp.float32)
    near_real, near_imag = density(partner_orbit, partner_orbit)
    self_real, self_imag = density(local_orbital_rows, local_orbital_rows)
    first_real = (kern_real * near_real - kern_imag * near_imag).astype(jnp.bfloat16)
    first_imag = (kern_real * near_imag + kern_imag * near_real).astype(jnp.bfloat16)
    second_real = (kern_real * self_real + kern_imag * self_imag).astype(jnp.bfloat16)
    second_imag = (kern_real * self_imag - kern_imag * self_real).astype(jnp.bfloat16)
    ones_real = product(first_real, local_orbital_rows[0]) - product(first_imag, local_orbital_rows[1])
    ones_imag = product(first_real, local_orbital_rows[1]) + product(first_imag, local_orbital_rows[0])
    twos_real = product(second_real, partner_orbit[0]) - product(second_imag, partner_orbit[1])
    twos_imag = product(second_real, partner_orbit[1]) + product(second_imag, partner_orbit[0])
    return project(local_orbital_rows, ones_real, ones_imag), project(partner_orbit, twos_real, twos_imag)


def reference(orbitals, kernels, pair_kdiff, stored_kernel_index):
    kcount = orbitals.shape[0]
    firsts = []
    seconds = []
    for kpoint in range(kcount):
        partner_orbit = orbitals[(kpoint - 1) % kcount]
        kernel_slot = stored_kernel_index[pair_kdiff[kpoint]].astype(jnp.int32)
        kernel = lax.dynamic_index_in_dim(kernels, kernel_slot, 0, keepdims=False)
        first_term, second_term = pair_terms(orbitals[kpoint], partner_orbit, kernel)
        firsts.append(first_term)
        seconds.append(second_term)
    results = [firsts[kpoint] + seconds[(kpoint + 1) % kcount] for kpoint in range(kcount)]
    return jnp.stack(results)
```

```python
import functools

import jax
import jax.numpy as jnp
import numpy as np
from jax import lax
from jax.experimental import pallas as pl
from jax.experimental.pallas import tpu as pltpu
from jax.sharding import PartitionSpec as P

NB = 432
SLAB = 64
NY, NX, NZ = 4, 2, 8
GROUPS = NY * NX
BLOCK = NZ * SLAB
KEEP = 16
VMEM = 56 * 1024 * 1024

OFFSETS = [(dy, dx) for dy in range(NY) for dx in range(NX)]
Z_OFFSETS = [0, 1, -1, 2, -2, 3, -3, 4]


def band_route(dy, dx, dz):
    route = []
    for y in range(NY):
        for x in range(NX):
            for z in range(NZ):
                there = ((y + dy) % NY * NX + (x + dx) % NX) * NZ + (z + dz) % NZ
                route.append(((y * NX + x) * NZ + z, there))
    return route


def shift(block, dy, dx, dz):
    return lax.ppermute(block, "band", band_route(dy, dx, dz))


def swap_groups(block, bit):
    return lax.ppermute(block, "kgrp", [(k, k ^ bit) for k in range(4)])


def dot(a, b, dims):
    return lax.dot_general(a, b, ((dims[0], dims[1]), ((), ())), preferred_element_type=jnp.float32)


def pack_body(slot_ref, dest_ref, kernels_ref, *refs):
    outs, sem = refs[:GROUPS], refs[GROUPS]
    copies = []
    for which in range(2):
        for i in range(GROUPS):
            start = pl.multiple_of(dest_ref[i] * BLOCK, BLOCK)
            copies.append(
                pltpu.make_async_copy(
                    kernels_ref.at[slot_ref[which], :, :, pl.ds(start, BLOCK)],
                    outs[i].at[which],
                    sem.at[which, i],
                )
            )
    for copy in copies:
        copy.start()
    for copy in copies:
        copy.wait()


def pack(slots, dests, kernels):
    piece = jax.ShapeDtypeStruct((2, 2, SLAB, BLOCK), jnp.bfloat16)
    return pl.pallas_call(
        pack_body,
        out_shape=[piece] * GROUPS,
        in_specs=[
            pl.BlockSpec(memory_space=pltpu.SMEM),
            pl.BlockSpec(memory_space=pltpu.SMEM),
            pl.BlockSpec(memory_space=pl.ANY),
        ],
        out_specs=[pl.BlockSpec(memory_space=pl.ANY)] * GROUPS,
        scratch_shapes=[pltpu.SemaphoreType.DMA((2, GROUPS))],
        name="pack",
    )(slots, dests, kernels)


def mix_body(n_rows, n_cols, place_ref, sign_ref, *refs):
    rows, refs = refs[:n_rows], refs[n_rows:]
    cols, refs = refs[:n_cols], refs[n_cols:]
    kerns, refs = refs[:GROUPS], refs[GROUPS:]
    m_ref, row_ref, col_ref, other_rows, other_cols = refs
    for i in range(GROUPS):
        at = pl.ds(i * SLAB, SLAB)
        row_ref[:, at, :] = rows[i][0]
        other_rows[:, at, :] = rows[i][1]
    for i in range(NZ):
        at = pl.ds(pl.multiple_of(place_ref[i] * SLAB, SLAB), SLAB)
        col_ref[:, at, :] = cols[i][0]
        other_cols[:, at, :] = cols[i][1]
    last = ((1,), (1,))
    per = 2 * SLAB
    for part in range(GROUPS // 2):
        at = pl.ds(part * per, per)
        total_re = total_im = None
        for which, (a_ref, b_ref) in enumerate(((row_ref, col_ref), (other_rows, other_cols))):
            a_re, a_im = a_ref[0, at, :], a_ref[1, at, :]
            p_re = dot(a_re, b_ref[0], last) + dot(a_im, b_ref[1], last)
            p_im = dot(a_im, b_ref[0], last) - dot(a_re, b_ref[1], last)
            sign = sign_ref[which]
            k_re = jnp.concatenate(
                [kerns[2 * part][which, 0], kerns[2 * part + 1][which, 0]], axis=0
            ).astype(jnp.float32)
            k_im = jnp.concatenate(
                [kerns[2 * part][which, 1], kerns[2 * part + 1][which, 1]], axis=0
            ).astype(jnp.float32) * sign
            m_re = k_re * p_re - k_im * p_im
            m_im = k_re * p_im + k_im * p_re
            total_re = m_re if total_re is None else total_re + m_re
            total_im = m_im if total_im is None else total_im + m_im
        m_ref[0, at, :] = total_re.astype(jnp.bfloat16)
        m_ref[1, at, :] = total_im.astype(jnp.bfloat16)


def mix(place, sign, rows, cols, kerns):
    vmem = pl.BlockSpec(memory_space=pltpu.VMEM)
    smem = pl.BlockSpec(memory_space=pltpu.SMEM)
    points = jax.ShapeDtypeStruct((2, BLOCK, NB), jnp.bfloat16)
    return pl.pallas_call(
        functools.partial(mix_body, len(rows), len(cols)),
        out_shape=[jax.ShapeDtypeStruct((2, BLOCK, BLOCK), jnp.bfloat16), points, points],
        in_specs=[smem, smem] + [vmem] * (len(rows) + len(cols) + len(kerns)),
        out_specs=[vmem] * 3,
        scratch_shapes=[pltpu.VMEM((2, BLOCK, NB), jnp.bfloat16)] * 2,
        compiler_params=pltpu.CompilerParams(vmem_limit_bytes=VMEM),
        name="mix",
    )(place, sign, *rows, *cols, *kerns)


def project_body(m_ref, row_ref, col_ref, out_ref, x_ref):
    mid = ((1,), (0,))
    first = ((0,), (0,))
    m_re, m_im = m_ref[0], m_ref[1]
    c_re, c_im = col_ref[0], col_ref[1]
    y_re = (dot(m_re, c_re, mid) - dot(m_im, c_im, mid)).astype(jnp.bfloat16)
    y_im = (dot(m_re, c_im, mid) + dot(m_im, c_re, mid)).astype(jnp.bfloat16)
    r_re, r_im = row_ref[0], row_ref[1]
    x_ref[:, pl.ds(NB, 8), :] = jnp.zeros((2, 8, NB), jnp.float32)
    x_ref[0, pl.ds(0, NB), :] = -(dot(r_re, y_re, first) + dot(r_im, y_im, first))
    x_ref[1, pl.ds(0, NB), :] = dot(r_im, y_re, first) - dot(r_re, y_im, first)
    for d in range(GROUPS * NZ):
        at = pl.ds(27 * d // 4, 8)
        window = jnp.concatenate([x_ref[0, at, :], x_ref[1, at, :]], axis=0)
        out_ref[d] = window.astype(jnp.bfloat16)


def project(m, rows, cols):
    vmem = pl.BlockSpec(memory_space=pltpu.VMEM)
    return pl.pallas_call(
        project_body,
        out_shape=jax.ShapeDtypeStruct((GROUPS * NZ, KEEP, NB), jnp.bfloat16),
        in_specs=[vmem] * 3,
        out_specs=vmem,
        scratch_shapes=[pltpu.VMEM((2, NB + 8, NB), jnp.float32)],
        compiler_params=pltpu.CompilerParams(vmem_limit_bytes=VMEM),
        name="project",
    )(m, rows, cols)


def reduce_windows(windows):
    over_yx = [[g * NZ + z for g in range(GROUPS)] for z in range(NZ)]
    over_z = [[g * NZ + z for z in range(NZ)] for g in range(GROUPS)]
    parts = windows.reshape(GROUPS, NZ, KEEP, NB)
    parts = lax.all_to_all(parts, "band", 0, 0, axis_index_groups=over_yx)
    parts = jnp.sum(parts.astype(jnp.float32), axis=0)
    parts = lax.all_to_all(parts, "band", 0, 0, axis_index_groups=over_z)
    return jnp.sum(parts, axis=0)


def on_device(orbitals, kernels, pair_kdiff, stored_kernel_index):
    group = lax.axis_index("kgrp")
    band = lax.axis_index("band")
    y, x, z = band // (NX * NZ), band // NZ % NX, band % NZ
    odd = group % 2

    own = orbitals[0]
    diff_core = swap_groups(pair_kdiff, 1)
    diff_far = swap_groups(pair_kdiff, 2)
    far = swap_groups(own, 2)

    first = jnp.where(odd == 1, pair_kdiff[0], diff_core[0])
    second = jnp.where(odd == 1, diff_core[0], diff_far[0])
    slots = jnp.stack([stored_kernel_index[first], stored_kernel_index[second]])
    sign_own = jnp.where(odd == 1, -1.0, 1.0).astype(jnp.float32)
    sign = jnp.stack([sign_own, -sign_own])
    dests = jnp.stack([(y + dy) % NY * NX + (x + dx) % NX for dy, dx in OFFSETS])
    sends = pack(slots, dests, kernels)
    kerns = [sends[0]] + [
        shift(block, dy, dx, 0) for block, (dy, dx) in zip(sends[1:], OFFSETS[1:])
    ]

    both = jnp.stack([own, far])
    up, down = both, both
    cols = [both]
    for _ in range(3):
        up, down = shift(up, 0, 0, 1), shift(down, 0, 0, -1)
        cols += [down, up]
    last = jnp.stack([shift(up[0], 0, 0, 1), shift(down[1], 0, 0, -1)])
    cols.append(last)
    pair = jnp.stack([both, shift(both, 0, 1, 0)])
    up, down = shift(pair, 1, 0, 0), shift(pair, -1, 0, 0)
    over = jnp.stack([shift(up[:, 0], 1, 0, 0), shift(down[:, 1], -1, 0, 0)], axis=1)
    rows = [block[i] for block in (pair, up, over, down) for i in range(NX)]

    place = jnp.stack([(z + dz) % NZ for dz in Z_OFFSETS])
    m_out, own_rows, own_cols = mix(place, sign, rows, cols, kerns)
    m_own = swap_groups(m_out, 1)
    total = reduce_windows(project(m_own, own_rows, own_cols))
    flat = total.reshape(2, 8 * NB)
    flat = lax.dynamic_slice(flat, (0, band * 27 % 4 * 108), (2, 27 * 108))
    return flat[None]


def solution(mesh):
    return jax.shard_map(
        on_device,
        mesh=mesh,
        in_specs=(P("kgrp", None, "band", None), P(None, None, "band", None), P("kgrp"), P()),
        out_specs=P("kgrp", None, "band"),
        check_vma=False,
    )
```

```python
import functools

import jax
import jax.numpy as jnp
import numpy as np
from jax import lax
from jax.experimental import pallas as pl
from jax.experimental.pallas import tpu as pltpu
from jax.sharding import PartitionSpec as P

NB = 432
SLAB = 64
NY, NX, NZ = 4, 2, 8
GROUPS = NY * NX
BLOCK = NZ * SLAB
KEEP = 16
VMEM = 56 * 1024 * 1024

OFFSETS = [(dy, dx) for dy in range(NY) for dx in range(NX)]
Z_OFFSETS = [0, 1, -1, 2, -2, 3, -3, 4]


def band_route(dy, dx, dz):
    route = []
    for y in range(NY):
        for x in range(NX):
            for z in range(NZ):
                there = ((y + dy) % NY * NX + (x + dx) % NX) * NZ + (z + dz) % NZ
                route.append(((y * NX + x) * NZ + z, there))
    return route


def shift(block, dy, dx, dz):
    return lax.ppermute(block, "band", band_route(dy, dx, dz))


def swap_groups(block, bit):
    return lax.ppermute(block, "kgrp", [(k, k ^ bit) for k in range(4)])


def dot(a, b, dims):
    return lax.dot_general(a, b, ((dims[0], dims[1]), ((), ())), preferred_element_type=jnp.float32)


def pack_body(slot_ref, dest_ref, kernels_ref, *refs):
    outs, held, sem = refs[:GROUPS], refs[GROUPS], refs[GROUPS + 1]
    copies = [
        pltpu.make_async_copy(kernels_ref.at[slot_ref[which]], held.at[which], sem.at[which])
        for which in range(2)
    ]
    for copy in copies:
        copy.start()
    for which, copy in enumerate(copies):
        copy.wait()
        for i in range(GROUPS):
            start = pl.multiple_of(dest_ref[i] * BLOCK, BLOCK)
            outs[i][which] = held[which, :, :, pl.ds(start, BLOCK)]


def pack(slots, dests, kernels):
    piece = jax.ShapeDtypeStruct((2, 2, SLAB, BLOCK), jnp.bfloat16)
    return pl.pallas_call(
        pack_body,
        out_shape=[piece] * GROUPS,
        in_specs=[
            pl.BlockSpec(memory_space=pltpu.SMEM),
            pl.BlockSpec(memory_space=pltpu.SMEM),
            pl.BlockSpec(memory_space=pl.ANY),
        ],
        out_specs=[pl.BlockSpec(memory_space=pltpu.VMEM)] * GROUPS,
        scratch_shapes=[
            pltpu.VMEM((2, 2, SLAB, GROUPS * BLOCK), jnp.bfloat16),
            pltpu.SemaphoreType.DMA((2,)),
        ],
        compiler_params=pltpu.CompilerParams(vmem_limit_bytes=VMEM),
        name="pack",
    )(slots, dests, kernels)


def mix_body(n_rows, n_cols, place_ref, sign_ref, *refs):
    rows, refs = refs[:n_rows], refs[n_rows:]
    cols, refs = refs[:n_cols], refs[n_cols:]
    kerns, refs = refs[:GROUPS], refs[GROUPS:]
    m_ref, row_ref, col_ref, other_rows, other_cols = refs
    for i in range(GROUPS):
        at = pl.ds(i * SLAB, SLAB)
        row_ref[:, at, :] = rows[i][0]
        other_rows[:, at, :] = rows[i][1]
    for i in range(NZ):
        at = pl.ds(pl.multiple_of(place_ref[i] * SLAB, SLAB), SLAB)
        col_ref[:, at, :] = cols[i][0]
        other_cols[:, at, :] = cols[i][1]
    last = ((1,), (1,))
    per = BLOCK // 2
    for part in range(2):
        at = pl.ds(part * per, per)
        total_re = total_im = None
        for which, (a_ref, b_ref) in enumerate(((row_ref, col_ref), (other_rows, other_cols))):
            a_re, a_im, b_re, b_im = a_ref[0], a_ref[1], b_ref[0, at, :], b_ref[1, at, :]
            p_re = dot(a_re, b_re, last) + dot(a_im, b_im, last)
            p_im = dot(a_im, b_re, last) - dot(a_re, b_im, last)
            k_re = jnp.concatenate([k[which, 0, :, at] for k in kerns], axis=0).astype(jnp.float32)
            k_im = jnp.concatenate([k[which, 1, :, at] for k in kerns], axis=0).astype(jnp.float32)
            k_im = k_im * sign_ref[which]
            m_re = k_re * p_re - k_im * p_im
            m_im = k_re * p_im + k_im * p_re
            total_re = m_re if total_re is None else total_re + m_re
            total_im = m_im if total_im is None else total_im + m_im
        m_ref[0, :, at] = total_re.astype(jnp.bfloat16)
        m_ref[1, :, at] = total_im.astype(jnp.bfloat16)


def mix(place, sign, rows, cols, kerns):
    vmem = pl.BlockSpec(memory_space=pltpu.VMEM)
    smem = pl.BlockSpec(memory_space=pltpu.SMEM)
    points = jax.ShapeDtypeStruct((2, BLOCK, NB), jnp.bfloat16)
    return pl.pallas_call(
        functools.partial(mix_body, len(rows), len(cols)),
        out_shape=[jax.ShapeDtypeStruct((2, BLOCK, BLOCK), jnp.bfloat16), points, points],
        in_specs=[smem, smem] + [vmem] * (len(rows) + len(cols) + len(kerns)),
        out_specs=[vmem] * 3,
        scratch_shapes=[pltpu.VMEM((2, BLOCK, NB), jnp.bfloat16)] * 2,
        compiler_params=pltpu.CompilerParams(vmem_limit_bytes=VMEM),
        name="mix",
    )(place, sign, *rows, *cols, *kerns)


def halves(value):
    high = value.astype(jnp.bfloat16)
    return high, (value - high.astype(jnp.float32)).astype(jnp.bfloat16)


def project_body(m_ref, row_ref, col_ref, out_ref, x_ref):
    mid = ((1,), (0,))
    first = ((0,), (0,))
    m_re, m_im = m_ref[0], m_ref[1]
    c_re, c_im = col_ref[0], col_ref[1]
    y_re = halves(dot(m_re, c_re, mid) - dot(m_im, c_im, mid))
    y_im = halves(dot(m_re, c_im, mid) + dot(m_im, c_re, mid))
    r_re, r_im = row_ref[0], row_ref[1]

    def meet(a, pair):
        return dot(a, pair[0], first) + dot(a, pair[1], first)

    x_ref[:, pl.ds(NB, 8), :] = jnp.zeros((2, 8, NB), jnp.float32)
    x_ref[0, pl.ds(0, NB), :] = -(meet(r_re, y_re) + meet(r_im, y_im))
    x_ref[1, pl.ds(0, NB), :] = meet(r_im, y_re) - meet(r_re, y_im)
    for d in range(GROUPS * NZ):
        at = pl.ds(27 * d // 4, 8)
        window = jnp.concatenate([x_ref[0, at, :], x_ref[1, at, :]], axis=0)
        out_ref[d] = window.astype(jnp.bfloat16)


def project(m, rows, cols):
    vmem = pl.BlockSpec(memory_space=pltpu.VMEM)
    return pl.pallas_call(
        project_body,
        out_shape=jax.ShapeDtypeStruct((GROUPS * NZ, KEEP, NB), jnp.bfloat16),
        in_specs=[vmem] * 3,
        out_specs=vmem,
        scratch_shapes=[pltpu.VMEM((2, NB + 8, NB), jnp.float32)],
        compiler_params=pltpu.CompilerParams(vmem_limit_bytes=VMEM),
        name="project",
    )(m, rows, cols)


def reduce_windows(windows):
    over_yx = [[g * NZ + z for g in range(GROUPS)] for z in range(NZ)]
    over_z = [[g * NZ + z for z in range(NZ)] for g in range(GROUPS)]
    parts = windows.reshape(GROUPS, NZ, KEEP, NB)
    parts = lax.all_to_all(parts, "band", 0, 0, axis_index_groups=over_yx)
    parts = jnp.sum(parts.astype(jnp.float32), axis=0)
    parts = lax.all_to_all(parts, "band", 0, 0, axis_index_groups=over_z)
    return jnp.sum(parts, axis=0)


def on_device(orbitals, kernels, pair_kdiff, stored_kernel_index):
    group = lax.axis_index("kgrp")
    band = lax.axis_index("band")
    y, x, z = band // (NX * NZ), band // NZ % NX, band % NZ
    odd = group % 2

    own = orbitals[0]
    diff_core = swap_groups(pair_kdiff, 1)
    diff_far = swap_groups(pair_kdiff, 2)
    far = swap_groups(own, 2)

    first = jnp.where(odd == 1, pair_kdiff[0], diff_core[0])
    second = jnp.where(odd == 1, diff_core[0], diff_far[0])
    slots = jnp.stack([stored_kernel_index[first], stored_kernel_index[second]])
    sign_own = jnp.where(odd == 1, -1.0, 1.0).astype(jnp.float32)
    sign = jnp.stack([sign_own, -sign_own])
    dests = jnp.stack([(y + dy) % NY * NX + (x + dx) % NX for dy, dx in OFFSETS])
    sends = pack(slots, dests, kernels)
    kerns = [sends[0]] + [
        shift(block, dy, dx, 0) for block, (dy, dx) in zip(sends[1:], OFFSETS[1:])
    ]

    both = jnp.stack([own, far])
    up, down = both, both
    cols = [both]
    for _ in range(3):
        up, down = shift(up, 0, 0, 1), shift(down, 0, 0, -1)
        cols += [down, up]
    last = jnp.stack([shift(up[0], 0, 0, 1), shift(down[1], 0, 0, -1)])
    cols.append(last)
    pair = jnp.stack([both, shift(both, 0, 1, 0)])
    up, down = shift(pair, 1, 0, 0), shift(pair, -1, 0, 0)
    over = jnp.stack([shift(up[:, 0], 1, 0, 0), shift(down[:, 1], -1, 0, 0)], axis=1)
    rows = [block[i] for block in (pair, up, over, down) for i in range(NX)]

    place = jnp.stack([(z + dz) % NZ for dz in Z_OFFSETS])
    m_out, own_rows, own_cols = mix(place, sign, rows, cols, kerns)
    m_own = swap_groups(m_out, 1)
    total = reduce_windows(project(m_own, own_rows, own_cols))
    flat = total.reshape(2, 8 * NB)
    flat = lax.dynamic_slice(flat, (0, band * 27 % 4 * 108), (2, 27 * 108))
    return flat[None]


def solution(mesh):
    return jax.shard_map(
        on_device,
        mesh=mesh,
        in_specs=(P("kgrp", None, "band", None), P(None, None, "band", None), P("kgrp"), P()),
        out_specs=P("kgrp", None, "band"),
        check_vma=False,
    )
```

```python
import functools

import jax
import jax.numpy as jnp
import numpy as np
from jax import lax
from jax.experimental import pallas as pl
from jax.experimental.pallas import tpu as pltpu
from jax.sharding import PartitionSpec as P

NB = 432
SLAB = 64
NY, NX, NZ = 4, 2, 8
GROUPS = NY * NX
BLOCK = NZ * SLAB
WHOLE = 384
LANES = 2 * WHOLE + 128
VMEM = 56 * 1024 * 1024

OFFSETS = [(0, 0), (0, 1), (1, 0), (1, 1), (2, 0), (2, 1), (3, 0), (3, 1)]


def band_route(dy, dx, dz):
    route = []
    for y in range(NY):
        for x in range(NX):
            for z in range(NZ):
                there = ((y + dy) % NY * NX + (x + dx) % NX) * NZ + (z + dz) % NZ
                route.append(((y * NX + x) * NZ + z, there))
    return route


def shift(block, dy, dx, dz):
    return lax.ppermute(block, "band", band_route(dy, dx, dz))


def swap_groups(block, bit):
    return lax.ppermute(block, "kgrp", [(k, k ^ bit) for k in range(4)])


def dot(a, b, dims):
    return lax.dot_general(a, b, ((dims[0], dims[1]), ((), ())), preferred_element_type=jnp.float32)


def pack_body(slot_ref, kernels_ref, *refs):
    outs, held, sem = refs[:2], refs[2], refs[3]
    copies = [
        pltpu.make_async_copy(kernels_ref.at[slot_ref[which]], held.at[which], sem.at[which])
        for which in range(2)
    ]
    for copy in copies:
        copy.start()
    for which, copy in enumerate(copies):
        copy.wait()
        for i in range(GROUPS):
            outs[which][i] = held[which, :, :, pl.ds(i * BLOCK, BLOCK)]


def pack(slots, kernels):
    piece = jax.ShapeDtypeStruct((GROUPS, 2, SLAB, BLOCK), jnp.bfloat16)
    return pl.pallas_call(
        pack_body,
        out_shape=[piece] * 2,
        in_specs=[pl.BlockSpec(memory_space=pltpu.SMEM), pl.BlockSpec(memory_space=pl.ANY)],
        out_specs=[pl.BlockSpec(memory_space=pltpu.VMEM)] * 2,
        scratch_shapes=[
            pltpu.VMEM((2, 2, SLAB, GROUPS * BLOCK), jnp.bfloat16),
            pltpu.SemaphoreType.DMA((2,)),
        ],
        compiler_params=pltpu.CompilerParams(vmem_limit_bytes=VMEM),
        name="pack",
    )(slots, kernels)


def mix_body(place_ref, sign_ref, *refs):
    rows, refs = refs[:GROUPS], refs[GROUPS:]
    gathered_ref, kerns, refs = refs[0], refs[1:3], refs[3:]
    m_ref, row_ref, col_ref, other_rows, other_cols = refs
    for i in range(GROUPS):
        at = pl.ds(pl.multiple_of(place_ref[i] * SLAB, SLAB), SLAB)
        row_ref[:, at, :] = rows[i][0]
        other_rows[:, at, :] = rows[i][1]
    for i in range(NZ):
        at = pl.ds(i * SLAB, SLAB)
        col_ref[:, at, :] = gathered_ref[i, 0]
        other_cols[:, at, :] = gathered_ref[i, 1]
    last = ((1,), (1,))
    per = BLOCK // 2
    for part in range(2):
        at = pl.ds(part * per, per)
        total_re = total_im = None
        for which, (a_ref, b_ref) in enumerate(((row_ref, col_ref), (other_rows, other_cols))):
            a_re, a_im, b_re, b_im = a_ref[0], a_ref[1], b_ref[0, at, :], b_ref[1, at, :]
            p_re = dot(a_re, b_re, last) + dot(a_im, b_im, last)
            p_im = dot(a_im, b_re, last) - dot(a_re, b_im, last)
            k_re = kerns[which][:, 0, :, at].reshape(BLOCK, per).astype(jnp.float32)
            k_im = kerns[which][:, 1, :, at].reshape(BLOCK, per).astype(jnp.float32)
            k_im = k_im * sign_ref[which]
            m_re = k_re * p_re - k_im * p_im
            m_im = k_re * p_im + k_im * p_re
            total_re = m_re if total_re is None else total_re + m_re
            total_im = m_im if total_im is None else total_im + m_im
        m_ref[0, :, at] = total_re.astype(jnp.bfloat16)
        m_ref[1, :, at] = total_im.astype(jnp.bfloat16)


def mix(place, sign, rows, gathered, kerns):
    vmem = pl.BlockSpec(memory_space=pltpu.VMEM)
    smem = pl.BlockSpec(memory_space=pltpu.SMEM)
    points = jax.ShapeDtypeStruct((2, BLOCK, NB), jnp.bfloat16)
    return pl.pallas_call(
        mix_body,
        out_shape=[jax.ShapeDtypeStruct((2, BLOCK, BLOCK), jnp.bfloat16), points, points],
        in_specs=[smem, smem] + [vmem] * (GROUPS + 3),
        out_specs=[vmem] * 3,
        scratch_shapes=[pltpu.VMEM((2, BLOCK, NB), jnp.bfloat16)] * 2,
        compiler_params=pltpu.CompilerParams(vmem_limit_bytes=VMEM),
        name="mix",
    )(place, sign, *rows, gathered, *kerns)


def halves(value):
    high = value.astype(jnp.bfloat16)
    return high, (value - high.astype(jnp.float32)).astype(jnp.bfloat16)


def project_body(m_ref, row_ref, col_ref, out_ref, x_ref):
    mid = ((1,), (0,))
    first = ((0,), (0,))
    m_re, m_im = m_ref[0], m_ref[1]
    c_re, c_im = col_ref[0], col_ref[1]
    y_re = halves(dot(m_re, c_re, mid) - dot(m_im, c_im, mid))
    y_im = halves(dot(m_re, c_im, mid) + dot(m_im, c_re, mid))
    r_re, r_im = row_ref[0], row_ref[1]

    def meet(a, pair):
        return dot(a, pair[0], first) + dot(a, pair[1], first)

    x_re = -(meet(r_re, y_re) + meet(r_im, y_im))
    x_im = meet(r_im, y_re) - meet(r_re, y_im)
    gap = jnp.zeros((NB, 64 - (NB - WHOLE)), jnp.float32)
    x_ref[pl.ds(NB, 8), :] = jnp.zeros((8, LANES), jnp.float32)
    x_ref[pl.ds(0, NB), pl.ds(0, WHOLE)] = x_re[:, :WHOLE]
    x_ref[pl.ds(0, NB), pl.ds(WHOLE, WHOLE)] = x_im[:, :WHOLE]
    x_ref[pl.ds(0, NB), pl.ds(2 * WHOLE, 128)] = jnp.concatenate(
        [x_re[:, WHOLE:], gap, x_im[:, WHOLE:], gap], axis=1
    )
    for d in range(GROUPS * NZ):
        out_ref[d] = x_ref[pl.ds(27 * d // 4, 8), :].astype(jnp.bfloat16)


def project(m, rows, cols):
    vmem = pl.BlockSpec(memory_space=pltpu.VMEM)
    return pl.pallas_call(
        project_body,
        out_shape=jax.ShapeDtypeStruct((GROUPS * NZ, 8, LANES), jnp.bfloat16),
        in_specs=[vmem] * 3,
        out_specs=vmem,
        scratch_shapes=[pltpu.VMEM((NB + 8, LANES), jnp.float32)],
        compiler_params=pltpu.CompilerParams(vmem_limit_bytes=VMEM),
        name="project",
    )(m, rows, cols)


def reduce_windows(windows):
    parts = lax.all_to_all(windows, "band", 0, 0)
    total = jnp.sum(parts.astype(jnp.float32), axis=0)
    tail = 2 * WHOLE
    rest = NB - WHOLE
    real = jnp.concatenate([total[:, :WHOLE], total[:, tail : tail + rest]], axis=1)
    imag = jnp.concatenate([total[:, WHOLE:tail], total[:, tail + 64 : tail + 64 + rest]], axis=1)
    return jnp.stack([real, imag])


def on_device(orbitals, kernels, pair_kdiff, stored_kernel_index):
    group = lax.axis_index("kgrp")
    band = lax.axis_index("band")
    y, x, z = band // (NX * NZ), band // NZ % NX, band % NZ
    odd = group % 2

    own = orbitals[0]
    diff_core = swap_groups(pair_kdiff, 1)
    diff_far = swap_groups(pair_kdiff, 2)
    far = swap_groups(own, 2)

    first = jnp.where(odd == 1, pair_kdiff[0], diff_core[0])
    second = jnp.where(odd == 1, diff_core[0], diff_far[0])
    slots = jnp.stack([stored_kernel_index[first], stored_kernel_index[second]])
    sign_own = jnp.where(odd == 1, -1.0, 1.0).astype(jnp.float32)
    sign = jnp.stack([sign_own, -sign_own])
    over_yx = [[g * NZ + z_at for g in range(GROUPS)] for z_at in range(NZ)]
    over_z = [[g * NZ + z_at for z_at in range(NZ)] for g in range(GROUPS)]
    kerns = [
        lax.all_to_all(block, "band", 0, 0, axis_index_groups=over_yx)
        for block in pack(slots, kernels)
    ]

    both = jnp.stack([own, far])
    gathered = lax.all_gather(both, "band", axis_index_groups=over_z)
    pair = jnp.stack([both, shift(both, 0, 1, 0)])
    up, down = shift(pair, 1, 0, 0), shift(pair, -1, 0, 0)
    over = jnp.stack([shift(up[:, 0], 1, 0, 0), shift(down[:, 1], -1, 0, 0)], axis=1)
    rows = [block[i] for block in (pair, up, over, down) for i in range(NX)]

    place = jnp.stack([(y - dy) % NY * NX + (x - dx) % NX for dy, dx in OFFSETS])
    m_out, own_rows, own_cols = mix(place, sign, rows, gathered, kerns)
    m_own = swap_groups(m_out, 1)
    total = reduce_windows(project(m_own, own_rows, own_cols))
    flat = total.reshape(2, 8 * NB)
    flat = lax.dynamic_slice(flat, (0, band * 27 % 4 * 108), (2, 27 * 108))
    return flat[None]


def solution(mesh):
    return jax.shard_map(
        on_device,
        mesh=mesh,
        in_specs=(P("kgrp", None, "band", None), P(None, None, "band", None), P("kgrp"), P()),
        out_specs=P("kgrp", None, "band"),
        check_vma=False,
    )
```

```python
import functools

import jax
import jax.numpy as jnp
import numpy as np
from jax import lax
from jax.experimental import pallas as pl
from jax.experimental.pallas import tpu as pltpu
from jax.sharding import PartitionSpec as P

NB = 432
SLAB = 64
NY, NX, NZ = 4, 2, 8
GROUPS = NY * NX
BLOCK = NZ * SLAB
WHOLE = 384
LANES = 2 * WHOLE + 128
VMEM = 56 * 1024 * 1024

OFFSETS = [(dy, dx) for dx in range(NX) for dy in range(NY)]


def band_route(dy, dx, dz):
    route = []
    for y in range(NY):
        for x in range(NX):
            for z in range(NZ):
                there = ((y + dy) % NY * NX + (x + dx) % NX) * NZ + (z + dz) % NZ
                route.append(((y * NX + x) * NZ + z, there))
    return route


def shift(block, dy, dx, dz):
    return lax.ppermute(block, "band", band_route(dy, dx, dz))


def swap_groups(block, bit):
    return lax.ppermute(block, "kgrp", [(k, k ^ bit) for k in range(4)])


def other_side(block):
    route = [(i, j) for i, j in band_route(0, 1, 0)]
    both = [((k ^ 2) * 64 + i, k * 64 + j) for k in range(4) for i, j in route]
    return lax.ppermute(block, ("kgrp", "band"), both)


def dot(a, b, dims):
    return lax.dot_general(a, b, ((dims[0], dims[1]), ((), ())), preferred_element_type=jnp.float32)


def pack_body(odd_ref, own_ref, core_ref, far_ref, stored_ref, kernels_ref, out_ref, held, sem):
    odd = odd_ref[0] == 1
    own, core, far = stored_ref[own_ref[0]], stored_ref[core_ref[0]], stored_ref[far_ref[0]]
    shared = jnp.where(odd, own, core)
    single = jnp.where(odd, core, far)
    copies = [
        pltpu.make_async_copy(kernels_ref.at[shared, odd_ref[0]], held.at[0], sem.at[0]),
        pltpu.make_async_copy(kernels_ref.at[single, 0], held.at[1], sem.at[1]),
        pltpu.make_async_copy(kernels_ref.at[single, 1], held.at[2], sem.at[2]),
    ]
    for copy in copies:
        copy.start()
    for which, copy in enumerate(copies):
        copy.wait()
        for i in range(GROUPS):
            out_ref[i, which] = held[which, :, pl.ds(i * BLOCK, BLOCK)]


def pack(odd, own, core, far, stored, kernels):
    smem = pl.BlockSpec(memory_space=pltpu.SMEM)
    return pl.pallas_call(
        pack_body,
        out_shape=jax.ShapeDtypeStruct((GROUPS, 3, SLAB, BLOCK), jnp.bfloat16),
        in_specs=[smem] * 5 + [pl.BlockSpec(memory_space=pl.ANY)],
        out_specs=pl.BlockSpec(memory_space=pltpu.VMEM),
        scratch_shapes=[
            pltpu.VMEM((3, SLAB, GROUPS * BLOCK), jnp.bfloat16),
            pltpu.SemaphoreType.DMA((3,)),
        ],
        compiler_params=pltpu.CompilerParams(vmem_limit_bytes=VMEM),
        name="pack",
    )(odd, own, core, far, stored, kernels)


def mix_body(place_ref, odd_ref, *refs):
    near_ref, own_side, far_side, gathered_ref, kern_ref, half_ref = refs[:6]
    m_ref, row_ref, col_ref, other_rows, other_cols = refs[6:]
    for i in range(NY):
        at = pl.ds(pl.multiple_of(place_ref[i] * SLAB, SLAB), SLAB)
        row_ref[:, at, :] = near_ref[i, 0]
        other_rows[:, at, :] = near_ref[i, 1]
        at = pl.ds(pl.multiple_of(place_ref[NY + i] * SLAB, SLAB), SLAB)
        row_ref[:, at, :] = own_side[i]
        other_rows[:, at, :] = far_side[i]
    for i in range(NZ):
        at = pl.ds(i * SLAB, SLAB)
        col_ref[:, at, :] = gathered_ref[i, 0]
        other_cols[:, at, :] = gathered_ref[i, 1]
    last = ((1,), (1,))
    per = BLOCK // 2
    odd = odd_ref[0] == 1
    sign = jnp.where(odd, -1.0, 1.0).astype(jnp.float32)

    def density(a_ref, b_ref, at):
        a_re, a_im, b_re, b_im = a_ref[0], a_ref[1], b_ref[0, at, :], b_ref[1, at, :]
        p_re = dot(a_re, b_re, last) + dot(a_im, b_im, last)
        p_im = dot(a_im, b_re, last) - dot(a_re, b_im, last)
        return p_re, p_im

    for part in range(2):
        at = pl.ds(part * per, per)
        p_re, p_im = density(row_ref, col_ref, at)
        mine = kern_ref[:, 0, :, at].reshape(BLOCK, per)
        other = half_ref[:, :, at].reshape(BLOCK, per)
        k_re = jnp.where(odd, other, mine).astype(jnp.float32)
        k_im = jnp.where(odd, mine, other).astype(jnp.float32) * sign
        total_re = k_re * p_re - k_im * p_im
        total_im = k_re * p_im + k_im * p_re
        p_re, p_im = density(other_rows, other_cols, at)
        k_re = kern_ref[:, 1, :, at].reshape(BLOCK, per).astype(jnp.float32)
        k_im = kern_ref[:, 2, :, at].reshape(BLOCK, per).astype(jnp.float32) * -sign
        total_re += k_re * p_re - k_im * p_im
        total_im += k_re * p_im + k_im * p_re
        m_ref[0, :, at] = total_re.astype(jnp.bfloat16)
        m_ref[1, :, at] = total_im.astype(jnp.bfloat16)


def mix(place, odd, *arrays):
    vmem = pl.BlockSpec(memory_space=pltpu.VMEM)
    smem = pl.BlockSpec(memory_space=pltpu.SMEM)
    points = jax.ShapeDtypeStruct((2, BLOCK, NB), jnp.bfloat16)
    return pl.pallas_call(
        mix_body,
        out_shape=[jax.ShapeDtypeStruct((2, BLOCK, BLOCK), jnp.bfloat16), points, points],
        in_specs=[smem, smem] + [vmem] * len(arrays),
        out_specs=[vmem] * 3,
        scratch_shapes=[pltpu.VMEM((2, BLOCK, NB), jnp.bfloat16)] * 2,
        compiler_params=pltpu.CompilerParams(vmem_limit_bytes=VMEM),
        name="mix",
    )(place, odd, *arrays)


def halves(value):
    high = value.astype(jnp.bfloat16)
    return high, (value - high.astype(jnp.float32)).astype(jnp.bfloat16)


def project_body(m_ref, row_ref, col_ref, out_ref, x_ref):
    mid = ((1,), (0,))
    first = ((0,), (0,))
    m_re, m_im = m_ref[0], m_ref[1]
    c_re, c_im = col_ref[0], col_ref[1]
    y_re = halves(dot(m_re, c_re, mid) - dot(m_im, c_im, mid))
    y_im = halves(dot(m_re, c_im, mid) + dot(m_im, c_re, mid))
    r_re, r_im = row_ref[0], row_ref[1]

    def meet(a, pair):
        return dot(a, pair[0], first) + dot(a, pair[1], first)

    x_re = -(meet(r_re, y_re) + meet(r_im, y_im))
    x_im = meet(r_im, y_re) - meet(r_re, y_im)
    gap = jnp.zeros((NB, 64 - (NB - WHOLE)), jnp.float32)
    x_ref[pl.ds(NB, 8), :] = jnp.zeros((8, LANES), jnp.float32)
    x_ref[pl.ds(0, NB), pl.ds(0, WHOLE)] = x_re[:, :WHOLE]
    x_ref[pl.ds(0, NB), pl.ds(WHOLE, WHOLE)] = x_im[:, :WHOLE]
    x_ref[pl.ds(0, NB), pl.ds(2 * WHOLE, 128)] = jnp.concatenate(
        [x_re[:, WHOLE:], gap, x_im[:, WHOLE:], gap], axis=1
    )
    for d in range(GROUPS * NZ):
        out_ref[d] = x_ref[pl.ds(27 * d // 4, 8), :].astype(jnp.bfloat16)


def project(m, rows, cols):
    vmem = pl.BlockSpec(memory_space=pltpu.VMEM)
    return pl.pallas_call(
        project_body,
        out_shape=jax.ShapeDtypeStruct((GROUPS * NZ, 8, LANES), jnp.bfloat16),
        in_specs=[vmem] * 3,
        out_specs=vmem,
        scratch_shapes=[pltpu.VMEM((NB + 8, LANES), jnp.float32)],
        compiler_params=pltpu.CompilerParams(vmem_limit_bytes=VMEM),
        name="project",
    )(m, rows, cols)


def reduce_windows(windows):
    parts = lax.all_to_all(windows, "band", 0, 0)
    total = jnp.sum(parts.astype(jnp.float32), axis=0)
    tail = 2 * WHOLE
    rest = NB - WHOLE
    real = jnp.concatenate([total[:, :WHOLE], total[:, tail : tail + rest]], axis=1)
    imag = jnp.concatenate([total[:, WHOLE:tail], total[:, tail + 64 : tail + 64 + rest]], axis=1)
    return jnp.stack([real, imag])


def on_device(orbitals, kernels, pair_kdiff, stored_kernel_index):
    group = lax.axis_index("kgrp")
    band = lax.axis_index("band")
    y, x, z = band // (NX * NZ), band // NZ % NX, band % NZ
    odd = (group % 2).reshape(1)

    own = orbitals[0]
    diff_core = swap_groups(pair_kdiff, 1)
    diff_far = swap_groups(pair_kdiff, 2)
    far = swap_groups(own, 2)

    over_yx = [[g * NZ + z_at for g in range(GROUPS)] for z_at in range(NZ)]
    over_z = [[g * NZ + z_at for z_at in range(NZ)] for g in range(GROUPS)]
    sends = pack(odd, pair_kdiff, diff_core, diff_far, stored_kernel_index, kernels)
    kern = lax.all_to_all(sends, "band", 0, 0, axis_index_groups=over_yx)
    half = swap_groups(kern[:, 0], 1)

    both = jnp.stack([own, far])
    gathered = lax.all_gather(both, "band", axis_index_groups=over_z)
    up, down = shift(both, 1, 0, 0), shift(both, -1, 0, 0)
    over = jnp.stack([shift(up[0], 1, 0, 0), shift(down[1], -1, 0, 0)])
    near = jnp.stack([both, up, over, down])
    own_side = shift(near[:, 0], 0, 1, 0)
    far_side = other_side(near[:, 0])

    place = jnp.stack([(y - dy) % NY * NX + (x - dx) % NX for dy, dx in OFFSETS])
    m_out, own_rows, own_cols = mix(place, odd, near, own_side, far_side, gathered, kern, half)
    m_own = swap_groups(m_out, 1)
    total = reduce_windows(project(m_own, own_rows, own_cols))
    flat = total.reshape(2, 8 * NB)
    flat = lax.dynamic_slice(flat, (0, band * 27 % 4 * 108), (2, 27 * 108))
    return flat[None]


def solution(mesh):
    return jax.shard_map(
        on_device,
        mesh=mesh,
        in_specs=(P("kgrp", None, "band", None), P(None, None, "band", None), P("kgrp"), P()),
        out_specs=P("kgrp", None, "band"),
        check_vma=False,
    )
```

```python
import functools

import jax
import jax.numpy as jnp
import numpy as np
from jax import lax
from jax.experimental import pallas as pl
from jax.experimental.pallas import tpu as pltpu
from jax.sharding import PartitionSpec as P

NB = 432
SLAB = 64
NY, NX, NZ = 4, 2, 8
GROUPS = NY * NX
BLOCK = NZ * SLAB
WHOLE = 384
LANES = 2 * WHOLE + 128
VMEM = 56 * 1024 * 1024

OFFSETS = [(dy, dx) for dx in range(NX) for dy in range(NY)]


def band_route(dy, dx, dz):
    route = []
    for y in range(NY):
        for x in range(NX):
            for z in range(NZ):
                there = ((y + dy) % NY * NX + (x + dx) % NX) * NZ + (z + dz) % NZ
                route.append(((y * NX + x) * NZ + z, there))
    return route


def shift(block, dy, dx, dz):
    return lax.ppermute(block, "band", band_route(dy, dx, dz))


def swap_groups(block, bit):
    return lax.ppermute(block, "kgrp", [(k, k ^ bit) for k in range(4)])


def other_side(block):
    route = [(i, j) for i, j in band_route(0, 1, 0)]
    both = [((k ^ 2) * 64 + i, k * 64 + j) for k in range(4) for i, j in route]
    return lax.ppermute(block, ("kgrp", "band"), both)


def dot(a, b, dims):
    return lax.dot_general(a, b, ((dims[0], dims[1]), ((), ())), preferred_element_type=jnp.float32)


def pack_body(odd_ref, own_ref, core_ref, far_ref, stored_ref, kernels_ref, out_ref, held, sem):
    odd = odd_ref[0] == 1
    own, core, far = stored_ref[own_ref[0]], stored_ref[core_ref[0]], stored_ref[far_ref[0]]
    shared = jnp.where(odd, own, core)
    single = jnp.where(odd, core, far)
    copies = [
        pltpu.make_async_copy(kernels_ref.at[shared, odd_ref[0]], held.at[0], sem.at[0]),
        pltpu.make_async_copy(kernels_ref.at[single, 0], held.at[1], sem.at[1]),
        pltpu.make_async_copy(kernels_ref.at[single, 1], held.at[2], sem.at[2]),
    ]
    for copy in copies:
        copy.start()
    for which, copy in enumerate(copies):
        copy.wait()
        for i in range(GROUPS):
            out_ref[i, which] = held[which, :, pl.ds(i * BLOCK, BLOCK)]


def pack(odd, own, core, far, stored, kernels):
    smem = pl.BlockSpec(memory_space=pltpu.SMEM)
    return pl.pallas_call(
        pack_body,
        out_shape=jax.ShapeDtypeStruct((GROUPS, 3, SLAB, BLOCK), jnp.bfloat16),
        in_specs=[smem] * 5 + [pl.BlockSpec(memory_space=pl.ANY)],
        out_specs=pl.BlockSpec(memory_space=pltpu.VMEM),
        scratch_shapes=[
            pltpu.VMEM((3, SLAB, GROUPS * BLOCK), jnp.bfloat16),
            pltpu.SemaphoreType.DMA((3,)),
        ],
        compiler_params=pltpu.CompilerParams(vmem_limit_bytes=VMEM),
        name="pack",
    )(odd, own, core, far, stored, kernels)


def mix_body(place_ref, odd_ref, *refs):
    near_ref, own_side, far_side, gathered_ref, kern_ref, half_ref = refs[:6]
    m_ref, row_ref, col_ref, other_rows, other_cols = refs[6:]
    for i in range(NY):
        at = pl.ds(pl.multiple_of(place_ref[i] * SLAB, SLAB), SLAB)
        row_ref[:, at, :] = near_ref[i, 0]
        other_rows[:, at, :] = near_ref[i, 1]
        at = pl.ds(pl.multiple_of(place_ref[NY + i] * SLAB, SLAB), SLAB)
        row_ref[:, at, :] = own_side[i]
        other_rows[:, at, :] = far_side[i]
    for i in range(NZ):
        at = pl.ds(i * SLAB, SLAB)
        col_ref[:, at, :] = gathered_ref[i, 0]
        other_cols[:, at, :] = gathered_ref[i, 1]
    last = ((1,), (1,))
    per = BLOCK // 2
    odd = odd_ref[0] == 1
    sign = jnp.where(odd, -1.0, 1.0).astype(jnp.float32)

    def density(a_ref, b_ref, at):
        a_re, a_im, b_re, b_im = a_ref[0], a_ref[1], b_ref[0, at, :], b_ref[1, at, :]
        p_re = dot(a_re, b_re, last) + dot(a_im, b_im, last)
        p_im = dot(a_im, b_re, last) - dot(a_re, b_im, last)
        return p_re, p_im

    for part in range(2):
        at = pl.ds(part * per, per)
        p_re, p_im = density(row_ref, col_ref, at)
        mine = kern_ref[:, 0, :, at].reshape(BLOCK, per)
        other = half_ref[:, :, at].reshape(BLOCK, per)
        k_re = jnp.where(odd, other, mine).astype(jnp.float32)
        k_im = jnp.where(odd, mine, other).astype(jnp.float32) * sign
        total_re = k_re * p_re - k_im * p_im
        total_im = k_re * p_im + k_im * p_re
        p_re, p_im = density(other_rows, other_cols, at)
        k_re = kern_ref[:, 1, :, at].reshape(BLOCK, per).astype(jnp.float32)
        k_im = kern_ref[:, 2, :, at].reshape(BLOCK, per).astype(jnp.float32) * -sign
        total_re += k_re * p_re - k_im * p_im
        total_im += k_re * p_im + k_im * p_re
        m_ref[0, :, at] = total_re.astype(jnp.bfloat16)
        m_ref[1, :, at] = total_im.astype(jnp.bfloat16)


def mix(place, odd, *arrays):
    vmem = pl.BlockSpec(memory_space=pltpu.VMEM)
    smem = pl.BlockSpec(memory_space=pltpu.SMEM)
    points = jax.ShapeDtypeStruct((2, BLOCK, NB), jnp.bfloat16)
    return pl.pallas_call(
        mix_body,
        out_shape=[jax.ShapeDtypeStruct((2, BLOCK, BLOCK), jnp.bfloat16), points, points],
        in_specs=[smem, smem] + [vmem] * len(arrays),
        out_specs=[vmem] * 3,
        scratch_shapes=[pltpu.VMEM((2, BLOCK, NB), jnp.bfloat16)] * 2,
        compiler_params=pltpu.CompilerParams(vmem_limit_bytes=VMEM),
        name="mix",
    )(place, odd, *arrays)


def halves(value):
    high = value.astype(jnp.bfloat16)
    return high, (value - high.astype(jnp.float32)).astype(jnp.bfloat16)


def project_body(m_ref, row_ref, col_ref, out_ref, x_ref):
    mid = ((1,), (0,))
    first = ((0,), (0,))
    m_re, m_im = m_ref[0], m_ref[1]
    c_re, c_im = col_ref[0], col_ref[1]
    y_re = halves(dot(m_re, c_re, mid) - dot(m_im, c_im, mid))
    y_im = halves(dot(m_re, c_im, mid) + dot(m_im, c_re, mid))
    r_re, r_im = row_ref[0], row_ref[1]

    def meet(a, pair):
        return dot(a, pair[0], first) + dot(a, pair[1], first)

    x_re = -(meet(r_re, y_re) + meet(r_im, y_im))
    x_im = meet(r_im, y_re) - meet(r_re, y_im)
    gap = jnp.zeros((NB, 64 - (NB - WHOLE)), jnp.float32)
    x_ref[pl.ds(NB, 8), :] = jnp.zeros((8, LANES), jnp.float32)
    x_ref[pl.ds(0, NB), pl.ds(0, WHOLE)] = x_re[:, :WHOLE]
    x_ref[pl.ds(0, NB), pl.ds(WHOLE, WHOLE)] = x_im[:, :WHOLE]
    x_ref[pl.ds(0, NB), pl.ds(2 * WHOLE, 128)] = jnp.concatenate(
        [x_re[:, WHOLE:], gap, x_im[:, WHOLE:], gap], axis=1
    )
    for d in range(GROUPS * NZ):
        out_ref[d] = x_ref[pl.ds(27 * d // 4, 8), :].astype(jnp.bfloat16)


def project(m, rows, cols):
    vmem = pl.BlockSpec(memory_space=pltpu.VMEM)
    return pl.pallas_call(
        project_body,
        out_shape=jax.ShapeDtypeStruct((GROUPS * NZ, 8, LANES), jnp.bfloat16),
        in_specs=[vmem] * 3,
        out_specs=vmem,
        scratch_shapes=[pltpu.VMEM((NB + 8, LANES), jnp.float32)],
        compiler_params=pltpu.CompilerParams(vmem_limit_bytes=VMEM),
        name="project",
    )(m, rows, cols)


def reduce_windows(windows):
    parts = lax.all_to_all(windows, "band", 0, 0)
    total = jnp.sum(parts.astype(jnp.float32), axis=0)
    tail = 2 * WHOLE
    rest = NB - WHOLE
    real = jnp.concatenate([total[:, :WHOLE], total[:, tail : tail + rest]], axis=1)
    imag = jnp.concatenate([total[:, WHOLE:tail], total[:, tail + 64 : tail + 64 + rest]], axis=1)
    return jnp.stack([real, imag])


def on_device(orbitals, kernels, pair_kdiff, stored_kernel_index):
    group = lax.axis_index("kgrp")
    band = lax.axis_index("band")
    y, x, z = band // (NX * NZ), band // NZ % NX, band % NZ
    odd = (group % 2).reshape(1)

    own = orbitals[0]
    diff_core = swap_groups(pair_kdiff, 1)
    diff_far = swap_groups(pair_kdiff, 2)
    far = swap_groups(own, 2)

    over_yx = [[g * NZ + z_at for g in range(GROUPS)] for z_at in range(NZ)]
    over_z = [[g * NZ + z_at for z_at in range(NZ)] for g in range(GROUPS)]
    sends = pack(odd, pair_kdiff, diff_core, diff_far, stored_kernel_index, kernels)
    both = jnp.stack([own, far])
    gathered = lax.all_gather(both, "band", axis_index_groups=over_z)
    up, down = shift(both, 1, 0, 0), shift(both, -1, 0, 0)
    sends, up, down = lax.optimization_barrier((sends, up, down))
    kern = lax.all_to_all(sends, "band", 0, 0, axis_index_groups=over_yx)
    half = swap_groups(kern[:, 0], 1)
    over = shift(down, -1, 0, 0)
    near = jnp.stack([both, up, over, down])
    own_side = shift(near[:, 0], 0, 1, 0)
    far_side = other_side(near[:, 0])

    place = jnp.stack([(y - dy) % NY * NX + (x - dx) % NX for dy, dx in OFFSETS])
    m_out, own_rows, own_cols = mix(place, odd, near, own_side, far_side, gathered, kern, half)
    m_own = swap_groups(m_out, 1)
    total = reduce_windows(project(m_own, own_rows, own_cols))
    flat = total.reshape(2, 8 * NB)
    flat = lax.dynamic_slice(flat, (0, band * 27 % 4 * 108), (2, 27 * 108))
    return flat[None]


def solution(mesh):
    return jax.shard_map(
        on_device,
        mesh=mesh,
        in_specs=(P("kgrp", None, "band", None), P(None, None, "band", None), P("kgrp"), P()),
        out_specs=P("kgrp", None, "band"),
        check_vma=False,
    )
```

```python
import functools

import jax
import jax.numpy as jnp
import numpy as np
from jax import lax
from jax.experimental import pallas as pl
from jax.experimental.pallas import tpu as pltpu
from jax.sharding import PartitionSpec as P

NB = 432
SLAB = 64
NY, NX, NZ = 4, 2, 8
GROUPS = NY * NX
BLOCK = NZ * SLAB
WHOLE = 384
LANES = 2 * WHOLE + 128
VMEM = 56 * 1024 * 1024

OFFSETS = [(dy, dx) for dx in range(NX) for dy in range(NY)]


def band_route(dy, dx, dz):
    route = []
    for y in range(NY):
        for x in range(NX):
            for z in range(NZ):
                there = ((y + dy) % NY * NX + (x + dx) % NX) * NZ + (z + dz) % NZ
                route.append(((y * NX + x) * NZ + z, there))
    return route


def shift(block, dy, dx, dz):
    return lax.ppermute(block, "band", band_route(dy, dx, dz))


def swap_groups(block, bit):
    return lax.ppermute(block, "kgrp", [(k, k ^ bit) for k in range(4)])


def other_side(block):
    route = [(i, j) for i, j in band_route(0, 1, 0)]
    both = [((k ^ 2) * 64 + i, k * 64 + j) for k in range(4) for i, j in route]
    return lax.ppermute(block, ("kgrp", "band"), both)


def dot(a, b, dims):
    return lax.dot_general(a, b, ((dims[0], dims[1]), ((), ())), preferred_element_type=jnp.float32)


def pack_body(odd_ref, own_ref, core_ref, far_ref, stored_ref, kernels_ref, out_ref, held, sem):
    odd = odd_ref[0] == 1
    own, core, far = stored_ref[own_ref[0]], stored_ref[core_ref[0]], stored_ref[far_ref[0]]
    shared = jnp.where(odd, own, core)
    single = jnp.where(odd, core, far)
    copies = [
        pltpu.make_async_copy(kernels_ref.at[shared, odd_ref[0]], held.at[0], sem.at[0]),
        pltpu.make_async_copy(kernels_ref.at[single, 0], held.at[1], sem.at[1]),
        pltpu.make_async_copy(kernels_ref.at[single, 1], held.at[2], sem.at[2]),
    ]
    for copy in copies:
        copy.start()
    for which, copy in enumerate(copies):
        copy.wait()
        for i in range(GROUPS):
            out_ref[i, which] = held[which, :, pl.ds(i * BLOCK, BLOCK)]


def pack(odd, own, core, far, stored, kernels):
    smem = pl.BlockSpec(memory_space=pltpu.SMEM)
    return pl.pallas_call(
        pack_body,
        out_shape=jax.ShapeDtypeStruct((GROUPS, 3, SLAB, BLOCK), jnp.bfloat16),
        in_specs=[smem] * 5 + [pl.BlockSpec(memory_space=pl.ANY)],
        out_specs=pl.BlockSpec(memory_space=pltpu.VMEM),
        scratch_shapes=[
            pltpu.VMEM((3, SLAB, GROUPS * BLOCK), jnp.bfloat16),
            pltpu.SemaphoreType.DMA((3,)),
        ],
        compiler_params=pltpu.CompilerParams(vmem_limit_bytes=VMEM),
        name="pack",
    )(odd, own, core, far, stored, kernels)


def mix_body(place_ref, odd_ref, *refs):
    near_ref, own_side, far_side, gathered_ref, kern_ref, half_ref = refs[:6]
    m_ref, row_ref, col_ref, other_rows, other_cols = refs[6:]
    for i in range(NY):
        at = pl.ds(pl.multiple_of(place_ref[i] * SLAB, SLAB), SLAB)
        row_ref[:, at, :] = near_ref[i, 0]
        other_rows[:, at, :] = near_ref[i, 1]
        at = pl.ds(pl.multiple_of(place_ref[NY + i] * SLAB, SLAB), SLAB)
        row_ref[:, at, :] = own_side[i]
        other_rows[:, at, :] = far_side[i]
    for i in range(NZ):
        at = pl.ds(i * SLAB, SLAB)
        col_ref[:, at, :] = gathered_ref[i, 0]
        other_cols[:, at, :] = gathered_ref[i, 1]
    last = ((1,), (1,))
    per = BLOCK // 2
    odd = odd_ref[0] == 1
    sign = jnp.where(odd, -1.0, 1.0).astype(jnp.float32)

    def density(a_ref, b_ref, at):
        a_re, a_im, b_re, b_im = a_ref[0], a_ref[1], b_ref[0, at, :], b_ref[1, at, :]
        p_re = dot(a_re, b_re, last) + dot(a_im, b_im, last)
        p_im = dot(a_im, b_re, last) - dot(a_re, b_im, last)
        return p_re, p_im

    for part in range(2):
        at = pl.ds(part * per, per)
        p_re, p_im = density(row_ref, col_ref, at)
        mine = kern_ref[:, 0, :, at].reshape(BLOCK, per)
        other = half_ref[:, :, at].reshape(BLOCK, per)
        k_re = jnp.where(odd, other, mine).astype(jnp.float32)
        k_im = jnp.where(odd, mine, other).astype(jnp.float32) * sign
        total_re = k_re * p_re - k_im * p_im
        total_im = k_re * p_im + k_im * p_re
        p_re, p_im = density(other_rows, other_cols, at)
        k_re = kern_ref[:, 1, :, at].reshape(BLOCK, per).astype(jnp.float32)
        k_im = kern_ref[:, 2, :, at].reshape(BLOCK, per).astype(jnp.float32) * -sign
        total_re += k_re * p_re - k_im * p_im
        total_im += k_re * p_im + k_im * p_re
        m_ref[0, :, at] = total_re.astype(jnp.bfloat16)
        m_ref[1, :, at] = total_im.astype(jnp.bfloat16)


def mix(place, odd, *arrays):
    vmem = pl.BlockSpec(memory_space=pltpu.VMEM)
    smem = pl.BlockSpec(memory_space=pltpu.SMEM)
    points = jax.ShapeDtypeStruct((2, BLOCK, NB), jnp.bfloat16)
    return pl.pallas_call(
        mix_body,
        out_shape=[jax.ShapeDtypeStruct((2, BLOCK, BLOCK), jnp.bfloat16), points, points],
        in_specs=[smem, smem] + [vmem] * len(arrays),
        out_specs=[vmem] * 3,
        scratch_shapes=[pltpu.VMEM((2, BLOCK, NB), jnp.bfloat16)] * 2,
        compiler_params=pltpu.CompilerParams(vmem_limit_bytes=VMEM),
        name="mix",
    )(place, odd, *arrays)


def halves(value):
    high = value.astype(jnp.bfloat16)
    return high, (value - high.astype(jnp.float32)).astype(jnp.bfloat16)


def project_body(m_ref, row_ref, col_ref, out_ref, x_ref):
    mid = ((1,), (0,))
    first = ((0,), (0,))
    m_re, m_im = m_ref[0], m_ref[1]
    c_re, c_im = col_ref[0], col_ref[1]
    y_re = halves(dot(m_re, c_re, mid) - dot(m_im, c_im, mid))
    y_im = halves(dot(m_re, c_im, mid) + dot(m_im, c_re, mid))
    r_re, r_im = row_ref[0], row_ref[1]

    def meet(a, pair):
        return dot(a, pair[0], first) + dot(a, pair[1], first)

    x_re = -(meet(r_re, y_re) + meet(r_im, y_im))
    x_im = meet(r_im, y_re) - meet(r_re, y_im)
    gap = jnp.zeros((NB, 64 - (NB - WHOLE)), jnp.float32)
    x_ref[pl.ds(NB, 8), :] = jnp.zeros((8, LANES), jnp.float32)
    x_ref[pl.ds(0, NB), pl.ds(0, WHOLE)] = x_re[:, :WHOLE]
    x_ref[pl.ds(0, NB), pl.ds(WHOLE, WHOLE)] = x_im[:, :WHOLE]
    x_ref[pl.ds(0, NB), pl.ds(2 * WHOLE, 128)] = jnp.concatenate(
        [x_re[:, WHOLE:], gap, x_im[:, WHOLE:], gap], axis=1
    )
    for d in range(GROUPS * NZ):
        out_ref[d] = x_ref[pl.ds(27 * d // 4, 8), :].astype(jnp.bfloat16)


def project(m, rows, cols):
    vmem = pl.BlockSpec(memory_space=pltpu.VMEM)
    return pl.pallas_call(
        project_body,
        out_shape=jax.ShapeDtypeStruct((GROUPS * NZ, 8, LANES), jnp.bfloat16),
        in_specs=[vmem] * 3,
        out_specs=vmem,
        scratch_shapes=[pltpu.VMEM((NB + 8, LANES), jnp.float32)],
        compiler_params=pltpu.CompilerParams(vmem_limit_bytes=VMEM),
        name="project",
    )(m, rows, cols)


def reduce_windows(windows):
    parts = lax.all_to_all(windows, "band", 0, 0)
    total = jnp.sum(parts.astype(jnp.float32), axis=0)
    tail = 2 * WHOLE
    rest = NB - WHOLE
    real = jnp.concatenate([total[:, :WHOLE], total[:, tail : tail + rest]], axis=1)
    imag = jnp.concatenate([total[:, WHOLE:tail], total[:, tail + 64 : tail + 64 + rest]], axis=1)
    return jnp.stack([real, imag])


def on_device(orbitals, kernels, pair_kdiff, stored_kernel_index):
    group = lax.axis_index("kgrp")
    band = lax.axis_index("band")
    y, x, z = band // (NX * NZ), band // NZ % NX, band % NZ
    odd = (group % 2).reshape(1)

    own = orbitals[0]
    diff_core = swap_groups(pair_kdiff, 1)
    diff_far = swap_groups(pair_kdiff, 2)
    far = swap_groups(own, 2)

    over_yx = [[g * NZ + z_at for g in range(GROUPS)] for z_at in range(NZ)]
    over_z = [[g * NZ + z_at for z_at in range(NZ)] for g in range(GROUPS)]
    sends = pack(odd, pair_kdiff, diff_core, diff_far, stored_kernel_index, kernels)
    both = jnp.stack([own, far])
    gathered = lax.all_gather(both, "band", axis_index_groups=over_z)
    up, down = shift(both, 1, 0, 0), shift(both, -1, 0, 0)
    sends, up, down = lax.optimization_barrier((sends, up, down))
    kern = lax.all_to_all(sends, "band", 0, 0, axis_index_groups=over_yx)
    half = swap_groups(kern[:, 0], 1)
    over = shift(up, 1, 0, 0)
    near = jnp.stack([both, up, over, down])
    own_side = shift(near[:, 0], 0, 1, 0)
    far_side = other_side(near[:, 0])

    place = jnp.stack([(y - dy) % NY * NX + (x - dx) % NX for dy, dx in OFFSETS])
    m_out, own_rows, own_cols = mix(place, odd, near, own_side, far_side, gathered, kern, half)
    m_own = swap_groups(m_out, 1)
    total = reduce_windows(project(m_own, own_rows, own_cols))
    flat = total.reshape(2, 8 * NB)
    flat = lax.dynamic_slice(flat, (0, band * 27 % 4 * 108), (2, 27 * 108))
    return flat[None]


def solution(mesh):
    return jax.shard_map(
        on_device,
        mesh=mesh,
        in_specs=(P("kgrp", None, "band", None), P(None, None, "band", None), P("kgrp"), P()),
        out_specs=P("kgrp", None, "band"),
        check_vma=False,
    )
```

```python
import functools

import jax
import jax.numpy as jnp
import numpy as np
from jax import lax
from jax.experimental import pallas as pl
from jax.experimental.pallas import tpu as pltpu
from jax.sharding import PartitionSpec as P

NB = 432
SLAB = 64
NY, NX, NZ = 4, 2, 8
GROUPS = NY * NX
BLOCK = NZ * SLAB
WHOLE = 384
LANES = 2 * WHOLE + 128
VMEM = 56 * 1024 * 1024

OFFSETS = [(dy, dx) for dx in range(NX) for dy in range(NY)]


def band_route(dy, dx, dz):
    route = []
    for y in range(NY):
        for x in range(NX):
            for z in range(NZ):
                there = ((y + dy) % NY * NX + (x + dx) % NX) * NZ + (z + dz) % NZ
                route.append(((y * NX + x) * NZ + z, there))
    return route


def shift(block, dy, dx, dz):
    return lax.ppermute(block, "band", band_route(dy, dx, dz))


def swap_groups(block, bit):
    return lax.ppermute(block, "kgrp", [(k, k ^ bit) for k in range(4)])


def other_side(block):
    route = [(i, j) for i, j in band_route(0, 1, 0)]
    both = [((k ^ 2) * 64 + i, k * 64 + j) for k in range(4) for i, j in route]
    return lax.ppermute(block, ("kgrp", "band"), both)


def dot(a, b, dims):
    return lax.dot_general(a, b, ((dims[0], dims[1]), ((), ())), preferred_element_type=jnp.float32)


def pack_body(odd_ref, own_ref, core_ref, far_ref, stored_ref, dest_ref, kernels_ref, *refs):
    outs, held, sem = refs[:GROUPS], refs[GROUPS], refs[GROUPS + 1]
    odd = odd_ref[0] == 1
    own, core, far = stored_ref[own_ref[0]], stored_ref[core_ref[0]], stored_ref[far_ref[0]]
    shared = jnp.where(odd, own, core)
    single = jnp.where(odd, core, far)
    copies = [
        pltpu.make_async_copy(kernels_ref.at[shared, odd_ref[0]], held.at[0], sem.at[0]),
        pltpu.make_async_copy(kernels_ref.at[single, 0], held.at[1], sem.at[1]),
        pltpu.make_async_copy(kernels_ref.at[single, 1], held.at[2], sem.at[2]),
    ]
    for copy in copies:
        copy.start()
    for which, copy in enumerate(copies):
        copy.wait()
        for i in range(GROUPS):
            start = pl.multiple_of(dest_ref[i] * BLOCK, BLOCK)
            outs[i][which] = held[which, :, pl.ds(start, BLOCK)]


def pack(odd, own, core, far, stored, dests, kernels):
    smem = pl.BlockSpec(memory_space=pltpu.SMEM)
    return pl.pallas_call(
        pack_body,
        out_shape=[jax.ShapeDtypeStruct((3, SLAB, BLOCK), jnp.bfloat16)] * GROUPS,
        in_specs=[smem] * 6 + [pl.BlockSpec(memory_space=pl.ANY)],
        out_specs=[pl.BlockSpec(memory_space=pltpu.VMEM)] * GROUPS,
        scratch_shapes=[
            pltpu.VMEM((3, SLAB, GROUPS * BLOCK), jnp.bfloat16),
            pltpu.SemaphoreType.DMA((3,)),
        ],
        compiler_params=pltpu.CompilerParams(vmem_limit_bytes=VMEM),
        name="pack",
    )(odd, own, core, far, stored, dests, kernels)


def mix_body(place_ref, odd_ref, *refs):
    near, (own_side, far_side, gathered_ref, half_ref) = refs[:NY], refs[NY : NY + 4]
    kerns, refs = refs[NY + 4 : NY + 4 + GROUPS], refs[NY + 4 + GROUPS :]
    m_ref, row_ref, col_ref, other_rows, other_cols, kern_ref = refs

    def rows_of(i):
        return pl.ds(pl.multiple_of(place_ref[i] * SLAB, SLAB), SLAB)

    for i in range(NY):
        row_ref[:, rows_of(i), :] = near[i][0]
        other_rows[:, rows_of(i), :] = near[i][1]
        row_ref[:, rows_of(NY + i), :] = own_side[i]
        other_rows[:, rows_of(NY + i), :] = far_side[i]
    for i in range(GROUPS):
        kern_ref[:3, rows_of(i), :] = kerns[i][...]
        kern_ref[3, rows_of(i), :] = half_ref[i]
    for i in range(NZ):
        at = pl.ds(i * SLAB, SLAB)
        col_ref[:, at, :] = gathered_ref[i, 0]
        other_cols[:, at, :] = gathered_ref[i, 1]
    last = ((1,), (1,))
    per = BLOCK // 2
    odd = odd_ref[0] == 1
    sign = jnp.where(odd, -1.0, 1.0).astype(jnp.float32)

    def density(a_ref, b_ref, at):
        a_re, a_im, b_re, b_im = a_ref[0], a_ref[1], b_ref[0, at, :], b_ref[1, at, :]
        p_re = dot(a_re, b_re, last) + dot(a_im, b_im, last)
        p_im = dot(a_im, b_re, last) - dot(a_re, b_im, last)
        return p_re, p_im

    for part in range(2):
        at = pl.ds(part * per, per)
        p_re, p_im = density(row_ref, col_ref, at)
        mine, other = kern_ref[0, :, at], kern_ref[3, :, at]
        k_re = jnp.where(odd, other, mine).astype(jnp.float32)
        k_im = jnp.where(odd, mine, other).astype(jnp.float32) * sign
        total_re = k_re * p_re - k_im * p_im
        total_im = k_re * p_im + k_im * p_re
        p_re, p_im = density(other_rows, other_cols, at)
        k_re = kern_ref[1, :, at].astype(jnp.float32)
        k_im = kern_ref[2, :, at].astype(jnp.float32) * -sign
        total_re += k_re * p_re - k_im * p_im
        total_im += k_re * p_im + k_im * p_re
        m_ref[0, :, at] = total_re.astype(jnp.bfloat16)
        m_ref[1, :, at] = total_im.astype(jnp.bfloat16)


def mix(place, odd, *arrays):
    vmem = pl.BlockSpec(memory_space=pltpu.VMEM)
    smem = pl.BlockSpec(memory_space=pltpu.SMEM)
    points = jax.ShapeDtypeStruct((2, BLOCK, NB), jnp.bfloat16)
    return pl.pallas_call(
        mix_body,
        out_shape=[jax.ShapeDtypeStruct((2, BLOCK, BLOCK), jnp.bfloat16), points, points],
        in_specs=[smem, smem] + [vmem] * len(arrays),
        out_specs=[vmem] * 3,
        scratch_shapes=[pltpu.VMEM((2, BLOCK, NB), jnp.bfloat16)] * 2
        + [pltpu.VMEM((4, BLOCK, BLOCK), jnp.bfloat16)],
        compiler_params=pltpu.CompilerParams(vmem_limit_bytes=VMEM),
        name="mix",
    )(place, odd, *arrays)


def halves(value):
    high = value.astype(jnp.bfloat16)
    return high, (value - high.astype(jnp.float32)).astype(jnp.bfloat16)


def project_body(m_ref, row_ref, col_ref, out_ref, x_ref):
    mid = ((1,), (0,))
    first = ((0,), (0,))
    m_re, m_im = m_ref[0], m_ref[1]
    c_re, c_im = col_ref[0], col_ref[1]
    y_re = halves(dot(m_re, c_re, mid) - dot(m_im, c_im, mid))
    y_im = halves(dot(m_re, c_im, mid) + dot(m_im, c_re, mid))
    r_re, r_im = row_ref[0], row_ref[1]

    def meet(a, pair):
        return dot(a, pair[0], first) + dot(a, pair[1], first)

    x_re = -(meet(r_re, y_re) + meet(r_im, y_im))
    x_im = meet(r_im, y_re) - meet(r_re, y_im)
    gap = jnp.zeros((NB, 64 - (NB - WHOLE)), jnp.float32)
    x_ref[pl.ds(NB, 8), :] = jnp.zeros((8, LANES), jnp.float32)
    x_ref[pl.ds(0, NB), pl.ds(0, WHOLE)] = x_re[:, :WHOLE]
    x_ref[pl.ds(0, NB), pl.ds(WHOLE, WHOLE)] = x_im[:, :WHOLE]
    x_ref[pl.ds(0, NB), pl.ds(2 * WHOLE, 128)] = jnp.concatenate(
        [x_re[:, WHOLE:], gap, x_im[:, WHOLE:], gap], axis=1
    )
    for d in range(GROUPS * NZ):
        out_ref[d] = x_ref[pl.ds(27 * d // 4, 8), :].astype(jnp.bfloat16)


def project(m, rows, cols):
    vmem = pl.BlockSpec(memory_space=pltpu.VMEM)
    return pl.pallas_call(
        project_body,
        out_shape=jax.ShapeDtypeStruct((GROUPS * NZ, 8, LANES), jnp.bfloat16),
        in_specs=[vmem] * 3,
        out_specs=vmem,
        scratch_shapes=[pltpu.VMEM((NB + 8, LANES), jnp.float32)],
        compiler_params=pltpu.CompilerParams(vmem_limit_bytes=VMEM),
        name="project",
    )(m, rows, cols)


def reduce_windows(windows):
    parts = lax.all_to_all(windows, "band", 0, 0)
    total = jnp.sum(parts.astype(jnp.float32), axis=0)
    tail = 2 * WHOLE
    rest = NB - WHOLE
    real = jnp.concatenate([total[:, :WHOLE], total[:, tail : tail + rest]], axis=1)
    imag = jnp.concatenate([total[:, WHOLE:tail], total[:, tail + 64 : tail + 64 + rest]], axis=1)
    return jnp.stack([real, imag])


def on_device(orbitals, kernels, pair_kdiff, stored_kernel_index):
    group = lax.axis_index("kgrp")
    band = lax.axis_index("band")
    y, x, z = band // (NX * NZ), band // NZ % NX, band % NZ
    odd = (group % 2).reshape(1)

    own = orbitals[0]
    diff_core = swap_groups(pair_kdiff, 1)
    diff_far = swap_groups(pair_kdiff, 2)
    far = swap_groups(own, 2)

    over_z = [[g * NZ + z_at for z_at in range(NZ)] for g in range(GROUPS)]
    dests = jnp.stack([(y + dy) % NY * NX + (x + dx) % NX for dy, dx in OFFSETS])
    sends = pack(odd, pair_kdiff, diff_core, diff_far, stored_kernel_index, dests, kernels)

    both = jnp.stack([own, far])
    gathered = lax.all_gather(both, "band", axis_index_groups=over_z)
    up, down = shift(both, 1, 0, 0), shift(both, -1, 0, 0)
    sends, up, down = lax.optimization_barrier((sends, up, down))
    over = shift(up, 1, 0, 0)
    kerns = {(0, 0): sends[0]}
    send_of = dict(zip(OFFSETS, sends))
    for offset in ((2, 0), (2, 1), (1, 0), (3, 0)):
        kerns[offset] = shift(send_of[offset], *offset, 0)
    later = ((1, 1), (3, 1), (0, 1))
    held, over = lax.optimization_barrier(([send_of[offset] for offset in later], over))
    near = [both, up, over, down]
    owns = jnp.stack([block[0] for block in near])
    own_side, far_side = shift(owns, 0, 1, 0), other_side(owns)
    for offset, block in zip(later, held):
        kerns[offset] = shift(block, *offset, 0)
    kerns = [kerns[offset] for offset in OFFSETS]
    half = swap_groups(jnp.stack([block[0] for block in kerns]), 1)

    place = jnp.stack([(y - dy) % NY * NX + (x - dx) % NX for dy, dx in OFFSETS])
    m_out, own_rows, own_cols = mix(
        place, odd, *near, own_side, far_side, gathered, half, *kerns
    )
    m_own = swap_groups(m_out, 1)
    total = reduce_windows(project(m_own, own_rows, own_cols))
    flat = total.reshape(2, 8 * NB)
    flat = lax.dynamic_slice(flat, (0, band * 27 % 4 * 108), (2, 27 * 108))
    return flat[None]


def solution(mesh):
    return jax.shard_map(
        on_device,
        mesh=mesh,
        in_specs=(P("kgrp", None, "band", None), P(None, None, "band", None), P("kgrp"), P()),
        out_specs=P("kgrp", None, "band"),
        check_vma=False,
    )
```

```python
import functools

import jax
import jax.numpy as jnp
import numpy as np
from jax import lax
from jax.experimental import pallas as pl
from jax.experimental.pallas import tpu as pltpu
from jax.sharding import PartitionSpec as P

NB = 432
SLAB = 64
NY, NX, NZ = 4, 2, 8
GROUPS = NY * NX
BLOCK = NZ * SLAB
WHOLE = 384
LANES = 2 * WHOLE + 128
VMEM = 56 * 1024 * 1024


def band_route(dy, dx, dz):
    route = []
    for y in range(NY):
        for x in range(NX):
            for z in range(NZ):
                there = ((y + dy) % NY * NX + (x + dx) % NX) * NZ + (z + dz) % NZ
                route.append(((y * NX + x) * NZ + z, there))
    return route


def shift(block, dy, dx, dz):
    return lax.ppermute(block, "band", band_route(dy, dx, dz))


def swap_groups(block, bit):
    return lax.ppermute(block, "kgrp", [(k, k ^ bit) for k in range(4)])


def other_side(block):
    route = [(i, j) for i, j in band_route(0, 1, 0)]
    both = [((k ^ 2) * 64 + i, k * 64 + j) for k in range(4) for i, j in route]
    return lax.ppermute(block, ("kgrp", "band"), both)


def dot(a, b, dims):
    return lax.dot_general(a, b, ((dims[0], dims[1]), ((), ())), preferred_element_type=jnp.float32)


def pack_body(odd_ref, own_ref, core_ref, far_ref, stored_ref, kernels_ref, out_ref, held, sem):
    odd = odd_ref[0] == 1
    own, core, far = stored_ref[own_ref[0]], stored_ref[core_ref[0]], stored_ref[far_ref[0]]
    shared = jnp.where(odd, own, core)
    single = jnp.where(odd, core, far)
    copies = [
        pltpu.make_async_copy(kernels_ref.at[shared, odd_ref[0]], held.at[0], sem.at[0]),
        pltpu.make_async_copy(kernels_ref.at[single, 0], held.at[1], sem.at[1]),
        pltpu.make_async_copy(kernels_ref.at[single, 1], held.at[2], sem.at[2]),
    ]
    for copy in copies:
        copy.start()
    for which, copy in enumerate(copies):
        copy.wait()
        for i in range(GROUPS):
            out_ref[i, which] = held[which, :, pl.ds(i * BLOCK, BLOCK)]


def pack(odd, own, core, far, stored, kernels):
    smem = pl.BlockSpec(memory_space=pltpu.SMEM)
    return pl.pallas_call(
        pack_body,
        out_shape=jax.ShapeDtypeStruct((GROUPS, 3, SLAB, BLOCK), jnp.bfloat16),
        in_specs=[smem] * 5 + [pl.BlockSpec(memory_space=pl.ANY)],
        out_specs=pl.BlockSpec(memory_space=pltpu.VMEM),
        scratch_shapes=[
            pltpu.VMEM((3, SLAB, GROUPS * BLOCK), jnp.bfloat16),
            pltpu.SemaphoreType.DMA((3,)),
        ],
        compiler_params=pltpu.CompilerParams(vmem_limit_bytes=VMEM),
        name="pack",
    )(odd, own, core, far, stored, kernels)


def mix_body(place_ref, odd_ref, *refs):
    rows, (gathered_ref, kern_ref, half_ref) = refs[:NY], refs[NY : NY + 3]
    m_ref, row_ref, col_ref, other_rows, other_cols = refs[NY + 3 :]
    for i in range(NY):
        for side in range(NX):
            at = pl.ds(pl.multiple_of(place_ref[i * NX + side] * SLAB, SLAB), SLAB)
            row_ref[:, at, :] = rows[i][2 * side]
            other_rows[:, at, :] = rows[i][2 * side + 1]
    for i in range(NZ):
        at = pl.ds(i * SLAB, SLAB)
        col_ref[:, at, :] = gathered_ref[i, 0]
        other_cols[:, at, :] = gathered_ref[i, 1]
    last = ((1,), (1,))
    per = BLOCK // 2
    odd = odd_ref[0] == 1
    sign = jnp.where(odd, -1.0, 1.0).astype(jnp.float32)

    def density(a_ref, b_ref, at):
        a_re, a_im, b_re, b_im = a_ref[0], a_ref[1], b_ref[0, at, :], b_ref[1, at, :]
        p_re = dot(a_re, b_re, last) + dot(a_im, b_im, last)
        p_im = dot(a_im, b_re, last) - dot(a_re, b_im, last)
        return p_re, p_im

    for part in range(2):
        at = pl.ds(part * per, per)
        p_re, p_im = density(row_ref, col_ref, at)
        mine = kern_ref[:, 0, :, at].reshape(BLOCK, per)
        other = half_ref[:, :, at].reshape(BLOCK, per)
        k_re = jnp.where(odd, other, mine).astype(jnp.float32)
        k_im = jnp.where(odd, mine, other).astype(jnp.float32) * sign
        total_re = k_re * p_re - k_im * p_im
        total_im = k_re * p_im + k_im * p_re
        p_re, p_im = density(other_rows, other_cols, at)
        k_re = kern_ref[:, 1, :, at].reshape(BLOCK, per).astype(jnp.float32)
        k_im = kern_ref[:, 2, :, at].reshape(BLOCK, per).astype(jnp.float32) * -sign
        total_re += k_re * p_re - k_im * p_im
        total_im += k_re * p_im + k_im * p_re
        m_ref[0, :, at] = total_re.astype(jnp.bfloat16)
        m_ref[1, :, at] = total_im.astype(jnp.bfloat16)


def mix(place, odd, *arrays):
    vmem = pl.BlockSpec(memory_space=pltpu.VMEM)
    smem = pl.BlockSpec(memory_space=pltpu.SMEM)
    points = jax.ShapeDtypeStruct((2, BLOCK, NB), jnp.bfloat16)
    return pl.pallas_call(
        mix_body,
        out_shape=[jax.ShapeDtypeStruct((2, BLOCK, BLOCK), jnp.bfloat16), points, points],
        in_specs=[smem, smem] + [vmem] * len(arrays),
        out_specs=[vmem] * 3,
        scratch_shapes=[pltpu.VMEM((2, BLOCK, NB), jnp.bfloat16)] * 2,
        compiler_params=pltpu.CompilerParams(vmem_limit_bytes=VMEM),
        name="mix",
    )(place, odd, *arrays)


def halves(value):
    high = value.astype(jnp.bfloat16)
    return high, (value - high.astype(jnp.float32)).astype(jnp.bfloat16)


def project_body(m_ref, row_ref, col_ref, out_ref, x_ref):
    mid = ((1,), (0,))
    first = ((0,), (0,))
    m_re, m_im = m_ref[0], m_ref[1]
    c_re, c_im = col_ref[0], col_ref[1]
    y_re = halves(dot(m_re, c_re, mid) - dot(m_im, c_im, mid))
    y_im = halves(dot(m_re, c_im, mid) + dot(m_im, c_re, mid))
    r_re, r_im = row_ref[0], row_ref[1]

    def meet(a, pair):
        return dot(a, pair[0], first) + dot(a, pair[1], first)

    x_re = -(meet(r_re, y_re) + meet(r_im, y_im))
    x_im = meet(r_im, y_re) - meet(r_re, y_im)
    gap = jnp.zeros((NB, 64 - (NB - WHOLE)), jnp.float32)
    x_ref[pl.ds(NB, 8), :] = jnp.zeros((8, LANES), jnp.float32)
    x_ref[pl.ds(0, NB), pl.ds(0, WHOLE)] = x_re[:, :WHOLE]
    x_ref[pl.ds(0, NB), pl.ds(WHOLE, WHOLE)] = x_im[:, :WHOLE]
    x_ref[pl.ds(0, NB), pl.ds(2 * WHOLE, 128)] = jnp.concatenate(
        [x_re[:, WHOLE:], gap, x_im[:, WHOLE:], gap], axis=1
    )
    for d in range(GROUPS * NZ):
        out_ref[d] = x_ref[pl.ds(27 * d // 4, 8), :].astype(jnp.bfloat16)


def project(m, rows, cols):
    vmem = pl.BlockSpec(memory_space=pltpu.VMEM)
    return pl.pallas_call(
        project_body,
        out_shape=jax.ShapeDtypeStruct((GROUPS * NZ, 8, LANES), jnp.bfloat16),
        in_specs=[vmem] * 3,
        out_specs=vmem,
        scratch_shapes=[pltpu.VMEM((NB + 8, LANES), jnp.float32)],
        compiler_params=pltpu.CompilerParams(vmem_limit_bytes=VMEM),
        name="project",
    )(m, rows, cols)


def reduce_windows(windows):
    parts = lax.all_to_all(windows, "band", 0, 0)
    total = jnp.sum(parts.astype(jnp.float32), axis=0)
    tail = 2 * WHOLE
    rest = NB - WHOLE
    real = jnp.concatenate([total[:, :WHOLE], total[:, tail : tail + rest]], axis=1)
    imag = jnp.concatenate([total[:, WHOLE:tail], total[:, tail + 64 : tail + 64 + rest]], axis=1)
    return jnp.stack([real, imag])


def on_device(orbitals, kernels, pair_kdiff, stored_kernel_index):
    group = lax.axis_index("kgrp")
    band = lax.axis_index("band")
    y, x, z = band // (NX * NZ), band // NZ % NX, band % NZ
    odd = (group % 2).reshape(1)

    own = orbitals[0]
    diff_core = swap_groups(pair_kdiff, 1)
    diff_far = swap_groups(pair_kdiff, 2)
    far = swap_groups(own, 2)
    own_side, far_side = shift(own, 0, 1, 0), other_side(own)

    over_yx = [[g * NZ + z_at for g in range(GROUPS)] for z_at in range(NZ)]
    over_z = [[g * NZ + z_at for z_at in range(NZ)] for g in range(GROUPS)]
    sends = pack(odd, pair_kdiff, diff_core, diff_far, stored_kernel_index, kernels)

    gathered = lax.all_gather(jnp.stack([own, far]), "band", axis_index_groups=over_z)
    four = jnp.stack([own, far, own_side, far_side])
    up, down = shift(four, 1, 0, 0), shift(four, -1, 0, 0)
    sends, up, down = lax.optimization_barrier((sends, up, down))
    over = shift(up, 1, 0, 0)
    kern = lax.all_to_all(sends, "band", 0, 0, axis_index_groups=over_yx)
    half = swap_groups(kern[:, 0], 1)

    place = jnp.stack([(y - dy) % NY * NX + (x - dx) % NX for dy in range(NY) for dx in range(NX)])
    m_out, own_rows, own_cols = mix(place, odd, four, up, over, down, gathered, kern, half)
    m_own = swap_groups(m_out, 1)
    total = reduce_windows(project(m_own, own_rows, own_cols))
    flat = total.reshape(2, 8 * NB)
    flat = lax.dynamic_slice(flat, (0, band * 27 % 4 * 108), (2, 27 * 108))
    return flat[None]


def solution(mesh):
    return jax.shard_map(
        on_device,
        mesh=mesh,
        in_specs=(P("kgrp", None, "band", None), P(None, None, "band", None), P("kgrp"), P()),
        out_specs=P("kgrp", None, "band"),
        check_vma=False,
    )
```

```python
import functools

import jax
import jax.numpy as jnp
import numpy as np
from jax import lax
from jax.experimental import pallas as pl
from jax.experimental.pallas import tpu as pltpu
from jax.sharding import PartitionSpec as P

NB = 432
SLAB = 64
NY, NX, NZ = 4, 2, 8
GROUPS = NY * NX
BLOCK = NZ * SLAB
WHOLE = 384
LANES = 2 * WHOLE + 128
VMEM = 56 * 1024 * 1024


def band_route(dy, dx, dz):
    route = []
    for y in range(NY):
        for x in range(NX):
            for z in range(NZ):
                there = ((y + dy) % NY * NX + (x + dx) % NX) * NZ + (z + dz) % NZ
                route.append(((y * NX + x) * NZ + z, there))
    return route


def shift(block, dy, dx, dz):
    return lax.ppermute(block, "band", band_route(dy, dx, dz))


def swap_groups(block, bit):
    return lax.ppermute(block, "kgrp", [(k, k ^ bit) for k in range(4)])


def other_side(block):
    route = [(i, j) for i, j in band_route(0, 1, 0)]
    both = [((k ^ 2) * 64 + i, k * 64 + j) for k in range(4) for i, j in route]
    return lax.ppermute(block, ("kgrp", "band"), both)


def dot(a, b, dims):
    return lax.dot_general(a, b, ((dims[0], dims[1]), ((), ())), preferred_element_type=jnp.float32)


def pack_body(odd_ref, own_ref, core_ref, far_ref, stored_ref, kernels_ref, shared_ref, single_ref, held, sem):
    odd = odd_ref[0] == 1
    own, core, far = stored_ref[own_ref[0]], stored_ref[core_ref[0]], stored_ref[far_ref[0]]
    shared = jnp.where(odd, own, core)
    single = jnp.where(odd, core, far)
    copies = [
        pltpu.make_async_copy(kernels_ref.at[shared, odd_ref[0]], held.at[0], sem.at[0]),
        pltpu.make_async_copy(kernels_ref.at[single, 0], held.at[1], sem.at[1]),
        pltpu.make_async_copy(kernels_ref.at[single, 1], held.at[2], sem.at[2]),
    ]
    for copy in copies:
        copy.start()
    for which, copy in enumerate(copies):
        copy.wait()
        for i in range(GROUPS):
            block = held[which, :, pl.ds(i * BLOCK, BLOCK)]
            if which == 0:
                shared_ref[i] = block
            else:
                single_ref[i, which - 1] = block


def pack(odd, own, core, far, stored, kernels):
    smem = pl.BlockSpec(memory_space=pltpu.SMEM)
    return pl.pallas_call(
        pack_body,
        out_shape=[
            jax.ShapeDtypeStruct((GROUPS, SLAB, BLOCK), jnp.bfloat16),
            jax.ShapeDtypeStruct((GROUPS, 2, SLAB, BLOCK), jnp.bfloat16),
        ],
        in_specs=[smem] * 5 + [pl.BlockSpec(memory_space=pl.ANY)],
        out_specs=[pl.BlockSpec(memory_space=pltpu.VMEM)] * 2,
        scratch_shapes=[
            pltpu.VMEM((3, SLAB, GROUPS * BLOCK), jnp.bfloat16),
            pltpu.SemaphoreType.DMA((3,)),
        ],
        compiler_params=pltpu.CompilerParams(vmem_limit_bytes=VMEM),
        name="pack",
    )(odd, own, core, far, stored, kernels)


def mix_body(place_ref, odd_ref, *refs):
    four_ref, up_ref, over_here, over_side, down_ref, gathered_ref = refs[:6]
    mine_ref, half_ref, kern_ref = refs[6:9]
    m_ref, row_ref, col_ref, other_rows, other_cols = refs[9:]
    rows = ((four_ref, four_ref), (up_ref, up_ref), (over_here, over_side), (down_ref, down_ref))
    for i in range(NY):
        for side in range(NX):
            at = pl.ds(pl.multiple_of(place_ref[i * NX + side] * SLAB, SLAB), SLAB)
            piece = rows[i][side]
            first = 0 if piece is over_side else 2 * side
            row_ref[:, at, :] = piece[first]
            other_rows[:, at, :] = piece[first + 1]
    for i in range(NZ):
        at = pl.ds(i * SLAB, SLAB)
        col_ref[:, at, :] = gathered_ref[i, 0]
        other_cols[:, at, :] = gathered_ref[i, 1]
    last = ((1,), (1,))
    per = BLOCK // 2
    odd = odd_ref[0] == 1
    sign = jnp.where(odd, -1.0, 1.0).astype(jnp.float32)

    def density(a_ref, b_ref, at):
        a_re, a_im, b_re, b_im = a_ref[0], a_ref[1], b_ref[0, at, :], b_ref[1, at, :]
        p_re = dot(a_re, b_re, last) + dot(a_im, b_im, last)
        p_im = dot(a_im, b_re, last) - dot(a_re, b_im, last)
        return p_re, p_im

    for part in range(2):
        at = pl.ds(part * per, per)
        p_re, p_im = density(row_ref, col_ref, at)
        mine = mine_ref[:, :, at].reshape(BLOCK, per)
        other = half_ref[:, :, at].reshape(BLOCK, per)
        k_re = jnp.where(odd, other, mine).astype(jnp.float32)
        k_im = jnp.where(odd, mine, other).astype(jnp.float32) * sign
        total_re = k_re * p_re - k_im * p_im
        total_im = k_re * p_im + k_im * p_re
        p_re, p_im = density(other_rows, other_cols, at)
        k_re = kern_ref[:, 0, :, at].reshape(BLOCK, per).astype(jnp.float32)
        k_im = kern_ref[:, 1, :, at].reshape(BLOCK, per).astype(jnp.float32) * -sign
        total_re += k_re * p_re - k_im * p_im
        total_im += k_re * p_im + k_im * p_re
        m_ref[0, :, at] = total_re.astype(jnp.bfloat16)
        m_ref[1, :, at] = total_im.astype(jnp.bfloat16)


def mix(place, odd, *arrays):
    vmem = pl.BlockSpec(memory_space=pltpu.VMEM)
    smem = pl.BlockSpec(memory_space=pltpu.SMEM)
    points = jax.ShapeDtypeStruct((2, BLOCK, NB), jnp.bfloat16)
    return pl.pallas_call(
        mix_body,
        out_shape=[jax.ShapeDtypeStruct((2, BLOCK, BLOCK), jnp.bfloat16), points, points],
        in_specs=[smem, smem] + [vmem] * len(arrays),
        out_specs=[vmem] * 3,
        scratch_shapes=[pltpu.VMEM((2, BLOCK, NB), jnp.bfloat16)] * 2,
        compiler_params=pltpu.CompilerParams(vmem_limit_bytes=VMEM),
        name="mix",
    )(place, odd, *arrays)


def halves(value):
    high = value.astype(jnp.bfloat16)
    return high, (value - high.astype(jnp.float32)).astype(jnp.bfloat16)


def project_body(m_ref, row_ref, col_ref, out_ref, x_ref):
    mid = ((1,), (0,))
    first = ((0,), (0,))
    m_re, m_im = m_ref[0], m_ref[1]
    c_re, c_im = col_ref[0], col_ref[1]
    y_re = halves(dot(m_re, c_re, mid) - dot(m_im, c_im, mid))
    y_im = halves(dot(m_re, c_im, mid) + dot(m_im, c_re, mid))
    r_re, r_im = row_ref[0], row_ref[1]

    def meet(a, pair):
        return dot(a, pair[0], first) + dot(a, pair[1], first)

    x_re = -(meet(r_re, y_re) + meet(r_im, y_im))
    x_im = meet(r_im, y_re) - meet(r_re, y_im)
    gap = jnp.zeros((NB, 64 - (NB - WHOLE)), jnp.float32)
    x_ref[pl.ds(NB, 8), :] = jnp.zeros((8, LANES), jnp.float32)
    x_ref[pl.ds(0, NB), pl.ds(0, WHOLE)] = x_re[:, :WHOLE]
    x_ref[pl.ds(0, NB), pl.ds(WHOLE, WHOLE)] = x_im[:, :WHOLE]
    x_ref[pl.ds(0, NB), pl.ds(2 * WHOLE, 128)] = jnp.concatenate(
        [x_re[:, WHOLE:], gap, x_im[:, WHOLE:], gap], axis=1
    )
    for d in range(GROUPS * NZ):
        out_ref[d] = x_ref[pl.ds(27 * d // 4, 8), :].astype(jnp.bfloat16)


def project(m, rows, cols):
    vmem = pl.BlockSpec(memory_space=pltpu.VMEM)
    return pl.pallas_call(
        project_body,
        out_shape=jax.ShapeDtypeStruct((GROUPS * NZ, 8, LANES), jnp.bfloat16),
        in_specs=[vmem] * 3,
        out_specs=vmem,
        scratch_shapes=[pltpu.VMEM((NB + 8, LANES), jnp.float32)],
        compiler_params=pltpu.CompilerParams(vmem_limit_bytes=VMEM),
        name="project",
    )(m, rows, cols)


def reduce_windows(windows):
    parts = lax.all_to_all(windows, "band", 0, 0)
    total = jnp.sum(parts.astype(jnp.float32), axis=0)
    tail = 2 * WHOLE
    rest = NB - WHOLE
    real = jnp.concatenate([total[:, :WHOLE], total[:, tail : tail + rest]], axis=1)
    imag = jnp.concatenate([total[:, WHOLE:tail], total[:, tail + 64 : tail + 64 + rest]], axis=1)
    return jnp.stack([real, imag])


def on_device(orbitals, kernels, pair_kdiff, stored_kernel_index):
    group = lax.axis_index("kgrp")
    band = lax.axis_index("band")
    y, x, z = band // (NX * NZ), band // NZ % NX, band % NZ
    odd = (group % 2).reshape(1)

    own = orbitals[0]
    diff_core = swap_groups(pair_kdiff, 1)
    diff_far = swap_groups(pair_kdiff, 2)
    far = swap_groups(own, 2)
    own_side, far_side = shift(own, 0, 1, 0), other_side(own)
    far, own_side, far_side = lax.optimization_barrier((far, own_side, far_side))

    over_yx = [[g * NZ + z_at for g in range(GROUPS)] for z_at in range(NZ)]
    over_z = [[g * NZ + z_at for z_at in range(NZ)] for g in range(GROUPS)]
    sends = pack(odd, pair_kdiff, diff_core, diff_far, stored_kernel_index, kernels)

    gathered = lax.all_gather(jnp.stack([own, far]), "band", axis_index_groups=over_z)
    four = jnp.stack([own, far, own_side, far_side])
    up, down = shift(four, 1, 0, 0), shift(four, -1, 0, 0)
    shared, single = sends
    shared, up, down = lax.optimization_barrier((shared, up, down))
    over = shift(up[:2], 1, 0, 0), shift(down[2:], -1, 0, 0)
    mine = lax.all_to_all(shared, "band", 0, 0, axis_index_groups=over_yx)
    half = swap_groups(mine, 1)
    single, over = lax.optimization_barrier((single, over))
    kern = lax.all_to_all(single, "band", 0, 0, axis_index_groups=over_yx)

    place = jnp.stack([(y - dy) % NY * NX + (x - dx) % NX for dy in range(NY) for dx in range(NX)])
    m_out, own_rows, own_cols = mix(
        place, odd, four, up, *over, down, gathered, mine, half, kern
    )
    m_own = swap_groups(m_out, 1)
    total = reduce_windows(project(m_own, own_rows, own_cols))
    flat = total.reshape(2, 8 * NB)
    flat = lax.dynamic_slice(flat, (0, band * 27 % 4 * 108), (2, 27 * 108))
    return flat[None]


def solution(mesh):
    return jax.shard_map(
        on_device,
        mesh=mesh,
        in_specs=(P("kgrp", None, "band", None), P(None, None, "band", None), P("kgrp"), P()),
        out_specs=P("kgrp", None, "band"),
        check_vma=False,
    )
```

```python
import jax
import jax.numpy as jnp
from jax import lax
from jax.experimental import pallas as pl
from jax.experimental.pallas import tpu as pltpu
from jax.sharding import PartitionSpec as P

NB = 432
SLAB = 64
NY, NX, NZ = 4, 2, 8
GROUPS = NY * NX
BLOCK = NZ * SLAB
WHOLE = 384
REST = NB - WHOLE
TAIL = 2 * WHOLE
LANES = TAIL + 128
VMEM = 24 * 1024 * 1024

IN_VMEM = pl.BlockSpec(memory_space=pltpu.VMEM)
IN_SMEM = pl.BlockSpec(memory_space=pltpu.SMEM)
ANYWHERE = pl.BlockSpec(memory_space=pl.ANY)
PARAMS = pltpu.CompilerParams(vmem_limit_bytes=VMEM)


def band_route(dy, dx, dz):
    route = []
    for y in range(NY):
        for x in range(NX):
            for z in range(NZ):
                there = ((y + dy) % NY * NX + (x + dx) % NX) * NZ + (z + dz) % NZ
                route.append(((y * NX + x) * NZ + z, there))
    return route


def shift(block, dy, dx, dz):
    return lax.ppermute(block, "band", band_route(dy, dx, dz))


def swap_groups(block, bit):
    return lax.ppermute(block, "kgrp", [(k, k ^ bit) for k in range(4)])


def other_side(block):
    route = [(i, j) for i, j in band_route(0, 1, 0)]
    both = [((k ^ 2) * 64 + i, k * 64 + j) for k in range(4) for i, j in route]
    return lax.ppermute(block, ("kgrp", "band"), both)


def dot(a, b, a_axis, b_axis):
    dims = (((a_axis,), (b_axis,)), ((), ()))
    return lax.dot_general(a, b, dims, preferred_element_type=jnp.float32)


def near(array):
    return pltpu.with_memory_space_constraint(array, pltpu.VMEM)


def lay_body(orbit_ref, out_ref):
    gap = jnp.zeros((SLAB, 64 - REST), jnp.float32)
    real, imag = orbit_ref[0, 0], orbit_ref[0, 1]
    out_ref[:, :WHOLE] = real[:, :WHOLE]
    out_ref[:, WHOLE:TAIL] = imag[:, :WHOLE]
    last = [real[:, WHOLE:].astype(jnp.float32), gap, imag[:, WHOLE:].astype(jnp.float32), gap]
    out_ref[:, TAIL:] = jnp.concatenate(last, axis=1).astype(jnp.bfloat16)


def lay(orbitals):
    return pl.pallas_call(
        lay_body,
        out_shape=pltpu.VMEM((SLAB, LANES), jnp.bfloat16),
        in_specs=[IN_VMEM],
        out_specs=IN_VMEM,
        name="lay",
    )(orbitals)


def turned(rows):
    last = rows[:, TAIL:].astype(jnp.float32)
    lane = lax.broadcasted_iota(jnp.int32, last.shape, 1)
    last = pltpu.roll(last, 64, 1) * jnp.where(lane < 64, 1.0, -1.0)
    return jnp.concatenate(
        [rows[:, WHOLE:TAIL], -rows[:, :WHOLE], last.astype(rows.dtype)], axis=1
    )


def pack_body(odd_ref, own_ref, core_ref, far_ref, stored_ref, kernels_ref, shared_ref, single_ref, sem):
    odd = odd_ref[0] == 1
    own, core, far = stored_ref[own_ref[0]], stored_ref[core_ref[0]], stored_ref[far_ref[0]]
    shared = jnp.where(odd, own, core)
    single = jnp.where(odd, core, far)
    copies = []
    for i in range(GROUPS):
        at = pl.ds(i * BLOCK, BLOCK)
        copies += [
            pltpu.make_async_copy(
                kernels_ref.at[shared, odd_ref[0], :, at], shared_ref.at[i], sem.at[0, i]
            ),
            pltpu.make_async_copy(
                kernels_ref.at[single, :, :, at], single_ref.at[i], sem.at[1, i]
            ),
        ]
    for copy in copies:
        copy.start()
    for copy in copies:
        copy.wait()


def pack(odd, own, core, far, stored, kernels):
    return pl.pallas_call(
        pack_body,
        out_shape=[
            pltpu.VMEM((GROUPS, SLAB, BLOCK), jnp.bfloat16),
            pltpu.VMEM((GROUPS, 2, SLAB, BLOCK), jnp.bfloat16),
        ],
        in_specs=[IN_SMEM] * 5 + [ANYWHERE],
        out_specs=[IN_VMEM] * 2,
        scratch_shapes=[pltpu.SemaphoreType.DMA((2, GROUPS))],
        compiler_params=PARAMS,
        name="pack",
    )(odd, own, core, far, stored, kernels)


def mix_body(place_ref, odd_ref, *refs):
    four_ref, up_ref, over_here, over_side, down_ref, gathered_ref = refs[:6]
    mine_ref, half_ref, kern_ref = refs[6:9]
    m_ref, row_ref, col_ref, other_rows, other_cols = refs[9:]
    rows = ((four_ref, four_ref), (up_ref, up_ref), (over_here, over_side), (down_ref, down_ref))
    for i in range(NY):
        for side in range(NX):
            at = pl.ds(pl.multiple_of(place_ref[i * NX + side] * SLAB, SLAB), SLAB)
            piece = rows[i][side]
            first = 0 if piece is over_side else 2 * side
            row_ref[at, :] = piece[first]
            other_rows[at, :] = piece[first + 1]
    for i in range(NZ):
        at = pl.ds(i * SLAB, SLAB)
        col_ref[at, :] = gathered_ref[i, 0]
        other_cols[at, :] = gathered_ref[i, 1]
    per = BLOCK // 2
    odd = odd_ref[0] == 1
    sign = jnp.where(odd, -1.0, 1.0).astype(jnp.float32)
    a, a_other = row_ref[...], other_rows[...]
    a_turned, other_turned = turned(a), turned(a_other)
    for part in range(2):
        at = pl.ds(part * per, per)
        b = col_ref[at, :]
        p_re, p_im = dot(a, b, 1, 1), dot(a_turned, b, 1, 1)
        mine = mine_ref[:, :, at].reshape(BLOCK, per)
        other = half_ref[:, :, at].reshape(BLOCK, per)
        k_re = jnp.where(odd, other, mine).astype(jnp.float32)
        k_im = jnp.where(odd, mine, other).astype(jnp.float32) * sign
        total_re = k_re * p_re - k_im * p_im
        total_im = k_re * p_im + k_im * p_re
        b = other_cols[at, :]
        p_re, p_im = dot(a_other, b, 1, 1), dot(other_turned, b, 1, 1)
        k_re = kern_ref[:, 0, :, at].reshape(BLOCK, per).astype(jnp.float32)
        k_im = kern_ref[:, 1, :, at].reshape(BLOCK, per).astype(jnp.float32) * -sign
        total_re += k_re * p_re - k_im * p_im
        total_im += k_re * p_im + k_im * p_re
        m_ref[:, at] = total_re.astype(jnp.bfloat16)
        m_ref[:, pl.ds(BLOCK + part * per, per)] = total_im.astype(jnp.bfloat16)


def mix(place, odd, *arrays):
    points = pltpu.VMEM((BLOCK, LANES), jnp.bfloat16)
    return pl.pallas_call(
        mix_body,
        out_shape=[pltpu.VMEM((BLOCK, 2 * BLOCK), jnp.bfloat16), points, points],
        in_specs=[IN_SMEM] * 2 + [IN_VMEM] * len(arrays),
        out_specs=[IN_VMEM] * 3,
        scratch_shapes=[pltpu.VMEM((BLOCK, LANES), jnp.bfloat16)] * 2,
        compiler_params=PARAMS,
        name="mix",
    )(place, odd, *map(near, arrays))


def prepare_body(row_ref, col_ref, left_ref, right_ref):
    flipped = row_ref[...].T
    left_ref[pl.ds(0, WHOLE), :BLOCK] = flipped[:WHOLE]
    left_ref[pl.ds(WHOLE, REST), :BLOCK] = flipped[TAIL : TAIL + REST]
    left_ref[pl.ds(0, WHOLE), BLOCK:] = flipped[WHOLE:TAIL]
    left_ref[pl.ds(WHOLE, REST), BLOCK:] = flipped[TAIL + 64 : TAIL + 64 + REST]
    col = col_ref[...]
    right_ref[pl.ds(0, BLOCK), :] = col
    right_ref[pl.ds(BLOCK, BLOCK), :] = -turned(col)


def prepare(rows, cols):
    return pl.pallas_call(
        prepare_body,
        out_shape=[
            pltpu.VMEM((NB, 2 * BLOCK), jnp.bfloat16),
            pltpu.VMEM((2 * BLOCK, LANES), jnp.bfloat16),
        ],
        in_specs=[IN_VMEM] * 2,
        out_specs=[IN_VMEM] * 2,
        compiler_params=PARAMS,
        name="prepare",
    )(near(rows), near(cols))


def project_body(m_ref, left_ref, right_ref, out_ref, x_ref):
    y = dot(m_ref[...], right_ref[...], 1, 0)
    high = y.astype(jnp.bfloat16)
    low = (y - high.astype(jnp.float32)).astype(jnp.bfloat16)
    left = left_ref[...]
    x = dot(left, jnp.concatenate([high, turned(high)], axis=0), 1, 0)
    x += dot(left, jnp.concatenate([low, turned(low)], axis=0), 1, 0)
    x_ref[pl.ds(0, NB), :] = -x
    x_ref[pl.ds(NB, 8), :] = jnp.zeros((8, LANES), jnp.float32)
    for d in range(GROUPS * NZ):
        out_ref[d] = x_ref[pl.ds(27 * d // 4, 8), :].astype(jnp.bfloat16)


def project(m, left, right):
    return pl.pallas_call(
        project_body,
        out_shape=pltpu.VMEM((GROUPS * NZ, 8, LANES), jnp.bfloat16),
        in_specs=[IN_VMEM] * 3,
        out_specs=IN_VMEM,
        scratch_shapes=[pltpu.VMEM((NB + 8, LANES), jnp.float32)],
        compiler_params=PARAMS,
        name="project",
    )(near(m), near(left), near(right))


def bundle_body(own_ref, far_ref, own_side, far_side, four_ref, both_ref):
    for i, ref in enumerate((own_ref, far_ref, own_side, far_side)):
        four_ref[i] = ref[...]
    both_ref[0] = own_ref[...]
    both_ref[1] = far_ref[...]


def bundle(*blocks):
    return pl.pallas_call(
        bundle_body,
        out_shape=[
            pltpu.VMEM((4, SLAB, LANES), jnp.bfloat16),
            jax.ShapeDtypeStruct((2, SLAB, LANES), jnp.bfloat16),
        ],
        in_specs=[IN_VMEM] * 4,
        out_specs=[IN_VMEM] * 2,
        compiler_params=PARAMS,
        name="bundle",
    )(*map(near, blocks))


def reduce_windows(windows):
    parts = lax.all_to_all(windows, "band", 0, 0)
    total = jnp.sum(parts.astype(jnp.float32), axis=0)
    real = jnp.concatenate([total[:, :WHOLE], total[:, TAIL : TAIL + REST]], axis=1)
    imag = jnp.concatenate([total[:, WHOLE:TAIL], total[:, TAIL + 64 : TAIL + 64 + REST]], axis=1)
    return jnp.stack([real, imag])


def on_device(orbitals, kernels, pair_kdiff, stored_kernel_index):
    group = lax.axis_index("kgrp")
    band = lax.axis_index("band")
    y, x = band // (NX * NZ), band // NZ % NX
    odd = (group % 2).reshape(1)

    own = lay(orbitals)
    first = (
        swap_groups(pair_kdiff, 1),
        swap_groups(pair_kdiff, 2),
        swap_groups(own, 2),
        shift(own, 0, 1, 0),
        other_side(own),
    )
    diff_core, diff_far, far, own_side, far_side = lax.optimization_barrier(first)

    over_yx = [[g * NZ + z for g in range(GROUPS)] for z in range(NZ)]
    over_z = [[g * NZ + z for z in range(NZ)] for g in range(GROUPS)]
    four, both = bundle(own, far, own_side, far_side)
    gathered = lax.all_gather(both, "band", axis_index_groups=over_z)
    up, down = shift(four, 1, 0, 0), shift(four, -1, 0, 0)
    over = shift(up[:2], 1, 0, 0), shift(down[2:], -1, 0, 0)

    shared, single = pack(odd, pair_kdiff, diff_core, diff_far, stored_kernel_index, kernels)
    mine = lax.all_to_all(shared, "band", 0, 0, axis_index_groups=over_yx)
    half = swap_groups(mine, 1)
    single, over = lax.optimization_barrier((single, over))
    kern = lax.all_to_all(single, "band", 0, 0, axis_index_groups=over_yx)

    place = jnp.stack([(y - dy) % NY * NX + (x - dx) % NX for dy in range(NY) for dx in range(NX)])
    m_out, rows, cols = mix(
        place, odd, four, up, *over, down, gathered, mine, half, kern
    )
    m_own = swap_groups(m_out, 1)
    left, right = prepare(rows, cols)
    total = reduce_windows(project(m_own, left, right))
    flat = total.reshape(2, 8 * NB)
    flat = lax.dynamic_slice(flat, (0, band * 27 % 4 * 108), (2, 27 * 108))
    return flat[None]


def solution(mesh):
    return jax.shard_map(
        on_device,
        mesh=mesh,
        in_specs=(P("kgrp", None, "band", None), P(None, None, "band", None), P("kgrp"), P()),
        out_specs=P("kgrp", None, "band"),
        check_vma=False,
    )
```

```python
import jax
import jax.numpy as jnp
from jax import lax
from jax.experimental import pallas as pl
from jax.experimental.pallas import tpu as pltpu
from jax.sharding import PartitionSpec as P

NB = 432
SLAB = 64
NY, NX, NZ = 4, 2, 8
GROUPS = NY * NX
BLOCK = NZ * SLAB
WHOLE = 384
REST = NB - WHOLE
TAIL = 2 * WHOLE
LANES = TAIL + 128
VMEM = 24 * 1024 * 1024

IN_VMEM = pl.BlockSpec(memory_space=pltpu.VMEM)
IN_SMEM = pl.BlockSpec(memory_space=pltpu.SMEM)
ANYWHERE = pl.BlockSpec(memory_space=pl.ANY)
PARAMS = pltpu.CompilerParams(vmem_limit_bytes=VMEM)


def band_route(dy, dx, dz):
    route = []
    for y in range(NY):
        for x in range(NX):
            for z in range(NZ):
                there = ((y + dy) % NY * NX + (x + dx) % NX) * NZ + (z + dz) % NZ
                route.append(((y * NX + x) * NZ + z, there))
    return route


def shift(block, dy, dx, dz):
    return lax.ppermute(block, "band", band_route(dy, dx, dz))


def swap_groups(block, bit):
    return lax.ppermute(block, "kgrp", [(k, k ^ bit) for k in range(4)])


def other_side(block):
    route = [(i, j) for i, j in band_route(0, 1, 0)]
    both = [((k ^ 2) * 64 + i, k * 64 + j) for k in range(4) for i, j in route]
    return lax.ppermute(block, ("kgrp", "band"), both)


def dot(a, b, a_axis, b_axis):
    dims = (((a_axis,), (b_axis,)), ((), ()))
    return lax.dot_general(a, b, dims, preferred_element_type=jnp.float32)


def near(array):
    return pltpu.with_memory_space_constraint(array, pltpu.VMEM)


def away(array):
    return pltpu.with_memory_space_constraint(array, pltpu.HBM)


def lay_body(orbit_ref, out_ref):
    gap = jnp.zeros((SLAB, 64 - REST), jnp.float32)
    real, imag = orbit_ref[0, 0], orbit_ref[0, 1]
    out_ref[:, :WHOLE] = real[:, :WHOLE]
    out_ref[:, WHOLE:TAIL] = imag[:, :WHOLE]
    last = [real[:, WHOLE:].astype(jnp.float32), gap, imag[:, WHOLE:].astype(jnp.float32), gap]
    out_ref[:, TAIL:] = jnp.concatenate(last, axis=1).astype(jnp.bfloat16)


def lay(orbitals):
    return pl.pallas_call(
        lay_body,
        out_shape=pltpu.VMEM((SLAB, LANES), jnp.bfloat16),
        in_specs=[IN_VMEM],
        out_specs=IN_VMEM,
        name="lay",
    )(orbitals)


def turned(rows):
    last = rows[:, TAIL:].astype(jnp.float32)
    lane = lax.broadcasted_iota(jnp.int32, last.shape, 1)
    last = pltpu.roll(last, 64, 1) * jnp.where(lane < 64, 1.0, -1.0)
    return jnp.concatenate(
        [rows[:, WHOLE:TAIL], -rows[:, :WHOLE], last.astype(rows.dtype)], axis=1
    )


def pack_body(odd_ref, own_ref, core_ref, far_ref, stored_ref, kernels_ref, shared_ref, single_ref, sem):
    odd = odd_ref[0] == 1
    own, core, far = stored_ref[own_ref[0]], stored_ref[core_ref[0]], stored_ref[far_ref[0]]
    shared = jnp.where(odd, own, core)
    single = jnp.where(odd, core, far)
    copies = []
    for i in range(GROUPS):
        at = pl.ds(i * BLOCK, BLOCK)
        copies += [
            pltpu.make_async_copy(
                kernels_ref.at[shared, odd_ref[0], :, at], shared_ref.at[i], sem.at[0, i]
            ),
            pltpu.make_async_copy(
                kernels_ref.at[single, :, :, at], single_ref.at[i], sem.at[1, i]
            ),
        ]
    for copy in copies:
        copy.start()
    for copy in copies:
        copy.wait()


def pack(odd, own, core, far, stored, kernels):
    return pl.pallas_call(
        pack_body,
        out_shape=[
            pltpu.VMEM((GROUPS, SLAB, BLOCK), jnp.bfloat16),
            pltpu.VMEM((GROUPS, 2, SLAB, BLOCK), jnp.bfloat16),
        ],
        in_specs=[IN_SMEM] * 5 + [ANYWHERE],
        out_specs=[IN_VMEM] * 2,
        scratch_shapes=[pltpu.SemaphoreType.DMA((2, GROUPS))],
        compiler_params=PARAMS,
        name="pack",
    )(odd, own, core, far, stored, away(kernels))


def mix_body(place_ref, odd_ref, *refs):
    four_ref, up_ref, over_here, over_side, down_ref, gathered_ref = refs[:6]
    mine_ref, half_ref, kern_ref = refs[6:9]
    m_ref, row_ref, col_ref, other_rows, other_cols, sem = refs[9:]

    def row_at(dy, side):
        return pl.ds(pl.multiple_of(place_ref[dy * NX + side] * SLAB, SLAB), SLAB)

    moves = []
    for side, piece in enumerate((over_here, over_side)):
        moves.append((piece.at[0], row_ref.at[row_at(2, side), :]))
        moves.append((piece.at[1], other_rows.at[row_at(2, side), :]))
    for target, which in ((col_ref, 0), (other_cols, 1)):
        for i in range(NZ):
            moves.append((gathered_ref.at[i, which], target.at[pl.ds(i * SLAB, SLAB), :]))
    copies = [pltpu.make_async_copy(*move, sem.at[i]) for i, move in enumerate(moves)]
    for copy in copies:
        copy.start()
    for dy, piece in ((0, four_ref), (1, up_ref), (3, down_ref)):
        for side in range(NX):
            row_ref[row_at(dy, side), :] = piece[2 * side]
            other_rows[row_at(dy, side), :] = piece[2 * side + 1]
    for copy in copies:
        copy.wait()
    per = BLOCK // 2
    odd = odd_ref[0] == 1
    sign = jnp.where(odd, -1.0, 1.0).astype(jnp.float32)
    a, a_other = row_ref[...], other_rows[...]
    a_turned, other_turned = turned(a), turned(a_other)
    for part in range(2):
        at = pl.ds(part * per, per)
        b = col_ref[at, :]
        p_re, p_im = dot(a, b, 1, 1), dot(a_turned, b, 1, 1)
        mine = mine_ref[:, :, at].reshape(BLOCK, per)
        other = half_ref[:, :, at].reshape(BLOCK, per)
        k_re = jnp.where(odd, other, mine).astype(jnp.float32)
        k_im = jnp.where(odd, mine, other).astype(jnp.float32) * sign
        total_re = k_re * p_re - k_im * p_im
        total_im = k_re * p_im + k_im * p_re
        b = other_cols[at, :]
        p_re, p_im = dot(a_other, b, 1, 1), dot(other_turned, b, 1, 1)
        k_re = kern_ref[:, 0, :, at].reshape(BLOCK, per).astype(jnp.float32)
        k_im = kern_ref[:, 1, :, at].reshape(BLOCK, per).astype(jnp.float32) * -sign
        total_re += k_re * p_re - k_im * p_im
        total_im += k_re * p_im + k_im * p_re
        m_ref[:, at] = total_re.astype(jnp.bfloat16)
        m_ref[:, pl.ds(BLOCK + part * per, per)] = total_im.astype(jnp.bfloat16)


def mix(place, odd, four, up, over, down, gathered, *kerns):
    points = pltpu.VMEM((BLOCK, LANES), jnp.bfloat16)
    in_hbm = pl.BlockSpec(memory_space=pltpu.HBM)
    specs = [IN_VMEM] * 2 + [in_hbm] * 2 + [IN_VMEM, in_hbm] + [IN_VMEM] * 3
    arrays = [near(four), near(up), *map(away, over), near(down), away(gathered), *map(near, kerns)]
    return pl.pallas_call(
        mix_body,
        out_shape=[pltpu.VMEM((BLOCK, 2 * BLOCK), jnp.bfloat16), points, points],
        in_specs=[IN_SMEM] * 2 + specs,
        out_specs=[IN_VMEM] * 3,
        scratch_shapes=[pltpu.VMEM((BLOCK, LANES), jnp.bfloat16)] * 2
        + [pltpu.SemaphoreType.DMA((2 * NX + 2 * NZ,))],
        compiler_params=PARAMS,
        name="mix",
    )(place, odd, *arrays)


def prepare_body(row_ref, col_ref, left_ref, right_ref):
    flipped = row_ref[...].T
    left_ref[pl.ds(0, WHOLE), :BLOCK] = flipped[:WHOLE]
    left_ref[pl.ds(WHOLE, REST), :BLOCK] = flipped[TAIL : TAIL + REST]
    left_ref[pl.ds(0, WHOLE), BLOCK:] = flipped[WHOLE:TAIL]
    left_ref[pl.ds(WHOLE, REST), BLOCK:] = flipped[TAIL + 64 : TAIL + 64 + REST]
    col = col_ref[...]
    right_ref[pl.ds(0, BLOCK), :] = col
    right_ref[pl.ds(BLOCK, BLOCK), :] = -turned(col)


def prepare(rows, cols):
    return pl.pallas_call(
        prepare_body,
        out_shape=[
            pltpu.VMEM((NB, 2 * BLOCK), jnp.bfloat16),
            pltpu.VMEM((2 * BLOCK, LANES), jnp.bfloat16),
        ],
        in_specs=[IN_VMEM] * 2,
        out_specs=[IN_VMEM] * 2,
        compiler_params=PARAMS,
        name="prepare",
    )(near(rows), near(cols))


def project_body(m_ref, left_ref, right_ref, out_ref, x_ref, part_ref, sem):
    y = dot(m_ref[...], right_ref[...], 1, 0)
    high = y.astype(jnp.bfloat16)
    low = (y - high.astype(jnp.float32)).astype(jnp.bfloat16)
    high = jnp.concatenate([high, turned(high)], axis=0)
    low = jnp.concatenate([low, turned(low)], axis=0)
    x_ref[pl.ds(NB, 8), :] = jnp.zeros((8, LANES), jnp.float32)
    copies = []
    for part, (start, size) in enumerate(((0, 224), (224, 208))):
        at = pl.ds(start, size)
        x_ref[at, :] = -(dot(left_ref[at, :], high, 1, 0) + dot(left_ref[at, :], low, 1, 0))
        some = GROUPS * NZ // 2
        for d in range(part * some, (part + 1) * some):
            part_ref[d] = x_ref[pl.ds(27 * d // 4, 8), :].astype(jnp.bfloat16)
        chosen = pl.ds(part * some, some)
        copy = pltpu.make_async_copy(part_ref.at[chosen], out_ref.at[chosen], sem.at[part])
        copy.start()
        copies.append(copy)
    for copy in copies:
        copy.wait()


def project(m, left, right):
    windows = (GROUPS * NZ, 8, LANES)
    return pl.pallas_call(
        project_body,
        out_shape=jax.ShapeDtypeStruct(windows, jnp.bfloat16),
        in_specs=[IN_VMEM] * 3,
        out_specs=pl.BlockSpec(memory_space=pltpu.HBM),
        scratch_shapes=[
            pltpu.VMEM((NB + 8, LANES), jnp.float32),
            pltpu.VMEM(windows, jnp.bfloat16),
            pltpu.SemaphoreType.DMA((2,)),
        ],
        compiler_params=PARAMS,
        name="project",
    )(near(m), near(left), near(right))


def bundle_body(own_ref, far_ref, own_side, far_side, four_ref, both_ref):
    for i, ref in enumerate((own_ref, far_ref, own_side, far_side)):
        four_ref[i] = ref[...]
    both_ref[0] = own_ref[...]
    both_ref[1] = far_ref[...]


def bundle(*blocks):
    return pl.pallas_call(
        bundle_body,
        out_shape=[
            pltpu.VMEM((4, SLAB, LANES), jnp.bfloat16),
            jax.ShapeDtypeStruct((2, SLAB, LANES), jnp.bfloat16),
        ],
        in_specs=[IN_VMEM] * 4,
        out_specs=[IN_VMEM] * 2,
        compiler_params=PARAMS,
        name="bundle",
    )(*map(near, blocks))


def reduce_windows(windows):
    parts = lax.all_to_all(windows, "band", 0, 0)
    total = jnp.sum(parts.astype(jnp.float32), axis=0)
    real = jnp.concatenate([total[:, :WHOLE], total[:, TAIL : TAIL + REST]], axis=1)
    imag = jnp.concatenate([total[:, WHOLE:TAIL], total[:, TAIL + 64 : TAIL + 64 + REST]], axis=1)
    return jnp.stack([real, imag])


def on_device(orbitals, kernels, pair_kdiff, stored_kernel_index):
    group = lax.axis_index("kgrp")
    band = lax.axis_index("band")
    y, x = band // (NX * NZ), band // NZ % NX
    odd = (group % 2).reshape(1)

    own = lay(orbitals)
    first = (
        swap_groups(pair_kdiff, 1),
        swap_groups(pair_kdiff, 2),
        swap_groups(own, 2),
        shift(own, 0, 1, 0),
        other_side(own),
    )
    diff_core, diff_far = first[:2]
    far, own_side, far_side = lax.optimization_barrier(first)[2:]

    over_yx = [[g * NZ + z for g in range(GROUPS)] for z in range(NZ)]
    over_z = [[g * NZ + z for z in range(NZ)] for g in range(GROUPS)]
    four, both = bundle(own, far, own_side, far_side)
    gathered = lax.all_gather(both, "band", axis_index_groups=over_z)
    up, down = shift(four, 1, 0, 0), shift(four, -1, 0, 0)

    shared, single = pack(odd, pair_kdiff, diff_core, diff_far, stored_kernel_index, kernels)
    mine = lax.all_to_all(shared, "band", 0, 0, axis_index_groups=over_yx)
    half = swap_groups(mine, 1)
    single, up, down = lax.optimization_barrier((single, up, down))
    over = shift(up[:2], 1, 0, 0), shift(down[2:], -1, 0, 0)
    kern = lax.all_to_all(single, "band", 0, 0, axis_index_groups=over_yx)

    place = jnp.stack([(y - dy) % NY * NX + (x - dx) % NX for dy in range(NY) for dx in range(NX)])
    m_out, rows, cols = mix(place, odd, four, up, over, down, gathered, mine, half, kern)
    m_own = swap_groups(m_out, 1)
    left, right = prepare(rows, cols)
    total = reduce_windows(project(m_own, left, right))
    flat = total.reshape(2, 8 * NB)
    flat = lax.dynamic_slice(flat, (0, band * 27 % 4 * 108), (2, 27 * 108))
    return flat[None]


def solution(mesh):
    return jax.shard_map(
        on_device,
        mesh=mesh,
        in_specs=(P("kgrp", None, "band", None), P(None, None, "band", None), P("kgrp"), P()),
        out_specs=P("kgrp", None, "band"),
        check_vma=False,
    )
```

```python
import jax
import jax.numpy as jnp
from jax import lax
from jax.experimental import pallas as pl
from jax.experimental.pallas import tpu as pltpu
from jax.sharding import PartitionSpec as P

NB = 432
SLAB = 64
NY, NX, NZ = 4, 2, 8
GROUPS = NY * NX
BLOCK = NZ * SLAB
WHOLE = 384
REST = NB - WHOLE
TAIL = 2 * WHOLE
LANES = TAIL + 128
EARLY = 5
VMEM = 24 * 1024 * 1024

IN_VMEM = pl.BlockSpec(memory_space=pltpu.VMEM)
IN_SMEM = pl.BlockSpec(memory_space=pltpu.SMEM)
ANYWHERE = pl.BlockSpec(memory_space=pl.ANY)
PARAMS = pltpu.CompilerParams(vmem_limit_bytes=VMEM)


def band_route(dy, dx, dz):
    route = []
    for y in range(NY):
        for x in range(NX):
            for z in range(NZ):
                there = ((y + dy) % NY * NX + (x + dx) % NX) * NZ + (z + dz) % NZ
                route.append(((y * NX + x) * NZ + z, there))
    return route


def shift(block, dy, dx, dz):
    return lax.ppermute(block, "band", band_route(dy, dx, dz))


def swap_groups(block, bit):
    return lax.ppermute(block, "kgrp", [(k, k ^ bit) for k in range(4)])


def other_side(block):
    route = [(i, j) for i, j in band_route(0, 1, 0)]
    both = [((k ^ 2) * 64 + i, k * 64 + j) for k in range(4) for i, j in route]
    return lax.ppermute(block, ("kgrp", "band"), both)


def dot(a, b, a_axis, b_axis):
    dims = (((a_axis,), (b_axis,)), ((), ()))
    return lax.dot_general(a, b, dims, preferred_element_type=jnp.float32)


def near(array):
    return pltpu.with_memory_space_constraint(array, pltpu.VMEM)


def away(array):
    return pltpu.with_memory_space_constraint(array, pltpu.HBM)


def lay_body(orbit_ref, out_ref):
    gap = jnp.zeros((SLAB, 64 - REST), jnp.float32)
    real, imag = orbit_ref[0, 0], orbit_ref[0, 1]
    out_ref[:, :WHOLE] = real[:, :WHOLE]
    out_ref[:, WHOLE:TAIL] = imag[:, :WHOLE]
    last = [real[:, WHOLE:].astype(jnp.float32), gap, imag[:, WHOLE:].astype(jnp.float32), gap]
    out_ref[:, TAIL:] = jnp.concatenate(last, axis=1).astype(jnp.bfloat16)


def lay(orbitals):
    return pl.pallas_call(
        lay_body,
        out_shape=pltpu.VMEM((SLAB, LANES), jnp.bfloat16),
        in_specs=[IN_VMEM],
        out_specs=IN_VMEM,
        name="lay",
    )(orbitals)


def turned(rows):
    last = rows[:, TAIL:].astype(jnp.float32)
    lane = lax.broadcasted_iota(jnp.int32, last.shape, 1)
    last = pltpu.roll(last, 64, 1) * jnp.where(lane < 64, 1.0, -1.0)
    return jnp.concatenate(
        [rows[:, WHOLE:TAIL], -rows[:, :WHOLE], last.astype(rows.dtype)], axis=1
    )


def pack_body(odd_ref, own_ref, core_ref, far_ref, stored_ref, kernels_ref, shared_ref, single_ref, sem):
    odd = odd_ref[0] == 1
    own, core, far = stored_ref[own_ref[0]], stored_ref[core_ref[0]], stored_ref[far_ref[0]]
    shared = jnp.where(odd, own, core)
    single = jnp.where(odd, core, far)
    copies = []
    for i in range(GROUPS):
        at = pl.ds(i * BLOCK, BLOCK)
        copies += [
            pltpu.make_async_copy(
                kernels_ref.at[shared, odd_ref[0], :, at], shared_ref.at[i], sem.at[0, i]
            ),
            pltpu.make_async_copy(
                kernels_ref.at[single, :, :, at], single_ref.at[i], sem.at[1, i]
            ),
        ]
    for copy in copies:
        copy.start()
    for copy in copies:
        copy.wait()


def pack(odd, own, core, far, stored, kernels):
    return pl.pallas_call(
        pack_body,
        out_shape=[
            pltpu.VMEM((GROUPS, SLAB, BLOCK), jnp.bfloat16),
            pltpu.VMEM((GROUPS, 2, SLAB, BLOCK), jnp.bfloat16),
        ],
        in_specs=[IN_SMEM] * 5 + [ANYWHERE],
        out_specs=[IN_VMEM] * 2,
        scratch_shapes=[pltpu.SemaphoreType.DMA((2, GROUPS))],
        compiler_params=PARAMS,
        name="pack",
    )(odd, own, core, far, stored, away(kernels))


def mix_body(place_ref, slot_ref, odd_ref, *refs):
    four_ref, up_ref, over_here, over_side, down_ref = refs[:5]
    cols, (mine_ref, half_ref, kern_ref) = refs[5 : 5 + NZ], refs[5 + NZ : 8 + NZ]
    m_ref, row_ref, col_ref, other_rows, other_cols, sem = refs[8 + NZ :]

    def row_at(dy, side):
        return pl.ds(pl.multiple_of(place_ref[dy * NX + side] * SLAB, SLAB), SLAB)

    def col_at(i):
        return pl.ds(pl.multiple_of(slot_ref[i] * SLAB, SLAB), SLAB)

    moves = []
    for side, piece in enumerate((over_here, over_side)):
        moves.append((piece.at[0], row_ref.at[row_at(2, side), :]))
        moves.append((piece.at[1], other_rows.at[row_at(2, side), :]))
    for i, piece in enumerate(cols[:EARLY]):
        moves.append((piece.at[0], col_ref.at[col_at(i), :]))
        moves.append((piece.at[1], other_cols.at[col_at(i), :]))
    copies = [pltpu.make_async_copy(*move, sem.at[i]) for i, move in enumerate(moves)]
    for copy in copies:
        copy.start()
    for dy, piece in ((0, four_ref), (1, up_ref), (3, down_ref)):
        for side in range(NX):
            row_ref[row_at(dy, side), :] = piece[2 * side]
            other_rows[row_at(dy, side), :] = piece[2 * side + 1]
    for i in range(EARLY, NZ):
        col_ref[col_at(i), :] = cols[i][0]
        other_cols[col_at(i), :] = cols[i][1]
    for copy in copies:
        copy.wait()
    per = BLOCK // 2
    odd = odd_ref[0] == 1
    sign = jnp.where(odd, -1.0, 1.0).astype(jnp.float32)
    a, a_other = row_ref[...], other_rows[...]
    a_turned, other_turned = turned(a), turned(a_other)
    for part in range(2):
        at = pl.ds(part * per, per)
        b = col_ref[at, :]
        p_re, p_im = dot(a, b, 1, 1), dot(a_turned, b, 1, 1)
        mine = mine_ref[:, :, at].reshape(BLOCK, per)
        other = half_ref[:, :, at].reshape(BLOCK, per)
        k_re = jnp.where(odd, other, mine).astype(jnp.float32)
        k_im = jnp.where(odd, mine, other).astype(jnp.float32) * sign
        total_re = k_re * p_re - k_im * p_im
        total_im = k_re * p_im + k_im * p_re
        b = other_cols[at, :]
        p_re, p_im = dot(a_other, b, 1, 1), dot(other_turned, b, 1, 1)
        k_re = kern_ref[:, 0, :, at].reshape(BLOCK, per).astype(jnp.float32)
        k_im = kern_ref[:, 1, :, at].reshape(BLOCK, per).astype(jnp.float32) * -sign
        total_re += k_re * p_re - k_im * p_im
        total_im += k_re * p_im + k_im * p_re
        m_ref[:, at] = total_re.astype(jnp.bfloat16)
        m_ref[:, pl.ds(BLOCK + part * per, per)] = total_im.astype(jnp.bfloat16)


def mix(place, slots, odd, four, up, over, down, cols, *kerns):
    points = pltpu.VMEM((BLOCK, LANES), jnp.bfloat16)
    in_hbm = pl.BlockSpec(memory_space=pltpu.HBM)
    late = NZ - EARLY
    specs = [IN_VMEM] * 2 + [in_hbm] * 2 + [IN_VMEM] + [in_hbm] * EARLY + [IN_VMEM] * (late + 3)
    arrays = [near(four), near(up), *map(away, over), near(down)]
    arrays += [*map(away, cols[:EARLY]), *map(near, cols[EARLY:]), *map(near, kerns)]
    return pl.pallas_call(
        mix_body,
        out_shape=[pltpu.VMEM((BLOCK, 2 * BLOCK), jnp.bfloat16), points, points],
        in_specs=[IN_SMEM] * 3 + specs,
        out_specs=[IN_VMEM] * 3,
        scratch_shapes=[pltpu.VMEM((BLOCK, LANES), jnp.bfloat16)] * 2
        + [pltpu.SemaphoreType.DMA((2 * NX + 2 * EARLY,))],
        compiler_params=PARAMS,
        name="mix",
    )(place, slots, odd, *arrays)


def prepare_body(row_ref, col_ref, left_ref, right_ref):
    flipped = row_ref[...].T
    left_ref[pl.ds(0, WHOLE), :BLOCK] = flipped[:WHOLE]
    left_ref[pl.ds(WHOLE, REST), :BLOCK] = flipped[TAIL : TAIL + REST]
    left_ref[pl.ds(0, WHOLE), BLOCK:] = flipped[WHOLE:TAIL]
    left_ref[pl.ds(WHOLE, REST), BLOCK:] = flipped[TAIL + 64 : TAIL + 64 + REST]
    col = col_ref[...]
    right_ref[pl.ds(0, BLOCK), :] = col
    right_ref[pl.ds(BLOCK, BLOCK), :] = -turned(col)


def prepare(rows, cols):
    return pl.pallas_call(
        prepare_body,
        out_shape=[
            pltpu.VMEM((NB, 2 * BLOCK), jnp.bfloat16),
            pltpu.VMEM((2 * BLOCK, LANES), jnp.bfloat16),
        ],
        in_specs=[IN_VMEM] * 2,
        out_specs=[IN_VMEM] * 2,
        compiler_params=PARAMS,
        name="prepare",
    )(near(rows), near(cols))


def place_of(d):
    yx, z = d // NZ, d % NZ
    return (yx * 2 + z % 2) * (NZ // 2) + z // 2


def project_body(m_ref, left_ref, right_ref, out_ref, x_ref, part_ref, sem):
    y = dot(m_ref[...], right_ref[...], 1, 0)
    high = y.astype(jnp.bfloat16)
    low = (y - high.astype(jnp.float32)).astype(jnp.bfloat16)
    high = jnp.concatenate([high, turned(high)], axis=0)
    low = jnp.concatenate([low, turned(low)], axis=0)
    x_ref[pl.ds(NB, 8), :] = jnp.zeros((8, LANES), jnp.float32)
    copies = []
    for part, (start, size) in enumerate(((0, 224), (224, 208))):
        at = pl.ds(start, size)
        x_ref[at, :] = -(dot(left_ref[at, :], high, 1, 0) + dot(left_ref[at, :], low, 1, 0))
        some = GROUPS * NZ // 2
        for d in range(part * some, (part + 1) * some):
            part_ref[place_of(d)] = x_ref[pl.ds(27 * d // 4, 8), :].astype(jnp.bfloat16)
        chosen = pl.ds(part * some, some)
        copy = pltpu.make_async_copy(part_ref.at[chosen], out_ref.at[chosen], sem.at[part])
        copy.start()
        copies.append(copy)
    for copy in copies:
        copy.wait()


def project(m, left, right):
    windows = (GROUPS * NZ, 8, LANES)
    return pl.pallas_call(
        project_body,
        out_shape=jax.ShapeDtypeStruct(windows, jnp.bfloat16),
        in_specs=[IN_VMEM] * 3,
        out_specs=pl.BlockSpec(memory_space=pltpu.HBM),
        scratch_shapes=[
            pltpu.VMEM((NB + 8, LANES), jnp.float32),
            pltpu.VMEM(windows, jnp.bfloat16),
            pltpu.SemaphoreType.DMA((2,)),
        ],
        compiler_params=PARAMS,
        name="project",
    )(near(m), near(left), near(right))


def bundle_body(own_ref, far_ref, own_side, far_side, four_ref, both_ref):
    for i, ref in enumerate((own_ref, far_ref, own_side, far_side)):
        four_ref[i] = ref[...]
    both_ref[0] = own_ref[...]
    both_ref[1] = far_ref[...]


def bundle(*blocks):
    return pl.pallas_call(
        bundle_body,
        out_shape=[
            pltpu.VMEM((4, SLAB, LANES), jnp.bfloat16),
            pltpu.VMEM((2, SLAB, LANES), jnp.bfloat16),
        ],
        in_specs=[IN_VMEM] * 4,
        out_specs=[IN_VMEM] * 2,
        compiler_params=PARAMS,
        name="bundle",
    )(*map(near, blocks))


def reduce_windows(windows):
    quads = NZ // 2
    wide = [[g * NZ + 2 * j + i for g in range(GROUPS) for i in range(2)] for j in range(quads)]
    deep = [[g * NZ + 2 * j + i for j in range(quads)] for g in range(GROUPS) for i in range(2)]
    parts = windows.reshape(2 * GROUPS, quads, 8, LANES)
    parts = lax.all_to_all(parts, "band", 0, 0, axis_index_groups=wide)
    parts = jnp.sum(parts.astype(jnp.float32), axis=0)
    total = jnp.sum(lax.all_to_all(parts, "band", 0, 0, axis_index_groups=deep), axis=0)
    real = jnp.concatenate([total[:, :WHOLE], total[:, TAIL : TAIL + REST]], axis=1)
    imag = jnp.concatenate([total[:, WHOLE:TAIL], total[:, TAIL + 64 : TAIL + 64 + REST]], axis=1)
    return jnp.stack([real, imag])


def on_device(orbitals, kernels, pair_kdiff, stored_kernel_index):
    group = lax.axis_index("kgrp")
    band = lax.axis_index("band")
    y, x, z = band // (NX * NZ), band // NZ % NX, band % NZ
    odd = (group % 2).reshape(1)

    own = lay(orbitals)
    first = (
        swap_groups(pair_kdiff, 1),
        swap_groups(pair_kdiff, 2),
        swap_groups(own, 2),
        shift(own, 0, 1, 0),
        other_side(own),
    )
    diff_core, diff_far = first[:2]
    far, own_side, far_side = lax.optimization_barrier(first)[2:]

    over_yx = [[g * NZ + i for g in range(GROUPS)] for i in range(NZ)]
    four, both = bundle(own, far, own_side, far_side)
    cols, ahead, behind = [both], both, both
    for _ in range(3):
        ahead, behind = shift(ahead, 0, 0, 1), shift(behind, 0, 0, -1)
        cols += [ahead, behind]
    cols.append(shift(ahead, 0, 0, 1))
    up, down = shift(four, 1, 0, 0), shift(four, -1, 0, 0)

    shared, single = pack(odd, pair_kdiff, diff_core, diff_far, stored_kernel_index, kernels)
    mine = lax.all_to_all(shared, "band", 0, 0, axis_index_groups=over_yx)
    half = swap_groups(mine, 1)
    single, up, down = lax.optimization_barrier((single, up, down))
    over = shift(up[:2], 1, 0, 0), shift(down[2:], -1, 0, 0)
    kern = lax.all_to_all(single, "band", 0, 0, axis_index_groups=over_yx)

    place = jnp.stack([(y - dy) % NY * NX + (x - dx) % NX for dy in range(NY) for dx in range(NX)])
    slots = jnp.stack([(z + i) % NZ for i in (0, -1, 1, -2, 2, -3, 3, -4)])
    m_out, rows, cols = mix(place, slots, odd, four, up, over, down, cols, mine, half, kern)
    m_own = swap_groups(m_out, 1)
    left, right = prepare(rows, cols)
    total = reduce_windows(project(m_own, left, right))
    flat = total.reshape(2, 8 * NB)
    flat = lax.dynamic_slice(flat, (0, band * 27 % 4 * 108), (2, 27 * 108))
    return flat[None]


def solution(mesh):
    return jax.shard_map(
        on_device,
        mesh=mesh,
        in_specs=(P("kgrp", None, "band", None), P(None, None, "band", None), P("kgrp"), P()),
        out_specs=P("kgrp", None, "band"),
        check_vma=False,
    )
```

```python
import jax
import jax.numpy as jnp
from jax import lax
from jax.experimental import pallas as pl
from jax.experimental.pallas import tpu as pltpu
from jax.sharding import PartitionSpec as P

NB = 432
SLAB = 64
NY, NX, NZ = 4, 2, 8
GROUPS = NY * NX
BLOCK = NZ * SLAB
WHOLE = 384
REST = NB - WHOLE
TAIL = 2 * WHOLE
LANES = TAIL + 128
EARLY = 5
VMEM = 24 * 1024 * 1024

IN_VMEM = pl.BlockSpec(memory_space=pltpu.VMEM)
IN_SMEM = pl.BlockSpec(memory_space=pltpu.SMEM)
ANYWHERE = pl.BlockSpec(memory_space=pl.ANY)
PARAMS = pltpu.CompilerParams(vmem_limit_bytes=VMEM)


def band_route(dy, dx, dz):
    route = []
    for y in range(NY):
        for x in range(NX):
            for z in range(NZ):
                there = ((y + dy) % NY * NX + (x + dx) % NX) * NZ + (z + dz) % NZ
                route.append(((y * NX + x) * NZ + z, there))
    return route


def shift(block, dy, dx, dz):
    return lax.ppermute(block, "band", band_route(dy, dx, dz))


def swap_groups(block, bit):
    return lax.ppermute(block, "kgrp", [(k, k ^ bit) for k in range(4)])


def other_side(block):
    route = [(i, j) for i, j in band_route(0, 1, 0)]
    both = [((k ^ 2) * 64 + i, k * 64 + j) for k in range(4) for i, j in route]
    return lax.ppermute(block, ("kgrp", "band"), both)


def dot(a, b, a_axis, b_axis):
    dims = (((a_axis,), (b_axis,)), ((), ()))
    return lax.dot_general(a, b, dims, preferred_element_type=jnp.float32)


def near(array):
    return pltpu.with_memory_space_constraint(array, pltpu.VMEM)


def away(array):
    return pltpu.with_memory_space_constraint(array, pltpu.HBM)


def lay_body(orbit_ref, out_ref):
    gap = jnp.zeros((SLAB, 64 - REST), jnp.float32)
    real, imag = orbit_ref[0, 0], orbit_ref[0, 1]
    out_ref[:, :WHOLE] = real[:, :WHOLE]
    out_ref[:, WHOLE:TAIL] = imag[:, :WHOLE]
    last = [real[:, WHOLE:].astype(jnp.float32), gap, imag[:, WHOLE:].astype(jnp.float32), gap]
    out_ref[:, TAIL:] = jnp.concatenate(last, axis=1).astype(jnp.bfloat16)


def lay(orbitals):
    return pl.pallas_call(
        lay_body,
        out_shape=pltpu.VMEM((SLAB, LANES), jnp.bfloat16),
        in_specs=[IN_VMEM],
        out_specs=IN_VMEM,
        name="lay",
    )(orbitals)


def turned(rows):
    last = rows[:, TAIL:].astype(jnp.float32)
    lane = lax.broadcasted_iota(jnp.int32, last.shape, 1)
    last = pltpu.roll(last, 64, 1) * jnp.where(lane < 64, 1.0, -1.0)
    return jnp.concatenate(
        [rows[:, WHOLE:TAIL], -rows[:, :WHOLE], last.astype(rows.dtype)], axis=1
    )


def pack_body(slot_ref, stored_ref, kernels_ref, out_ref, sem):
    planes = out_ref.shape[1]
    kernel = kernels_ref.at[stored_ref[slot_ref[0]]]
    copies = []
    for i in range(GROUPS):
        block = kernel.at[:, :, pl.ds(i * BLOCK, BLOCK)]
        if planes == 1:
            block = block.at[pl.ds(slot_ref[1], 1)]
        copies.append(pltpu.make_async_copy(block, out_ref.at[i], sem.at[i]))
    for copy in copies:
        copy.start()
    for copy in copies:
        copy.wait()


def pack(slot, stored, kernels, planes):
    return pl.pallas_call(
        pack_body,
        out_shape=jax.ShapeDtypeStruct((GROUPS, planes, SLAB, BLOCK), jnp.bfloat16),
        in_specs=[IN_SMEM] * 2 + [pl.BlockSpec(memory_space=pltpu.HBM)],
        out_specs=IN_VMEM,
        scratch_shapes=[pltpu.SemaphoreType.DMA((GROUPS,))],
        compiler_params=PARAMS,
        name="pack",
    )(slot, stored, away(kernels))


def mix_body(place_ref, slot_ref, odd_ref, *refs):
    four_ref, up_ref, over_here, over_side, down_ref = refs[:5]
    cols, (mine_ref, half_ref, kern_ref) = refs[5 : 5 + NZ], refs[5 + NZ : 8 + NZ]
    m_ref, row_ref, col_ref, other_rows, other_cols, sem = refs[8 + NZ :]

    def row_at(dy, side):
        return pl.ds(pl.multiple_of(place_ref[dy * NX + side] * SLAB, SLAB), SLAB)

    def col_at(i):
        return pl.ds(pl.multiple_of(slot_ref[i] * SLAB, SLAB), SLAB)

    moves = []
    for side, piece in enumerate((over_here, over_side)):
        moves.append((piece.at[0], row_ref.at[row_at(2, side), :]))
        moves.append((piece.at[1], other_rows.at[row_at(2, side), :]))
    for i, piece in enumerate(cols[:EARLY]):
        moves.append((piece.at[0], col_ref.at[col_at(i), :]))
        moves.append((piece.at[1], other_cols.at[col_at(i), :]))
    copies = [pltpu.make_async_copy(*move, sem.at[i]) for i, move in enumerate(moves)]
    for copy in copies:
        copy.start()
    for dy, piece in ((0, four_ref), (1, up_ref), (3, down_ref)):
        for side in range(NX):
            row_ref[row_at(dy, side), :] = piece[2 * side]
            other_rows[row_at(dy, side), :] = piece[2 * side + 1]
    for i in range(EARLY, NZ):
        col_ref[col_at(i), :] = cols[i][0]
        other_cols[col_at(i), :] = cols[i][1]
    for copy in copies:
        copy.wait()
    per = BLOCK // 2
    odd = odd_ref[0] == 1
    sign = jnp.where(odd, -1.0, 1.0).astype(jnp.float32)
    a, a_other = row_ref[...], other_rows[...]
    a_turned, other_turned = turned(a), turned(a_other)
    for part in range(2):
        at = pl.ds(part * per, per)
        b = col_ref[at, :]
        p_re, p_im = dot(a, b, 1, 1), dot(a_turned, b, 1, 1)
        mine = mine_ref[:, 0, :, at].reshape(BLOCK, per)
        other = half_ref[:, 0, :, at].reshape(BLOCK, per)
        k_re = jnp.where(odd, other, mine).astype(jnp.float32)
        k_im = jnp.where(odd, mine, other).astype(jnp.float32) * sign
        total_re = k_re * p_re - k_im * p_im
        total_im = k_re * p_im + k_im * p_re
        b = other_cols[at, :]
        p_re, p_im = dot(a_other, b, 1, 1), dot(other_turned, b, 1, 1)
        k_re = kern_ref[:, 0, :, at].reshape(BLOCK, per).astype(jnp.float32)
        k_im = kern_ref[:, 1, :, at].reshape(BLOCK, per).astype(jnp.float32) * -sign
        total_re += k_re * p_re - k_im * p_im
        total_im += k_re * p_im + k_im * p_re
        m_ref[:, at] = total_re.astype(jnp.bfloat16)
        m_ref[:, pl.ds(BLOCK + part * per, per)] = total_im.astype(jnp.bfloat16)


def mix(place, slots, odd, four, up, over, down, cols, *kerns):
    points = pltpu.VMEM((BLOCK, LANES), jnp.bfloat16)
    in_hbm = pl.BlockSpec(memory_space=pltpu.HBM)
    late = NZ - EARLY
    specs = [IN_VMEM] * 2 + [in_hbm] * 2 + [IN_VMEM] + [in_hbm] * EARLY + [IN_VMEM] * (late + 3)
    arrays = [near(four), near(up), *map(away, over), near(down)]
    arrays += [*map(away, cols[:EARLY]), *map(near, cols[EARLY:]), *map(near, kerns)]
    return pl.pallas_call(
        mix_body,
        out_shape=[pltpu.VMEM((BLOCK, 2 * BLOCK), jnp.bfloat16), points, points],
        in_specs=[IN_SMEM] * 3 + specs,
        out_specs=[IN_VMEM] * 3,
        scratch_shapes=[pltpu.VMEM((BLOCK, LANES), jnp.bfloat16)] * 2
        + [pltpu.SemaphoreType.DMA((2 * NX + 2 * EARLY,))],
        compiler_params=PARAMS,
        name="mix",
    )(place, slots, odd, *arrays)


def prepare_body(row_ref, col_ref, left_ref, right_ref):
    flipped = row_ref[...].T
    left_ref[pl.ds(0, WHOLE), :BLOCK] = flipped[:WHOLE]
    left_ref[pl.ds(WHOLE, REST), :BLOCK] = flipped[TAIL : TAIL + REST]
    left_ref[pl.ds(0, WHOLE), BLOCK:] = flipped[WHOLE:TAIL]
    left_ref[pl.ds(WHOLE, REST), BLOCK:] = flipped[TAIL + 64 : TAIL + 64 + REST]
    col = col_ref[...]
    right_ref[pl.ds(0, BLOCK), :] = col
    right_ref[pl.ds(BLOCK, BLOCK), :] = -turned(col)


def prepare(rows, cols):
    return pl.pallas_call(
        prepare_body,
        out_shape=[
            pltpu.VMEM((NB, 2 * BLOCK), jnp.bfloat16),
            pltpu.VMEM((2 * BLOCK, LANES), jnp.bfloat16),
        ],
        in_specs=[IN_VMEM] * 2,
        out_specs=[IN_VMEM] * 2,
        compiler_params=PARAMS,
        name="prepare",
    )(near(rows), near(cols))


def place_of(d):
    yx, z = d // NZ, d % NZ
    return (yx * 2 + z % 2) * (NZ // 2) + z // 2


def project_body(m_ref, left_ref, right_ref, out_ref, x_ref, part_ref, sem):
    y = dot(m_ref[...], right_ref[...], 1, 0)
    high = y.astype(jnp.bfloat16)
    low = (y - high.astype(jnp.float32)).astype(jnp.bfloat16)
    high = jnp.concatenate([high, turned(high)], axis=0)
    low = jnp.concatenate([low, turned(low)], axis=0)
    x_ref[pl.ds(NB, 8), :] = jnp.zeros((8, LANES), jnp.float32)
    copies = []
    for part, (start, size) in enumerate(((0, 224), (224, 208))):
        at = pl.ds(start, size)
        x_ref[at, :] = -(dot(left_ref[at, :], high, 1, 0) + dot(left_ref[at, :], low, 1, 0))
        some = GROUPS * NZ // 2
        for d in range(part * some, (part + 1) * some):
            part_ref[place_of(d)] = x_ref[pl.ds(27 * d // 4, 8), :].astype(jnp.bfloat16)
        chosen = pl.ds(part * some, some)
        copy = pltpu.make_async_copy(part_ref.at[chosen], out_ref.at[chosen], sem.at[part])
        copy.start()
        copies.append(copy)
    for copy in copies:
        copy.wait()


def project(m, left, right):
    windows = (GROUPS * NZ, 8, LANES)
    return pl.pallas_call(
        project_body,
        out_shape=jax.ShapeDtypeStruct(windows, jnp.bfloat16),
        in_specs=[IN_VMEM] * 3,
        out_specs=pl.BlockSpec(memory_space=pltpu.HBM),
        scratch_shapes=[
            pltpu.VMEM((NB + 8, LANES), jnp.float32),
            pltpu.VMEM(windows, jnp.bfloat16),
            pltpu.SemaphoreType.DMA((2,)),
        ],
        compiler_params=PARAMS,
        name="project",
    )(near(m), near(left), near(right))


def bundle_body(own_ref, far_ref, own_side, far_side, four_ref, both_ref):
    for i, ref in enumerate((own_ref, far_ref, own_side, far_side)):
        four_ref[i] = ref[...]
    both_ref[0] = own_ref[...]
    both_ref[1] = far_ref[...]


def bundle(*blocks):
    return pl.pallas_call(
        bundle_body,
        out_shape=[
            pltpu.VMEM((4, SLAB, LANES), jnp.bfloat16),
            pltpu.VMEM((2, SLAB, LANES), jnp.bfloat16),
        ],
        in_specs=[IN_VMEM] * 4,
        out_specs=[IN_VMEM] * 2,
        compiler_params=PARAMS,
        name="bundle",
    )(*map(near, blocks))


def reduce_windows(windows):
    quads = NZ // 2
    wide = [[g * NZ + 2 * j + i for g in range(GROUPS) for i in range(2)] for j in range(quads)]
    deep = [[g * NZ + 2 * j + i for j in range(quads)] for g in range(GROUPS) for i in range(2)]
    parts = windows.reshape(2 * GROUPS, quads, 8, LANES)
    parts = lax.all_to_all(parts, "band", 0, 0, axis_index_groups=wide)
    parts = jnp.sum(parts.astype(jnp.float32), axis=0)
    total = jnp.sum(lax.all_to_all(parts, "band", 0, 0, axis_index_groups=deep), axis=0)
    real = jnp.concatenate([total[:, :WHOLE], total[:, TAIL : TAIL + REST]], axis=1)
    imag = jnp.concatenate([total[:, WHOLE:TAIL], total[:, TAIL + 64 : TAIL + 64 + REST]], axis=1)
    return jnp.stack([real, imag])


def on_device(orbitals, kernels, pair_kdiff, stored_kernel_index):
    group = lax.axis_index("kgrp")
    band = lax.axis_index("band")
    y, x, z = band // (NX * NZ), band // NZ % NX, band % NZ
    odd = (group % 2).reshape(1)

    own = lay(orbitals)
    first = (
        swap_groups(pair_kdiff, 1),
        swap_groups(pair_kdiff, 2),
        swap_groups(own, 2),
        shift(own, 0, 1, 0),
        other_side(own),
    )
    diff_core, diff_far = first[:2]
    far, own_side, far_side = lax.optimization_barrier(first)[2:]

    over_yx = [[g * NZ + i for g in range(GROUPS)] for i in range(NZ)]
    four, both = bundle(own, far, own_side, far_side)
    sends = shift(four, 1, 0, 0), shift(four, -1, 0, 0), shift(both, 0, 0, 1), shift(both, 0, 0, -1)
    up, down, ahead, behind = lax.optimization_barrier(sends)
    cols = [both, ahead, behind]
    over = shift(up[:2], 1, 0, 0), shift(down[2:], -1, 0, 0)
    ahead, behind = shift(ahead, 0, 0, 1), shift(behind, 0, 0, -1)
    *over, ahead, behind = lax.optimization_barrier((*over, ahead, behind))
    cols += [ahead, behind]
    ahead, behind = shift(ahead, 0, 0, 1), shift(behind, 0, 0, -1)
    cols += [ahead, behind, shift(ahead, 0, 0, 1)]

    is_odd = odd[0] == 1
    shared = jnp.stack([jnp.where(is_odd, pair_kdiff[0], diff_core[0]), odd[0]])
    single = jnp.where(is_odd, diff_core, diff_far)
    shared = pack(shared, stored_kernel_index, kernels, 1)
    single = pack(single, stored_kernel_index, kernels, 2)
    mine = lax.all_to_all(shared, "band", 0, 0, axis_index_groups=over_yx)
    half = swap_groups(mine, 1)
    single, up, down = lax.optimization_barrier((single, up, down))
    kern = lax.all_to_all(single, "band", 0, 0, axis_index_groups=over_yx)

    place = jnp.stack([(y - dy) % NY * NX + (x - dx) % NX for dy in range(NY) for dx in range(NX)])
    slots = jnp.stack([(z + i) % NZ for i in (0, -1, 1, -2, 2, -3, 3, -4)])
    m_out, rows, cols = mix(place, slots, odd, four, up, over, down, cols, mine, half, kern)
    m_own = swap_groups(m_out, 1)
    left, right = prepare(rows, cols)
    total = reduce_windows(project(m_own, left, right))
    flat = total.reshape(2, 8 * NB)
    flat = lax.dynamic_slice(flat, (0, band * 27 % 4 * 108), (2, 27 * 108))
    return flat[None]


def solution(mesh):
    return jax.shard_map(
        on_device,
        mesh=mesh,
        in_specs=(P("kgrp", None, "band", None), P(None, None, "band", None), P("kgrp"), P()),
        out_specs=P("kgrp", None, "band"),
        check_vma=False,
    )
```

```python
import jax
import jax.numpy as jnp
from jax import lax
from jax.experimental import pallas as pl
from jax.experimental.pallas import tpu as pltpu
from jax.sharding import PartitionSpec as P

NB = 432
SLAB = 64
NY, NX, NZ = 4, 2, 8
GROUPS = NY * NX
BLOCK = NZ * SLAB
WHOLE = 384
REST = NB - WHOLE
TAIL = 2 * WHOLE
LANES = TAIL + 128
EARLY = 6
VMEM = 24 * 1024 * 1024

IN_VMEM = pl.BlockSpec(memory_space=pltpu.VMEM)
IN_SMEM = pl.BlockSpec(memory_space=pltpu.SMEM)
ANYWHERE = pl.BlockSpec(memory_space=pl.ANY)
PARAMS = pltpu.CompilerParams(vmem_limit_bytes=VMEM)


def band_route(dy, dx, dz):
    route = []
    for y in range(NY):
        for x in range(NX):
            for z in range(NZ):
                there = ((y + dy) % NY * NX + (x + dx) % NX) * NZ + (z + dz) % NZ
                route.append(((y * NX + x) * NZ + z, there))
    return route


def shift(block, dy, dx, dz):
    return lax.ppermute(block, "band", band_route(dy, dx, dz))


def swap_groups(block, bit):
    return lax.ppermute(block, "kgrp", [(k, k ^ bit) for k in range(4)])


def other_side(block):
    route = [(i, j) for i, j in band_route(0, 1, 0)]
    both = [((k ^ 2) * 64 + i, k * 64 + j) for k in range(4) for i, j in route]
    return lax.ppermute(block, ("kgrp", "band"), both)


def dot(a, b, a_axis, b_axis):
    dims = (((a_axis,), (b_axis,)), ((), ()))
    return lax.dot_general(a, b, dims, preferred_element_type=jnp.float32)


def near(array):
    return pltpu.with_memory_space_constraint(array, pltpu.VMEM)


def away(array):
    return pltpu.with_memory_space_constraint(array, pltpu.HBM)


def lay_body(orbit_ref, out_ref):
    gap = jnp.zeros((SLAB, 64 - REST), jnp.float32)
    real, imag = orbit_ref[0, 0], orbit_ref[0, 1]
    out_ref[:, :WHOLE] = real[:, :WHOLE]
    out_ref[:, WHOLE:TAIL] = imag[:, :WHOLE]
    last = [real[:, WHOLE:].astype(jnp.float32), gap, imag[:, WHOLE:].astype(jnp.float32), gap]
    out_ref[:, TAIL:] = jnp.concatenate(last, axis=1).astype(jnp.bfloat16)


def lay(orbitals):
    return pl.pallas_call(
        lay_body,
        out_shape=pltpu.VMEM((SLAB, LANES), jnp.bfloat16),
        in_specs=[IN_VMEM],
        out_specs=IN_VMEM,
        name="lay",
    )(orbitals)


def turned(rows):
    last = rows[:, TAIL:].astype(jnp.float32)
    lane = lax.broadcasted_iota(jnp.int32, last.shape, 1)
    last = pltpu.roll(last, 64, 1) * jnp.where(lane < 64, 1.0, -1.0)
    return jnp.concatenate(
        [rows[:, WHOLE:TAIL], -rows[:, :WHOLE], last.astype(rows.dtype)], axis=1
    )


def pack_body(odd_ref, own_ref, core_ref, far_ref, stored_ref, kernels_ref, out_ref, sem):
    odd = odd_ref[0] == 1
    own, core, far = stored_ref[own_ref[0]], stored_ref[core_ref[0]], stored_ref[far_ref[0]]
    shared = jnp.where(odd, own, core)
    single = jnp.where(odd, core, far)
    copies = []
    for i in range(GROUPS):
        at = pl.ds(i * BLOCK, BLOCK)
        half = kernels_ref.at[shared, odd_ref[0], :, at]
        copies.append(pltpu.make_async_copy(half, out_ref.at[i, 0], sem.at[0, i]))
        both = kernels_ref.at[single, :, :, at]
        copies.append(pltpu.make_async_copy(both, out_ref.at[i, pl.ds(1, 2)], sem.at[1, i]))
    for copy in copies:
        copy.start()
    for copy in copies:
        copy.wait()


def pack(odd, own, core, far, stored, kernels):
    return pl.pallas_call(
        pack_body,
        out_shape=jax.ShapeDtypeStruct((GROUPS, 3, SLAB, BLOCK), jnp.bfloat16),
        in_specs=[IN_SMEM] * 5 + [pl.BlockSpec(memory_space=pltpu.HBM)],
        out_specs=IN_VMEM,
        scratch_shapes=[pltpu.SemaphoreType.DMA((2, GROUPS))],
        compiler_params=PARAMS,
        name="pack",
    )(odd, own, core, far, stored, away(kernels))


def mix_body(place_ref, slot_ref, odd_ref, *refs):
    four_ref, up_ref, over_here, over_side, down_ref = refs[:5]
    cols, (half_ref, kern_ref) = refs[5 : 5 + NZ], refs[5 + NZ : 7 + NZ]
    m_ref, row_ref, col_ref, other_rows, other_cols, sem = refs[7 + NZ :]

    def row_at(dy, side):
        return pl.ds(pl.multiple_of(place_ref[dy * NX + side] * SLAB, SLAB), SLAB)

    def col_at(i):
        return pl.ds(pl.multiple_of(slot_ref[i] * SLAB, SLAB), SLAB)

    moves = []
    for side, piece in enumerate((over_here, over_side)):
        moves.append((piece.at[0], row_ref.at[row_at(2, side), :]))
        moves.append((piece.at[1], other_rows.at[row_at(2, side), :]))
    for i, piece in enumerate(cols[:EARLY]):
        moves.append((piece.at[0], col_ref.at[col_at(i), :]))
        moves.append((piece.at[1], other_cols.at[col_at(i), :]))
    copies = [pltpu.make_async_copy(*move, sem.at[i]) for i, move in enumerate(moves)]
    for copy in copies:
        copy.start()
    for dy, piece in ((0, four_ref), (1, up_ref), (3, down_ref)):
        for side in range(NX):
            row_ref[row_at(dy, side), :] = piece[2 * side]
            other_rows[row_at(dy, side), :] = piece[2 * side + 1]
    for i in range(EARLY, NZ):
        col_ref[col_at(i), :] = cols[i][0]
        other_cols[col_at(i), :] = cols[i][1]
    for copy in copies:
        copy.wait()
    per = BLOCK // 2
    odd = odd_ref[0] == 1
    sign = jnp.where(odd, -1.0, 1.0).astype(jnp.float32)
    a, a_other = row_ref[...], other_rows[...]
    a_turned, other_turned = turned(a), turned(a_other)
    for part in range(2):
        at = pl.ds(part * per, per)
        b = col_ref[at, :]
        p_re, p_im = dot(a, b, 1, 1), dot(a_turned, b, 1, 1)
        mine = kern_ref[:, 0, :, at].reshape(BLOCK, per)
        other = half_ref[:, :, at].reshape(BLOCK, per)
        k_re = jnp.where(odd, other, mine).astype(jnp.float32)
        k_im = jnp.where(odd, mine, other).astype(jnp.float32) * sign
        total_re = k_re * p_re - k_im * p_im
        total_im = k_re * p_im + k_im * p_re
        b = other_cols[at, :]
        p_re, p_im = dot(a_other, b, 1, 1), dot(other_turned, b, 1, 1)
        k_re = kern_ref[:, 1, :, at].reshape(BLOCK, per).astype(jnp.float32)
        k_im = kern_ref[:, 2, :, at].reshape(BLOCK, per).astype(jnp.float32) * -sign
        total_re += k_re * p_re - k_im * p_im
        total_im += k_re * p_im + k_im * p_re
        m_ref[:, at] = total_re.astype(jnp.bfloat16)
        m_ref[:, pl.ds(BLOCK + part * per, per)] = total_im.astype(jnp.bfloat16)


def mix(place, slots, odd, four, up, over, down, cols, *kerns):
    points = pltpu.VMEM((BLOCK, LANES), jnp.bfloat16)
    in_hbm = pl.BlockSpec(memory_space=pltpu.HBM)
    late = NZ - EARLY
    specs = [IN_VMEM] * 2 + [in_hbm] * 2 + [IN_VMEM] + [in_hbm] * EARLY + [IN_VMEM] * (late + 2)
    arrays = [near(four), near(up), *map(away, over), near(down)]
    arrays += [*map(away, cols[:EARLY]), *map(near, cols[EARLY:]), *map(near, kerns)]
    return pl.pallas_call(
        mix_body,
        out_shape=[pltpu.VMEM((BLOCK, 2 * BLOCK), jnp.bfloat16), points, points],
        in_specs=[IN_SMEM] * 3 + specs,
        out_specs=[IN_VMEM] * 3,
        scratch_shapes=[pltpu.VMEM((BLOCK, LANES), jnp.bfloat16)] * 2
        + [pltpu.SemaphoreType.DMA((2 * NX + 2 * EARLY,))],
        compiler_params=PARAMS,
        name="mix",
    )(place, slots, odd, *arrays)


def prepare_body(row_ref, col_ref, left_ref, right_ref):
    flipped = row_ref[...].T
    left_ref[pl.ds(0, WHOLE), :BLOCK] = flipped[:WHOLE]
    left_ref[pl.ds(WHOLE, REST), :BLOCK] = flipped[TAIL : TAIL + REST]
    left_ref[pl.ds(0, WHOLE), BLOCK:] = flipped[WHOLE:TAIL]
    left_ref[pl.ds(WHOLE, REST), BLOCK:] = flipped[TAIL + 64 : TAIL + 64 + REST]
    col = col_ref[...]
    right_ref[pl.ds(0, BLOCK), :] = col
    right_ref[pl.ds(BLOCK, BLOCK), :] = -turned(col)


def prepare(rows, cols):
    return pl.pallas_call(
        prepare_body,
        out_shape=[
            pltpu.VMEM((NB, 2 * BLOCK), jnp.bfloat16),
            pltpu.VMEM((2 * BLOCK, LANES), jnp.bfloat16),
        ],
        in_specs=[IN_VMEM] * 2,
        out_specs=[IN_VMEM] * 2,
        compiler_params=PARAMS,
        name="prepare",
    )(near(rows), near(cols))


def place_of(d):
    yx, z = d // NZ, d % NZ
    return (yx * 2 + z % 2) * (NZ // 2) + z // 2


def project_body(m_ref, left_ref, right_ref, out_ref, x_ref, part_ref, sem):
    y = dot(m_ref[...], right_ref[...], 1, 0)
    high = y.astype(jnp.bfloat16)
    low = (y - high.astype(jnp.float32)).astype(jnp.bfloat16)
    high = jnp.concatenate([high, turned(high)], axis=0)
    low = jnp.concatenate([low, turned(low)], axis=0)
    x_ref[pl.ds(NB, 8), :] = jnp.zeros((8, LANES), jnp.float32)
    copies = []
    for part, (start, size) in enumerate(((0, 224), (224, 208))):
        at = pl.ds(start, size)
        x_ref[at, :] = -(dot(left_ref[at, :], high, 1, 0) + dot(left_ref[at, :], low, 1, 0))
        some = GROUPS * NZ // 2
        for d in range(part * some, (part + 1) * some):
            part_ref[place_of(d)] = x_ref[pl.ds(27 * d // 4, 8), :].astype(jnp.bfloat16)
        chosen = pl.ds(part * some, some)
        copy = pltpu.make_async_copy(part_ref.at[chosen], out_ref.at[chosen], sem.at[part])
        copy.start()
        copies.append(copy)
    for copy in copies:
        copy.wait()


def project(m, left, right):
    windows = (GROUPS * NZ, 8, LANES)
    return pl.pallas_call(
        project_body,
        out_shape=jax.ShapeDtypeStruct(windows, jnp.bfloat16),
        in_specs=[IN_VMEM] * 3,
        out_specs=pl.BlockSpec(memory_space=pltpu.HBM),
        scratch_shapes=[
            pltpu.VMEM((NB + 8, LANES), jnp.float32),
            pltpu.VMEM(windows, jnp.bfloat16),
            pltpu.SemaphoreType.DMA((2,)),
        ],
        compiler_params=PARAMS,
        name="project",
    )(near(m), near(left), near(right))


def bundle_body(own_ref, far_ref, own_side, far_side, four_ref, both_ref):
    for i, ref in enumerate((own_ref, far_ref, own_side, far_side)):
        four_ref[i] = ref[...]
    both_ref[0] = own_ref[...]
    both_ref[1] = far_ref[...]


def bundle(*blocks):
    return pl.pallas_call(
        bundle_body,
        out_shape=[
            pltpu.VMEM((4, SLAB, LANES), jnp.bfloat16),
            pltpu.VMEM((2, SLAB, LANES), jnp.bfloat16),
        ],
        in_specs=[IN_VMEM] * 4,
        out_specs=[IN_VMEM] * 2,
        compiler_params=PARAMS,
        name="bundle",
    )(*map(near, blocks))


def reduce_windows(windows):
    quads = NZ // 2
    wide = [[g * NZ + 2 * j + i for g in range(GROUPS) for i in range(2)] for j in range(quads)]
    deep = [[g * NZ + 2 * j + i for j in range(quads)] for g in range(GROUPS) for i in range(2)]
    parts = windows.reshape(2 * GROUPS, quads, 8, LANES)
    parts = lax.all_to_all(parts, "band", 0, 0, axis_index_groups=wide)
    parts = jnp.sum(parts.astype(jnp.float32), axis=0)
    total = jnp.sum(lax.all_to_all(parts, "band", 0, 0, axis_index_groups=deep), axis=0)
    real = jnp.concatenate([total[:, :WHOLE], total[:, TAIL : TAIL + REST]], axis=1)
    imag = jnp.concatenate([total[:, WHOLE:TAIL], total[:, TAIL + 64 : TAIL + 64 + REST]], axis=1)
    return jnp.stack([real, imag])


def on_device(orbitals, kernels, pair_kdiff, stored_kernel_index):
    group = lax.axis_index("kgrp")
    band = lax.axis_index("band")
    y, x, z = band // (NX * NZ), band // NZ % NX, band % NZ
    odd = (group % 2).reshape(1)

    own = lay(orbitals)
    first = (
        swap_groups(pair_kdiff, 1),
        swap_groups(pair_kdiff, 2),
        swap_groups(own, 2),
        shift(own, 0, 1, 0),
        other_side(own),
    )
    diff_core, diff_far = first[:2]
    far, own_side, far_side = lax.optimization_barrier(first)[2:]

    over_yx = [[g * NZ + i for g in range(GROUPS)] for i in range(NZ)]
    sends = pack(odd, pair_kdiff, diff_core, diff_far, stored_kernel_index, kernels)
    kern = lax.all_to_all(sends, "band", 0, 0, axis_index_groups=over_yx)
    half = swap_groups(kern[:, 0], 1)

    four, both = bundle(own, far, own_side, far_side)
    opposite = shift(both, 0, 0, NZ // 2)
    steps = shift(four, 1, 0, 0), shift(four, -1, 0, 0), shift(both, 0, 0, 1), shift(both, 0, 0, -1)
    up, down, ahead, behind = lax.optimization_barrier(steps)
    over = shift(up[:2], 1, 0, 0), shift(down[2:], -1, 0, 0)
    cols = [both, ahead, behind]
    for _ in range(2):
        ahead, behind = shift(ahead, 0, 0, 1), shift(behind, 0, 0, -1)
        cols += [ahead, behind]
    cols.insert(3, opposite)

    place = jnp.stack([(y - dy) % NY * NX + (x - dx) % NX for dy in range(NY) for dx in range(NX)])
    slots = jnp.stack([(z + i) % NZ for i in (0, -1, 1, -4, -2, 2, -3, 3)])
    m_out, rows, cols = mix(place, slots, odd, four, up, over, down, cols, half, kern)
    m_own = swap_groups(m_out, 1)
    left, right = prepare(rows, cols)
    total = reduce_windows(project(m_own, left, right))
    flat = total.reshape(2, 8 * NB)
    flat = lax.dynamic_slice(flat, (0, band * 27 % 4 * 108), (2, 27 * 108))
    return flat[None]


def solution(mesh):
    return jax.shard_map(
        on_device,
        mesh=mesh,
        in_specs=(P("kgrp", None, "band", None), P(None, None, "band", None), P("kgrp"), P()),
        out_specs=P("kgrp", None, "band"),
        check_vma=False,
    )
```

```python
import jax
import jax.numpy as jnp
from jax import lax
from jax.experimental import pallas as pl
from jax.experimental.pallas import tpu as pltpu
from jax.sharding import PartitionSpec as P

NB = 432
SLAB = 64
NY, NX, NZ = 4, 2, 8
GROUPS = NY * NX
BLOCK = NZ * SLAB
WHOLE = 384
REST = NB - WHOLE
TAIL = 2 * WHOLE
LANES = TAIL + 128
EARLY = 6
VMEM = 24 * 1024 * 1024

IN_VMEM = pl.BlockSpec(memory_space=pltpu.VMEM)
IN_SMEM = pl.BlockSpec(memory_space=pltpu.SMEM)
ANYWHERE = pl.BlockSpec(memory_space=pl.ANY)
PARAMS = pltpu.CompilerParams(vmem_limit_bytes=VMEM)


def band_route(dy, dx, dz):
    route = []
    for y in range(NY):
        for x in range(NX):
            for z in range(NZ):
                there = ((y + dy) % NY * NX + (x + dx) % NX) * NZ + (z + dz) % NZ
                route.append(((y * NX + x) * NZ + z, there))
    return route


def shift(block, dy, dx, dz):
    return lax.ppermute(block, "band", band_route(dy, dx, dz))


def swap_groups(block, bit):
    return lax.ppermute(block, "kgrp", [(k, k ^ bit) for k in range(4)])


def other_side(block):
    route = [(i, j) for i, j in band_route(0, 1, 0)]
    both = [((k ^ 2) * 64 + i, k * 64 + j) for k in range(4) for i, j in route]
    return lax.ppermute(block, ("kgrp", "band"), both)


def dot(a, b, a_axis, b_axis):
    dims = (((a_axis,), (b_axis,)), ((), ()))
    return lax.dot_general(a, b, dims, preferred_element_type=jnp.float32)


def near(array):
    return pltpu.with_memory_space_constraint(array, pltpu.VMEM)


def away(array):
    return pltpu.with_memory_space_constraint(array, pltpu.HBM)


def lay_body(orbit_ref, out_ref):
    gap = jnp.zeros((SLAB, 64 - REST), jnp.float32)
    real, imag = orbit_ref[0, 0], orbit_ref[0, 1]
    out_ref[:, :WHOLE] = real[:, :WHOLE]
    out_ref[:, WHOLE:TAIL] = imag[:, :WHOLE]
    last = [real[:, WHOLE:].astype(jnp.float32), gap, imag[:, WHOLE:].astype(jnp.float32), gap]
    out_ref[:, TAIL:] = jnp.concatenate(last, axis=1).astype(jnp.bfloat16)


def lay(orbitals):
    return pl.pallas_call(
        lay_body,
        out_shape=pltpu.VMEM((SLAB, LANES), jnp.bfloat16),
        in_specs=[IN_VMEM],
        out_specs=IN_VMEM,
        name="lay",
    )(orbitals)


def turned(rows):
    last = rows[:, TAIL:].astype(jnp.float32)
    lane = lax.broadcasted_iota(jnp.int32, last.shape, 1)
    last = pltpu.roll(last, 64, 1) * jnp.where(lane < 64, 1.0, -1.0)
    return jnp.concatenate(
        [rows[:, WHOLE:TAIL], -rows[:, :WHOLE], last.astype(rows.dtype)], axis=1
    )


def pack_body(odd_ref, own_ref, core_ref, far_ref, stored_ref, kernels_ref, out_ref, sem):
    odd = odd_ref[0] == 1
    own, core, far = stored_ref[own_ref[0]], stored_ref[core_ref[0]], stored_ref[far_ref[0]]
    shared = jnp.where(odd, own, core)
    single = jnp.where(odd, core, far)
    copies = []
    for i in range(GROUPS):
        at = pl.ds(i * BLOCK, BLOCK)
        half = kernels_ref.at[shared, odd_ref[0], :, at]
        copies.append(pltpu.make_async_copy(half, out_ref.at[i, 0], sem.at[0, i]))
        both = kernels_ref.at[single, :, :, at]
        copies.append(pltpu.make_async_copy(both, out_ref.at[i, pl.ds(1, 2)], sem.at[1, i]))
    for copy in copies:
        copy.start()
    for copy in copies:
        copy.wait()


def pack(odd, own, core, far, stored, kernels):
    return pl.pallas_call(
        pack_body,
        out_shape=jax.ShapeDtypeStruct((GROUPS, 3, SLAB, BLOCK), jnp.bfloat16),
        in_specs=[IN_SMEM] * 5 + [pl.BlockSpec(memory_space=pltpu.HBM)],
        out_specs=IN_VMEM,
        scratch_shapes=[pltpu.SemaphoreType.DMA((2, GROUPS))],
        compiler_params=PARAMS,
        name="pack",
    )(odd, own, core, far, stored, away(kernels))


def mix_body(place_ref, slot_ref, odd_ref, *refs):
    four_ref, up_ref, over_here, over_side, down_ref = refs[:5]
    cols, (half_ref, kern_ref) = refs[5 : 5 + NZ], refs[5 + NZ : 7 + NZ]
    m_ref, row_ref, col_ref, other_rows, other_cols, sem = refs[7 + NZ :]

    def row_at(dy, side):
        return pl.ds(pl.multiple_of(place_ref[dy * NX + side] * SLAB, SLAB), SLAB)

    def col_at(i):
        return pl.ds(pl.multiple_of(slot_ref[i] * SLAB, SLAB), SLAB)

    moves = []
    for side, piece in enumerate((over_here, over_side)):
        moves.append((piece.at[0], row_ref.at[row_at(2, side), :]))
        moves.append((piece.at[1], other_rows.at[row_at(2, side), :]))
    for i, piece in enumerate(cols[:EARLY]):
        moves.append((piece.at[0], col_ref.at[col_at(i), :]))
        moves.append((piece.at[1], other_cols.at[col_at(i), :]))
    copies = [pltpu.make_async_copy(*move, sem.at[i]) for i, move in enumerate(moves)]
    for copy in copies:
        copy.start()
    for dy, piece in ((0, four_ref), (1, up_ref), (3, down_ref)):
        for side in range(NX):
            row_ref[row_at(dy, side), :] = piece[2 * side]
            other_rows[row_at(dy, side), :] = piece[2 * side + 1]
    for i in range(EARLY, NZ):
        col_ref[col_at(i), :] = cols[i][0]
        other_cols[col_at(i), :] = cols[i][1]
    for copy in copies:
        copy.wait()
    per = BLOCK // 2
    odd = odd_ref[0] == 1
    sign = jnp.where(odd, -1.0, 1.0).astype(jnp.float32)
    a, a_other = row_ref[...], other_rows[...]
    a_turned, other_turned = turned(a), turned(a_other)
    for part in range(2):
        at = pl.ds(part * per, per)
        b = col_ref[at, :]
        p_re, p_im = dot(a, b, 1, 1), dot(a_turned, b, 1, 1)
        mine = kern_ref[:, 0, :, at].reshape(BLOCK, per)
        other = half_ref[:, :, at].reshape(BLOCK, per)
        k_re = jnp.where(odd, other, mine).astype(jnp.float32)
        k_im = jnp.where(odd, mine, other).astype(jnp.float32) * sign
        total_re = k_re * p_re - k_im * p_im
        total_im = k_re * p_im + k_im * p_re
        b = other_cols[at, :]
        p_re, p_im = dot(a_other, b, 1, 1), dot(other_turned, b, 1, 1)
        k_re = kern_ref[:, 1, :, at].reshape(BLOCK, per).astype(jnp.float32)
        k_im = kern_ref[:, 2, :, at].reshape(BLOCK, per).astype(jnp.float32) * -sign
        total_re += k_re * p_re - k_im * p_im
        total_im += k_re * p_im + k_im * p_re
        m_ref[:, at] = total_re.astype(jnp.bfloat16)
        m_ref[:, pl.ds(BLOCK + part * per, per)] = total_im.astype(jnp.bfloat16)


def mix(place, slots, odd, four, up, over, down, cols, *kerns):
    points = pltpu.VMEM((BLOCK, LANES), jnp.bfloat16)
    in_hbm = pl.BlockSpec(memory_space=pltpu.HBM)
    late = NZ - EARLY
    specs = [IN_VMEM] * 2 + [in_hbm] * 2 + [IN_VMEM] + [in_hbm] * EARLY + [IN_VMEM] * (late + 2)
    arrays = [near(four), near(up), *map(away, over), near(down)]
    arrays += [*map(away, cols[:EARLY]), *map(near, cols[EARLY:]), *map(near, kerns)]
    return pl.pallas_call(
        mix_body,
        out_shape=[pltpu.VMEM((BLOCK, 2 * BLOCK), jnp.bfloat16), points, points],
        in_specs=[IN_SMEM] * 3 + specs,
        out_specs=[IN_VMEM] * 3,
        scratch_shapes=[pltpu.VMEM((BLOCK, LANES), jnp.bfloat16)] * 2
        + [pltpu.SemaphoreType.DMA((2 * NX + 2 * EARLY,))],
        compiler_params=PARAMS,
        name="mix",
    )(place, slots, odd, *arrays)


def prepare_body(row_ref, col_ref, left_ref, right_ref):
    flipped = row_ref[...].T
    left_ref[pl.ds(0, WHOLE), :BLOCK] = flipped[:WHOLE]
    left_ref[pl.ds(WHOLE, REST), :BLOCK] = flipped[TAIL : TAIL + REST]
    left_ref[pl.ds(0, WHOLE), BLOCK:] = flipped[WHOLE:TAIL]
    left_ref[pl.ds(WHOLE, REST), BLOCK:] = flipped[TAIL + 64 : TAIL + 64 + REST]
    col = col_ref[...]
    right_ref[pl.ds(0, BLOCK), :] = col
    right_ref[pl.ds(BLOCK, BLOCK), :] = -turned(col)


def prepare(rows, cols):
    return pl.pallas_call(
        prepare_body,
        out_shape=[
            pltpu.VMEM((NB, 2 * BLOCK), jnp.bfloat16),
            pltpu.VMEM((2 * BLOCK, LANES), jnp.bfloat16),
        ],
        in_specs=[IN_VMEM] * 2,
        out_specs=[IN_VMEM] * 2,
        compiler_params=PARAMS,
        name="prepare",
    )(near(rows), near(cols))


def place_of(d):
    yx, z = d // NZ, d % NZ
    return (yx * 2 + z % 2) * (NZ // 2) + z // 2


def project_body(m_ref, left_ref, right_ref, out_ref, x_ref, part_ref, sem):
    y = dot(m_ref[...], right_ref[...], 1, 0)
    high = y.astype(jnp.bfloat16)
    low = (y - high.astype(jnp.float32)).astype(jnp.bfloat16)
    high = jnp.concatenate([high, turned(high)], axis=0)
    low = jnp.concatenate([low, turned(low)], axis=0)
    x_ref[pl.ds(NB, 8), :] = jnp.zeros((8, LANES), jnp.float32)
    copies = []
    for part, (start, size) in enumerate(((0, 224), (224, 208))):
        at = pl.ds(start, size)
        x_ref[at, :] = -(dot(left_ref[at, :], high, 1, 0) + dot(left_ref[at, :], low, 1, 0))
        some = GROUPS * NZ // 2
        for d in range(part * some, (part + 1) * some):
            part_ref[place_of(d)] = x_ref[pl.ds(27 * d // 4, 8), :].astype(jnp.bfloat16)
        chosen = pl.ds(part * some, some)
        copy = pltpu.make_async_copy(part_ref.at[chosen], out_ref.at[chosen], sem.at[part])
        copy.start()
        copies.append(copy)
    for copy in copies:
        copy.wait()


def project(m, left, right):
    windows = (GROUPS * NZ, 8, LANES)
    return pl.pallas_call(
        project_body,
        out_shape=jax.ShapeDtypeStruct(windows, jnp.bfloat16),
        in_specs=[IN_VMEM] * 3,
        out_specs=pl.BlockSpec(memory_space=pltpu.HBM),
        scratch_shapes=[
            pltpu.VMEM((NB + 8, LANES), jnp.float32),
            pltpu.VMEM(windows, jnp.bfloat16),
            pltpu.SemaphoreType.DMA((2,)),
        ],
        compiler_params=PARAMS,
        name="project",
    )(near(m), near(left), near(right))


def bundle_body(own_ref, far_ref, own_side, far_side, four_ref, both_ref):
    for i, ref in enumerate((own_ref, far_ref, own_side, far_side)):
        four_ref[i] = ref[...]
    both_ref[0] = own_ref[...]
    both_ref[1] = far_ref[...]


def bundle(*blocks):
    return pl.pallas_call(
        bundle_body,
        out_shape=[
            pltpu.VMEM((4, SLAB, LANES), jnp.bfloat16),
            pltpu.VMEM((2, SLAB, LANES), jnp.bfloat16),
        ],
        in_specs=[IN_VMEM] * 4,
        out_specs=[IN_VMEM] * 2,
        compiler_params=PARAMS,
        name="bundle",
    )(*map(near, blocks))


def reduce_windows(windows):
    quads = NZ // 2
    wide = [[g * NZ + 2 * j + i for g in range(GROUPS) for i in range(2)] for j in range(quads)]
    deep = [[g * NZ + 2 * j + i for j in range(quads)] for g in range(GROUPS) for i in range(2)]
    parts = windows.reshape(2 * GROUPS, quads, 8, LANES)
    parts = lax.all_to_all(parts, "band", 0, 0, axis_index_groups=wide)
    parts = jnp.sum(parts.astype(jnp.float32), axis=0)
    total = jnp.sum(lax.all_to_all(parts, "band", 0, 0, axis_index_groups=deep), axis=0)
    real = jnp.concatenate([total[:, :WHOLE], total[:, TAIL : TAIL + REST]], axis=1)
    imag = jnp.concatenate([total[:, WHOLE:TAIL], total[:, TAIL + 64 : TAIL + 64 + REST]], axis=1)
    return jnp.stack([real, imag])


def on_device(orbitals, kernels, pair_kdiff, stored_kernel_index):
    group = lax.axis_index("kgrp")
    band = lax.axis_index("band")
    y, x, z = band // (NX * NZ), band // NZ % NX, band % NZ
    odd = (group % 2).reshape(1)

    own = lay(orbitals)
    first = (
        swap_groups(pair_kdiff, 1),
        swap_groups(pair_kdiff, 2),
        swap_groups(own, 2),
        shift(own, 0, 1, 0),
        other_side(own),
    )
    diff_core, diff_far = first[:2]
    far, own_side, far_side = lax.optimization_barrier(first)[2:]

    over_yx = [[g * NZ + i for g in range(GROUPS)] for i in range(NZ)]
    four, both = bundle(own, far, own_side, far_side)
    sends = pack(odd, pair_kdiff, diff_core, diff_far, stored_kernel_index, kernels)
    sends, four, both = lax.optimization_barrier((sends, four, both))
    kern = lax.all_to_all(sends, "band", 0, 0, axis_index_groups=over_yx)
    half = swap_groups(kern[:, 0], 1)
    opposite = shift(both, 0, 0, NZ // 2)
    steps = shift(four, 1, 0, 0), shift(four, -1, 0, 0), shift(both, 0, 0, 1), shift(both, 0, 0, -1)
    up, down, ahead, behind = lax.optimization_barrier(steps)
    over = shift(up[:2], 1, 0, 0), shift(down[2:], -1, 0, 0)
    cols = [both, ahead, behind]
    for _ in range(2):
        ahead, behind = shift(ahead, 0, 0, 1), shift(behind, 0, 0, -1)
        cols += [ahead, behind]
    cols.insert(3, opposite)

    place = jnp.stack([(y - dy) % NY * NX + (x - dx) % NX for dy in range(NY) for dx in range(NX)])
    slots = jnp.stack([(z + i) % NZ for i in (0, -1, 1, -4, -2, 2, -3, 3)])
    m_out, rows, cols = mix(place, slots, odd, four, up, over, down, cols, half, kern)
    m_own = swap_groups(m_out, 1)
    left, right = prepare(rows, cols)
    total = reduce_windows(project(m_own, left, right))
    flat = total.reshape(2, 8 * NB)
    flat = lax.dynamic_slice(flat, (0, band * 27 % 4 * 108), (2, 27 * 108))
    return flat[None]


def solution(mesh):
    return jax.shard_map(
        on_device,
        mesh=mesh,
        in_specs=(P("kgrp", None, "band", None), P(None, None, "band", None), P("kgrp"), P()),
        out_specs=P("kgrp", None, "band"),
        check_vma=False,
    )
```

```python
import jax
import jax.numpy as jnp
from jax import lax
from jax.experimental import pallas as pl
from jax.experimental.pallas import tpu as pltpu
from jax.sharding import PartitionSpec as P

NB = 432
SLAB = 64
NY, NX, NZ = 4, 2, 8
GROUPS = NY * NX
BLOCK = NZ * SLAB
WHOLE = 384
REST = NB - WHOLE
TAIL = 2 * WHOLE
LANES = TAIL + 128
VMEM = 24 * 1024 * 1024

IN_VMEM = pl.BlockSpec(memory_space=pltpu.VMEM)
IN_SMEM = pl.BlockSpec(memory_space=pltpu.SMEM)
ANYWHERE = pl.BlockSpec(memory_space=pl.ANY)
PARAMS = pltpu.CompilerParams(vmem_limit_bytes=VMEM)


def band_route(dy, dx, dz):
    route = []
    for y in range(NY):
        for x in range(NX):
            for z in range(NZ):
                there = ((y + dy) % NY * NX + (x + dx) % NX) * NZ + (z + dz) % NZ
                route.append(((y * NX + x) * NZ + z, there))
    return route


def shift(block, dy, dx, dz):
    return lax.ppermute(block, "band", band_route(dy, dx, dz))


def swap_groups(block, bit):
    return lax.ppermute(block, "kgrp", [(k, k ^ bit) for k in range(4)])


def other_side(block):
    route = [(i, j) for i, j in band_route(0, 1, 0)]
    both = [((k ^ 2) * 64 + i, k * 64 + j) for k in range(4) for i, j in route]
    return lax.ppermute(block, ("kgrp", "band"), both)


def dot(a, b, a_axis, b_axis):
    dims = (((a_axis,), (b_axis,)), ((), ()))
    return lax.dot_general(a, b, dims, preferred_element_type=jnp.float32)


def near(array):
    return pltpu.with_memory_space_constraint(array, pltpu.VMEM)


def away(array):
    return pltpu.with_memory_space_constraint(array, pltpu.HBM)


def lay_body(orbit_ref, out_ref):
    gap = jnp.zeros((SLAB, 64 - REST), jnp.float32)
    real, imag = orbit_ref[0, 0], orbit_ref[0, 1]
    out_ref[:, :WHOLE] = real[:, :WHOLE]
    out_ref[:, WHOLE:TAIL] = imag[:, :WHOLE]
    last = [real[:, WHOLE:].astype(jnp.float32), gap, imag[:, WHOLE:].astype(jnp.float32), gap]
    out_ref[:, TAIL:] = jnp.concatenate(last, axis=1).astype(jnp.bfloat16)


def lay(orbitals):
    return pl.pallas_call(
        lay_body,
        out_shape=pltpu.VMEM((SLAB, LANES), jnp.bfloat16),
        in_specs=[IN_VMEM],
        out_specs=IN_VMEM,
        name="lay",
    )(orbitals)


def turned(rows):
    last = rows[:, TAIL:].astype(jnp.float32)
    lane = lax.broadcasted_iota(jnp.int32, last.shape, 1)
    last = pltpu.roll(last, 64, 1) * jnp.where(lane < 64, 1.0, -1.0)
    return jnp.concatenate(
        [rows[:, WHOLE:TAIL], -rows[:, :WHOLE], last.astype(rows.dtype)], axis=1
    )


def pack_body(odd_ref, own_ref, core_ref, far_ref, stored_ref, kernels_ref, shared_ref, single_ref, sem):
    odd = odd_ref[0] == 1
    own, core, far = stored_ref[own_ref[0]], stored_ref[core_ref[0]], stored_ref[far_ref[0]]
    shared = jnp.where(odd, own, core)
    single = jnp.where(odd, core, far)
    copies = []
    for i in range(GROUPS):
        at = pl.ds(i * BLOCK, BLOCK)
        copies += [
            pltpu.make_async_copy(
                kernels_ref.at[shared, odd_ref[0], :, at], shared_ref.at[i], sem.at[0, i]
            ),
            pltpu.make_async_copy(
                kernels_ref.at[single, :, :, at], single_ref.at[i], sem.at[1, i]
            ),
        ]
    for copy in copies:
        copy.start()
    for copy in copies:
        copy.wait()


def pack(odd, own, core, far, stored, kernels):
    return pl.pallas_call(
        pack_body,
        out_shape=[
            pltpu.VMEM((GROUPS, SLAB, BLOCK), jnp.bfloat16),
            pltpu.VMEM((GROUPS, 2, SLAB, BLOCK), jnp.bfloat16),
        ],
        in_specs=[IN_SMEM] * 5 + [ANYWHERE],
        out_specs=[IN_VMEM] * 2,
        scratch_shapes=[pltpu.SemaphoreType.DMA((2, GROUPS))],
        compiler_params=PARAMS,
        name="pack",
    )(odd, own, core, far, stored, away(kernels))


def mix_body(place_ref, odd_ref, *refs):
    four_ref, up_ref, over_here, over_side, down_ref, gathered_ref = refs[:6]
    mine_ref, half_ref, kern_ref = refs[6:9]
    m_ref, row_ref, col_ref, other_rows, other_cols, sem = refs[9:]

    def row_at(dy, side):
        return pl.ds(pl.multiple_of(place_ref[dy * NX + side] * SLAB, SLAB), SLAB)

    moves = []
    for side, piece in enumerate((over_here, over_side)):
        moves.append((piece.at[0], row_ref.at[row_at(2, side), :]))
        moves.append((piece.at[1], other_rows.at[row_at(2, side), :]))
    for target, which in ((col_ref, 0), (other_cols, 1)):
        for i in range(NZ):
            moves.append((gathered_ref.at[i, which], target.at[pl.ds(i * SLAB, SLAB), :]))
    copies = [pltpu.make_async_copy(*move, sem.at[i]) for i, move in enumerate(moves)]
    for copy in copies:
        copy.start()
    for dy, piece in ((0, four_ref), (1, up_ref), (3, down_ref)):
        for side in range(NX):
            row_ref[row_at(dy, side), :] = piece[2 * side]
            other_rows[row_at(dy, side), :] = piece[2 * side + 1]
    for copy in copies:
        copy.wait()
    per = BLOCK // 2
    odd = odd_ref[0] == 1
    sign = jnp.where(odd, -1.0, 1.0).astype(jnp.float32)
    a, a_other = row_ref[...], other_rows[...]
    a_turned, other_turned = turned(a), turned(a_other)
    for part in range(2):
        at = pl.ds(part * per, per)
        b = col_ref[at, :]
        p_re, p_im = dot(a, b, 1, 1), dot(a_turned, b, 1, 1)
        mine = mine_ref[:, :, at].reshape(BLOCK, per)
        other = half_ref[:, :, at].reshape(BLOCK, per)
        k_re = jnp.where(odd, other, mine).astype(jnp.float32)
        k_im = jnp.where(odd, mine, other).astype(jnp.float32) * sign
        total_re = k_re * p_re - k_im * p_im
        total_im = k_re * p_im + k_im * p_re
        b = other_cols[at, :]
        p_re, p_im = dot(a_other, b, 1, 1), dot(other_turned, b, 1, 1)
        k_re = kern_ref[:, 0, :, at].reshape(BLOCK, per).astype(jnp.float32)
        k_im = kern_ref[:, 1, :, at].reshape(BLOCK, per).astype(jnp.float32) * -sign
        total_re += k_re * p_re - k_im * p_im
        total_im += k_re * p_im + k_im * p_re
        m_ref[:, at] = total_re.astype(jnp.bfloat16)
        m_ref[:, pl.ds(BLOCK + part * per, per)] = total_im.astype(jnp.bfloat16)


def mix(place, odd, four, up, over, down, gathered, *kerns):
    points = pltpu.VMEM((BLOCK, LANES), jnp.bfloat16)
    in_hbm = pl.BlockSpec(memory_space=pltpu.HBM)
    specs = [IN_VMEM] * 2 + [in_hbm] * 2 + [IN_VMEM, in_hbm] + [IN_VMEM] * 3
    arrays = [near(four), near(up), *map(away, over), near(down), away(gathered), *map(near, kerns)]
    return pl.pallas_call(
        mix_body,
        out_shape=[pltpu.VMEM((BLOCK, 2 * BLOCK), jnp.bfloat16), points, points],
        in_specs=[IN_SMEM] * 2 + specs,
        out_specs=[IN_VMEM] * 3,
        scratch_shapes=[pltpu.VMEM((BLOCK, LANES), jnp.bfloat16)] * 2
        + [pltpu.SemaphoreType.DMA((2 * NX + 2 * NZ,))],
        compiler_params=PARAMS,
        name="mix",
    )(place, odd, *arrays)


def prepare_body(row_ref, col_ref, left_ref, right_ref):
    flipped = row_ref[...].T
    left_ref[pl.ds(0, WHOLE), :BLOCK] = flipped[:WHOLE]
    left_ref[pl.ds(WHOLE, REST), :BLOCK] = flipped[TAIL : TAIL + REST]
    left_ref[pl.ds(0, WHOLE), BLOCK:] = flipped[WHOLE:TAIL]
    left_ref[pl.ds(WHOLE, REST), BLOCK:] = flipped[TAIL + 64 : TAIL + 64 + REST]
    col = col_ref[...]
    right_ref[pl.ds(0, BLOCK), :] = col
    right_ref[pl.ds(BLOCK, BLOCK), :] = -turned(col)


def prepare(rows, cols):
    return pl.pallas_call(
        prepare_body,
        out_shape=[
            pltpu.VMEM((NB, 2 * BLOCK), jnp.bfloat16),
            pltpu.VMEM((2 * BLOCK, LANES), jnp.bfloat16),
        ],
        in_specs=[IN_VMEM] * 2,
        out_specs=[IN_VMEM] * 2,
        compiler_params=PARAMS,
        name="prepare",
    )(near(rows), near(cols))


def place_of(d):
    yx, z = d // NZ, d % NZ
    return (yx * 2 + z % 2) * (NZ // 2) + z // 2


def project_body(m_ref, left_ref, right_ref, out_ref, x_ref, part_ref, sem):
    y = dot(m_ref[...], right_ref[...], 1, 0)
    high = y.astype(jnp.bfloat16)
    low = (y - high.astype(jnp.float32)).astype(jnp.bfloat16)
    high = jnp.concatenate([high, turned(high)], axis=0)
    low = jnp.concatenate([low, turned(low)], axis=0)
    x_ref[pl.ds(NB, 8), :] = jnp.zeros((8, LANES), jnp.float32)
    copies = []
    for part, (start, size) in enumerate(((0, 224), (224, 208))):
        at = pl.ds(start, size)
        x_ref[at, :] = -(dot(left_ref[at, :], high, 1, 0) + dot(left_ref[at, :], low, 1, 0))
        some = GROUPS * NZ // 2
        for d in range(part * some, (part + 1) * some):
            part_ref[place_of(d)] = x_ref[pl.ds(27 * d // 4, 8), :].astype(jnp.bfloat16)
        chosen = pl.ds(part * some, some)
        copy = pltpu.make_async_copy(part_ref.at[chosen], out_ref.at[chosen], sem.at[part])
        copy.start()
        copies.append(copy)
    for copy in copies:
        copy.wait()


def project(m, left, right):
    windows = (GROUPS * NZ, 8, LANES)
    return pl.pallas_call(
        project_body,
        out_shape=jax.ShapeDtypeStruct(windows, jnp.bfloat16),
        in_specs=[IN_VMEM] * 3,
        out_specs=pl.BlockSpec(memory_space=pltpu.HBM),
        scratch_shapes=[
            pltpu.VMEM((NB + 8, LANES), jnp.float32),
            pltpu.VMEM(windows, jnp.bfloat16),
            pltpu.SemaphoreType.DMA((2,)),
        ],
        compiler_params=PARAMS,
        name="project",
    )(near(m), near(left), near(right))


def bundle_body(*refs):
    *blocks, out_ref = refs
    for i, ref in enumerate(blocks):
        out_ref[i] = ref[...]


def bundle(*blocks):
    return pl.pallas_call(
        bundle_body,
        out_shape=jax.ShapeDtypeStruct((len(blocks), SLAB, LANES), jnp.bfloat16),
        in_specs=[IN_VMEM] * len(blocks),
        out_specs=IN_VMEM,
        compiler_params=PARAMS,
        name="bundle",
    )(*map(near, blocks))


def reduce_windows(windows):
    quads = NZ // 2
    wide = [[g * NZ + 2 * j + i for g in range(GROUPS) for i in range(2)] for j in range(quads)]
    deep = [[g * NZ + 2 * j + i for j in range(quads)] for g in range(GROUPS) for i in range(2)]
    parts = windows.reshape(2 * GROUPS, quads, 8, LANES)
    parts = lax.all_to_all(parts, "band", 0, 0, axis_index_groups=wide)
    parts = jnp.sum(parts.astype(jnp.float32), axis=0)
    total = jnp.sum(lax.all_to_all(parts, "band", 0, 0, axis_index_groups=deep), axis=0)
    real = jnp.concatenate([total[:, :WHOLE], total[:, TAIL : TAIL + REST]], axis=1)
    imag = jnp.concatenate([total[:, WHOLE:TAIL], total[:, TAIL + 64 : TAIL + 64 + REST]], axis=1)
    return jnp.stack([real, imag])


def on_device(orbitals, kernels, pair_kdiff, stored_kernel_index):
    group = lax.axis_index("kgrp")
    band = lax.axis_index("band")
    y, x = band // (NX * NZ), band // NZ % NX
    odd = (group % 2).reshape(1)

    own = lay(orbitals)
    first = swap_groups(pair_kdiff, 1), swap_groups(pair_kdiff, 2), swap_groups(own, 2)
    diff_core, diff_far, far = lax.optimization_barrier(first)

    over_yx = [[g * NZ + z for g in range(GROUPS)] for z in range(NZ)]
    over_z = [[g * NZ + z for z in range(NZ)] for g in range(GROUPS)]
    gathered = lax.all_gather(bundle(own, far), "band", axis_index_groups=over_z)
    four = bundle(own, far, shift(own, 0, 1, 0), other_side(own))
    up, down = shift(four, 1, 0, 0), shift(four, -1, 0, 0)

    shared, single = pack(odd, pair_kdiff, diff_core, diff_far, stored_kernel_index, kernels)
    mine = lax.all_to_all(shared, "band", 0, 0, axis_index_groups=over_yx)
    half = swap_groups(mine, 1)
    single, up, down = lax.optimization_barrier((single, up, down))
    over = shift(up[:2], 1, 0, 0), shift(down[2:], -1, 0, 0)
    kern = lax.all_to_all(single, "band", 0, 0, axis_index_groups=over_yx)

    place = jnp.stack([(y - dy) % NY * NX + (x - dx) % NX for dy in range(NY) for dx in range(NX)])
    m_out, rows, cols = mix(place, odd, four, up, over, down, gathered, mine, half, kern)
    m_own = swap_groups(m_out, 1)
    left, right = prepare(rows, cols)
    total = reduce_windows(project(m_own, left, right))
    flat = total.reshape(2, 8 * NB)
    flat = lax.dynamic_slice(flat, (0, band * 27 % 4 * 108), (2, 27 * 108))
    return flat[None]


def solution(mesh):
    return jax.shard_map(
        on_device,
        mesh=mesh,
        in_specs=(P("kgrp", None, "band", None), P(None, None, "band", None), P("kgrp"), P()),
        out_specs=P("kgrp", None, "band"),
        check_vma=False,
    )
```

```python
import jax
import jax.numpy as jnp
from jax import lax
from jax.experimental import pallas as pl
from jax.experimental.pallas import tpu as pltpu
from jax.sharding import PartitionSpec as P

NB = 432
SLAB = 64
NY, NX, NZ = 4, 2, 8
GROUPS = NY * NX
BLOCK = NZ * SLAB
WHOLE = 384
REST = NB - WHOLE
TAIL = 2 * WHOLE
LANES = TAIL + 128
EARLY = 5
VMEM = 24 * 1024 * 1024

IN_VMEM = pl.BlockSpec(memory_space=pltpu.VMEM)
IN_SMEM = pl.BlockSpec(memory_space=pltpu.SMEM)
ANYWHERE = pl.BlockSpec(memory_space=pl.ANY)
PARAMS = pltpu.CompilerParams(vmem_limit_bytes=VMEM)


def band_route(dy, dx, dz):
    route = []
    for y in range(NY):
        for x in range(NX):
            for z in range(NZ):
                there = ((y + dy) % NY * NX + (x + dx) % NX) * NZ + (z + dz) % NZ
                route.append(((y * NX + x) * NZ + z, there))
    return route


def shift(block, dy, dx, dz):
    return lax.ppermute(block, "band", band_route(dy, dx, dz))


def swap_groups(block, bit):
    return lax.ppermute(block, "kgrp", [(k, k ^ bit) for k in range(4)])


def other_side(block):
    route = [(i, j) for i, j in band_route(0, 1, 0)]
    both = [((k ^ 2) * 64 + i, k * 64 + j) for k in range(4) for i, j in route]
    return lax.ppermute(block, ("kgrp", "band"), both)


def dot(a, b, a_axis, b_axis):
    dims = (((a_axis,), (b_axis,)), ((), ()))
    return lax.dot_general(a, b, dims, preferred_element_type=jnp.float32)


def near(array):
    return pltpu.with_memory_space_constraint(array, pltpu.VMEM)


def away(array):
    return pltpu.with_memory_space_constraint(array, pltpu.HBM)


def lay_body(orbit_ref, out_ref):
    gap = jnp.zeros((SLAB, 64 - REST), jnp.float32)
    real, imag = orbit_ref[0, 0], orbit_ref[0, 1]
    out_ref[:, :WHOLE] = real[:, :WHOLE]
    out_ref[:, WHOLE:TAIL] = imag[:, :WHOLE]
    last = [real[:, WHOLE:].astype(jnp.float32), gap, imag[:, WHOLE:].astype(jnp.float32), gap]
    out_ref[:, TAIL:] = jnp.concatenate(last, axis=1).astype(jnp.bfloat16)


def lay(orbitals):
    return pl.pallas_call(
        lay_body,
        out_shape=pltpu.VMEM((SLAB, LANES), jnp.bfloat16),
        in_specs=[IN_VMEM],
        out_specs=IN_VMEM,
        name="lay",
    )(orbitals)


def turned(rows):
    last = rows[:, TAIL:].astype(jnp.float32)
    lane = lax.broadcasted_iota(jnp.int32, last.shape, 1)
    last = pltpu.roll(last, 64, 1) * jnp.where(lane < 64, 1.0, -1.0)
    return jnp.concatenate(
        [rows[:, WHOLE:TAIL], -rows[:, :WHOLE], last.astype(rows.dtype)], axis=1
    )


def pack_body(odd_ref, own_ref, core_ref, far_ref, stored_ref, kernels_ref, shared_ref, single_ref, sem):
    odd = odd_ref[0] == 1
    own, core, far = stored_ref[own_ref[0]], stored_ref[core_ref[0]], stored_ref[far_ref[0]]
    shared = jnp.where(odd, own, core)
    single = jnp.where(odd, core, far)
    copies = []
    for i in range(GROUPS):
        at = pl.ds(i * BLOCK, BLOCK)
        copies += [
            pltpu.make_async_copy(
                kernels_ref.at[shared, odd_ref[0], :, at], shared_ref.at[i], sem.at[0, i]
            ),
            pltpu.make_async_copy(
                kernels_ref.at[single, :, :, at], single_ref.at[i], sem.at[1, i]
            ),
        ]
    for copy in copies:
        copy.start()
    for copy in copies:
        copy.wait()


def pack(odd, own, core, far, stored, kernels):
    return pl.pallas_call(
        pack_body,
        out_shape=[
            pltpu.VMEM((GROUPS, SLAB, BLOCK), jnp.bfloat16),
            pltpu.VMEM((GROUPS, 2, SLAB, BLOCK), jnp.bfloat16),
        ],
        in_specs=[IN_SMEM] * 5 + [ANYWHERE],
        out_specs=[IN_VMEM] * 2,
        scratch_shapes=[pltpu.SemaphoreType.DMA((2, GROUPS))],
        compiler_params=PARAMS,
        name="pack",
    )(odd, own, core, far, stored, away(kernels))


def mix_body(place_ref, slot_ref, odd_ref, *refs):
    four_ref, up_ref, over_here, over_side, down_ref = refs[:5]
    cols, (mine_ref, half_ref, kern_ref) = refs[5 : 5 + NZ], refs[5 + NZ : 8 + NZ]
    m_ref, row_ref, col_ref, other_rows, other_cols, sem = refs[8 + NZ :]

    def row_at(dy, side):
        return pl.ds(pl.multiple_of(place_ref[dy * NX + side] * SLAB, SLAB), SLAB)

    def col_at(i):
        return pl.ds(pl.multiple_of(slot_ref[i] * SLAB, SLAB), SLAB)

    moves = []
    for side, piece in enumerate((over_here, over_side)):
        moves.append((piece.at[0], row_ref.at[row_at(2, side), :]))
        moves.append((piece.at[1], other_rows.at[row_at(2, side), :]))
    for i, piece in enumerate(cols[:EARLY]):
        moves.append((piece.at[0], col_ref.at[col_at(i), :]))
        moves.append((piece.at[1], other_cols.at[col_at(i), :]))
    copies = [pltpu.make_async_copy(*move, sem.at[i]) for i, move in enumerate(moves)]
    for copy in copies:
        copy.start()
    for dy, piece in ((0, four_ref), (1, up_ref), (3, down_ref)):
        for side in range(NX):
            row_ref[row_at(dy, side), :] = piece[2 * side]
            other_rows[row_at(dy, side), :] = piece[2 * side + 1]
    for i in range(EARLY, NZ):
        col_ref[col_at(i), :] = cols[i][0]
        other_cols[col_at(i), :] = cols[i][1]
    for copy in copies:
        copy.wait()
    per = BLOCK // 2
    odd = odd_ref[0] == 1
    sign = jnp.where(odd, -1.0, 1.0).astype(jnp.float32)
    a, a_other = row_ref[...], other_rows[...]
    a_turned, other_turned = turned(a), turned(a_other)
    for part in range(2):
        at = pl.ds(part * per, per)
        b = col_ref[at, :]
        p_re, p_im = dot(a, b, 1, 1), dot(a_turned, b, 1, 1)
        mine = mine_ref[:, :, at].reshape(BLOCK, per)
        other = half_ref[:, :, at].reshape(BLOCK, per)
        k_re = jnp.where(odd, other, mine).astype(jnp.float32)
        k_im = jnp.where(odd, mine, other).astype(jnp.float32) * sign
        total_re = k_re * p_re - k_im * p_im
        total_im = k_re * p_im + k_im * p_re
        b = other_cols[at, :]
        p_re, p_im = dot(a_other, b, 1, 1), dot(other_turned, b, 1, 1)
        k_re = kern_ref[:, 0, :, at].reshape(BLOCK, per).astype(jnp.float32)
        k_im = kern_ref[:, 1, :, at].reshape(BLOCK, per).astype(jnp.float32) * -sign
        total_re += k_re * p_re - k_im * p_im
        total_im += k_re * p_im + k_im * p_re
        m_ref[:, at] = total_re.astype(jnp.bfloat16)
        m_ref[:, pl.ds(BLOCK + part * per, per)] = total_im.astype(jnp.bfloat16)


def mix(place, slots, odd, four, up, over, down, cols, *kerns):
    points = pltpu.VMEM((BLOCK, LANES), jnp.bfloat16)
    in_hbm = pl.BlockSpec(memory_space=pltpu.HBM)
    late = NZ - EARLY
    specs = [IN_VMEM] * 2 + [in_hbm] * 2 + [IN_VMEM] + [in_hbm] * EARLY + [IN_VMEM] * (late + 3)
    arrays = [near(four), near(up), *map(away, over), near(down)]
    arrays += [*map(away, cols[:EARLY]), *map(near, cols[EARLY:]), *map(near, kerns)]
    return pl.pallas_call(
        mix_body,
        out_shape=[pltpu.VMEM((BLOCK, 2 * BLOCK), jnp.bfloat16), points, points],
        in_specs=[IN_SMEM] * 3 + specs,
        out_specs=[IN_VMEM] * 3,
        scratch_shapes=[pltpu.VMEM((BLOCK, LANES), jnp.bfloat16)] * 2
        + [pltpu.SemaphoreType.DMA((2 * NX + 2 * EARLY,))],
        compiler_params=PARAMS,
        name="mix",
    )(place, slots, odd, *arrays)


def prepare_body(row_ref, col_ref, left_ref, right_ref):
    flipped = row_ref[...].T
    left_ref[pl.ds(0, WHOLE), :BLOCK] = flipped[:WHOLE]
    left_ref[pl.ds(WHOLE, REST), :BLOCK] = flipped[TAIL : TAIL + REST]
    left_ref[pl.ds(0, WHOLE), BLOCK:] = flipped[WHOLE:TAIL]
    left_ref[pl.ds(WHOLE, REST), BLOCK:] = flipped[TAIL + 64 : TAIL + 64 + REST]
    col = col_ref[...]
    right_ref[pl.ds(0, BLOCK), :] = col
    right_ref[pl.ds(BLOCK, BLOCK), :] = -turned(col)


def prepare(rows, cols):
    return pl.pallas_call(
        prepare_body,
        out_shape=[
            pltpu.VMEM((NB, 2 * BLOCK), jnp.bfloat16),
            pltpu.VMEM((2 * BLOCK, LANES), jnp.bfloat16),
        ],
        in_specs=[IN_VMEM] * 2,
        out_specs=[IN_VMEM] * 2,
        compiler_params=PARAMS,
        name="prepare",
    )(near(rows), near(cols))


def place_of(d):
    yx, z = d // NZ, d % NZ
    return (yx * 2 + z % 2) * (NZ // 2) + z // 2


def project_body(m_ref, left_ref, right_ref, out_ref, x_ref, part_ref, sem):
    y = dot(m_ref[...], right_ref[...], 1, 0)
    high = y.astype(jnp.bfloat16)
    low = (y - high.astype(jnp.float32)).astype(jnp.bfloat16)
    high = jnp.concatenate([high, turned(high)], axis=0)
    low = jnp.concatenate([low, turned(low)], axis=0)
    x_ref[pl.ds(NB, 8), :] = jnp.zeros((8, LANES), jnp.float32)
    copies = []
    for part, (start, size) in enumerate(((0, 224), (224, 208))):
        at = pl.ds(start, size)
        x_ref[at, :] = -(dot(left_ref[at, :], high, 1, 0) + dot(left_ref[at, :], low, 1, 0))
        some = GROUPS * NZ // 2
        for d in range(part * some, (part + 1) * some):
            part_ref[place_of(d)] = x_ref[pl.ds(27 * d // 4, 8), :].astype(jnp.bfloat16)
        chosen = pl.ds(part * some, some)
        copy = pltpu.make_async_copy(part_ref.at[chosen], out_ref.at[chosen], sem.at[part])
        copy.start()
        copies.append(copy)
    for copy in copies:
        copy.wait()


def project(m, left, right):
    windows = (GROUPS * NZ, 8, LANES)
    return pl.pallas_call(
        project_body,
        out_shape=jax.ShapeDtypeStruct(windows, jnp.bfloat16),
        in_specs=[IN_VMEM] * 3,
        out_specs=pl.BlockSpec(memory_space=pltpu.HBM),
        scratch_shapes=[
            pltpu.VMEM((NB + 8, LANES), jnp.float32),
            pltpu.VMEM(windows, jnp.bfloat16),
            pltpu.SemaphoreType.DMA((2,)),
        ],
        compiler_params=PARAMS,
        name="project",
    )(near(m), near(left), near(right))


def bundle_body(own_ref, far_ref, own_side, far_side, four_ref, both_ref):
    for i, ref in enumerate((own_ref, far_ref, own_side, far_side)):
        four_ref[i] = ref[...]
    both_ref[0] = own_ref[...]
    both_ref[1] = far_ref[...]


def bundle(*blocks):
    return pl.pallas_call(
        bundle_body,
        out_shape=[
            pltpu.VMEM((4, SLAB, LANES), jnp.bfloat16),
            pltpu.VMEM((2, SLAB, LANES), jnp.bfloat16),
        ],
        in_specs=[IN_VMEM] * 4,
        out_specs=[IN_VMEM] * 2,
        compiler_params=PARAMS,
        name="bundle",
    )(*map(near, blocks))


def reduce_windows(windows):
    quads = NZ // 2
    wide = [[g * NZ + 2 * j + i for g in range(GROUPS) for i in range(2)] for j in range(quads)]
    deep = [[g * NZ + 2 * j + i for j in range(quads)] for g in range(GROUPS) for i in range(2)]
    parts = windows.reshape(2 * GROUPS, quads, 8, LANES)
    parts = lax.all_to_all(parts, "band", 0, 0, axis_index_groups=wide)
    parts = jnp.sum(parts.astype(jnp.float32), axis=0)
    total = jnp.sum(lax.all_to_all(parts, "band", 0, 0, axis_index_groups=deep), axis=0)
    real = jnp.concatenate([total[:, :WHOLE], total[:, TAIL : TAIL + REST]], axis=1)
    imag = jnp.concatenate([total[:, WHOLE:TAIL], total[:, TAIL + 64 : TAIL + 64 + REST]], axis=1)
    return jnp.stack([real, imag])


def on_device(orbitals, kernels, pair_kdiff, stored_kernel_index):
    group = lax.axis_index("kgrp")
    band = lax.axis_index("band")
    y, x, z = band // (NX * NZ), band // NZ % NX, band % NZ
    odd = (group % 2).reshape(1)

    own = lay(orbitals)
    first = (
        swap_groups(pair_kdiff, 1),
        swap_groups(pair_kdiff, 2),
        swap_groups(own, 2),
        shift(own, 0, 1, 0),
        other_side(own),
    )
    diff_core, diff_far = first[:2]
    far, own_side, far_side = lax.optimization_barrier(first)[2:]

    over_yx = [[g * NZ + i for g in range(GROUPS)] for i in range(NZ)]
    shared, single = pack(odd, pair_kdiff, diff_core, diff_far, stored_kernel_index, kernels)

    four, both = bundle(own, far, own_side, far_side)
    steps = shift(four, 1, 0, 0), shift(four, -1, 0, 0), shift(both, 0, 0, 1), shift(both, 0, 0, -1)
    up, down, ahead, behind, shared, single = lax.optimization_barrier((*steps, shared, single))
    over = shift(up[:2], 1, 0, 0), shift(down[2:], -1, 0, 0)
    mine = lax.all_to_all(shared, "band", 0, 0, axis_index_groups=over_yx)
    half = swap_groups(mine, 1)
    kern = lax.all_to_all(single, "band", 0, 0, axis_index_groups=over_yx)
    cols = [both, ahead, behind]
    for _ in range(2):
        ahead, behind = shift(ahead, 0, 0, 1), shift(behind, 0, 0, -1)
        cols += [ahead, behind]
    cols.append(shift(ahead, 0, 0, 1))

    place = jnp.stack([(y - dy) % NY * NX + (x - dx) % NX for dy in range(NY) for dx in range(NX)])
    slots = jnp.stack([(z + i) % NZ for i in (0, -1, 1, -2, 2, -3, 3, -4)])
    m_out, rows, cols = mix(place, slots, odd, four, up, over, down, cols, mine, half, kern)
    m_own = swap_groups(m_out, 1)
    left, right = prepare(rows, cols)
    total = reduce_windows(project(m_own, left, right))
    flat = total.reshape(2, 8 * NB)
    flat = lax.dynamic_slice(flat, (0, band * 27 % 4 * 108), (2, 27 * 108))
    return flat[None]


def solution(mesh):
    return jax.shard_map(
        on_device,
        mesh=mesh,
        in_specs=(P("kgrp", None, "band", None), P(None, None, "band", None), P("kgrp"), P()),
        out_specs=P("kgrp", None, "band"),
        check_vma=False,
    )
```

```python
import jax
import jax.numpy as jnp
from jax import lax
from jax.experimental import pallas as pl
from jax.experimental.pallas import tpu as pltpu
from jax.sharding import PartitionSpec as P

NB = 432
SLAB = 64
NY, NX, NZ = 4, 2, 8
GROUPS = NY * NX
BLOCK = NZ * SLAB
WHOLE = 384
REST = NB - WHOLE
TAIL = 2 * WHOLE
LANES = TAIL + 128
EARLY = 5
VMEM = 24 * 1024 * 1024

IN_VMEM = pl.BlockSpec(memory_space=pltpu.VMEM)
IN_SMEM = pl.BlockSpec(memory_space=pltpu.SMEM)
ANYWHERE = pl.BlockSpec(memory_space=pl.ANY)
PARAMS = pltpu.CompilerParams(vmem_limit_bytes=VMEM)


def band_route(dy, dx, dz):
    route = []
    for y in range(NY):
        for x in range(NX):
            for z in range(NZ):
                there = ((y + dy) % NY * NX + (x + dx) % NX) * NZ + (z + dz) % NZ
                route.append(((y * NX + x) * NZ + z, there))
    return route


def shift(block, dy, dx, dz):
    return lax.ppermute(block, "band", band_route(dy, dx, dz))


def swap_groups(block, bit):
    return lax.ppermute(block, "kgrp", [(k, k ^ bit) for k in range(4)])


def other_side(block):
    route = [(i, j) for i, j in band_route(0, 1, 0)]
    both = [((k ^ 2) * 64 + i, k * 64 + j) for k in range(4) for i, j in route]
    return lax.ppermute(block, ("kgrp", "band"), both)


def dot(a, b, a_axis, b_axis):
    dims = (((a_axis,), (b_axis,)), ((), ()))
    return lax.dot_general(a, b, dims, preferred_element_type=jnp.float32)


def near(array):
    return pltpu.with_memory_space_constraint(array, pltpu.VMEM)


def away(array):
    return pltpu.with_memory_space_constraint(array, pltpu.HBM)


def lay_body(orbit_ref, out_ref):
    gap = jnp.zeros((SLAB, 64 - REST), jnp.float32)
    real, imag = orbit_ref[0, 0], orbit_ref[0, 1]
    out_ref[:, :WHOLE] = real[:, :WHOLE]
    out_ref[:, WHOLE:TAIL] = imag[:, :WHOLE]
    last = [real[:, WHOLE:].astype(jnp.float32), gap, imag[:, WHOLE:].astype(jnp.float32), gap]
    out_ref[:, TAIL:] = jnp.concatenate(last, axis=1).astype(jnp.bfloat16)


def lay(orbitals):
    return pl.pallas_call(
        lay_body,
        out_shape=pltpu.VMEM((SLAB, LANES), jnp.bfloat16),
        in_specs=[IN_VMEM],
        out_specs=IN_VMEM,
        name="lay",
    )(orbitals)


def turned(rows):
    last = rows[:, TAIL:].astype(jnp.float32)
    lane = lax.broadcasted_iota(jnp.int32, last.shape, 1)
    last = pltpu.roll(last, 64, 1) * jnp.where(lane < 64, 1.0, -1.0)
    return jnp.concatenate(
        [rows[:, WHOLE:TAIL], -rows[:, :WHOLE], last.astype(rows.dtype)], axis=1
    )


def pack_body(odd_ref, own_ref, core_ref, far_ref, stored_ref, kernels_ref, out_ref, sem):
    odd = odd_ref[0] == 1
    own, core, far = stored_ref[own_ref[0]], stored_ref[core_ref[0]], stored_ref[far_ref[0]]
    shared = jnp.where(odd, own, core)
    single = jnp.where(odd, core, far)
    copies = []
    for i in range(GROUPS):
        at = pl.ds(i * BLOCK, BLOCK)
        half = kernels_ref.at[shared, odd_ref[0], :, at]
        copies.append(pltpu.make_async_copy(half, out_ref.at[i, 0], sem.at[0, i]))
        both = kernels_ref.at[single, :, :, at]
        copies.append(pltpu.make_async_copy(both, out_ref.at[i, pl.ds(1, 2)], sem.at[1, i]))
    for copy in copies:
        copy.start()
    for copy in copies:
        copy.wait()


def pack(odd, own, core, far, stored, kernels):
    return pl.pallas_call(
        pack_body,
        out_shape=jax.ShapeDtypeStruct((GROUPS, 3, SLAB, BLOCK), jnp.bfloat16),
        in_specs=[IN_SMEM] * 5 + [pl.BlockSpec(memory_space=pltpu.HBM)],
        out_specs=IN_VMEM,
        scratch_shapes=[pltpu.SemaphoreType.DMA((2, GROUPS))],
        compiler_params=PARAMS,
        name="pack",
    )(odd, own, core, far, stored, away(kernels))


def mix_body(place_ref, slot_ref, odd_ref, *refs):
    four_ref, up_ref, over_here, over_side, down_ref = refs[:5]
    cols, (half_ref, kern_ref) = refs[5 : 5 + NZ], refs[5 + NZ : 7 + NZ]
    m_ref, row_ref, col_ref, other_rows, other_cols, sem = refs[7 + NZ :]

    def row_at(dy, side):
        return pl.ds(pl.multiple_of(place_ref[dy * NX + side] * SLAB, SLAB), SLAB)

    def col_at(i):
        return pl.ds(pl.multiple_of(slot_ref[i] * SLAB, SLAB), SLAB)

    moves = []
    for side, piece in enumerate((over_here, over_side)):
        moves.append((piece.at[0], row_ref.at[row_at(2, side), :]))
        moves.append((piece.at[1], other_rows.at[row_at(2, side), :]))
    for i, piece in enumerate(cols[:EARLY]):
        moves.append((piece.at[0], col_ref.at[col_at(i), :]))
        moves.append((piece.at[1], other_cols.at[col_at(i), :]))
    copies = [pltpu.make_async_copy(*move, sem.at[i]) for i, move in enumerate(moves)]
    for copy in copies:
        copy.start()
    for dy, piece in ((0, four_ref), (1, up_ref), (3, down_ref)):
        for side in range(NX):
            row_ref[row_at(dy, side), :] = piece[2 * side]
            other_rows[row_at(dy, side), :] = piece[2 * side + 1]
    for i in range(EARLY, NZ):
        col_ref[col_at(i), :] = cols[i][0]
        other_cols[col_at(i), :] = cols[i][1]
    for copy in copies:
        copy.wait()
    per = BLOCK // 2
    odd = odd_ref[0] == 1
    sign = jnp.where(odd, -1.0, 1.0).astype(jnp.float32)
    a, a_other = row_ref[...], other_rows[...]
    a_turned, other_turned = turned(a), turned(a_other)
    for part in range(2):
        at = pl.ds(part * per, per)
        b = col_ref[at, :]
        p_re, p_im = dot(a, b, 1, 1), dot(a_turned, b, 1, 1)
        mine = kern_ref[:, 0, :, at].reshape(BLOCK, per)
        other = half_ref[:, :, at].reshape(BLOCK, per)
        k_re = jnp.where(odd, other, mine).astype(jnp.float32)
        k_im = jnp.where(odd, mine, other).astype(jnp.float32) * sign
        total_re = k_re * p_re - k_im * p_im
        total_im = k_re * p_im + k_im * p_re
        b = other_cols[at, :]
        p_re, p_im = dot(a_other, b, 1, 1), dot(other_turned, b, 1, 1)
        k_re = kern_ref[:, 1, :, at].reshape(BLOCK, per).astype(jnp.float32)
        k_im = kern_ref[:, 2, :, at].reshape(BLOCK, per).astype(jnp.float32) * -sign
        total_re += k_re * p_re - k_im * p_im
        total_im += k_re * p_im + k_im * p_re
        m_ref[:, at] = total_re.astype(jnp.bfloat16)
        m_ref[:, pl.ds(BLOCK + part * per, per)] = total_im.astype(jnp.bfloat16)


def mix(place, slots, odd, four, up, over, down, cols, *kerns):
    points = pltpu.VMEM((BLOCK, LANES), jnp.bfloat16)
    in_hbm = pl.BlockSpec(memory_space=pltpu.HBM)
    late = NZ - EARLY
    specs = [IN_VMEM] * 2 + [in_hbm] * 2 + [IN_VMEM] + [in_hbm] * EARLY + [IN_VMEM] * (late + 2)
    arrays = [near(four), near(up), *map(away, over), near(down)]
    arrays += [*map(away, cols[:EARLY]), *map(near, cols[EARLY:]), *map(near, kerns)]
    return pl.pallas_call(
        mix_body,
        out_shape=[pltpu.VMEM((BLOCK, 2 * BLOCK), jnp.bfloat16), points, points],
        in_specs=[IN_SMEM] * 3 + specs,
        out_specs=[IN_VMEM] * 3,
        scratch_shapes=[pltpu.VMEM((BLOCK, LANES), jnp.bfloat16)] * 2
        + [pltpu.SemaphoreType.DMA((2 * NX + 2 * EARLY,))],
        compiler_params=PARAMS,
        name="mix",
    )(place, slots, odd, *arrays)


def prepare_body(row_ref, col_ref, left_ref, right_ref):
    flipped = row_ref[...].T
    left_ref[pl.ds(0, WHOLE), :BLOCK] = flipped[:WHOLE]
    left_ref[pl.ds(WHOLE, REST), :BLOCK] = flipped[TAIL : TAIL + REST]
    left_ref[pl.ds(0, WHOLE), BLOCK:] = flipped[WHOLE:TAIL]
    left_ref[pl.ds(WHOLE, REST), BLOCK:] = flipped[TAIL + 64 : TAIL + 64 + REST]
    col = col_ref[...]
    right_ref[pl.ds(0, BLOCK), :] = col
    right_ref[pl.ds(BLOCK, BLOCK), :] = -turned(col)


def prepare(rows, cols):
    return pl.pallas_call(
        prepare_body,
        out_shape=[
            pltpu.VMEM((NB, 2 * BLOCK), jnp.bfloat16),
            pltpu.VMEM((2 * BLOCK, LANES), jnp.bfloat16),
        ],
        in_specs=[IN_VMEM] * 2,
        out_specs=[IN_VMEM] * 2,
        compiler_params=PARAMS,
        name="prepare",
    )(near(rows), near(cols))


def place_of(d):
    yx, z = d // NZ, d % NZ
    return (yx * 2 + z % 2) * (NZ // 2) + z // 2


def project_body(m_ref, left_ref, right_ref, out_ref, x_ref, part_ref, sem):
    y = dot(m_ref[...], right_ref[...], 1, 0)
    high = y.astype(jnp.bfloat16)
    low = (y - high.astype(jnp.float32)).astype(jnp.bfloat16)
    high = jnp.concatenate([high, turned(high)], axis=0)
    low = jnp.concatenate([low, turned(low)], axis=0)
    x_ref[pl.ds(NB, 8), :] = jnp.zeros((8, LANES), jnp.float32)
    copies = []
    for part, (start, size) in enumerate(((0, 224), (224, 208))):
        at = pl.ds(start, size)
        x_ref[at, :] = -(dot(left_ref[at, :], high, 1, 0) + dot(left_ref[at, :], low, 1, 0))
        some = GROUPS * NZ // 2
        for d in range(part * some, (part + 1) * some):
            part_ref[place_of(d)] = x_ref[pl.ds(27 * d // 4, 8), :].astype(jnp.bfloat16)
        chosen = pl.ds(part * some, some)
        copy = pltpu.make_async_copy(part_ref.at[chosen], out_ref.at[chosen], sem.at[part])
        copy.start()
        copies.append(copy)
    for copy in copies:
        copy.wait()


def project(m, left, right):
    windows = (GROUPS * NZ, 8, LANES)
    return pl.pallas_call(
        project_body,
        out_shape=jax.ShapeDtypeStruct(windows, jnp.bfloat16),
        in_specs=[IN_VMEM] * 3,
        out_specs=pl.BlockSpec(memory_space=pltpu.HBM),
        scratch_shapes=[
            pltpu.VMEM((NB + 8, LANES), jnp.float32),
            pltpu.VMEM(windows, jnp.bfloat16),
            pltpu.SemaphoreType.DMA((2,)),
        ],
        compiler_params=PARAMS,
        name="project",
    )(near(m), near(left), near(right))


def bundle_body(own_ref, far_ref, own_side, far_side, four_ref, both_ref):
    for i, ref in enumerate((own_ref, far_ref, own_side, far_side)):
        four_ref[i] = ref[...]
    both_ref[0] = own_ref[...]
    both_ref[1] = far_ref[...]


def bundle(*blocks):
    return pl.pallas_call(
        bundle_body,
        out_shape=[
            pltpu.VMEM((4, SLAB, LANES), jnp.bfloat16),
            pltpu.VMEM((2, SLAB, LANES), jnp.bfloat16),
        ],
        in_specs=[IN_VMEM] * 4,
        out_specs=[IN_VMEM] * 2,
        compiler_params=PARAMS,
        name="bundle",
    )(*map(near, blocks))


def reduce_windows(windows):
    quads = NZ // 2
    wide = [[g * NZ + 2 * j + i for g in range(GROUPS) for i in range(2)] for j in range(quads)]
    deep = [[g * NZ + 2 * j + i for j in range(quads)] for g in range(GROUPS) for i in range(2)]
    parts = windows.reshape(2 * GROUPS, quads, 8, LANES)
    parts = lax.all_to_all(parts, "band", 0, 0, axis_index_groups=wide)
    parts = jnp.sum(parts.astype(jnp.float32), axis=0)
    total = jnp.sum(lax.all_to_all(parts, "band", 0, 0, axis_index_groups=deep), axis=0)
    real = jnp.concatenate([total[:, :WHOLE], total[:, TAIL : TAIL + REST]], axis=1)
    imag = jnp.concatenate([total[:, WHOLE:TAIL], total[:, TAIL + 64 : TAIL + 64 + REST]], axis=1)
    return jnp.stack([real, imag])


def on_device(orbitals, kernels, pair_kdiff, stored_kernel_index):
    group = lax.axis_index("kgrp")
    band = lax.axis_index("band")
    y, x, z = band // (NX * NZ), band // NZ % NX, band % NZ
    odd = (group % 2).reshape(1)

    own = lay(orbitals)
    first = (
        swap_groups(pair_kdiff, 1),
        swap_groups(pair_kdiff, 2),
        swap_groups(own, 2),
        shift(own, 0, 1, 0),
        other_side(own),
    )
    diff_core, diff_far = first[:2]
    far, own_side, far_side = lax.optimization_barrier(first)[2:]

    over_yx = [[g * NZ + i for g in range(GROUPS)] for i in range(NZ)]
    sends = pack(odd, pair_kdiff, diff_core, diff_far, stored_kernel_index, kernels)

    four, both = bundle(own, far, own_side, far_side)
    up, down = shift(four, 1, 0, 0), shift(four, -1, 0, 0)
    steps = shift(both, 0, 0, 1), shift(both, 0, 0, -1)
    ahead, behind, sends = lax.optimization_barrier((*steps, sends))
    over = shift(up[:2], 1, 0, 0), shift(down[2:], -1, 0, 0)
    kern = lax.all_to_all(sends, "band", 0, 0, axis_index_groups=over_yx)
    cols = [both, ahead, behind]
    for _ in range(2):
        ahead, behind = shift(ahead, 0, 0, 1), shift(behind, 0, 0, -1)
        cols += [ahead, behind]
    cols.append(shift(ahead, 0, 0, 1))
    kern = lax.optimization_barrier((kern, ahead, behind))[0]
    half = swap_groups(kern[:, 0], 1)

    place = jnp.stack([(y - dy) % NY * NX + (x - dx) % NX for dy in range(NY) for dx in range(NX)])
    slots = jnp.stack([(z + i) % NZ for i in (0, -1, 1, -2, 2, -3, 3, -4)])
    m_out, rows, cols = mix(place, slots, odd, four, up, over, down, cols, half, kern)
    m_own = swap_groups(m_out, 1)
    left, right = prepare(rows, cols)
    total = reduce_windows(project(m_own, left, right))
    flat = total.reshape(2, 8 * NB)
    flat = lax.dynamic_slice(flat, (0, band * 27 % 4 * 108), (2, 27 * 108))
    return flat[None]


def solution(mesh):
    return jax.shard_map(
        on_device,
        mesh=mesh,
        in_specs=(P("kgrp", None, "band", None), P(None, None, "band", None), P("kgrp"), P()),
        out_specs=P("kgrp", None, "band"),
        check_vma=False,
    )
```

```python
import jax
import jax.numpy as jnp
from jax import lax
from jax.experimental import pallas as pl
from jax.experimental.pallas import tpu as pltpu
from jax.sharding import PartitionSpec as P

NB = 432
SLAB = 64
NY, NX, NZ = 4, 2, 8
GROUPS = NY * NX
BLOCK = NZ * SLAB
WHOLE = 384
REST = NB - WHOLE
TAIL = 2 * WHOLE
LANES = TAIL + 128
EARLY = 5
VMEM = 24 * 1024 * 1024

IN_VMEM = pl.BlockSpec(memory_space=pltpu.VMEM)
IN_SMEM = pl.BlockSpec(memory_space=pltpu.SMEM)
ANYWHERE = pl.BlockSpec(memory_space=pl.ANY)
PARAMS = pltpu.CompilerParams(vmem_limit_bytes=VMEM)


def band_route(dy, dx, dz):
    route = []
    for y in range(NY):
        for x in range(NX):
            for z in range(NZ):
                there = ((y + dy) % NY * NX + (x + dx) % NX) * NZ + (z + dz) % NZ
                route.append(((y * NX + x) * NZ + z, there))
    return route


def shift(block, dy, dx, dz):
    return lax.ppermute(block, "band", band_route(dy, dx, dz))


def swap_groups(block, bit):
    return lax.ppermute(block, "kgrp", [(k, k ^ bit) for k in range(4)])


def other_side(block):
    route = [(i, j) for i, j in band_route(0, 1, 0)]
    both = [((k ^ 2) * 64 + i, k * 64 + j) for k in range(4) for i, j in route]
    return lax.ppermute(block, ("kgrp", "band"), both)


def dot(a, b, a_axis, b_axis):
    dims = (((a_axis,), (b_axis,)), ((), ()))
    return lax.dot_general(a, b, dims, preferred_element_type=jnp.float32)


def near(array):
    return pltpu.with_memory_space_constraint(array, pltpu.VMEM)


def away(array):
    return pltpu.with_memory_space_constraint(array, pltpu.HBM)


def lay_body(orbit_ref, out_ref):
    gap = jnp.zeros((SLAB, 64 - REST), jnp.float32)
    real, imag = orbit_ref[0, 0], orbit_ref[0, 1]
    out_ref[:, :WHOLE] = real[:, :WHOLE]
    out_ref[:, WHOLE:TAIL] = imag[:, :WHOLE]
    last = [real[:, WHOLE:].astype(jnp.float32), gap, imag[:, WHOLE:].astype(jnp.float32), gap]
    out_ref[:, TAIL:] = jnp.concatenate(last, axis=1).astype(jnp.bfloat16)


def lay(orbitals):
    return pl.pallas_call(
        lay_body,
        out_shape=pltpu.VMEM((SLAB, LANES), jnp.bfloat16),
        in_specs=[IN_VMEM],
        out_specs=IN_VMEM,
        name="lay",
    )(orbitals)


def turned(rows):
    last = rows[:, TAIL:].astype(jnp.float32)
    lane = lax.broadcasted_iota(jnp.int32, last.shape, 1)
    last = pltpu.roll(last, 64, 1) * jnp.where(lane < 64, 1.0, -1.0)
    return jnp.concatenate(
        [rows[:, WHOLE:TAIL], -rows[:, :WHOLE], last.astype(rows.dtype)], axis=1
    )


def pack_body(odd_ref, own_ref, core_ref, far_ref, stored_ref, kernels_ref, out_ref, sem):
    odd = odd_ref[0] == 1
    own, core, far = stored_ref[own_ref[0]], stored_ref[core_ref[0]], stored_ref[far_ref[0]]
    shared = jnp.where(odd, own, core)
    single = jnp.where(odd, core, far)
    copies = []
    for i in range(GROUPS):
        at = pl.ds(i * BLOCK, BLOCK)
        half = kernels_ref.at[shared, odd_ref[0], :, at]
        copies.append(pltpu.make_async_copy(half, out_ref.at[i, 0], sem.at[0, i]))
        both = kernels_ref.at[single, :, :, at]
        copies.append(pltpu.make_async_copy(both, out_ref.at[i, pl.ds(1, 2)], sem.at[1, i]))
    for copy in copies:
        copy.start()
    for copy in copies:
        copy.wait()


def pack(odd, own, core, far, stored, kernels):
    return pl.pallas_call(
        pack_body,
        out_shape=jax.ShapeDtypeStruct((GROUPS, 3, SLAB, BLOCK), jnp.bfloat16),
        in_specs=[IN_SMEM] * 5 + [pl.BlockSpec(memory_space=pltpu.HBM)],
        out_specs=IN_VMEM,
        scratch_shapes=[pltpu.SemaphoreType.DMA((2, GROUPS))],
        compiler_params=PARAMS,
        name="pack",
    )(odd, own, core, far, stored, away(kernels))


def mix_body(place_ref, slot_ref, odd_ref, *refs):
    four_ref, up_ref, over_here, over_side, down_ref = refs[:5]
    cols, (half_ref, kern_ref) = refs[5 : 5 + NZ], refs[5 + NZ : 7 + NZ]
    m_ref, row_ref, col_ref, other_rows, other_cols, sem = refs[7 + NZ :]

    def row_at(dy, side):
        return pl.ds(pl.multiple_of(place_ref[dy * NX + side] * SLAB, SLAB), SLAB)

    def col_at(i):
        return pl.ds(pl.multiple_of(slot_ref[i] * SLAB, SLAB), SLAB)

    moves = []
    for side, piece in enumerate((over_here, over_side)):
        moves.append((piece.at[0], row_ref.at[row_at(2, side), :]))
        moves.append((piece.at[1], other_rows.at[row_at(2, side), :]))
    for i, piece in enumerate(cols[:EARLY]):
        moves.append((piece.at[0], col_ref.at[col_at(i), :]))
        moves.append((piece.at[1], other_cols.at[col_at(i), :]))
    copies = [pltpu.make_async_copy(*move, sem.at[i]) for i, move in enumerate(moves)]
    for copy in copies:
        copy.start()
    for dy, piece in ((0, four_ref), (1, up_ref), (3, down_ref)):
        for side in range(NX):
            row_ref[row_at(dy, side), :] = piece[2 * side]
            other_rows[row_at(dy, side), :] = piece[2 * side + 1]
    for i in range(EARLY, NZ):
        col_ref[col_at(i), :] = cols[i][0]
        other_cols[col_at(i), :] = cols[i][1]
    for copy in copies:
        copy.wait()
    per = BLOCK // 2
    odd = odd_ref[0] == 1
    sign = jnp.where(odd, -1.0, 1.0).astype(jnp.float32)
    a, a_other = row_ref[...], other_rows[...]
    a_turned, other_turned = turned(a), turned(a_other)
    for part in range(2):
        at = pl.ds(part * per, per)
        b = col_ref[at, :]
        p_re, p_im = dot(a, b, 1, 1), dot(a_turned, b, 1, 1)
        mine = kern_ref[:, 0, :, at].reshape(BLOCK, per)
        other = half_ref[:, :, at].reshape(BLOCK, per)
        k_re = jnp.where(odd, other, mine).astype(jnp.float32)
        k_im = jnp.where(odd, mine, other).astype(jnp.float32) * sign
        total_re = k_re * p_re - k_im * p_im
        total_im = k_re * p_im + k_im * p_re
        b = other_cols[at, :]
        p_re, p_im = dot(a_other, b, 1, 1), dot(other_turned, b, 1, 1)
        k_re = kern_ref[:, 1, :, at].reshape(BLOCK, per).astype(jnp.float32)
        k_im = kern_ref[:, 2, :, at].reshape(BLOCK, per).astype(jnp.float32) * -sign
        total_re += k_re * p_re - k_im * p_im
        total_im += k_re * p_im + k_im * p_re
        m_ref[:, at] = total_re.astype(jnp.bfloat16)
        m_ref[:, pl.ds(BLOCK + part * per, per)] = total_im.astype(jnp.bfloat16)


def mix(place, slots, odd, four, up, over, down, cols, *kerns):
    points = pltpu.VMEM((BLOCK, LANES), jnp.bfloat16)
    in_hbm = pl.BlockSpec(memory_space=pltpu.HBM)
    late = NZ - EARLY
    specs = [IN_VMEM] * 2 + [in_hbm] * 2 + [IN_VMEM] + [in_hbm] * EARLY + [IN_VMEM] * (late + 2)
    arrays = [near(four), near(up), *map(away, over), near(down)]
    arrays += [*map(away, cols[:EARLY]), *map(near, cols[EARLY:]), *map(near, kerns)]
    return pl.pallas_call(
        mix_body,
        out_shape=[pltpu.VMEM((BLOCK, 2 * BLOCK), jnp.bfloat16), points, points],
        in_specs=[IN_SMEM] * 3 + specs,
        out_specs=[IN_VMEM] * 3,
        scratch_shapes=[pltpu.VMEM((BLOCK, LANES), jnp.bfloat16)] * 2
        + [pltpu.SemaphoreType.DMA((2 * NX + 2 * EARLY,))],
        compiler_params=PARAMS,
        name="mix",
    )(place, slots, odd, *arrays)


def prepare_body(row_ref, col_ref, left_ref, right_ref):
    flipped = row_ref[...].T
    left_ref[pl.ds(0, WHOLE), :BLOCK] = flipped[:WHOLE]
    left_ref[pl.ds(WHOLE, REST), :BLOCK] = flipped[TAIL : TAIL + REST]
    left_ref[pl.ds(0, WHOLE), BLOCK:] = flipped[WHOLE:TAIL]
    left_ref[pl.ds(WHOLE, REST), BLOCK:] = flipped[TAIL + 64 : TAIL + 64 + REST]
    col = col_ref[...]
    right_ref[pl.ds(0, BLOCK), :] = col
    right_ref[pl.ds(BLOCK, BLOCK), :] = -turned(col)


def prepare(rows, cols):
    return pl.pallas_call(
        prepare_body,
        out_shape=[
            pltpu.VMEM((NB, 2 * BLOCK), jnp.bfloat16),
            pltpu.VMEM((2 * BLOCK, LANES), jnp.bfloat16),
        ],
        in_specs=[IN_VMEM] * 2,
        out_specs=[IN_VMEM] * 2,
        compiler_params=PARAMS,
        name="prepare",
    )(near(rows), near(cols))


def place_of(d):
    yx, z = d // NZ, d % NZ
    return (yx * 2 + z % 2) * (NZ // 2) + z // 2


def project_body(m_ref, left_ref, right_ref, out_ref, x_ref, part_ref, sem):
    y = dot(m_ref[...], right_ref[...], 1, 0)
    high = y.astype(jnp.bfloat16)
    low = (y - high.astype(jnp.float32)).astype(jnp.bfloat16)
    high = jnp.concatenate([high, turned(high)], axis=0)
    low = jnp.concatenate([low, turned(low)], axis=0)
    x_ref[pl.ds(NB, 8), :] = jnp.zeros((8, LANES), jnp.float32)
    copies = []
    for part, (start, size) in enumerate(((0, 224), (224, 208))):
        at = pl.ds(start, size)
        x_ref[at, :] = -(dot(left_ref[at, :], high, 1, 0) + dot(left_ref[at, :], low, 1, 0))
        some = GROUPS * NZ // 2
        for d in range(part * some, (part + 1) * some):
            part_ref[place_of(d)] = x_ref[pl.ds(27 * d // 4, 8), :].astype(jnp.bfloat16)
        chosen = pl.ds(part * some, some)
        copy = pltpu.make_async_copy(part_ref.at[chosen], out_ref.at[chosen], sem.at[part])
        copy.start()
        copies.append(copy)
    for copy in copies:
        copy.wait()


def project(m, left, right):
    windows = (GROUPS * NZ, 8, LANES)
    return pl.pallas_call(
        project_body,
        out_shape=jax.ShapeDtypeStruct(windows, jnp.bfloat16),
        in_specs=[IN_VMEM] * 3,
        out_specs=pl.BlockSpec(memory_space=pltpu.HBM),
        scratch_shapes=[
            pltpu.VMEM((NB + 8, LANES), jnp.float32),
            pltpu.VMEM(windows, jnp.bfloat16),
            pltpu.SemaphoreType.DMA((2,)),
        ],
        compiler_params=PARAMS,
        name="project",
    )(near(m), near(left), near(right))


def bundle_body(own_ref, far_ref, own_side, far_side, four_ref, both_ref):
    for i, ref in enumerate((own_ref, far_ref, own_side, far_side)):
        four_ref[i] = ref[...]
    both_ref[0] = own_ref[...]
    both_ref[1] = far_ref[...]


def bundle(*blocks):
    return pl.pallas_call(
        bundle_body,
        out_shape=[
            pltpu.VMEM((4, SLAB, LANES), jnp.bfloat16),
            pltpu.VMEM((2, SLAB, LANES), jnp.bfloat16),
        ],
        in_specs=[IN_VMEM] * 4,
        out_specs=[IN_VMEM] * 2,
        compiler_params=PARAMS,
        name="bundle",
    )(*map(near, blocks))


def reduce_windows(windows):
    quads = NZ // 2
    wide = [[g * NZ + 2 * j + i for g in range(GROUPS) for i in range(2)] for j in range(quads)]
    deep = [[g * NZ + 2 * j + i for j in range(quads)] for g in range(GROUPS) for i in range(2)]
    parts = windows.reshape(2 * GROUPS, quads, 8, LANES)
    parts = lax.all_to_all(parts, "band", 0, 0, axis_index_groups=wide)
    parts = jnp.sum(parts.astype(jnp.float32), axis=0)
    total = jnp.sum(lax.all_to_all(parts, "band", 0, 0, axis_index_groups=deep), axis=0)
    real = jnp.concatenate([total[:, :WHOLE], total[:, TAIL : TAIL + REST]], axis=1)
    imag = jnp.concatenate([total[:, WHOLE:TAIL], total[:, TAIL + 64 : TAIL + 64 + REST]], axis=1)
    return jnp.stack([real, imag])


def on_device(orbitals, kernels, pair_kdiff, stored_kernel_index):
    group = lax.axis_index("kgrp")
    band = lax.axis_index("band")
    y, x, z = band // (NX * NZ), band // NZ % NX, band % NZ
    odd = (group % 2).reshape(1)

    own = lay(orbitals)
    first = (
        swap_groups(pair_kdiff, 1),
        swap_groups(pair_kdiff, 2),
        swap_groups(own, 2),
        shift(own, 0, 1, 0),
        other_side(own),
    )
    diff_core, diff_far = first[:2]
    far, own_side, far_side = lax.optimization_barrier(first)[2:]

    over_yx = [[g * NZ + i for g in range(GROUPS)] for i in range(NZ)]
    sends = pack(odd, pair_kdiff, diff_core, diff_far, stored_kernel_index, kernels)

    four, both = bundle(own, far, own_side, far_side)
    steps = shift(four, 1, 0, 0), shift(four, -1, 0, 0), shift(both, 0, 0, 1), shift(both, 0, 0, -1)
    up, down, ahead, behind, sends = lax.optimization_barrier((*steps, sends))
    over = shift(up[:2], 1, 0, 0), shift(down[2:], -1, 0, 0)
    kern = lax.all_to_all(sends, "band", 0, 0, axis_index_groups=over_yx)
    cols = [both, ahead, behind]
    for _ in range(2):
        ahead, behind = shift(ahead, 0, 0, 1), shift(behind, 0, 0, -1)
        cols += [ahead, behind]
    cols.append(shift(ahead, 0, 0, 1))
    kern, over, cols = lax.optimization_barrier((kern, over, cols))
    half = swap_groups(kern[:, 0], 1)

    place = jnp.stack([(y - dy) % NY * NX + (x - dx) % NX for dy in range(NY) for dx in range(NX)])
    slots = jnp.stack([(z + i) % NZ for i in (0, -1, 1, -2, 2, -3, 3, -4)])
    m_out, rows, cols = mix(place, slots, odd, four, up, over, down, cols, half, kern)
    m_own = swap_groups(m_out, 1)
    left, right = prepare(rows, cols)
    total = reduce_windows(project(m_own, left, right))
    flat = total.reshape(2, 8 * NB)
    flat = lax.dynamic_slice(flat, (0, band * 27 % 4 * 108), (2, 27 * 108))
    return flat[None]


def solution(mesh):
    return jax.shard_map(
        on_device,
        mesh=mesh,
        in_specs=(P("kgrp", None, "band", None), P(None, None, "band", None), P("kgrp"), P()),
        out_specs=P("kgrp", None, "band"),
        check_vma=False,
    )
```

```python
import jax
import jax.numpy as jnp
from jax import lax
from jax.experimental import pallas as pl
from jax.experimental.pallas import tpu as pltpu
from jax.sharding import PartitionSpec as P

NB = 432
SLAB = 64
NY, NX, NZ = 4, 2, 8
GROUPS = NY * NX
BLOCK = NZ * SLAB
WHOLE = 384
REST = NB - WHOLE
TAIL = 2 * WHOLE
LANES = TAIL + 128
VMEM = 24 * 1024 * 1024

IN_VMEM = pl.BlockSpec(memory_space=pltpu.VMEM)
IN_SMEM = pl.BlockSpec(memory_space=pltpu.SMEM)
ANYWHERE = pl.BlockSpec(memory_space=pl.ANY)
PARAMS = pltpu.CompilerParams(vmem_limit_bytes=VMEM)


def band_route(dy, dx, dz):
    route = []
    for y in range(NY):
        for x in range(NX):
            for z in range(NZ):
                there = ((y + dy) % NY * NX + (x + dx) % NX) * NZ + (z + dz) % NZ
                route.append(((y * NX + x) * NZ + z, there))
    return route


def shift(block, dy, dx, dz):
    return lax.ppermute(block, "band", band_route(dy, dx, dz))


def swap_groups(block, bit):
    return lax.ppermute(block, "kgrp", [(k, k ^ bit) for k in range(4)])


def other_side(block):
    route = [(i, j) for i, j in band_route(0, 1, 0)]
    both = [((k ^ 2) * 64 + i, k * 64 + j) for k in range(4) for i, j in route]
    return lax.ppermute(block, ("kgrp", "band"), both)


def dot(a, b, a_axis, b_axis):
    dims = (((a_axis,), (b_axis,)), ((), ()))
    return lax.dot_general(a, b, dims, preferred_element_type=jnp.float32)


def near(array):
    return pltpu.with_memory_space_constraint(array, pltpu.VMEM)


def away(array):
    return pltpu.with_memory_space_constraint(array, pltpu.HBM)


def lay_body(orbit_ref, out_ref):
    gap = jnp.zeros((SLAB, 64 - REST), jnp.float32)
    real, imag = orbit_ref[0, 0], orbit_ref[0, 1]
    out_ref[:, :WHOLE] = real[:, :WHOLE]
    out_ref[:, WHOLE:TAIL] = imag[:, :WHOLE]
    last = [real[:, WHOLE:].astype(jnp.float32), gap, imag[:, WHOLE:].astype(jnp.float32), gap]
    out_ref[:, TAIL:] = jnp.concatenate(last, axis=1).astype(jnp.bfloat16)


def lay(orbitals):
    return pl.pallas_call(
        lay_body,
        out_shape=pltpu.VMEM((SLAB, LANES), jnp.bfloat16),
        in_specs=[IN_VMEM],
        out_specs=IN_VMEM,
        name="lay",
    )(orbitals)


def turned(rows):
    last = rows[:, TAIL:].astype(jnp.float32)
    lane = lax.broadcasted_iota(jnp.int32, last.shape, 1)
    last = pltpu.roll(last, 64, 1) * jnp.where(lane < 64, 1.0, -1.0)
    return jnp.concatenate(
        [rows[:, WHOLE:TAIL], -rows[:, :WHOLE], last.astype(rows.dtype)], axis=1
    )


def pack_body(odd_ref, own_ref, core_ref, far_ref, stored_ref, kernels_ref, out_ref, sem):
    odd = odd_ref[0] == 1
    own, core, far = stored_ref[own_ref[0]], stored_ref[core_ref[0]], stored_ref[far_ref[0]]
    shared = jnp.where(odd, own, core)
    single = jnp.where(odd, core, far)
    copies = []
    for i in range(GROUPS):
        at = pl.ds(i * BLOCK, BLOCK)
        half = kernels_ref.at[shared, odd_ref[0], :, at]
        copies.append(pltpu.make_async_copy(half, out_ref.at[i, 0], sem.at[0, i]))
        both = kernels_ref.at[single, :, :, at]
        copies.append(pltpu.make_async_copy(both, out_ref.at[i, pl.ds(1, 2)], sem.at[1, i]))
    for copy in copies:
        copy.start()
    for copy in copies:
        copy.wait()


def pack(odd, own, core, far, stored, kernels):
    return pl.pallas_call(
        pack_body,
        out_shape=jax.ShapeDtypeStruct((GROUPS, 3, SLAB, BLOCK), jnp.bfloat16),
        in_specs=[IN_SMEM] * 5 + [pl.BlockSpec(memory_space=pltpu.HBM)],
        out_specs=IN_VMEM,
        scratch_shapes=[pltpu.SemaphoreType.DMA((2, GROUPS))],
        compiler_params=PARAMS,
        name="pack",
    )(odd, own, core, far, stored, away(kernels))


def density_body(place_ref, slot_ref, *refs):
    four_ref, up_ref, over_here, over_side, down_ref = refs[:5]
    cols = refs[5 : 5 + NZ]
    own_ref, far_ref, row_ref, col_ref, other_rows, other_cols, sem = refs[5 + NZ :]

    def row_at(dy, side):
        return pl.ds(pl.multiple_of(place_ref[dy * NX + side] * SLAB, SLAB), SLAB)

    moves = []
    for i, piece in enumerate(cols):
        at = pl.ds(pl.multiple_of(slot_ref[i] * SLAB, SLAB), SLAB)
        moves.append((piece.at[0], col_ref.at[at, :]))
        moves.append((piece.at[1], other_cols.at[at, :]))
    for side, piece in enumerate((over_here, over_side)):
        moves.append((piece.at[0], row_ref.at[row_at(2, side), :]))
        moves.append((piece.at[1], other_rows.at[row_at(2, side), :]))
    copies = [pltpu.make_async_copy(*move, sem.at[i]) for i, move in enumerate(moves)]
    for copy in copies:
        copy.start()
    for dy, piece in ((0, four_ref), (1, up_ref), (3, down_ref)):
        for side in range(NX):
            row_ref[row_at(dy, side), :] = piece[2 * side]
            other_rows[row_at(dy, side), :] = piece[2 * side + 1]
    for copy in copies:
        copy.wait()
    for rows, columns, out in ((row_ref, col_ref, own_ref), (other_rows, other_cols, far_ref)):
        a, b = rows[...], columns[...]
        out[:, :BLOCK] = dot(a, b, 1, 1)
        out[:, BLOCK:] = dot(turned(a), b, 1, 1)


def density(place, slots, four, up, over, down, cols):
    product = pltpu.VMEM((BLOCK, 2 * BLOCK), jnp.float32)
    points = pltpu.VMEM((BLOCK, LANES), jnp.bfloat16)
    in_hbm = pl.BlockSpec(memory_space=pltpu.HBM)
    specs = [IN_VMEM] * 2 + [in_hbm] * 2 + [IN_VMEM] + [in_hbm] * NZ
    arrays = [near(four), near(up), *map(away, over), near(down), *map(away, cols)]
    return pl.pallas_call(
        density_body,
        out_shape=[product, product, points, points],
        in_specs=[IN_SMEM] * 2 + specs,
        out_specs=[IN_VMEM] * 4,
        scratch_shapes=[pltpu.VMEM((BLOCK, LANES), jnp.bfloat16)] * 2
        + [pltpu.SemaphoreType.DMA((2 * NX + 2 * NZ,))],
        compiler_params=PARAMS,
        name="density",
    )(place, slots, *arrays)


def mix_body(odd_ref, own_ref, far_ref, half_ref, kern_ref, m_ref):
    odd = odd_ref[0] == 1
    sign = jnp.where(odd, -1.0, 1.0).astype(jnp.float32)
    for i in range(GROUPS):
        at = pl.ds(i * SLAB, SLAB)
        mine, other = kern_ref[i, 0], half_ref[i]
        k_re = jnp.where(odd, other, mine).astype(jnp.float32)
        k_im = jnp.where(odd, mine, other).astype(jnp.float32) * sign
        p_re, p_im = own_ref[at, :BLOCK], own_ref[at, BLOCK:]
        total_re = k_re * p_re - k_im * p_im
        total_im = k_re * p_im + k_im * p_re
        k_re = kern_ref[i, 1].astype(jnp.float32)
        k_im = kern_ref[i, 2].astype(jnp.float32) * -sign
        p_re, p_im = far_ref[at, :BLOCK], far_ref[at, BLOCK:]
        total_re += k_re * p_re - k_im * p_im
        total_im += k_re * p_im + k_im * p_re
        m_ref[at, :BLOCK] = total_re.astype(jnp.bfloat16)
        m_ref[at, BLOCK:] = total_im.astype(jnp.bfloat16)


def mix(odd, *arrays):
    return pl.pallas_call(
        mix_body,
        out_shape=pltpu.VMEM((BLOCK, 2 * BLOCK), jnp.bfloat16),
        in_specs=[IN_SMEM] + [IN_VMEM] * 4,
        out_specs=IN_VMEM,
        compiler_params=PARAMS,
        name="mix",
    )(odd, *map(near, arrays))


def prepare_body(row_ref, col_ref, left_ref, right_ref):
    flipped = row_ref[...].T
    left_ref[pl.ds(0, WHOLE), :BLOCK] = flipped[:WHOLE]
    left_ref[pl.ds(WHOLE, REST), :BLOCK] = flipped[TAIL : TAIL + REST]
    left_ref[pl.ds(0, WHOLE), BLOCK:] = flipped[WHOLE:TAIL]
    left_ref[pl.ds(WHOLE, REST), BLOCK:] = flipped[TAIL + 64 : TAIL + 64 + REST]
    col = col_ref[...]
    right_ref[pl.ds(0, BLOCK), :] = col
    right_ref[pl.ds(BLOCK, BLOCK), :] = -turned(col)


def prepare(rows, cols):
    return pl.pallas_call(
        prepare_body,
        out_shape=[
            pltpu.VMEM((NB, 2 * BLOCK), jnp.bfloat16),
            pltpu.VMEM((2 * BLOCK, LANES), jnp.bfloat16),
        ],
        in_specs=[IN_VMEM] * 2,
        out_specs=[IN_VMEM] * 2,
        compiler_params=PARAMS,
        name="prepare",
    )(near(rows), near(cols))


def place_of(d):
    yx, z = d // NZ, d % NZ
    return (yx * 2 + z % 2) * (NZ // 2) + z // 2


def project_body(m_ref, left_ref, right_ref, out_ref, x_ref, part_ref, sem):
    y = dot(m_ref[...], right_ref[...], 1, 0)
    high = y.astype(jnp.bfloat16)
    low = (y - high.astype(jnp.float32)).astype(jnp.bfloat16)
    high = jnp.concatenate([high, turned(high)], axis=0)
    low = jnp.concatenate([low, turned(low)], axis=0)
    x_ref[pl.ds(NB, 8), :] = jnp.zeros((8, LANES), jnp.float32)
    copies = []
    for part, (start, size) in enumerate(((0, 224), (224, 208))):
        at = pl.ds(start, size)
        x_ref[at, :] = -(dot(left_ref[at, :], high, 1, 0) + dot(left_ref[at, :], low, 1, 0))
        some = GROUPS * NZ // 2
        for d in range(part * some, (part + 1) * some):
            part_ref[place_of(d)] = x_ref[pl.ds(27 * d // 4, 8), :].astype(jnp.bfloat16)
        chosen = pl.ds(part * some, some)
        copy = pltpu.make_async_copy(part_ref.at[chosen], out_ref.at[chosen], sem.at[part])
        copy.start()
        copies.append(copy)
    for copy in copies:
        copy.wait()


def project(m, left, right):
    windows = (GROUPS * NZ, 8, LANES)
    return pl.pallas_call(
        project_body,
        out_shape=jax.ShapeDtypeStruct(windows, jnp.bfloat16),
        in_specs=[IN_VMEM] * 3,
        out_specs=pl.BlockSpec(memory_space=pltpu.HBM),
        scratch_shapes=[
            pltpu.VMEM((NB + 8, LANES), jnp.float32),
            pltpu.VMEM(windows, jnp.bfloat16),
            pltpu.SemaphoreType.DMA((2,)),
        ],
        compiler_params=PARAMS,
        name="project",
    )(near(m), near(left), near(right))


def bundle_body(own_ref, far_ref, own_side, far_side, four_ref, both_ref):
    for i, ref in enumerate((own_ref, far_ref, own_side, far_side)):
        four_ref[i] = ref[...]
    both_ref[0] = own_ref[...]
    both_ref[1] = far_ref[...]


def bundle(*blocks):
    return pl.pallas_call(
        bundle_body,
        out_shape=[
            pltpu.VMEM((4, SLAB, LANES), jnp.bfloat16),
            pltpu.VMEM((2, SLAB, LANES), jnp.bfloat16),
        ],
        in_specs=[IN_VMEM] * 4,
        out_specs=[IN_VMEM] * 2,
        compiler_params=PARAMS,
        name="bundle",
    )(*map(near, blocks))


def reduce_windows(windows):
    quads = NZ // 2
    wide = [[g * NZ + 2 * j + i for g in range(GROUPS) for i in range(2)] for j in range(quads)]
    deep = [[g * NZ + 2 * j + i for j in range(quads)] for g in range(GROUPS) for i in range(2)]
    parts = windows.reshape(2 * GROUPS, quads, 8, LANES)
    parts = lax.all_to_all(parts, "band", 0, 0, axis_index_groups=wide)
    parts = jnp.sum(parts.astype(jnp.float32), axis=0)
    total = jnp.sum(lax.all_to_all(parts, "band", 0, 0, axis_index_groups=deep), axis=0)
    real = jnp.concatenate([total[:, :WHOLE], total[:, TAIL : TAIL + REST]], axis=1)
    imag = jnp.concatenate([total[:, WHOLE:TAIL], total[:, TAIL + 64 : TAIL + 64 + REST]], axis=1)
    return jnp.stack([real, imag])


def on_device(orbitals, kernels, pair_kdiff, stored_kernel_index):
    group = lax.axis_index("kgrp")
    band = lax.axis_index("band")
    y, x, z = band // (NX * NZ), band // NZ % NX, band % NZ
    odd = (group % 2).reshape(1)

    own = lay(orbitals)
    first = (
        swap_groups(pair_kdiff, 1),
        swap_groups(pair_kdiff, 2),
        swap_groups(own, 2),
        shift(own, 0, 1, 0),
        other_side(own),
    )
    diff_core, diff_far = first[:2]
    far, own_side, far_side = lax.optimization_barrier(first)[2:]

    over_yx = [[g * NZ + i for g in range(GROUPS)] for i in range(NZ)]
    sends = pack(odd, pair_kdiff, diff_core, diff_far, stored_kernel_index, kernels)

    four, both = bundle(own, far, own_side, far_side)
    steps = shift(four, 1, 0, 0), shift(four, -1, 0, 0), shift(both, 0, 0, 1), shift(both, 0, 0, -1)
    up, down, ahead, behind, sends = lax.optimization_barrier((*steps, sends))
    over = shift(up[:2], 1, 0, 0), shift(down[2:], -1, 0, 0)
    kern = lax.all_to_all(sends, "band", 0, 0, axis_index_groups=over_yx)
    cols = [both, ahead, behind]
    for _ in range(2):
        ahead, behind = shift(ahead, 0, 0, 1), shift(behind, 0, 0, -1)
        cols += [ahead, behind]
    cols.append(shift(ahead, 0, 0, 1))
    kern, over, cols = lax.optimization_barrier((kern, over, cols))
    half = swap_groups(kern[:, 0], 1)

    place = jnp.stack([(y - dy) % NY * NX + (x - dx) % NX for dy in range(NY) for dx in range(NX)])
    slots = jnp.stack([(z + i) % NZ for i in (0, -1, 1, -2, 2, -3, 3, -4)])
    p_own, p_far, rows, cols = density(place, slots, four, up, over, down, cols)
    m_own = swap_groups(mix(odd, p_own, p_far, half, kern), 1)
    left, right = prepare(rows, cols)
    total = reduce_windows(project(m_own, left, right))
    flat = total.reshape(2, 8 * NB)
    flat = lax.dynamic_slice(flat, (0, band * 27 % 4 * 108), (2, 27 * 108))
    return flat[None]


def solution(mesh):
    return jax.shard_map(
        on_device,
        mesh=mesh,
        in_specs=(P("kgrp", None, "band", None), P(None, None, "band", None), P("kgrp"), P()),
        out_specs=P("kgrp", None, "band"),
        check_vma=False,
    )
```

```python
import jax
import jax.numpy as jnp
from jax import lax
from jax.experimental import pallas as pl
from jax.experimental.pallas import tpu as pltpu
from jax.sharding import PartitionSpec as P

NB = 432
SLAB = 64
NY, NX, NZ = 4, 2, 8
GROUPS = NY * NX
BLOCK = NZ * SLAB
WHOLE = 384
REST = NB - WHOLE
TAIL = 2 * WHOLE
LANES = TAIL + 128
Z_ORDER = (0, -1, 1, -2, 2, -3, 3, -4)
VMEM = 24 * 1024 * 1024

IN_VMEM = pl.BlockSpec(memory_space=pltpu.VMEM)
IN_SMEM = pl.BlockSpec(memory_space=pltpu.SMEM)
ANYWHERE = pl.BlockSpec(memory_space=pl.ANY)
PARAMS = pltpu.CompilerParams(vmem_limit_bytes=VMEM)


def band_route(dy, dx, dz):
    route = []
    for y in range(NY):
        for x in range(NX):
            for z in range(NZ):
                there = ((y + dy) % NY * NX + (x + dx) % NX) * NZ + (z + dz) % NZ
                route.append(((y * NX + x) * NZ + z, there))
    return route


def shift(block, dy, dx, dz):
    return lax.ppermute(block, "band", band_route(dy, dx, dz))


def swap_groups(block, bit):
    return lax.ppermute(block, "kgrp", [(k, k ^ bit) for k in range(4)])


def other_side(block):
    route = [(i, j) for i, j in band_route(0, 1, 0)]
    both = [((k ^ 2) * 64 + i, k * 64 + j) for k in range(4) for i, j in route]
    return lax.ppermute(block, ("kgrp", "band"), both)


def dot(a, b, a_axis, b_axis):
    dims = (((a_axis,), (b_axis,)), ((), ()))
    return lax.dot_general(a, b, dims, preferred_element_type=jnp.float32)


def near(array):
    return pltpu.with_memory_space_constraint(array, pltpu.VMEM)


def away(array):
    return pltpu.with_memory_space_constraint(array, pltpu.HBM)


def lay_body(orbit_ref, out_ref):
    gap = jnp.zeros((SLAB, 64 - REST), jnp.float32)
    real, imag = orbit_ref[0, 0], orbit_ref[0, 1]
    out_ref[:, :WHOLE] = real[:, :WHOLE]
    out_ref[:, WHOLE:TAIL] = imag[:, :WHOLE]
    last = [real[:, WHOLE:].astype(jnp.float32), gap, imag[:, WHOLE:].astype(jnp.float32), gap]
    out_ref[:, TAIL:] = jnp.concatenate(last, axis=1).astype(jnp.bfloat16)


def lay(orbitals):
    return pl.pallas_call(
        lay_body,
        out_shape=pltpu.VMEM((SLAB, LANES), jnp.bfloat16),
        in_specs=[IN_VMEM],
        out_specs=IN_VMEM,
        name="lay",
    )(orbitals)


def turned(rows):
    last = rows[:, TAIL:].astype(jnp.float32)
    lane = lax.broadcasted_iota(jnp.int32, last.shape, 1)
    last = pltpu.roll(last, 64, 1) * jnp.where(lane < 64, 1.0, -1.0)
    return jnp.concatenate(
        [rows[:, WHOLE:TAIL], -rows[:, :WHOLE], last.astype(rows.dtype)], axis=1
    )


def pack_body(odd_ref, own_ref, core_ref, far_ref, stored_ref, kernels_ref, out_ref, sem):
    odd = odd_ref[0] == 1
    own, core, far = stored_ref[own_ref[0]], stored_ref[core_ref[0]], stored_ref[far_ref[0]]
    shared = jnp.where(odd, own, core)
    single = jnp.where(odd, core, far)
    copies = []
    for i in range(GROUPS):
        at = pl.ds(i * BLOCK, BLOCK)
        half = kernels_ref.at[shared, odd_ref[0], :, at]
        copies.append(pltpu.make_async_copy(half, out_ref.at[i, 0], sem.at[0, i]))
        both = kernels_ref.at[single, :, :, at]
        copies.append(pltpu.make_async_copy(both, out_ref.at[i, pl.ds(1, 2)], sem.at[1, i]))
    for copy in copies:
        copy.start()
    for copy in copies:
        copy.wait()


def pack(odd, own, core, far, stored, kernels):
    return pl.pallas_call(
        pack_body,
        out_shape=jax.ShapeDtypeStruct((GROUPS, 3, SLAB, BLOCK), jnp.bfloat16),
        in_specs=[IN_SMEM] * 5 + [pl.BlockSpec(memory_space=pltpu.HBM)],
        out_specs=IN_VMEM,
        scratch_shapes=[pltpu.SemaphoreType.DMA((2, GROUPS))],
        compiler_params=PARAMS,
        name="pack",
    )(odd, own, core, far, stored, away(kernels))


def density_body(band_ref, *refs):
    four_ref, up_ref, over_here, over_side, down_ref = refs[:5]
    cols = refs[5 : 5 + NZ]
    own_ref, far_ref, row_ref, col_ref, other_rows, other_cols, sem = refs[5 + NZ :]

    band = band_ref[0]
    y, x, z = band // (NX * NZ), band // NZ % NX, band % NZ

    def row_at(dy, side):
        place = (y + NY - dy) % NY * NX + (x + side) % NX
        return pl.ds(pl.multiple_of(place * SLAB, SLAB), SLAB)

    def col_at(dz):
        return pl.ds(pl.multiple_of((z + NZ + dz) % NZ * SLAB, SLAB), SLAB)

    moves = []
    for piece, dz in zip(cols[:-1], Z_ORDER):
        moves.append((piece.at[0], col_ref.at[col_at(dz), :]))
        moves.append((piece.at[1], other_cols.at[col_at(dz), :]))
    copies = [pltpu.make_async_copy(*move, sem.at[i]) for i, move in enumerate(moves)]
    for copy in copies:
        copy.start()
    for dy, piece in ((0, four_ref), (1, up_ref), (3, down_ref)):
        for side in range(NX):
            row_ref[row_at(dy, side), :] = piece[2 * side]
            other_rows[row_at(dy, side), :] = piece[2 * side + 1]
    for side, piece in enumerate((over_here, over_side)):
        row_ref[row_at(2, side), :] = piece[0]
        other_rows[row_at(2, side), :] = piece[1]
    col_ref[col_at(Z_ORDER[-1]), :] = cols[-1][0]
    other_cols[col_at(Z_ORDER[-1]), :] = cols[-1][1]
    for copy in copies:
        copy.wait()
    for rows, columns, out in ((row_ref, col_ref, own_ref), (other_rows, other_cols, far_ref)):
        a, b = rows[...], columns[...]
        out[:, :BLOCK] = dot(a, b, 1, 1)
        out[:, BLOCK:] = dot(turned(a), b, 1, 1)


def density(band, four, up, over, down, cols):
    product = pltpu.VMEM((BLOCK, 2 * BLOCK), jnp.float32)
    points = pltpu.VMEM((BLOCK, LANES), jnp.bfloat16)
    in_hbm = pl.BlockSpec(memory_space=pltpu.HBM)
    specs = [IN_VMEM] * 5 + [in_hbm] * (NZ - 1) + [IN_VMEM]
    arrays = [*map(near, (four, up, *over, down)), *map(away, cols[:-1]), near(cols[-1])]
    return pl.pallas_call(
        density_body,
        out_shape=[product, product, points, points],
        in_specs=[IN_SMEM] + specs,
        out_specs=[IN_VMEM] * 4,
        scratch_shapes=[pltpu.VMEM((BLOCK, LANES), jnp.bfloat16)] * 2
        + [pltpu.SemaphoreType.DMA((2 * (NZ - 1),))],
        compiler_params=PARAMS,
        name="density",
    )(band, *arrays)


def mix_body(odd_ref, own_ref, far_ref, core_ref, kern_ref, m_ref):
    odd = odd_ref[0] == 1
    sign = jnp.where(odd, -1.0, 1.0).astype(jnp.float32)
    for i in range(GROUPS):
        at = pl.ds(i * SLAB, SLAB)
        mine, other = kern_ref[i, 0], core_ref[i, 0]
        k_re = jnp.where(odd, other, mine).astype(jnp.float32)
        k_im = jnp.where(odd, mine, other).astype(jnp.float32) * sign
        p_re, p_im = own_ref[at, :BLOCK], own_ref[at, BLOCK:]
        total_re = k_re * p_re - k_im * p_im
        total_im = k_re * p_im + k_im * p_re
        k_re = kern_ref[i, 1].astype(jnp.float32)
        k_im = kern_ref[i, 2].astype(jnp.float32) * -sign
        p_re, p_im = far_ref[at, :BLOCK], far_ref[at, BLOCK:]
        total_re += k_re * p_re - k_im * p_im
        total_im += k_re * p_im + k_im * p_re
        m_ref[at, :BLOCK] = total_re.astype(jnp.bfloat16)
        m_ref[at, BLOCK:] = total_im.astype(jnp.bfloat16)


def mix(odd, *arrays):
    return pl.pallas_call(
        mix_body,
        out_shape=pltpu.VMEM((BLOCK, 2 * BLOCK), jnp.bfloat16),
        in_specs=[IN_SMEM] + [IN_VMEM] * 4,
        out_specs=IN_VMEM,
        compiler_params=PARAMS,
        name="mix",
    )(odd, *map(near, arrays))


def prepare_body(row_ref, col_ref, left_ref, right_ref):
    flipped = row_ref[...].T
    left_ref[pl.ds(0, WHOLE), :BLOCK] = flipped[:WHOLE]
    left_ref[pl.ds(WHOLE, REST), :BLOCK] = flipped[TAIL : TAIL + REST]
    left_ref[pl.ds(0, WHOLE), BLOCK:] = flipped[WHOLE:TAIL]
    left_ref[pl.ds(WHOLE, REST), BLOCK:] = flipped[TAIL + 64 : TAIL + 64 + REST]
    col = col_ref[...]
    right_ref[pl.ds(0, BLOCK), :] = col
    right_ref[pl.ds(BLOCK, BLOCK), :] = -turned(col)


def prepare(rows, cols):
    return pl.pallas_call(
        prepare_body,
        out_shape=[
            pltpu.VMEM((NB, 2 * BLOCK), jnp.bfloat16),
            pltpu.VMEM((2 * BLOCK, LANES), jnp.bfloat16),
        ],
        in_specs=[IN_VMEM] * 2,
        out_specs=[IN_VMEM] * 2,
        compiler_params=PARAMS,
        name="prepare",
    )(near(rows), near(cols))


def place_of(d):
    yx, z = d // NZ, d % NZ
    return (yx * 2 + z % 2) * (NZ // 2) + z // 2


def project_body(m_ref, left_ref, right_ref, out_ref, x_ref, part_ref, sem):
    y = dot(m_ref[...], right_ref[...], 1, 0)
    high = y.astype(jnp.bfloat16)
    low = (y - high.astype(jnp.float32)).astype(jnp.bfloat16)
    high = jnp.concatenate([high, turned(high)], axis=0)
    low = jnp.concatenate([low, turned(low)], axis=0)
    x_ref[pl.ds(NB, 8), :] = jnp.zeros((8, LANES), jnp.float32)
    copies = []
    for part, (start, size) in enumerate(((0, 224), (224, 208))):
        at = pl.ds(start, size)
        x_ref[at, :] = -(dot(left_ref[at, :], high, 1, 0) + dot(left_ref[at, :], low, 1, 0))
        some = GROUPS * NZ // 2
        for d in range(part * some, (part + 1) * some):
            part_ref[place_of(d)] = x_ref[pl.ds(27 * d // 4, 8), :].astype(jnp.bfloat16)
        chosen = pl.ds(part * some, some)
        copy = pltpu.make_async_copy(part_ref.at[chosen], out_ref.at[chosen], sem.at[part])
        copy.start()
        copies.append(copy)
    for copy in copies:
        copy.wait()


def project(m, left, right):
    windows = (GROUPS * NZ, 8, LANES)
    return pl.pallas_call(
        project_body,
        out_shape=jax.ShapeDtypeStruct(windows, jnp.bfloat16),
        in_specs=[IN_VMEM] * 3,
        out_specs=pl.BlockSpec(memory_space=pltpu.HBM),
        scratch_shapes=[
            pltpu.VMEM((NB + 8, LANES), jnp.float32),
            pltpu.VMEM(windows, jnp.bfloat16),
            pltpu.SemaphoreType.DMA((2,)),
        ],
        compiler_params=PARAMS,
        name="project",
    )(near(m), near(left), near(right))


def bundle_body(own_ref, far_ref, own_side, far_side, four_ref, both_ref):
    for i, ref in enumerate((own_ref, far_ref, own_side, far_side)):
        four_ref[i] = ref[...]
    both_ref[0] = own_ref[...]
    both_ref[1] = far_ref[...]


def bundle(*blocks):
    return pl.pallas_call(
        bundle_body,
        out_shape=[
            pltpu.VMEM((4, SLAB, LANES), jnp.bfloat16),
            pltpu.VMEM((2, SLAB, LANES), jnp.bfloat16),
        ],
        in_specs=[IN_VMEM] * 4,
        out_specs=[IN_VMEM] * 2,
        compiler_params=PARAMS,
        name="bundle",
    )(*map(near, blocks))


def reduce_windows(windows):
    quads = NZ // 2
    wide = [[g * NZ + 2 * j + i for g in range(GROUPS) for i in range(2)] for j in range(quads)]
    deep = [[g * NZ + 2 * j + i for j in range(quads)] for g in range(GROUPS) for i in range(2)]
    parts = windows.reshape(2 * GROUPS, quads, 8, LANES)
    parts = lax.all_to_all(parts, "band", 0, 0, axis_index_groups=wide)
    parts = jnp.sum(parts.astype(jnp.float32), axis=0)
    total = jnp.sum(lax.all_to_all(parts, "band", 0, 0, axis_index_groups=deep), axis=0)
    real = jnp.concatenate([total[:, :WHOLE], total[:, TAIL : TAIL + REST]], axis=1)
    imag = jnp.concatenate([total[:, WHOLE:TAIL], total[:, TAIL + 64 : TAIL + 64 + REST]], axis=1)
    return jnp.stack([real, imag])


def on_device(orbitals, kernels, pair_kdiff, stored_kernel_index):
    group = lax.axis_index("kgrp")
    band = lax.axis_index("band")
    odd = (group % 2).reshape(1)

    own = lay(orbitals)
    first = (
        swap_groups(pair_kdiff, 1),
        swap_groups(pair_kdiff, 2),
        swap_groups(own, 2),
        shift(own, 0, 1, 0),
        other_side(own),
    )
    diff_core, diff_far = first[:2]
    far, own_side, far_side = lax.optimization_barrier(first)[2:]

    over_yx = [[g * NZ + i for g in range(GROUPS)] for i in range(NZ)]
    sends = pack(odd, pair_kdiff, diff_core, diff_far, stored_kernel_index, kernels)

    four, both = bundle(own, far, own_side, far_side)
    steps = shift(four, 1, 0, 0), shift(four, -1, 0, 0), shift(both, 0, 0, 1), shift(both, 0, 0, -1)
    up, down, ahead, behind, sends = lax.optimization_barrier((*steps, sends))
    over = shift(up[:2], 1, 0, 0), shift(down[2:], -1, 0, 0)
    kern = lax.all_to_all(sends, "band", 0, 0, axis_index_groups=over_yx)
    cols = [both, ahead, behind]
    for _ in range(2):
        ahead, behind = shift(ahead, 0, 0, 1), shift(behind, 0, 0, -1)
        cols += [ahead, behind]
    cols.append(shift(ahead, 0, 0, 1))
    kern, over, cols = lax.optimization_barrier((kern, over, cols))
    kern_core = swap_groups(kern, 1)

    p_own, p_far, rows, cols = density(band.reshape(1), four, up, over, down, cols)
    m_own = swap_groups(mix(odd, p_own, p_far, kern_core, kern), 1)
    left, right = prepare(rows, cols)
    total = reduce_windows(project(m_own, left, right))
    flat = total.reshape(2, 8 * NB)
    flat = lax.dynamic_slice(flat, (0, band * 27 % 4 * 108), (2, 27 * 108))
    return flat[None]


def solution(mesh):
    return jax.shard_map(
        on_device,
        mesh=mesh,
        in_specs=(P("kgrp", None, "band", None), P(None, None, "band", None), P("kgrp"), P()),
        out_specs=P("kgrp", None, "band"),
        check_vma=False,
    )
```

```python
import jax
import jax.numpy as jnp
from jax import lax
from jax.experimental import pallas as pl
from jax.experimental.pallas import tpu as pltpu
from jax.sharding import PartitionSpec as P

NB = 432
SLAB = 64
NY, NX, NZ = 4, 2, 8
GROUPS = NY * NX
BLOCK = NZ * SLAB
WHOLE = 384
REST = NB - WHOLE
TAIL = 2 * WHOLE
LANES = TAIL + 128
Z_ORDER = (0, -1, 1, -2, 2, -3, 3, -4)
VMEM = 24 * 1024 * 1024

IN_VMEM = pl.BlockSpec(memory_space=pltpu.VMEM)
IN_SMEM = pl.BlockSpec(memory_space=pltpu.SMEM)
ANYWHERE = pl.BlockSpec(memory_space=pl.ANY)
PARAMS = pltpu.CompilerParams(vmem_limit_bytes=VMEM)


def band_route(dy, dx, dz):
    route = []
    for y in range(NY):
        for x in range(NX):
            for z in range(NZ):
                there = ((y + dy) % NY * NX + (x + dx) % NX) * NZ + (z + dz) % NZ
                route.append(((y * NX + x) * NZ + z, there))
    return route


def shift(block, dy, dx, dz):
    return lax.ppermute(block, "band", band_route(dy, dx, dz))


def swap_groups(block, bit):
    return lax.ppermute(block, "kgrp", [(k, k ^ bit) for k in range(4)])


def other_side(block):
    route = [(i, j) for i, j in band_route(0, 1, 0)]
    both = [((k ^ 2) * 64 + i, k * 64 + j) for k in range(4) for i, j in route]
    return lax.ppermute(block, ("kgrp", "band"), both)


def dot(a, b, a_axis, b_axis):
    dims = (((a_axis,), (b_axis,)), ((), ()))
    return lax.dot_general(a, b, dims, preferred_element_type=jnp.float32)


def near(array):
    return pltpu.with_memory_space_constraint(array, pltpu.VMEM)


def away(array):
    return pltpu.with_memory_space_constraint(array, pltpu.HBM)


def lay_body(orbit_ref, out_ref):
    gap = jnp.zeros((SLAB, 64 - REST), jnp.float32)
    real, imag = orbit_ref[0, 0], orbit_ref[0, 1]
    out_ref[:, :WHOLE] = real[:, :WHOLE]
    out_ref[:, WHOLE:TAIL] = imag[:, :WHOLE]
    last = [real[:, WHOLE:].astype(jnp.float32), gap, imag[:, WHOLE:].astype(jnp.float32), gap]
    out_ref[:, TAIL:] = jnp.concatenate(last, axis=1).astype(jnp.bfloat16)


def lay(orbitals):
    return pl.pallas_call(
        lay_body,
        out_shape=pltpu.VMEM((SLAB, LANES), jnp.bfloat16),
        in_specs=[IN_VMEM],
        out_specs=IN_VMEM,
        name="lay",
    )(orbitals)


def turned(rows):
    last = rows[:, TAIL:].astype(jnp.float32)
    lane = lax.broadcasted_iota(jnp.int32, last.shape, 1)
    last = pltpu.roll(last, 64, 1) * jnp.where(lane < 64, 1.0, -1.0)
    return jnp.concatenate(
        [rows[:, WHOLE:TAIL], -rows[:, :WHOLE], last.astype(rows.dtype)], axis=1
    )


def pack_body(odd_ref, own_ref, core_ref, far_ref, stored_ref, kernels_ref, out_ref, sem):
    odd = odd_ref[0] == 1
    own, core, far = stored_ref[own_ref[0]], stored_ref[core_ref[0]], stored_ref[far_ref[0]]
    shared = jnp.where(odd, own, core)
    single = jnp.where(odd, core, far)
    copies = []
    for i in range(GROUPS):
        at = pl.ds(i * BLOCK, BLOCK)
        half = kernels_ref.at[shared, odd_ref[0], :, at]
        copies.append(pltpu.make_async_copy(half, out_ref.at[i, 0], sem.at[0, i]))
        both = kernels_ref.at[single, :, :, at]
        copies.append(pltpu.make_async_copy(both, out_ref.at[i, pl.ds(1, 2)], sem.at[1, i]))
    for copy in copies:
        copy.start()
    for copy in copies:
        copy.wait()


def pack(odd, own, core, far, stored, kernels):
    return pl.pallas_call(
        pack_body,
        out_shape=jax.ShapeDtypeStruct((GROUPS, 3, SLAB, BLOCK), jnp.bfloat16),
        in_specs=[IN_SMEM] * 5 + [pl.BlockSpec(memory_space=pltpu.HBM)],
        out_specs=IN_VMEM,
        scratch_shapes=[pltpu.SemaphoreType.DMA((2, GROUPS))],
        compiler_params=PARAMS,
        name="pack",
    )(odd, own, core, far, stored, away(kernels))


def density_body(band_ref, *refs):
    steps, (own_side, far_side), cols = refs[:NY], refs[NY : NY + 2], refs[NY + 2 : NY + 2 + NZ]
    own_ref, far_ref, row_ref, col_ref, other_rows, other_cols, sem = refs[NY + 2 + NZ :]
    band = band_ref[0]
    y, x, z = band // (NX * NZ), band // NZ % NX, band % NZ

    def row_at(dy, side):
        place = (y + NY - dy) % NY * NX + (x + side) % NX
        return pl.ds(pl.multiple_of(place * SLAB, SLAB), SLAB)

    moves = []
    for piece, dz in zip(cols, Z_ORDER):
        at = pl.ds(pl.multiple_of((z + NZ + dz) % NZ * SLAB, SLAB), SLAB)
        moves.append((piece.at[0], col_ref.at[at, :]))
        moves.append((piece.at[1], other_cols.at[at, :]))
    for dy, piece in enumerate(steps):
        moves.append((piece.at[0], row_ref.at[row_at(dy, 0), :]))
        moves.append((piece.at[1], other_rows.at[row_at(dy, 0), :]))
        moves.append((own_side.at[dy], row_ref.at[row_at(dy, 1), :]))
        moves.append((far_side.at[dy], other_rows.at[row_at(dy, 1), :]))
    copies = [pltpu.make_async_copy(*move, sem.at[i]) for i, move in enumerate(moves)]
    for copy in copies:
        copy.start()
    for copy in copies:
        copy.wait()
    for rows, columns, out in ((row_ref, col_ref, own_ref), (other_rows, other_cols, far_ref)):
        a, b = rows[...], columns[...]
        out[:, :BLOCK] = dot(a, b, 1, 1)
        out[:, BLOCK:] = dot(turned(a), b, 1, 1)


def density(band, *arrays):
    product = pltpu.VMEM((BLOCK, 2 * BLOCK), jnp.float32)
    points = pltpu.VMEM((BLOCK, LANES), jnp.bfloat16)
    in_hbm = pl.BlockSpec(memory_space=pltpu.HBM)
    return pl.pallas_call(
        density_body,
        out_shape=[product, product, points, points],
        in_specs=[IN_SMEM] + [in_hbm] * len(arrays),
        out_specs=[IN_VMEM] * 4,
        scratch_shapes=[pltpu.VMEM((BLOCK, LANES), jnp.bfloat16)] * 2
        + [pltpu.SemaphoreType.DMA((4 * NY + 2 * NZ,))],
        compiler_params=PARAMS,
        name="density",
    )(band, *map(away, arrays))


def mix_body(odd_ref, own_ref, far_ref, half_ref, kern_ref, m_ref):
    odd = odd_ref[0] == 1
    sign = jnp.where(odd, -1.0, 1.0).astype(jnp.float32)
    for i in range(GROUPS):
        at = pl.ds(i * SLAB, SLAB)
        mine, other = kern_ref[i, 0], half_ref[i]
        k_re = jnp.where(odd, other, mine).astype(jnp.float32)
        k_im = jnp.where(odd, mine, other).astype(jnp.float32) * sign
        p_re, p_im = own_ref[at, :BLOCK], own_ref[at, BLOCK:]
        total_re = k_re * p_re - k_im * p_im
        total_im = k_re * p_im + k_im * p_re
        k_re = kern_ref[i, 1].astype(jnp.float32)
        k_im = kern_ref[i, 2].astype(jnp.float32) * -sign
        p_re, p_im = far_ref[at, :BLOCK], far_ref[at, BLOCK:]
        total_re += k_re * p_re - k_im * p_im
        total_im += k_re * p_im + k_im * p_re
        m_ref[at, :BLOCK] = total_re.astype(jnp.bfloat16)
        m_ref[at, BLOCK:] = total_im.astype(jnp.bfloat16)


def mix(odd, *arrays):
    return pl.pallas_call(
        mix_body,
        out_shape=pltpu.VMEM((BLOCK, 2 * BLOCK), jnp.bfloat16),
        in_specs=[IN_SMEM] + [IN_VMEM] * 4,
        out_specs=IN_VMEM,
        compiler_params=PARAMS,
        name="mix",
    )(odd, *map(near, arrays))


def prepare_body(row_ref, col_ref, left_ref, right_ref):
    flipped = row_ref[...].T
    left_ref[pl.ds(0, WHOLE), :BLOCK] = flipped[:WHOLE]
    left_ref[pl.ds(WHOLE, REST), :BLOCK] = flipped[TAIL : TAIL + REST]
    left_ref[pl.ds(0, WHOLE), BLOCK:] = flipped[WHOLE:TAIL]
    left_ref[pl.ds(WHOLE, REST), BLOCK:] = flipped[TAIL + 64 : TAIL + 64 + REST]
    col = col_ref[...]
    right_ref[pl.ds(0, BLOCK), :] = col
    right_ref[pl.ds(BLOCK, BLOCK), :] = -turned(col)


def prepare(rows, cols):
    return pl.pallas_call(
        prepare_body,
        out_shape=[
            pltpu.VMEM((NB, 2 * BLOCK), jnp.bfloat16),
            pltpu.VMEM((2 * BLOCK, LANES), jnp.bfloat16),
        ],
        in_specs=[IN_VMEM] * 2,
        out_specs=[IN_VMEM] * 2,
        compiler_params=PARAMS,
        name="prepare",
    )(near(rows), near(cols))


def place_of(d):
    yx, z = d // NZ, d % NZ
    return (yx * 2 + z % 2) * (NZ // 2) + z // 2


def project_body(m_ref, left_ref, right_ref, out_ref, x_ref, part_ref, sem):
    y = dot(m_ref[...], right_ref[...], 1, 0)
    high = y.astype(jnp.bfloat16)
    low = (y - high.astype(jnp.float32)).astype(jnp.bfloat16)
    high = jnp.concatenate([high, turned(high)], axis=0)
    low = jnp.concatenate([low, turned(low)], axis=0)
    x_ref[pl.ds(NB, 8), :] = jnp.zeros((8, LANES), jnp.float32)
    copies = []
    for part, (start, size) in enumerate(((0, 224), (224, 208))):
        at = pl.ds(start, size)
        x_ref[at, :] = -(dot(left_ref[at, :], high, 1, 0) + dot(left_ref[at, :], low, 1, 0))
        some = GROUPS * NZ // 2
        for d in range(part * some, (part + 1) * some):
            part_ref[place_of(d)] = x_ref[pl.ds(27 * d // 4, 8), :].astype(jnp.bfloat16)
        chosen = pl.ds(part * some, some)
        copy = pltpu.make_async_copy(part_ref.at[chosen], out_ref.at[chosen], sem.at[part])
        copy.start()
        copies.append(copy)
    for copy in copies:
        copy.wait()


def project(m, left, right):
    windows = (GROUPS * NZ, 8, LANES)
    return pl.pallas_call(
        project_body,
        out_shape=jax.ShapeDtypeStruct(windows, jnp.bfloat16),
        in_specs=[IN_VMEM] * 3,
        out_specs=pl.BlockSpec(memory_space=pltpu.HBM),
        scratch_shapes=[
            pltpu.VMEM((NB + 8, LANES), jnp.float32),
            pltpu.VMEM(windows, jnp.bfloat16),
            pltpu.SemaphoreType.DMA((2,)),
        ],
        compiler_params=PARAMS,
        name="project",
    )(near(m), near(left), near(right))


def bundle_body(*refs):
    *blocks, out_ref = refs
    for i, ref in enumerate(blocks):
        out_ref[i] = ref[...]


def bundle(*blocks):
    return pl.pallas_call(
        bundle_body,
        out_shape=pltpu.VMEM((len(blocks), SLAB, LANES), jnp.bfloat16),
        in_specs=[IN_VMEM] * len(blocks),
        out_specs=IN_VMEM,
        compiler_params=PARAMS,
        name="bundle",
    )(*map(near, blocks))


def reduce_windows(windows):
    quads = NZ // 2
    wide = [[g * NZ + 2 * j + i for g in range(GROUPS) for i in range(2)] for j in range(quads)]
    deep = [[g * NZ + 2 * j + i for j in range(quads)] for g in range(GROUPS) for i in range(2)]
    parts = windows.reshape(2 * GROUPS, quads, 8, LANES)
    parts = lax.all_to_all(parts, "band", 0, 0, axis_index_groups=wide)
    parts = jnp.sum(parts.astype(jnp.float32), axis=0)
    total = jnp.sum(lax.all_to_all(parts, "band", 0, 0, axis_index_groups=deep), axis=0)
    real = jnp.concatenate([total[:, :WHOLE], total[:, TAIL : TAIL + REST]], axis=1)
    imag = jnp.concatenate([total[:, WHOLE:TAIL], total[:, TAIL + 64 : TAIL + 64 + REST]], axis=1)
    return jnp.stack([real, imag])


def on_device(orbitals, kernels, pair_kdiff, stored_kernel_index):
    group = lax.axis_index("kgrp")
    band = lax.axis_index("band")
    odd = (group % 2).reshape(1)

    own = lay(orbitals)
    first = swap_groups(pair_kdiff, 1), swap_groups(pair_kdiff, 2), swap_groups(own, 2)
    diff_core, diff_far, far = lax.optimization_barrier(first)

    over_yx = [[g * NZ + i for g in range(GROUPS)] for i in range(NZ)]
    sends = pack(odd, pair_kdiff, diff_core, diff_far, stored_kernel_index, kernels)

    both = bundle(own, far)
    steps = [shift(both, 1, 0, 0), shift(both, -1, 0, 0), shift(both, 0, 0, 1), shift(both, 0, 0, -1)]
    up, down, ahead, behind, sends = lax.optimization_barrier((*steps, sends))
    over = shift(up, 1, 0, 0)
    kern = lax.all_to_all(sends, "band", 0, 0, axis_index_groups=over_yx)
    cols = [both, ahead, behind]
    for _ in range(2):
        ahead, behind = shift(ahead, 0, 0, 1), shift(behind, 0, 0, -1)
        cols += [ahead, behind]
    cols.append(shift(ahead, 0, 0, 1))
    owns = bundle(own, up[0], over[0], down[0])
    sides = shift(owns, 0, 1, 0), other_side(owns)
    kern, over, sides, cols = lax.optimization_barrier((kern, over, sides, cols))
    half = swap_groups(kern[:, 0], 1)

    p_own, p_far, rows, cols = density(band.reshape(1), both, up, over, down, *sides, *cols)
    m_own = swap_groups(mix(odd, p_own, p_far, half, kern), 1)
    left, right = prepare(rows, cols)
    total = reduce_windows(project(m_own, left, right))
    flat = total.reshape(2, 8 * NB)
    flat = lax.dynamic_slice(flat, (0, band * 27 % 4 * 108), (2, 27 * 108))
    return flat[None]


def solution(mesh):
    return jax.shard_map(
        on_device,
        mesh=mesh,
        in_specs=(P("kgrp", None, "band", None), P(None, None, "band", None), P("kgrp"), P()),
        out_specs=P("kgrp", None, "band"),
        check_vma=False,
    )
```

```python
import jax
import jax.numpy as jnp
from jax import lax
from jax.experimental import pallas as pl
from jax.experimental.pallas import tpu as pltpu
from jax.sharding import PartitionSpec as P

NB = 432
SLAB = 64
NY, NX, NZ = 4, 2, 8
GROUPS = NY * NX
BLOCK = NZ * SLAB
WHOLE = 384
REST = NB - WHOLE
TAIL = 2 * WHOLE
LANES = TAIL + 128
Z_ORDER = (0, -1, 1, -2, 2, -3, 3, -4)
VMEM = 24 * 1024 * 1024

IN_VMEM = pl.BlockSpec(memory_space=pltpu.VMEM)
IN_SMEM = pl.BlockSpec(memory_space=pltpu.SMEM)
ANYWHERE = pl.BlockSpec(memory_space=pl.ANY)
PARAMS = pltpu.CompilerParams(vmem_limit_bytes=VMEM)


def band_route(dy, dx, dz):
    route = []
    for y in range(NY):
        for x in range(NX):
            for z in range(NZ):
                there = ((y + dy) % NY * NX + (x + dx) % NX) * NZ + (z + dz) % NZ
                route.append(((y * NX + x) * NZ + z, there))
    return route


def shift(block, dy, dx, dz):
    return lax.ppermute(block, "band", band_route(dy, dx, dz))


def swap_groups(block, bit):
    return lax.ppermute(block, "kgrp", [(k, k ^ bit) for k in range(4)])


def other_side(block):
    route = [(i, j) for i, j in band_route(0, 1, 0)]
    both = [((k ^ 2) * 64 + i, k * 64 + j) for k in range(4) for i, j in route]
    return lax.ppermute(block, ("kgrp", "band"), both)


def dot(a, b, a_axis, b_axis):
    dims = (((a_axis,), (b_axis,)), ((), ()))
    return lax.dot_general(a, b, dims, preferred_element_type=jnp.float32)


def near(array):
    return pltpu.with_memory_space_constraint(array, pltpu.VMEM)


def away(array):
    return pltpu.with_memory_space_constraint(array, pltpu.HBM)


def lay_body(orbit_ref, out_ref):
    gap = jnp.zeros((SLAB, 64 - REST), jnp.float32)
    real, imag = orbit_ref[0, 0], orbit_ref[0, 1]
    out_ref[:, :WHOLE] = real[:, :WHOLE]
    out_ref[:, WHOLE:TAIL] = imag[:, :WHOLE]
    last = [real[:, WHOLE:].astype(jnp.float32), gap, imag[:, WHOLE:].astype(jnp.float32), gap]
    out_ref[:, TAIL:] = jnp.concatenate(last, axis=1).astype(jnp.bfloat16)


def lay(orbitals):
    return pl.pallas_call(
        lay_body,
        out_shape=pltpu.VMEM((SLAB, LANES), jnp.bfloat16),
        in_specs=[IN_VMEM],
        out_specs=IN_VMEM,
        name="lay",
    )(orbitals)


def turned(rows):
    last = rows[:, TAIL:].astype(jnp.float32)
    lane = lax.broadcasted_iota(jnp.int32, last.shape, 1)
    last = pltpu.roll(last, 64, 1) * jnp.where(lane < 64, 1.0, -1.0)
    return jnp.concatenate(
        [rows[:, WHOLE:TAIL], -rows[:, :WHOLE], last.astype(rows.dtype)], axis=1
    )


def pack_body(odd_ref, own_ref, core_ref, far_ref, stored_ref, kernels_ref, out_ref, held, sem, out_sem):
    odd = odd_ref[0] == 1
    own, core, far = stored_ref[own_ref[0]], stored_ref[core_ref[0]], stored_ref[far_ref[0]]
    shared = jnp.where(odd, own, core)
    single = jnp.where(odd, core, far)
    copies = []
    for i in range(GROUPS):
        at = pl.ds(i * BLOCK, BLOCK)
        half = kernels_ref.at[shared, odd_ref[0], :, at]
        copies.append(pltpu.make_async_copy(half, held.at[i, 0], sem.at[0, i]))
        both = kernels_ref.at[single, :, :, at]
        copies.append(pltpu.make_async_copy(both, held.at[i, pl.ds(1, 2)], sem.at[1, i]))
    for copy in copies:
        copy.start()
    sent = []
    for i in range(GROUPS):
        copies[2 * i].wait()
        copies[2 * i + 1].wait()
        sent.append(pltpu.make_async_copy(held.at[i], out_ref.at[i], out_sem.at[i]))
        sent[i].start()
    for copy in sent:
        copy.wait()


def pack(odd, own, core, far, stored, kernels):
    blocks = (GROUPS, 3, SLAB, BLOCK)
    in_hbm = pl.BlockSpec(memory_space=pltpu.HBM)
    return pl.pallas_call(
        pack_body,
        out_shape=jax.ShapeDtypeStruct(blocks, jnp.bfloat16),
        in_specs=[IN_SMEM] * 5 + [in_hbm],
        out_specs=in_hbm,
        scratch_shapes=[
            pltpu.VMEM(blocks, jnp.bfloat16),
            pltpu.SemaphoreType.DMA((2, GROUPS)),
            pltpu.SemaphoreType.DMA((GROUPS,)),
        ],
        compiler_params=PARAMS,
        name="pack",
    )(odd, own, core, far, away(stored), away(kernels))


def density_body(band_ref, *refs):
    four_ref, up_ref, over_here, over_side, down_ref = refs[:5]
    cols = refs[5 : 5 + NZ]
    own_ref, far_ref, row_ref, col_ref, other_rows, other_cols, sem = refs[5 + NZ :]

    band = band_ref[0]
    y, x, z = band // (NX * NZ), band // NZ % NX, band % NZ

    def row_at(dy, side):
        place = (y + NY - dy) % NY * NX + (x + side) % NX
        return pl.ds(pl.multiple_of(place * SLAB, SLAB), SLAB)

    moves = []
    for piece, dz in zip(cols, Z_ORDER):
        at = pl.ds(pl.multiple_of((z + NZ + dz) % NZ * SLAB, SLAB), SLAB)
        moves.append((piece.at[0], col_ref.at[at, :]))
        moves.append((piece.at[1], other_cols.at[at, :]))
    for side, piece in enumerate((over_here, over_side)):
        moves.append((piece.at[0], row_ref.at[row_at(2, side), :]))
        moves.append((piece.at[1], other_rows.at[row_at(2, side), :]))
    copies = [pltpu.make_async_copy(*move, sem.at[i]) for i, move in enumerate(moves)]
    for copy in copies:
        copy.start()
    for dy, piece in ((0, four_ref), (1, up_ref), (3, down_ref)):
        for side in range(NX):
            row_ref[row_at(dy, side), :] = piece[2 * side]
            other_rows[row_at(dy, side), :] = piece[2 * side + 1]
    for copy in copies:
        copy.wait()
    for rows, columns, out in ((row_ref, col_ref, own_ref), (other_rows, other_cols, far_ref)):
        a, b = rows[...], columns[...]
        out[:, :BLOCK] = dot(a, b, 1, 1)
        out[:, BLOCK:] = dot(turned(a), b, 1, 1)


def density(band, four, up, over, down, cols):
    product = pltpu.VMEM((BLOCK, 2 * BLOCK), jnp.float32)
    points = pltpu.VMEM((BLOCK, LANES), jnp.bfloat16)
    in_hbm = pl.BlockSpec(memory_space=pltpu.HBM)
    specs = [IN_VMEM] * 2 + [in_hbm] * 2 + [IN_VMEM] + [in_hbm] * NZ
    arrays = [near(four), near(up), *map(away, over), near(down), *map(away, cols)]
    return pl.pallas_call(
        density_body,
        out_shape=[product, product, points, points],
        in_specs=[IN_SMEM] + specs,
        out_specs=[IN_VMEM] * 4,
        scratch_shapes=[pltpu.VMEM((BLOCK, LANES), jnp.bfloat16)] * 2
        + [pltpu.SemaphoreType.DMA((2 * NX + 2 * NZ,))],
        compiler_params=PARAMS,
        name="density",
    )(band, *arrays)


def mix_body(odd_ref, own_ref, far_ref, core_ref, kern_ref, m_ref):
    odd = odd_ref[0] == 1
    sign = jnp.where(odd, -1.0, 1.0).astype(jnp.float32)
    for i in range(GROUPS):
        at = pl.ds(i * SLAB, SLAB)
        mine, other = kern_ref[i, 0], core_ref[i, 0]
        k_re = jnp.where(odd, other, mine).astype(jnp.float32)
        k_im = jnp.where(odd, mine, other).astype(jnp.float32) * sign
        p_re, p_im = own_ref[at, :BLOCK], own_ref[at, BLOCK:]
        total_re = k_re * p_re - k_im * p_im
        total_im = k_re * p_im + k_im * p_re
        k_re = kern_ref[i, 1].astype(jnp.float32)
        k_im = kern_ref[i, 2].astype(jnp.float32) * -sign
        p_re, p_im = far_ref[at, :BLOCK], far_ref[at, BLOCK:]
        total_re += k_re * p_re - k_im * p_im
        total_im += k_re * p_im + k_im * p_re
        m_ref[at, :BLOCK] = total_re.astype(jnp.bfloat16)
        m_ref[at, BLOCK:] = total_im.astype(jnp.bfloat16)


def mix(odd, *arrays):
    return pl.pallas_call(
        mix_body,
        out_shape=pltpu.VMEM((BLOCK, 2 * BLOCK), jnp.bfloat16),
        in_specs=[IN_SMEM] + [IN_VMEM] * 4,
        out_specs=IN_VMEM,
        compiler_params=PARAMS,
        name="mix",
    )(odd, *map(near, arrays))


def prepare_body(row_ref, col_ref, left_ref, right_ref):
    flipped = row_ref[...].T
    left_ref[pl.ds(0, WHOLE), :BLOCK] = flipped[:WHOLE]
    left_ref[pl.ds(WHOLE, REST), :BLOCK] = flipped[TAIL : TAIL + REST]
    left_ref[pl.ds(0, WHOLE), BLOCK:] = flipped[WHOLE:TAIL]
    left_ref[pl.ds(WHOLE, REST), BLOCK:] = flipped[TAIL + 64 : TAIL + 64 + REST]
    col = col_ref[...]
    right_ref[pl.ds(0, BLOCK), :] = col
    right_ref[pl.ds(BLOCK, BLOCK), :] = -turned(col)


def prepare(rows, cols):
    return pl.pallas_call(
        prepare_body,
        out_shape=[
            pltpu.VMEM((NB, 2 * BLOCK), jnp.bfloat16),
            pltpu.VMEM((2 * BLOCK, LANES), jnp.bfloat16),
        ],
        in_specs=[IN_VMEM] * 2,
        out_specs=[IN_VMEM] * 2,
        compiler_params=PARAMS,
        name="prepare",
    )(near(rows), near(cols))


def place_of(d):
    yx, z = d // NZ, d % NZ
    return (yx * 2 + z % 2) * (NZ // 2) + z // 2


def project_body(m_ref, left_ref, right_ref, out_ref, x_ref, part_ref, sem):
    y = dot(m_ref[...], right_ref[...], 1, 0)
    high = y.astype(jnp.bfloat16)
    low = (y - high.astype(jnp.float32)).astype(jnp.bfloat16)
    high = jnp.concatenate([high, turned(high)], axis=0)
    low = jnp.concatenate([low, turned(low)], axis=0)
    x_ref[pl.ds(NB, 8), :] = jnp.zeros((8, LANES), jnp.float32)
    copies = []
    for part, (start, size) in enumerate(((0, 224), (224, 208))):
        at = pl.ds(start, size)
        x_ref[at, :] = -(dot(left_ref[at, :], high, 1, 0) + dot(left_ref[at, :], low, 1, 0))
        some = GROUPS * NZ // 2
        for d in range(part * some, (part + 1) * some):
            part_ref[place_of(d)] = x_ref[pl.ds(27 * d // 4, 8), :].astype(jnp.bfloat16)
        chosen = pl.ds(part * some, some)
        copy = pltpu.make_async_copy(part_ref.at[chosen], out_ref.at[chosen], sem.at[part])
        copy.start()
        copies.append(copy)
    for copy in copies:
        copy.wait()


def project(m, left, right):
    windows = (GROUPS * NZ, 8, LANES)
    return pl.pallas_call(
        project_body,
        out_shape=jax.ShapeDtypeStruct(windows, jnp.bfloat16),
        in_specs=[IN_VMEM] * 3,
        out_specs=pl.BlockSpec(memory_space=pltpu.HBM),
        scratch_shapes=[
            pltpu.VMEM((NB + 8, LANES), jnp.float32),
            pltpu.VMEM(windows, jnp.bfloat16),
            pltpu.SemaphoreType.DMA((2,)),
        ],
        compiler_params=PARAMS,
        name="project",
    )(near(m), near(left), near(right))


def bundle_body(own_ref, far_ref, own_side, far_side, four_ref, both_ref):
    for i, ref in enumerate((own_ref, far_ref, own_side, far_side)):
        four_ref[i] = ref[...]
    both_ref[0] = own_ref[...]
    both_ref[1] = far_ref[...]


def bundle(*blocks):
    return pl.pallas_call(
        bundle_body,
        out_shape=[
            pltpu.VMEM((4, SLAB, LANES), jnp.bfloat16),
            pltpu.VMEM((2, SLAB, LANES), jnp.bfloat16),
        ],
        in_specs=[IN_VMEM] * 4,
        out_specs=[IN_VMEM] * 2,
        compiler_params=PARAMS,
        name="bundle",
    )(*map(near, blocks))


def reduce_windows(windows):
    quads = NZ // 2
    wide = [[g * NZ + 2 * j + i for g in range(GROUPS) for i in range(2)] for j in range(quads)]
    deep = [[g * NZ + 2 * j + i for j in range(quads)] for g in range(GROUPS) for i in range(2)]
    parts = windows.reshape(2 * GROUPS, quads, 8, LANES)
    parts = lax.all_to_all(parts, "band", 0, 0, axis_index_groups=wide)
    parts = jnp.sum(parts.astype(jnp.float32), axis=0)
    total = jnp.sum(lax.all_to_all(parts, "band", 0, 0, axis_index_groups=deep), axis=0)
    real = jnp.concatenate([total[:, :WHOLE], total[:, TAIL : TAIL + REST]], axis=1)
    imag = jnp.concatenate([total[:, WHOLE:TAIL], total[:, TAIL + 64 : TAIL + 64 + REST]], axis=1)
    return jnp.stack([real, imag])


def on_device(orbitals, kernels, pair_kdiff, stored_kernel_index):
    group = lax.axis_index("kgrp")
    band = lax.axis_index("band")
    odd = (group % 2).reshape(1)

    own = lay(orbitals)
    first = (
        swap_groups(pair_kdiff, 1),
        swap_groups(pair_kdiff, 2),
        swap_groups(own, 2),
        shift(own, 0, 1, 0),
        other_side(own),
    )
    diff_core, diff_far = first[:2]
    far, own_side, far_side = lax.optimization_barrier(first)[2:]

    over_yx = [[g * NZ + i for g in range(GROUPS)] for i in range(NZ)]
    sends = pack(odd, pair_kdiff, diff_core, diff_far, stored_kernel_index, kernels)

    four, both = bundle(own, far, own_side, far_side)
    steps = shift(four, 1, 0, 0), shift(four, -1, 0, 0), shift(both, 0, 0, 1), shift(both, 0, 0, -1)
    up, down, ahead, behind, sends = lax.optimization_barrier((*steps, sends))
    over = shift(up[:2], 1, 0, 0), shift(down[2:], -1, 0, 0)
    kern = lax.all_to_all(sends, "band", 0, 0, axis_index_groups=over_yx)
    cols = [both, ahead, behind]
    for _ in range(2):
        ahead, behind = shift(ahead, 0, 0, 1), shift(behind, 0, 0, -1)
        cols += [ahead, behind]
    cols.append(shift(ahead, 0, 0, 1))
    kern, over, cols = lax.optimization_barrier((kern, over, cols))
    kern_core = swap_groups(kern, 1)

    p_own, p_far, rows, cols = density(band.reshape(1), four, up, over, down, cols)
    m_own = swap_groups(mix(odd, p_own, p_far, kern_core, kern), 1)
    left, right = prepare(rows, cols)
    total = reduce_windows(project(m_own, left, right))
    flat = total.reshape(2, 8 * NB)
    flat = lax.dynamic_slice(flat, (0, band * 27 % 4 * 108), (2, 27 * 108))
    return flat[None]


def solution(mesh):
    return jax.shard_map(
        on_device,
        mesh=mesh,
        in_specs=(P("kgrp", None, "band", None), P(None, None, "band", None), P("kgrp"), P()),
        out_specs=P("kgrp", None, "band"),
        check_vma=False,
    )
```

```python
import jax
import jax.numpy as jnp
from jax import lax
from jax.experimental import pallas as pl
from jax.experimental.pallas import tpu as pltpu
from jax.sharding import PartitionSpec as P

NB = 432
SLAB = 64
NY, NX, NZ = 4, 2, 8
GROUPS = NY * NX
BLOCK = NZ * SLAB
WHOLE = 384
REST = NB - WHOLE
TAIL = 2 * WHOLE
LANES = TAIL + 128
Z_ORDER = (0, -1, 1, -2, 2, -3, 3, -4)
VMEM = 24 * 1024 * 1024

IN_VMEM = pl.BlockSpec(memory_space=pltpu.VMEM)
IN_SMEM = pl.BlockSpec(memory_space=pltpu.SMEM)
ANYWHERE = pl.BlockSpec(memory_space=pl.ANY)
PARAMS = pltpu.CompilerParams(vmem_limit_bytes=VMEM)


def band_route(dy, dx, dz):
    route = []
    for y in range(NY):
        for x in range(NX):
            for z in range(NZ):
                there = ((y + dy) % NY * NX + (x + dx) % NX) * NZ + (z + dz) % NZ
                route.append(((y * NX + x) * NZ + z, there))
    return route


def shift(block, dy, dx, dz):
    return lax.ppermute(block, "band", band_route(dy, dx, dz))


def swap_groups(block, bit):
    return lax.ppermute(block, "kgrp", [(k, k ^ bit) for k in range(4)])


def other_side(block):
    route = [(i, j) for i, j in band_route(0, 1, 0)]
    both = [((k ^ 2) * 64 + i, k * 64 + j) for k in range(4) for i, j in route]
    return lax.ppermute(block, ("kgrp", "band"), both)


def dot(a, b, a_axis, b_axis):
    dims = (((a_axis,), (b_axis,)), ((), ()))
    return lax.dot_general(a, b, dims, preferred_element_type=jnp.float32)


def near(array):
    return pltpu.with_memory_space_constraint(array, pltpu.VMEM)


def away(array):
    return pltpu.with_memory_space_constraint(array, pltpu.HBM)


def lay_body(orbit_ref, out_ref):
    gap = jnp.zeros((SLAB, 64 - REST), jnp.float32)
    real, imag = orbit_ref[0, 0], orbit_ref[0, 1]
    out_ref[:, :WHOLE] = real[:, :WHOLE]
    out_ref[:, WHOLE:TAIL] = imag[:, :WHOLE]
    last = [real[:, WHOLE:].astype(jnp.float32), gap, imag[:, WHOLE:].astype(jnp.float32), gap]
    out_ref[:, TAIL:] = jnp.concatenate(last, axis=1).astype(jnp.bfloat16)


def lay(orbitals):
    return pl.pallas_call(
        lay_body,
        out_shape=pltpu.VMEM((SLAB, LANES), jnp.bfloat16),
        in_specs=[IN_VMEM],
        out_specs=IN_VMEM,
        name="lay",
    )(orbitals)


def turned(rows):
    last = rows[:, TAIL:].astype(jnp.float32)
    lane = lax.broadcasted_iota(jnp.int32, last.shape, 1)
    last = pltpu.roll(last, 64, 1) * jnp.where(lane < 64, 1.0, -1.0)
    return jnp.concatenate(
        [rows[:, WHOLE:TAIL], -rows[:, :WHOLE], last.astype(rows.dtype)], axis=1
    )


def pack_body(odd_ref, own_ref, core_ref, far_ref, stored_ref, kernels_ref, out_ref, sem):
    odd = odd_ref[0] == 1
    own, core, far = stored_ref[own_ref[0]], stored_ref[core_ref[0]], stored_ref[far_ref[0]]
    shared = jnp.where(odd, own, core)
    single = jnp.where(odd, core, far)
    copies = []
    for i in range(GROUPS):
        at = pl.ds(i * BLOCK, BLOCK)
        half = kernels_ref.at[shared, odd_ref[0], :, at]
        copies.append(pltpu.make_async_copy(half, out_ref.at[i, 0], sem.at[0, i]))
        both = kernels_ref.at[single, :, :, at]
        copies.append(pltpu.make_async_copy(both, out_ref.at[i, pl.ds(1, 2)], sem.at[1, i]))
    for copy in copies:
        copy.start()
    for copy in copies:
        copy.wait()


def pack(odd, own, core, far, stored, kernels):
    return pl.pallas_call(
        pack_body,
        out_shape=jax.ShapeDtypeStruct((GROUPS, 3, SLAB, BLOCK), jnp.bfloat16),
        in_specs=[IN_SMEM] * 5 + [pl.BlockSpec(memory_space=pltpu.HBM)],
        out_specs=IN_VMEM,
        scratch_shapes=[pltpu.SemaphoreType.DMA((2, GROUPS))],
        compiler_params=PARAMS,
        name="pack",
    )(odd, own, core, far, stored, away(kernels))


def density_body(band_ref, *refs):
    four_ref, up_ref, over_here, over_side, down_ref = refs[:5]
    cols = refs[5 : 5 + NZ]
    own_ref, far_ref, row_ref, col_ref, other_rows, other_cols, sem = refs[5 + NZ :]

    band = band_ref[0]
    y, x, z = band // (NX * NZ), band // NZ % NX, band % NZ

    def row_at(dy, side):
        place = (y + NY - dy) % NY * NX + (x + side) % NX
        return pl.ds(pl.multiple_of(place * SLAB, SLAB), SLAB)

    moves = []
    for piece, dz in zip(cols, Z_ORDER):
        at = pl.ds(pl.multiple_of((z + NZ + dz) % NZ * SLAB, SLAB), SLAB)
        moves.append((piece.at[0], col_ref.at[at, :]))
        moves.append((piece.at[1], other_cols.at[at, :]))
    for side, piece in enumerate((over_here, over_side)):
        moves.append((piece.at[0], row_ref.at[row_at(2, side), :]))
        moves.append((piece.at[1], other_rows.at[row_at(2, side), :]))
    copies = [pltpu.make_async_copy(*move, sem.at[i]) for i, move in enumerate(moves)]
    for copy in copies:
        copy.start()
    for dy, piece in ((0, four_ref), (1, up_ref), (3, down_ref)):
        for side in range(NX):
            row_ref[row_at(dy, side), :] = piece[2 * side]
            other_rows[row_at(dy, side), :] = piece[2 * side + 1]
    for copy in copies:
        copy.wait()
    for rows, columns, out in ((row_ref, col_ref, own_ref), (other_rows, other_cols, far_ref)):
        a, b = rows[...], columns[...]
        out[:, :BLOCK] = dot(a, b, 1, 1)
        out[:, BLOCK:] = dot(turned(a), b, 1, 1)


def density(band, four, up, over, down, cols):
    product = pltpu.VMEM((BLOCK, 2 * BLOCK), jnp.float32)
    points = pltpu.VMEM((BLOCK, LANES), jnp.bfloat16)
    in_hbm = pl.BlockSpec(memory_space=pltpu.HBM)
    specs = [IN_VMEM] * 2 + [in_hbm] * 2 + [IN_VMEM] + [in_hbm] * NZ
    arrays = [near(four), near(up), *map(away, over), near(down), *map(away, cols)]
    return pl.pallas_call(
        density_body,
        out_shape=[product, product, points, points],
        in_specs=[IN_SMEM] + specs,
        out_specs=[IN_VMEM] * 4,
        scratch_shapes=[pltpu.VMEM((BLOCK, LANES), jnp.bfloat16)] * 2
        + [pltpu.SemaphoreType.DMA((2 * NX + 2 * NZ,))],
        compiler_params=PARAMS,
        name="density",
    )(band, *arrays)


def mix_body(odd_ref, own_ref, far_ref, half_ref, kern_ref, m_ref):
    odd = odd_ref[0] == 1
    sign = jnp.where(odd, -1.0, 1.0).astype(jnp.float32)
    for i in range(GROUPS):
        at = pl.ds(i * SLAB, SLAB)
        mine, other = kern_ref[i, 0], half_ref[i]
        k_re = jnp.where(odd, other, mine).astype(jnp.float32)
        k_im = jnp.where(odd, mine, other).astype(jnp.float32) * sign
        p_re, p_im = own_ref[at, :BLOCK], own_ref[at, BLOCK:]
        total_re = k_re * p_re - k_im * p_im
        total_im = k_re * p_im + k_im * p_re
        k_re = kern_ref[i, 1].astype(jnp.float32)
        k_im = kern_ref[i, 2].astype(jnp.float32) * -sign
        p_re, p_im = far_ref[at, :BLOCK], far_ref[at, BLOCK:]
        total_re += k_re * p_re - k_im * p_im
        total_im += k_re * p_im + k_im * p_re
        m_ref[at, :BLOCK] = total_re.astype(jnp.bfloat16)
        m_ref[at, BLOCK:] = total_im.astype(jnp.bfloat16)


def mix(odd, *arrays):
    return pl.pallas_call(
        mix_body,
        out_shape=pltpu.VMEM((BLOCK, 2 * BLOCK), jnp.bfloat16),
        in_specs=[IN_SMEM] + [IN_VMEM] * 4,
        out_specs=IN_VMEM,
        compiler_params=PARAMS,
        name="mix",
    )(odd, *map(near, arrays))


def prepare_body(row_ref, col_ref, left_ref, right_ref):
    flipped = row_ref[...].T
    left_ref[pl.ds(0, WHOLE), :BLOCK] = flipped[:WHOLE]
    left_ref[pl.ds(WHOLE, REST), :BLOCK] = flipped[TAIL : TAIL + REST]
    left_ref[pl.ds(0, WHOLE), BLOCK:] = flipped[WHOLE:TAIL]
    left_ref[pl.ds(WHOLE, REST), BLOCK:] = flipped[TAIL + 64 : TAIL + 64 + REST]
    col = col_ref[...]
    right_ref[pl.ds(0, BLOCK), :] = col
    right_ref[pl.ds(BLOCK, BLOCK), :] = -turned(col)


def prepare(rows, cols):
    return pl.pallas_call(
        prepare_body,
        out_shape=[
            pltpu.VMEM((NB, 2 * BLOCK), jnp.bfloat16),
            pltpu.VMEM((2 * BLOCK, LANES), jnp.bfloat16),
        ],
        in_specs=[IN_VMEM] * 2,
        out_specs=[IN_VMEM] * 2,
        compiler_params=PARAMS,
        name="prepare",
    )(near(rows), near(cols))


def place_of(d):
    yx, z = d // NZ, d % NZ
    return (yx * 2 + z % 2) * (NZ // 2) + z // 2


def project_body(m_ref, left_ref, right_ref, out_ref, x_ref, part_ref, sem):
    y = dot(m_ref[...], right_ref[...], 1, 0)
    high = y.astype(jnp.bfloat16)
    low = (y - high.astype(jnp.float32)).astype(jnp.bfloat16)
    high = jnp.concatenate([high, turned(high)], axis=0)
    low = jnp.concatenate([low, turned(low)], axis=0)
    x_ref[pl.ds(NB, 8), :] = jnp.zeros((8, LANES), jnp.float32)
    copies = []
    for part, (start, size) in enumerate(((0, 224), (224, 208))):
        at = pl.ds(start, size)
        x_ref[at, :] = -(dot(left_ref[at, :], high, 1, 0) + dot(left_ref[at, :], low, 1, 0))
        some = GROUPS * NZ // 2
        for d in range(part * some, (part + 1) * some):
            part_ref[place_of(d)] = x_ref[pl.ds(27 * d // 4, 8), :].astype(jnp.bfloat16)
        chosen = pl.ds(part * some, some)
        copy = pltpu.make_async_copy(part_ref.at[chosen], out_ref.at[chosen], sem.at[part])
        copy.start()
        copies.append(copy)
    for copy in copies:
        copy.wait()


def project(m, left, right):
    windows = (GROUPS * NZ, 8, LANES)
    return pl.pallas_call(
        project_body,
        out_shape=jax.ShapeDtypeStruct(windows, jnp.bfloat16),
        in_specs=[IN_VMEM] * 3,
        out_specs=pl.BlockSpec(memory_space=pltpu.HBM),
        scratch_shapes=[
            pltpu.VMEM((NB + 8, LANES), jnp.float32),
            pltpu.VMEM(windows, jnp.bfloat16),
            pltpu.SemaphoreType.DMA((2,)),
        ],
        compiler_params=PARAMS,
        name="project",
    )(near(m), near(left), near(right))


def bundle_body(own_ref, far_ref, own_side, far_side, four_ref, both_ref):
    for i, ref in enumerate((own_ref, far_ref, own_side, far_side)):
        four_ref[i] = ref[...]
    both_ref[0] = own_ref[...]
    both_ref[1] = far_ref[...]


def bundle(*blocks):
    return pl.pallas_call(
        bundle_body,
        out_shape=[
            pltpu.VMEM((4, SLAB, LANES), jnp.bfloat16),
            pltpu.VMEM((2, SLAB, LANES), jnp.bfloat16),
        ],
        in_specs=[IN_VMEM] * 4,
        out_specs=[IN_VMEM] * 2,
        compiler_params=PARAMS,
        name="bundle",
    )(*map(near, blocks))


def reduce_windows(windows):
    quads = NZ // 2
    wide = [[g * NZ + 2 * j + i for g in range(GROUPS) for i in range(2)] for j in range(quads)]
    deep = [[g * NZ + 2 * j + i for j in range(quads)] for g in range(GROUPS) for i in range(2)]
    parts = windows.reshape(2 * GROUPS, quads, 8, LANES)
    parts = lax.all_to_all(parts, "band", 0, 0, axis_index_groups=wide)
    parts = jnp.sum(parts.astype(jnp.float32), axis=0)
    total = jnp.sum(lax.all_to_all(parts, "band", 0, 0, axis_index_groups=deep), axis=0)
    real = jnp.concatenate([total[:, :WHOLE], total[:, TAIL : TAIL + REST]], axis=1)
    imag = jnp.concatenate([total[:, WHOLE:TAIL], total[:, TAIL + 64 : TAIL + 64 + REST]], axis=1)
    return jnp.stack([real, imag])


def on_device(orbitals, kernels, pair_kdiff, stored_kernel_index):
    group = lax.axis_index("kgrp")
    band = lax.axis_index("band")
    odd = (group % 2).reshape(1)

    own = lay(orbitals)
    first = (
        swap_groups(pair_kdiff, 1),
        swap_groups(pair_kdiff, 2),
        swap_groups(own, 2),
        shift(own, 0, 1, 0),
        other_side(own),
    )
    diff_core, diff_far = first[:2]
    far, own_side, far_side = lax.optimization_barrier(first)[2:]

    over_yx = [[g * NZ + i for g in range(GROUPS)] for i in range(NZ)]
    sends = pack(odd, pair_kdiff, diff_core, diff_far, stored_kernel_index, kernels)

    four, both = bundle(own, far, own_side, far_side)
    steps = shift(four, 1, 0, 0), shift(four, -1, 0, 0), shift(both, 0, 0, 1), shift(both, 0, 0, -1)
    up, down, ahead, behind, sends = lax.optimization_barrier((*steps, sends))
    over = shift(up[:2], 1, 0, 0), shift(down[2:], -1, 0, 0)
    kern = lax.all_to_all(sends, "band", 0, 0, axis_index_groups=over_yx)
    cols = [both, ahead, behind]
    for _ in range(2):
        ahead, behind = shift(ahead, 0, 0, 1), shift(behind, 0, 0, -1)
        cols += [ahead, behind]
    cols.append(shift(ahead, 0, 0, 1))
    late = sum(block[0, 0, :1] for block in (*over, cols[-1]))
    kern = lax.optimization_barrier((kern, late))[0]
    half = swap_groups(kern[:, 0], 1)

    p_own, p_far, rows, cols = density(band.reshape(1), four, up, over, down, cols)
    m_own = swap_groups(mix(odd, p_own, p_far, half, kern), 1)
    left, right = prepare(rows, cols)
    total = reduce_windows(project(m_own, left, right))
    flat = total.reshape(2, 8 * NB)
    flat = lax.dynamic_slice(flat, (0, band * 27 % 4 * 108), (2, 27 * 108))
    return flat[None]


def solution(mesh):
    return jax.shard_map(
        on_device,
        mesh=mesh,
        in_specs=(P("kgrp", None, "band", None), P(None, None, "band", None), P("kgrp"), P()),
        out_specs=P("kgrp", None, "band"),
        check_vma=False,
    )
```

```python
import jax
import jax.numpy as jnp
from jax import lax
from jax.experimental import pallas as pl
from jax.experimental.pallas import tpu as pltpu
from jax.sharding import PartitionSpec as P

NB = 432
SLAB = 64
NY, NX, NZ = 4, 2, 8
GROUPS = NY * NX
BLOCK = NZ * SLAB
WHOLE = 384
REST = NB - WHOLE
TAIL = 2 * WHOLE
LANES = TAIL + 128
VMEM = 24 * 1024 * 1024

IN_VMEM = pl.BlockSpec(memory_space=pltpu.VMEM)
IN_SMEM = pl.BlockSpec(memory_space=pltpu.SMEM)
ANYWHERE = pl.BlockSpec(memory_space=pl.ANY)
PARAMS = pltpu.CompilerParams(vmem_limit_bytes=VMEM)


def band_route(dy, dx, dz):
    route = []
    for y in range(NY):
        for x in range(NX):
            for z in range(NZ):
                there = ((y + dy) % NY * NX + (x + dx) % NX) * NZ + (z + dz) % NZ
                route.append(((y * NX + x) * NZ + z, there))
    return route


def shift(block, dy, dx, dz):
    return lax.ppermute(block, "band", band_route(dy, dx, dz))


def swap_groups(block, bit):
    return lax.ppermute(block, "kgrp", [(k, k ^ bit) for k in range(4)])


def other_side(block):
    route = [(i, j) for i, j in band_route(0, 1, 0)]
    both = [((k ^ 2) * 64 + i, k * 64 + j) for k in range(4) for i, j in route]
    return lax.ppermute(block, ("kgrp", "band"), both)


def dot(a, b, a_axis, b_axis):
    dims = (((a_axis,), (b_axis,)), ((), ()))
    return lax.dot_general(a, b, dims, preferred_element_type=jnp.float32)


def near(array):
    return pltpu.with_memory_space_constraint(array, pltpu.VMEM)


def away(array):
    return pltpu.with_memory_space_constraint(array, pltpu.HBM)


def lay_body(orbit_ref, out_ref):
    gap = jnp.zeros((SLAB, 64 - REST), jnp.float32)
    real, imag = orbit_ref[0, 0], orbit_ref[0, 1]
    out_ref[:, :WHOLE] = real[:, :WHOLE]
    out_ref[:, WHOLE:TAIL] = imag[:, :WHOLE]
    last = [real[:, WHOLE:].astype(jnp.float32), gap, imag[:, WHOLE:].astype(jnp.float32), gap]
    out_ref[:, TAIL:] = jnp.concatenate(last, axis=1).astype(jnp.bfloat16)


def lay(orbitals):
    return pl.pallas_call(
        lay_body,
        out_shape=pltpu.VMEM((SLAB, LANES), jnp.bfloat16),
        in_specs=[IN_VMEM],
        out_specs=IN_VMEM,
        name="lay",
    )(orbitals)


def turned(rows):
    last = rows[:, TAIL:].astype(jnp.float32)
    lane = lax.broadcasted_iota(jnp.int32, last.shape, 1)
    last = pltpu.roll(last, 64, 1) * jnp.where(lane < 64, 1.0, -1.0)
    return jnp.concatenate(
        [rows[:, WHOLE:TAIL], -rows[:, :WHOLE], last.astype(rows.dtype)], axis=1
    )


def pack_body(odd_ref, own_ref, core_ref, far_ref, stored_ref, kernels_ref, out_ref, sem):
    odd = odd_ref[0] == 1
    own, core, far = stored_ref[own_ref[0]], stored_ref[core_ref[0]], stored_ref[far_ref[0]]
    shared = jnp.where(odd, own, core)
    single = jnp.where(odd, core, far)
    copies = []
    for i in range(GROUPS):
        at = pl.ds(i * BLOCK, BLOCK)
        half = kernels_ref.at[shared, odd_ref[0], :, at]
        copies.append(pltpu.make_async_copy(half, out_ref.at[i, 0], sem.at[0, i]))
        both = kernels_ref.at[single, :, :, at]
        copies.append(pltpu.make_async_copy(both, out_ref.at[i, pl.ds(1, 2)], sem.at[1, i]))
    for copy in copies:
        copy.start()
    for copy in copies:
        copy.wait()


def pack(odd, own, core, far, stored, kernels):
    return pl.pallas_call(
        pack_body,
        out_shape=jax.ShapeDtypeStruct((GROUPS, 3, SLAB, BLOCK), jnp.bfloat16),
        in_specs=[IN_SMEM] * 5 + [pl.BlockSpec(memory_space=pltpu.HBM)],
        out_specs=IN_VMEM,
        scratch_shapes=[pltpu.SemaphoreType.DMA((2, GROUPS))],
        compiler_params=PARAMS,
        name="pack",
    )(odd, own, core, far, stored, away(kernels))


def density_body(place_ref, slot_ref, *refs):
    four_ref, up_ref, over_here, over_side, down_ref = refs[:5]
    cols = refs[5 : 5 + NZ]
    own_ref, far_ref, row_ref, col_ref, other_rows, other_cols, sem = refs[5 + NZ :]

    def row_at(dy, side):
        return pl.ds(pl.multiple_of(place_ref[dy * NX + side] * SLAB, SLAB), SLAB)

    moves = []
    for i, piece in enumerate(cols):
        at = pl.ds(pl.multiple_of(slot_ref[i] * SLAB, SLAB), SLAB)
        moves.append((piece.at[0], col_ref.at[at, :]))
        moves.append((piece.at[1], other_cols.at[at, :]))
    for side, piece in enumerate((over_here, over_side)):
        moves.append((piece.at[0], row_ref.at[row_at(2, side), :]))
        moves.append((piece.at[1], other_rows.at[row_at(2, side), :]))
    copies = [pltpu.make_async_copy(*move, sem.at[i]) for i, move in enumerate(moves)]
    for copy in copies:
        copy.start()
    for dy, piece in ((0, four_ref), (1, up_ref), (3, down_ref)):
        for side in range(NX):
            row_ref[row_at(dy, side), :] = piece[2 * side]
            other_rows[row_at(dy, side), :] = piece[2 * side + 1]
    for copy in copies:
        copy.wait()
    for rows, columns, out in ((row_ref, col_ref, own_ref), (other_rows, other_cols, far_ref)):
        a, b = rows[...], columns[...]
        out[:, :BLOCK] = dot(a, b, 1, 1)
        out[:, BLOCK:] = dot(turned(a), b, 1, 1)


def density(place, slots, four, up, over, down, cols):
    product = pltpu.VMEM((BLOCK, 2 * BLOCK), jnp.float32)
    points = pltpu.VMEM((BLOCK, LANES), jnp.bfloat16)
    in_hbm = pl.BlockSpec(memory_space=pltpu.HBM)
    specs = [IN_VMEM] * 2 + [in_hbm] * 2 + [IN_VMEM] + [in_hbm] * NZ
    arrays = [near(four), near(up), *map(away, over), near(down), *map(away, cols)]
    return pl.pallas_call(
        density_body,
        out_shape=[product, product, points, points],
        in_specs=[IN_SMEM] * 2 + specs,
        out_specs=[IN_VMEM] * 4,
        scratch_shapes=[pltpu.VMEM((BLOCK, LANES), jnp.bfloat16)] * 2
        + [pltpu.SemaphoreType.DMA((2 * NX + 2 * NZ,))],
        compiler_params=PARAMS,
        name="density",
    )(place, slots, *arrays)


def mix_body(odd_ref, own_ref, far_ref, half_ref, kern_ref, m_ref):
    odd = odd_ref[0] == 1
    sign = jnp.where(odd, -1.0, 1.0).astype(jnp.float32)
    for i in range(GROUPS):
        at = pl.ds(i * SLAB, SLAB)
        mine, other = kern_ref[i, 0], half_ref[i]
        k_re = jnp.where(odd, other, mine).astype(jnp.float32)
        k_im = jnp.where(odd, mine, other).astype(jnp.float32) * sign
        p_re, p_im = own_ref[at, :BLOCK], own_ref[at, BLOCK:]
        total_re = k_re * p_re - k_im * p_im
        total_im = k_re * p_im + k_im * p_re
        k_re = kern_ref[i, 1].astype(jnp.float32)
        k_im = kern_ref[i, 2].astype(jnp.float32) * -sign
        p_re, p_im = far_ref[at, :BLOCK], far_ref[at, BLOCK:]
        total_re += k_re * p_re - k_im * p_im
        total_im += k_re * p_im + k_im * p_re
        m_ref[at, :BLOCK] = total_re.astype(jnp.bfloat16)
        m_ref[at, BLOCK:] = total_im.astype(jnp.bfloat16)


def mix(odd, *arrays):
    return pl.pallas_call(
        mix_body,
        out_shape=pltpu.VMEM((BLOCK, 2 * BLOCK), jnp.bfloat16),
        in_specs=[IN_SMEM] + [IN_VMEM] * 4,
        out_specs=IN_VMEM,
        compiler_params=PARAMS,
        name="mix",
    )(odd, *map(near, arrays))


def prepare_body(row_ref, col_ref, left_ref, right_ref):
    flipped = row_ref[...].T
    left_ref[pl.ds(0, WHOLE), :BLOCK] = flipped[:WHOLE]
    left_ref[pl.ds(WHOLE, REST), :BLOCK] = flipped[TAIL : TAIL + REST]
    left_ref[pl.ds(0, WHOLE), BLOCK:] = flipped[WHOLE:TAIL]
    left_ref[pl.ds(WHOLE, REST), BLOCK:] = flipped[TAIL + 64 : TAIL + 64 + REST]
    col = col_ref[...]
    right_ref[pl.ds(0, BLOCK), :] = col
    right_ref[pl.ds(BLOCK, BLOCK), :] = -turned(col)


def prepare(rows, cols):
    return pl.pallas_call(
        prepare_body,
        out_shape=[
            pltpu.VMEM((NB, 2 * BLOCK), jnp.bfloat16),
            pltpu.VMEM((2 * BLOCK, LANES), jnp.bfloat16),
        ],
        in_specs=[IN_VMEM] * 2,
        out_specs=[IN_VMEM] * 2,
        compiler_params=PARAMS,
        name="prepare",
    )(near(rows), near(cols))


def window_at(place):
    outer, half = place // (NZ // 2), place % (NZ // 2)
    return outer // 2 * NZ + 2 * half + outer % 2


def project_body(m_ref, left_ref, right_ref, out_ref, x_ref, part_ref, sem):
    y = dot(m_ref[...], right_ref[...], 1, 0)
    high = y.astype(jnp.bfloat16)
    low = (y - high.astype(jnp.float32)).astype(jnp.bfloat16)
    high = jnp.concatenate([high, turned(high)], axis=0)
    low = jnp.concatenate([low, turned(low)], axis=0)
    x_ref[pl.ds(NB, 8), :] = jnp.zeros((8, LANES), jnp.float32)
    copies = []
    for part, (start, size) in enumerate(((0, 224), (224, 208))):
        at = pl.ds(start, size)
        x_ref[at, :] = -(dot(left_ref[at, :], high, 1, 0) + dot(left_ref[at, :], low, 1, 0))
        some = GROUPS * NZ // 4
        for pair in range(part * some, (part + 1) * some):
            starts = [27 * window_at(2 * pair + i) // 4 for i in range(2)]
            rows = [x_ref[pl.ds(first, 8), :] for first in starts]
            part_ref[pair] = jnp.concatenate(rows, axis=0).astype(jnp.bfloat16)
        chosen = pl.ds(part * some, some)
        copy = pltpu.make_async_copy(part_ref.at[chosen], out_ref.at[chosen], sem.at[part])
        copy.start()
        copies.append(copy)
    for copy in copies:
        copy.wait()


def project(m, left, right):
    windows = (GROUPS * NZ // 2, 16, LANES)
    return pl.pallas_call(
        project_body,
        out_shape=jax.ShapeDtypeStruct(windows, jnp.bfloat16),
        in_specs=[IN_VMEM] * 3,
        out_specs=pl.BlockSpec(memory_space=pltpu.HBM),
        scratch_shapes=[
            pltpu.VMEM((NB + 8, LANES), jnp.float32),
            pltpu.VMEM(windows, jnp.bfloat16),
            pltpu.SemaphoreType.DMA((2,)),
        ],
        compiler_params=PARAMS,
        name="project",
    )(near(m), near(left), near(right))


def bundle_body(own_ref, far_ref, own_side, far_side, four_ref, both_ref):
    for i, ref in enumerate((own_ref, far_ref, own_side, far_side)):
        four_ref[i] = ref[...]
    both_ref[0] = own_ref[...]
    both_ref[1] = far_ref[...]


def bundle(*blocks):
    return pl.pallas_call(
        bundle_body,
        out_shape=[
            pltpu.VMEM((4, SLAB, LANES), jnp.bfloat16),
            pltpu.VMEM((2, SLAB, LANES), jnp.bfloat16),
        ],
        in_specs=[IN_VMEM] * 4,
        out_specs=[IN_VMEM] * 2,
        compiler_params=PARAMS,
        name="bundle",
    )(*map(near, blocks))


def reduce_windows(windows):
    quads = NZ // 2
    wide = [[g * NZ + 2 * j + i for g in range(GROUPS) for i in range(2)] for j in range(quads)]
    deep = [[g * NZ + 2 * j + i for j in range(quads)] for g in range(GROUPS) for i in range(2)]
    parts = windows.reshape(2 * GROUPS, quads, 8, LANES)
    parts = lax.all_to_all(parts, "band", 0, 0, axis_index_groups=wide)
    parts = jnp.sum(parts.astype(jnp.float32), axis=0)
    total = jnp.sum(lax.all_to_all(parts, "band", 0, 0, axis_index_groups=deep), axis=0)
    real = jnp.concatenate([total[:, :WHOLE], total[:, TAIL : TAIL + REST]], axis=1)
    imag = jnp.concatenate([total[:, WHOLE:TAIL], total[:, TAIL + 64 : TAIL + 64 + REST]], axis=1)
    return jnp.stack([real, imag])


def on_device(orbitals, kernels, pair_kdiff, stored_kernel_index):
    group = lax.axis_index("kgrp")
    band = lax.axis_index("band")
    y, x, z = band // (NX * NZ), band // NZ % NX, band % NZ
    odd = (group % 2).reshape(1)

    own = lay(orbitals)
    first = (
        swap_groups(pair_kdiff, 1),
        swap_groups(pair_kdiff, 2),
        swap_groups(own, 2),
        shift(own, 0, 1, 0),
        other_side(own),
    )
    diff_core, diff_far = first[:2]
    far, own_side, far_side = lax.optimization_barrier(first)[2:]

    over_yx = [[g * NZ + i for g in range(GROUPS)] for i in range(NZ)]
    sends = pack(odd, pair_kdiff, diff_core, diff_far, stored_kernel_index, kernels)

    four, both = bundle(own, far, own_side, far_side)
    steps = shift(four, 1, 0, 0), shift(four, -1, 0, 0), shift(both, 0, 0, 1), shift(both, 0, 0, -1)
    up, down, ahead, behind, sends = lax.optimization_barrier((*steps, sends))
    over = shift(up[:2], 1, 0, 0), shift(down[2:], -1, 0, 0)
    kern = lax.all_to_all(sends, "band", 0, 0, axis_index_groups=over_yx)
    cols = [both, ahead, behind]
    for _ in range(2):
        ahead, behind = shift(ahead, 0, 0, 1), shift(behind, 0, 0, -1)
        cols += [ahead, behind]
    cols.append(shift(ahead, 0, 0, 1))
    kern, over, cols = lax.optimization_barrier((kern, over, cols))
    half = swap_groups(kern[:, 0], 1)

    place = jnp.stack([(y - dy) % NY * NX + (x - dx) % NX for dy in range(NY) for dx in range(NX)])
    slots = jnp.stack([(z + i) % NZ for i in (0, -1, 1, -2, 2, -3, 3, -4)])
    p_own, p_far, rows, cols = density(place, slots, four, up, over, down, cols)
    m_own = swap_groups(mix(odd, p_own, p_far, half, kern), 1)
    left, right = prepare(rows, cols)
    total = reduce_windows(project(m_own, left, right))
    flat = total.reshape(2, 8 * NB)
    flat = lax.dynamic_slice(flat, (0, band * 27 % 4 * 108), (2, 27 * 108))
    return flat[None]


def solution(mesh):
    return jax.shard_map(
        on_device,
        mesh=mesh,
        in_specs=(P("kgrp", None, "band", None), P(None, None, "band", None), P("kgrp"), P()),
        out_specs=P("kgrp", None, "band"),
        check_vma=False,
    )
```

```python
import jax
import jax.numpy as jnp
from jax import lax
from jax.experimental import pallas as pl
from jax.experimental.pallas import tpu as pltpu
from jax.sharding import PartitionSpec as P

NB = 432
SLAB = 64
NY, NX, NZ = 4, 2, 8
GROUPS = NY * NX
BLOCK = NZ * SLAB
WHOLE = 384
REST = NB - WHOLE
TAIL = 2 * WHOLE
LANES = TAIL + 128
VMEM = 24 * 1024 * 1024

IN_VMEM = pl.BlockSpec(memory_space=pltpu.VMEM)
IN_SMEM = pl.BlockSpec(memory_space=pltpu.SMEM)
ANYWHERE = pl.BlockSpec(memory_space=pl.ANY)
PARAMS = pltpu.CompilerParams(vmem_limit_bytes=VMEM)


def band_route(dy, dx, dz):
    route = []
    for y in range(NY):
        for x in range(NX):
            for z in range(NZ):
                there = ((y + dy) % NY * NX + (x + dx) % NX) * NZ + (z + dz) % NZ
                route.append(((y * NX + x) * NZ + z, there))
    return route


def shift(block, dy, dx, dz):
    return lax.ppermute(block, "band", band_route(dy, dx, dz))


def swap_groups(block, bit):
    return lax.ppermute(block, "kgrp", [(k, k ^ bit) for k in range(4)])


def other_side(block):
    route = [(i, j) for i, j in band_route(0, 1, 0)]
    both = [((k ^ 2) * 64 + i, k * 64 + j) for k in range(4) for i, j in route]
    return lax.ppermute(block, ("kgrp", "band"), both)


def dot(a, b, a_axis, b_axis):
    dims = (((a_axis,), (b_axis,)), ((), ()))
    return lax.dot_general(a, b, dims, preferred_element_type=jnp.float32)


def near(array):
    return pltpu.with_memory_space_constraint(array, pltpu.VMEM)


def away(array):
    return pltpu.with_memory_space_constraint(array, pltpu.HBM)


def lay_body(orbit_ref, out_ref):
    gap = jnp.zeros((SLAB, 64 - REST), jnp.float32)
    real, imag = orbit_ref[0, 0], orbit_ref[0, 1]
    out_ref[:, :WHOLE] = real[:, :WHOLE]
    out_ref[:, WHOLE:TAIL] = imag[:, :WHOLE]
    last = [real[:, WHOLE:].astype(jnp.float32), gap, imag[:, WHOLE:].astype(jnp.float32), gap]
    out_ref[:, TAIL:] = jnp.concatenate(last, axis=1).astype(jnp.bfloat16)


def lay(orbitals):
    return pl.pallas_call(
        lay_body,
        out_shape=pltpu.VMEM((SLAB, LANES), jnp.bfloat16),
        in_specs=[IN_VMEM],
        out_specs=IN_VMEM,
        name="lay",
    )(orbitals)


def turned(rows):
    last = rows[:, TAIL:].astype(jnp.float32)
    lane = lax.broadcasted_iota(jnp.int32, last.shape, 1)
    last = pltpu.roll(last, 64, 1) * jnp.where(lane < 64, 1.0, -1.0)
    return jnp.concatenate(
        [rows[:, WHOLE:TAIL], -rows[:, :WHOLE], last.astype(rows.dtype)], axis=1
    )


def pack_body(odd_ref, own_ref, core_ref, far_ref, stored_ref, kernels_ref, out_ref, sem):
    odd = odd_ref[0] == 1
    own, core, far = stored_ref[own_ref[0]], stored_ref[core_ref[0]], stored_ref[far_ref[0]]
    shared = jnp.where(odd, own, core)
    single = jnp.where(odd, core, far)
    copies = []
    for i in range(GROUPS):
        at = pl.ds(i * BLOCK, BLOCK)
        half = kernels_ref.at[shared, odd_ref[0], :, at]
        copies.append(pltpu.make_async_copy(half, out_ref.at[i, 0], sem.at[0, i]))
        both = kernels_ref.at[single, :, :, at]
        copies.append(pltpu.make_async_copy(both, out_ref.at[i, pl.ds(1, 2)], sem.at[1, i]))
    for copy in copies:
        copy.start()
    for copy in copies:
        copy.wait()


def pack(odd, own, core, far, stored, kernels):
    return pl.pallas_call(
        pack_body,
        out_shape=jax.ShapeDtypeStruct((GROUPS, 3, SLAB, BLOCK), jnp.bfloat16),
        in_specs=[IN_SMEM] * 5 + [pl.BlockSpec(memory_space=pltpu.HBM)],
        out_specs=IN_VMEM,
        scratch_shapes=[pltpu.SemaphoreType.DMA((2, GROUPS))],
        compiler_params=PARAMS,
        name="pack",
    )(odd, own, core, far, stored, away(kernels))


def density_body(place_ref, slot_ref, *refs):
    four_ref, up_ref, over_here, over_side, down_ref = refs[:5]
    cols = refs[5 : 5 + NZ]
    own_ref, far_ref, row_ref, col_ref, other_rows, other_cols, sem = refs[5 + NZ :]

    def row_at(dy, side):
        return pl.ds(pl.multiple_of(place_ref[dy * NX + side] * SLAB, SLAB), SLAB)

    moves = []
    for i, piece in enumerate(cols):
        at = pl.ds(pl.multiple_of(slot_ref[i] * SLAB, SLAB), SLAB)
        moves.append((piece.at[0], col_ref.at[at, :]))
        moves.append((piece.at[1], other_cols.at[at, :]))
    for side, piece in enumerate((over_here, over_side)):
        moves.append((piece.at[0], row_ref.at[row_at(2, side), :]))
        moves.append((piece.at[1], other_rows.at[row_at(2, side), :]))
    copies = [pltpu.make_async_copy(*move, sem.at[i]) for i, move in enumerate(moves)]
    for copy in copies:
        copy.start()
    for dy, piece in ((0, four_ref), (1, up_ref), (3, down_ref)):
        for side in range(NX):
            row_ref[row_at(dy, side), :] = piece[2 * side]
            other_rows[row_at(dy, side), :] = piece[2 * side + 1]
    for copy in copies:
        copy.wait()
    for rows, columns, out in ((row_ref, col_ref, own_ref), (other_rows, other_cols, far_ref)):
        a, b = rows[...], columns[...]
        out[:, :BLOCK] = dot(a, b, 1, 1)
        out[:, BLOCK:] = dot(turned(a), b, 1, 1)


def density(place, slots, four, up, over, down, cols):
    product = pltpu.VMEM((BLOCK, 2 * BLOCK), jnp.float32)
    points = pltpu.VMEM((BLOCK, LANES), jnp.bfloat16)
    specs = [IN_VMEM] * 2 + [ANYWHERE] * 2 + [IN_VMEM] + [ANYWHERE] * NZ
    arrays = [near(four), near(up), *over, near(down), *cols]
    return pl.pallas_call(
        density_body,
        out_shape=[product, product, points, points],
        in_specs=[IN_SMEM] * 2 + specs,
        out_specs=[IN_VMEM] * 4,
        scratch_shapes=[pltpu.VMEM((BLOCK, LANES), jnp.bfloat16)] * 2
        + [pltpu.SemaphoreType.DMA((2 * NX + 2 * NZ,))],
        compiler_params=PARAMS,
        name="density",
    )(place, slots, *arrays)


def mix_body(odd_ref, own_ref, far_ref, half_ref, kern_ref, m_ref):
    odd = odd_ref[0] == 1
    sign = jnp.where(odd, -1.0, 1.0).astype(jnp.float32)
    for i in range(GROUPS):
        at = pl.ds(i * SLAB, SLAB)
        mine, other = kern_ref[i, 0], half_ref[i]
        k_re = jnp.where(odd, other, mine).astype(jnp.float32)
        k_im = jnp.where(odd, mine, other).astype(jnp.float32) * sign
        p_re, p_im = own_ref[at, :BLOCK], own_ref[at, BLOCK:]
        total_re = k_re * p_re - k_im * p_im
        total_im = k_re * p_im + k_im * p_re
        k_re = kern_ref[i, 1].astype(jnp.float32)
        k_im = kern_ref[i, 2].astype(jnp.float32) * -sign
        p_re, p_im = far_ref[at, :BLOCK], far_ref[at, BLOCK:]
        total_re += k_re * p_re - k_im * p_im
        total_im += k_re * p_im + k_im * p_re
        m_ref[at, :BLOCK] = total_re.astype(jnp.bfloat16)
        m_ref[at, BLOCK:] = total_im.astype(jnp.bfloat16)


def mix(odd, *arrays):
    return pl.pallas_call(
        mix_body,
        out_shape=pltpu.VMEM((BLOCK, 2 * BLOCK), jnp.bfloat16),
        in_specs=[IN_SMEM] + [IN_VMEM] * 4,
        out_specs=IN_VMEM,
        compiler_params=PARAMS,
        name="mix",
    )(odd, *map(near, arrays))


def prepare_body(row_ref, col_ref, left_ref, right_ref):
    flipped = row_ref[...].T
    left_ref[pl.ds(0, WHOLE), :BLOCK] = flipped[:WHOLE]
    left_ref[pl.ds(WHOLE, REST), :BLOCK] = flipped[TAIL : TAIL + REST]
    left_ref[pl.ds(0, WHOLE), BLOCK:] = flipped[WHOLE:TAIL]
    left_ref[pl.ds(WHOLE, REST), BLOCK:] = flipped[TAIL + 64 : TAIL + 64 + REST]
    col = col_ref[...]
    right_ref[pl.ds(0, BLOCK), :] = col
    right_ref[pl.ds(BLOCK, BLOCK), :] = -turned(col)


def prepare(rows, cols):
    return pl.pallas_call(
        prepare_body,
        out_shape=[
            pltpu.VMEM((NB, 2 * BLOCK), jnp.bfloat16),
            pltpu.VMEM((2 * BLOCK, LANES), jnp.bfloat16),
        ],
        in_specs=[IN_VMEM] * 2,
        out_specs=[IN_VMEM] * 2,
        compiler_params=PARAMS,
        name="prepare",
    )(near(rows), near(cols))


def window_at(place):
    outer, half = place // (NZ // 2), place % (NZ // 2)
    return outer // 2 * NZ + 2 * half + outer % 2


def project_body(m_ref, left_ref, right_ref, out_ref, x_ref, part_ref, sem):
    y = dot(m_ref[...], right_ref[...], 1, 0)
    high = y.astype(jnp.bfloat16)
    low = (y - high.astype(jnp.float32)).astype(jnp.bfloat16)
    high = jnp.concatenate([high, turned(high)], axis=0)
    low = jnp.concatenate([low, turned(low)], axis=0)
    x_ref[pl.ds(NB, 8), :] = jnp.zeros((8, LANES), jnp.float32)
    copies = []
    for part, (start, size) in enumerate(((0, 224), (224, 208))):
        at = pl.ds(start, size)
        x_ref[at, :] = -(dot(left_ref[at, :], high, 1, 0) + dot(left_ref[at, :], low, 1, 0))
        some = GROUPS * NZ // 4
        for pair in range(part * some, (part + 1) * some):
            starts = [27 * window_at(2 * pair + i) // 4 for i in range(2)]
            rows = [x_ref[pl.ds(first, 8), :] for first in starts]
            part_ref[pair] = jnp.concatenate(rows, axis=0).astype(jnp.bfloat16)
        chosen = pl.ds(part * some, some)
        copy = pltpu.make_async_copy(part_ref.at[chosen], out_ref.at[chosen], sem.at[part])
        copy.start()
        copies.append(copy)
    for copy in copies:
        copy.wait()


def project(m, left, right):
    windows = (GROUPS * NZ // 2, 16, LANES)
    return pl.pallas_call(
        project_body,
        out_shape=jax.ShapeDtypeStruct(windows, jnp.bfloat16),
        in_specs=[IN_VMEM] * 3,
        out_specs=pl.BlockSpec(memory_space=pltpu.HBM),
        scratch_shapes=[
            pltpu.VMEM((NB + 8, LANES), jnp.float32),
            pltpu.VMEM(windows, jnp.bfloat16),
            pltpu.SemaphoreType.DMA((2,)),
        ],
        compiler_params=PARAMS,
        name="project",
    )(near(m), near(left), near(right))


def bundle_body(own_ref, far_ref, own_side, far_side, four_ref, both_ref):
    for i, ref in enumerate((own_ref, far_ref, own_side, far_side)):
        four_ref[i] = ref[...]
    both_ref[0] = own_ref[...]
    both_ref[1] = far_ref[...]


def bundle(*blocks):
    return pl.pallas_call(
        bundle_body,
        out_shape=[
            pltpu.VMEM((4, SLAB, LANES), jnp.bfloat16),
            pltpu.VMEM((2, SLAB, LANES), jnp.bfloat16),
        ],
        in_specs=[IN_VMEM] * 4,
        out_specs=[IN_VMEM] * 2,
        compiler_params=PARAMS,
        name="bundle",
    )(*map(near, blocks))


def reduce_windows(windows):
    quads = NZ // 2
    wide = [[g * NZ + 2 * j + i for g in range(GROUPS) for i in range(2)] for j in range(quads)]
    deep = [[g * NZ + 2 * j + i for j in range(quads)] for g in range(GROUPS) for i in range(2)]
    parts = windows.reshape(2 * GROUPS, quads, 8, LANES)
    parts = lax.all_to_all(parts, "band", 0, 0, axis_index_groups=wide)
    parts = jnp.sum(parts.astype(jnp.float32), axis=0)
    total = jnp.sum(lax.all_to_all(parts, "band", 0, 0, axis_index_groups=deep), axis=0)
    real = jnp.concatenate([total[:, :WHOLE], total[:, TAIL : TAIL + REST]], axis=1)
    imag = jnp.concatenate([total[:, WHOLE:TAIL], total[:, TAIL + 64 : TAIL + 64 + REST]], axis=1)
    return jnp.stack([real, imag])


def on_device(orbitals, kernels, pair_kdiff, stored_kernel_index):
    group = lax.axis_index("kgrp")
    band = lax.axis_index("band")
    y, x, z = band // (NX * NZ), band // NZ % NX, band % NZ
    odd = (group % 2).reshape(1)

    own = lay(orbitals)
    first = (
        swap_groups(pair_kdiff, 1),
        swap_groups(pair_kdiff, 2),
        swap_groups(own, 2),
        shift(own, 0, 1, 0),
        other_side(own),
    )
    diff_core, diff_far = first[:2]
    far, own_side, far_side = lax.optimization_barrier(first)[2:]

    over_yx = [[g * NZ + i for g in range(GROUPS)] for i in range(NZ)]
    sends = pack(odd, pair_kdiff, diff_core, diff_far, stored_kernel_index, kernels)

    four, both = bundle(own, far, own_side, far_side)
    steps = shift(four, 1, 0, 0), shift(four, -1, 0, 0), shift(both, 0, 0, 1), shift(both, 0, 0, -1)
    up, down, ahead, behind, sends = lax.optimization_barrier((*steps, sends))
    over = shift(up[:2], 1, 0, 0), shift(down[2:], -1, 0, 0)
    kern = lax.all_to_all(sends, "band", 0, 0, axis_index_groups=over_yx)
    cols = [both, ahead, behind]
    for _ in range(2):
        ahead, behind = shift(ahead, 0, 0, 1), shift(behind, 0, 0, -1)
        cols += [ahead, behind]
    cols.append(shift(ahead, 0, 0, 1))
    kern, over, cols = lax.optimization_barrier((kern, over, cols))
    half = swap_groups(kern[:, 0], 1)

    place = jnp.stack([(y - dy) % NY * NX + (x - dx) % NX for dy in range(NY) for dx in range(NX)])
    slots = jnp.stack([(z + i) % NZ for i in (0, -1, 1, -2, 2, -3, 3, -4)])
    p_own, p_far, rows, cols = density(place, slots, four, up, over, down, cols)
    m_own = swap_groups(mix(odd, p_own, p_far, half, kern), 1)
    left, right = prepare(rows, cols)
    total = reduce_windows(project(m_own, left, right))
    flat = total.reshape(2, 8 * NB)
    flat = lax.dynamic_slice(flat, (0, band * 27 % 4 * 108), (2, 27 * 108))
    return flat[None]


def solution(mesh):
    return jax.shard_map(
        on_device,
        mesh=mesh,
        in_specs=(P("kgrp", None, "band", None), P(None, None, "band", None), P("kgrp"), P()),
        out_specs=P("kgrp", None, "band"),
        check_vma=False,
    )
```

```python
import jax
import jax.numpy as jnp
from jax import lax
from jax.experimental import pallas as pl
from jax.experimental.pallas import tpu as pltpu
from jax.sharding import PartitionSpec as P

NB = 432
SLAB = 64
NY, NX, NZ = 4, 2, 8
GROUPS = NY * NX
BLOCK = NZ * SLAB
WHOLE = 384
REST = NB - WHOLE
TAIL = 2 * WHOLE
LANES = TAIL + 128
VMEM = 24 * 1024 * 1024

IN_VMEM = pl.BlockSpec(memory_space=pltpu.VMEM)
IN_SMEM = pl.BlockSpec(memory_space=pltpu.SMEM)
ANYWHERE = pl.BlockSpec(memory_space=pl.ANY)
PARAMS = pltpu.CompilerParams(vmem_limit_bytes=VMEM)


def band_route(dy, dx, dz):
    route = []
    for y in range(NY):
        for x in range(NX):
            for z in range(NZ):
                there = ((y + dy) % NY * NX + (x + dx) % NX) * NZ + (z + dz) % NZ
                route.append(((y * NX + x) * NZ + z, there))
    return route


def shift(block, dy, dx, dz):
    return lax.ppermute(block, "band", band_route(dy, dx, dz))


def swap_groups(block, bit):
    return lax.ppermute(block, "kgrp", [(k, k ^ bit) for k in range(4)])


def other_side(block):
    route = [(i, j) for i, j in band_route(0, 1, 0)]
    both = [((k ^ 2) * 64 + i, k * 64 + j) for k in range(4) for i, j in route]
    return lax.ppermute(block, ("kgrp", "band"), both)


def dot(a, b, a_axis, b_axis):
    dims = (((a_axis,), (b_axis,)), ((), ()))
    return lax.dot_general(a, b, dims, preferred_element_type=jnp.float32)


def near(array):
    return pltpu.with_memory_space_constraint(array, pltpu.VMEM)


def away(array):
    return pltpu.with_memory_space_constraint(array, pltpu.HBM)


def lay_body(orbit_ref, out_ref):
    gap = jnp.zeros((SLAB, 64 - REST), jnp.float32)
    real, imag = orbit_ref[0, 0], orbit_ref[0, 1]
    out_ref[:, :WHOLE] = real[:, :WHOLE]
    out_ref[:, WHOLE:TAIL] = imag[:, :WHOLE]
    last = [real[:, WHOLE:].astype(jnp.float32), gap, imag[:, WHOLE:].astype(jnp.float32), gap]
    out_ref[:, TAIL:] = jnp.concatenate(last, axis=1).astype(jnp.bfloat16)


def lay(orbitals):
    return pl.pallas_call(
        lay_body,
        out_shape=pltpu.VMEM((SLAB, LANES), jnp.bfloat16),
        in_specs=[IN_VMEM],
        out_specs=IN_VMEM,
        name="lay",
    )(orbitals)


def turned(rows):
    last = rows[:, TAIL:].astype(jnp.float32)
    lane = lax.broadcasted_iota(jnp.int32, last.shape, 1)
    last = pltpu.roll(last, 64, 1) * jnp.where(lane < 64, 1.0, -1.0)
    return jnp.concatenate(
        [rows[:, WHOLE:TAIL], -rows[:, :WHOLE], last.astype(rows.dtype)], axis=1
    )


def pack_body(odd_ref, own_ref, core_ref, far_ref, stored_ref, kernels_ref, out_ref, sem):
    odd = odd_ref[0] == 1
    own, core, far = stored_ref[own_ref[0]], stored_ref[core_ref[0]], stored_ref[far_ref[0]]
    shared = jnp.where(odd, own, core)
    single = jnp.where(odd, core, far)
    copies = []
    for i in range(GROUPS):
        at = pl.ds(i * BLOCK, BLOCK)
        half = kernels_ref.at[shared, odd_ref[0], :, at]
        copies.append(pltpu.make_async_copy(half, out_ref.at[i, 0], sem.at[0, i]))
        both = kernels_ref.at[single, :, :, at]
        copies.append(pltpu.make_async_copy(both, out_ref.at[i, pl.ds(1, 2)], sem.at[1, i]))
    for copy in copies:
        copy.start()
    for copy in copies:
        copy.wait()


def pack(odd, own, core, far, stored, kernels):
    return pl.pallas_call(
        pack_body,
        out_shape=jax.ShapeDtypeStruct((GROUPS, 3, SLAB, BLOCK), jnp.bfloat16),
        in_specs=[IN_SMEM] * 5 + [pl.BlockSpec(memory_space=pltpu.HBM)],
        out_specs=IN_VMEM,
        scratch_shapes=[pltpu.SemaphoreType.DMA((2, GROUPS))],
        compiler_params=PARAMS,
        name="pack",
    )(odd, own, core, far, stored, away(kernels))


def density_body(place_ref, slot_ref, *refs):
    four_ref, up_ref, over_here, over_side, down_ref = refs[:5]
    cols = refs[5 : 5 + NZ]
    own_ref, far_ref, row_ref, col_ref, other_rows, other_cols, sem = refs[5 + NZ :]

    def row_at(dy, side):
        return pl.ds(pl.multiple_of(place_ref[dy * NX + side] * SLAB, SLAB), SLAB)

    moves = []
    for i, piece in enumerate(cols):
        at = pl.ds(pl.multiple_of(slot_ref[i] * SLAB, SLAB), SLAB)
        moves.append((piece.at[0], col_ref.at[at, :]))
        moves.append((piece.at[1], other_cols.at[at, :]))
    for side, piece in enumerate((over_here, over_side)):
        moves.append((piece.at[0], row_ref.at[row_at(2, side), :]))
        moves.append((piece.at[1], other_rows.at[row_at(2, side), :]))
    for dy, piece in ((0, four_ref), (1, up_ref), (3, down_ref)):
        for side in range(NX):
            moves.append((piece.at[2 * side], row_ref.at[row_at(dy, side), :]))
            moves.append((piece.at[2 * side + 1], other_rows.at[row_at(dy, side), :]))
    copies = [pltpu.make_async_copy(*move, sem.at[i]) for i, move in enumerate(moves)]
    for copy in copies:
        copy.start()
    for copy in copies:
        copy.wait()
    for rows, columns, out in ((row_ref, col_ref, own_ref), (other_rows, other_cols, far_ref)):
        a, b = rows[...], columns[...]
        out[:, :BLOCK] = dot(a, b, 1, 1)
        out[:, BLOCK:] = dot(turned(a), b, 1, 1)


def density(place, slots, four, up, over, down, cols):
    product = pltpu.VMEM((BLOCK, 2 * BLOCK), jnp.float32)
    points = pltpu.VMEM((BLOCK, LANES), jnp.bfloat16)
    in_hbm = pl.BlockSpec(memory_space=pltpu.HBM)
    specs = [in_hbm] * (5 + NZ)
    arrays = map(away, (four, up, *over, down, *cols))
    return pl.pallas_call(
        density_body,
        out_shape=[product, product, points, points],
        in_specs=[IN_SMEM] * 2 + specs,
        out_specs=[IN_VMEM] * 4,
        scratch_shapes=[pltpu.VMEM((BLOCK, LANES), jnp.bfloat16)] * 2
        + [pltpu.SemaphoreType.DMA((2 * NX * NY + 2 * NZ,))],
        compiler_params=PARAMS,
        name="density",
    )(place, slots, *arrays)


def mix_body(odd_ref, own_ref, far_ref, core_ref, kern_ref, m_ref):
    odd = odd_ref[0] == 1
    sign = jnp.where(odd, -1.0, 1.0).astype(jnp.float32)
    for i in range(GROUPS):
        at = pl.ds(i * SLAB, SLAB)
        mine, other = kern_ref[i, 0], core_ref[i, 0]
        k_re = jnp.where(odd, other, mine).astype(jnp.float32)
        k_im = jnp.where(odd, mine, other).astype(jnp.float32) * sign
        p_re, p_im = own_ref[at, :BLOCK], own_ref[at, BLOCK:]
        total_re = k_re * p_re - k_im * p_im
        total_im = k_re * p_im + k_im * p_re
        k_re = kern_ref[i, 1].astype(jnp.float32)
        k_im = kern_ref[i, 2].astype(jnp.float32) * -sign
        p_re, p_im = far_ref[at, :BLOCK], far_ref[at, BLOCK:]
        total_re += k_re * p_re - k_im * p_im
        total_im += k_re * p_im + k_im * p_re
        m_ref[at, :BLOCK] = total_re.astype(jnp.bfloat16)
        m_ref[at, BLOCK:] = total_im.astype(jnp.bfloat16)


def mix(odd, *arrays):
    return pl.pallas_call(
        mix_body,
        out_shape=pltpu.VMEM((BLOCK, 2 * BLOCK), jnp.bfloat16),
        in_specs=[IN_SMEM] + [IN_VMEM] * 4,
        out_specs=IN_VMEM,
        compiler_params=PARAMS,
        name="mix",
    )(odd, *map(near, arrays))


def prepare_body(row_ref, col_ref, left_ref, right_ref):
    flipped = row_ref[...].T
    left_ref[pl.ds(0, WHOLE), :BLOCK] = flipped[:WHOLE]
    left_ref[pl.ds(WHOLE, REST), :BLOCK] = flipped[TAIL : TAIL + REST]
    left_ref[pl.ds(0, WHOLE), BLOCK:] = flipped[WHOLE:TAIL]
    left_ref[pl.ds(WHOLE, REST), BLOCK:] = flipped[TAIL + 64 : TAIL + 64 + REST]
    col = col_ref[...]
    right_ref[pl.ds(0, BLOCK), :] = col
    right_ref[pl.ds(BLOCK, BLOCK), :] = -turned(col)


def prepare(rows, cols):
    return pl.pallas_call(
        prepare_body,
        out_shape=[
            pltpu.VMEM((NB, 2 * BLOCK), jnp.bfloat16),
            pltpu.VMEM((2 * BLOCK, LANES), jnp.bfloat16),
        ],
        in_specs=[IN_VMEM] * 2,
        out_specs=[IN_VMEM] * 2,
        compiler_params=PARAMS,
        name="prepare",
    )(near(rows), near(cols))


def window_at(place):
    outer, half = place // (NZ // 2), place % (NZ // 2)
    return outer // 2 * NZ + 2 * half + outer % 2


def project_body(m_ref, left_ref, right_ref, out_ref, x_ref, part_ref, sem):
    y = dot(m_ref[...], right_ref[...], 1, 0)
    high = y.astype(jnp.bfloat16)
    low = (y - high.astype(jnp.float32)).astype(jnp.bfloat16)
    high = jnp.concatenate([high, turned(high)], axis=0)
    low = jnp.concatenate([low, turned(low)], axis=0)
    x_ref[pl.ds(NB, 8), :] = jnp.zeros((8, LANES), jnp.float32)
    copies = []
    for part, (start, size) in enumerate(((0, 224), (224, 208))):
        at = pl.ds(start, size)
        x_ref[at, :] = -(dot(left_ref[at, :], high, 1, 0) + dot(left_ref[at, :], low, 1, 0))
        some = GROUPS * NZ // 4
        for pair in range(part * some, (part + 1) * some):
            starts = [27 * window_at(2 * pair + i) // 4 for i in range(2)]
            rows = [x_ref[pl.ds(first, 8), :] for first in starts]
            part_ref[pair] = jnp.concatenate(rows, axis=0).astype(jnp.bfloat16)
        chosen = pl.ds(part * some, some)
        copy = pltpu.make_async_copy(part_ref.at[chosen], out_ref.at[chosen], sem.at[part])
        copy.start()
        copies.append(copy)
    for copy in copies:
        copy.wait()


def project(m, left, right):
    windows = (GROUPS * NZ // 2, 16, LANES)
    return pl.pallas_call(
        project_body,
        out_shape=jax.ShapeDtypeStruct(windows, jnp.bfloat16),
        in_specs=[IN_VMEM] * 3,
        out_specs=pl.BlockSpec(memory_space=pltpu.HBM),
        scratch_shapes=[
            pltpu.VMEM((NB + 8, LANES), jnp.float32),
            pltpu.VMEM(windows, jnp.bfloat16),
            pltpu.SemaphoreType.DMA((2,)),
        ],
        compiler_params=PARAMS,
        name="project",
    )(near(m), near(left), near(right))


def bundle_body(own_ref, far_ref, own_side, far_side, four_ref, both_ref):
    for i, ref in enumerate((own_ref, far_ref, own_side, far_side)):
        four_ref[i] = ref[...]
    both_ref[0] = own_ref[...]
    both_ref[1] = far_ref[...]


def bundle(*blocks):
    return pl.pallas_call(
        bundle_body,
        out_shape=[
            pltpu.VMEM((4, SLAB, LANES), jnp.bfloat16),
            pltpu.VMEM((2, SLAB, LANES), jnp.bfloat16),
        ],
        in_specs=[IN_VMEM] * 4,
        out_specs=[IN_VMEM] * 2,
        compiler_params=PARAMS,
        name="bundle",
    )(*map(near, blocks))


def reduce_windows(windows):
    quads = NZ // 2
    wide = [[g * NZ + 2 * j + i for g in range(GROUPS) for i in range(2)] for j in range(quads)]
    deep = [[g * NZ + 2 * j + i for j in range(quads)] for g in range(GROUPS) for i in range(2)]
    parts = windows.reshape(2 * GROUPS, quads, 8, LANES)
    parts = lax.all_to_all(parts, "band", 0, 0, axis_index_groups=wide)
    parts = jnp.sum(parts.astype(jnp.float32), axis=0)
    total = jnp.sum(lax.all_to_all(parts, "band", 0, 0, axis_index_groups=deep), axis=0)
    real = jnp.concatenate([total[:, :WHOLE], total[:, TAIL : TAIL + REST]], axis=1)
    imag = jnp.concatenate([total[:, WHOLE:TAIL], total[:, TAIL + 64 : TAIL + 64 + REST]], axis=1)
    return jnp.stack([real, imag])


def on_device(orbitals, kernels, pair_kdiff, stored_kernel_index):
    group = lax.axis_index("kgrp")
    band = lax.axis_index("band")
    y, x, z = band // (NX * NZ), band // NZ % NX, band % NZ
    odd = (group % 2).reshape(1)

    own = lay(orbitals)
    first = (
        swap_groups(pair_kdiff, 1),
        swap_groups(pair_kdiff, 2),
        swap_groups(own, 2),
        shift(own, 0, 1, 0),
        other_side(own),
    )
    diff_core, diff_far = first[:2]
    far, own_side, far_side = lax.optimization_barrier(first)[2:]

    over_yx = [[g * NZ + i for g in range(GROUPS)] for i in range(NZ)]
    sends = pack(odd, pair_kdiff, diff_core, diff_far, stored_kernel_index, kernels)

    four, both = bundle(own, far, own_side, far_side)
    steps = shift(four, 1, 0, 0), shift(four, -1, 0, 0), shift(both, 0, 0, 1), shift(both, 0, 0, -1)
    up, down, ahead, behind, sends = lax.optimization_barrier((*steps, sends))
    over = shift(up[:2], 1, 0, 0), shift(down[2:], -1, 0, 0)
    kern = lax.all_to_all(sends, "band", 0, 0, axis_index_groups=over_yx)
    cols = [both, ahead, behind]
    for _ in range(2):
        ahead, behind = shift(ahead, 0, 0, 1), shift(behind, 0, 0, -1)
        cols += [ahead, behind]
    cols.append(shift(ahead, 0, 0, 1))
    kern, over, cols = lax.optimization_barrier((kern, over, cols))
    kern_core = swap_groups(kern, 1)

    place = jnp.stack([(y - dy) % NY * NX + (x - dx) % NX for dy in range(NY) for dx in range(NX)])
    slots = jnp.stack([(z + i) % NZ for i in (0, -1, 1, -2, 2, -3, 3, -4)])
    p_own, p_far, rows, cols = density(place, slots, four, up, over, down, cols)
    m_own = swap_groups(mix(odd, p_own, p_far, kern_core, kern), 1)
    left, right = prepare(rows, cols)
    total = reduce_windows(project(m_own, left, right))
    flat = total.reshape(2, 8 * NB)
    flat = lax.dynamic_slice(flat, (0, band * 27 % 4 * 108), (2, 27 * 108))
    return flat[None]


def solution(mesh):
    return jax.shard_map(
        on_device,
        mesh=mesh,
        in_specs=(P("kgrp", None, "band", None), P(None, None, "band", None), P("kgrp"), P()),
        out_specs=P("kgrp", None, "band"),
        check_vma=False,
    )
```

```python
import functools

import jax
import jax.numpy as jnp
from jax import lax
from jax.experimental import pallas as pl
from jax.experimental.pallas import tpu as pltpu
from jax.sharding import PartitionSpec as P

NB = 432
SLAB = 64
NY, NX, NZ = 4, 2, 8
GROUPS = NY * NX
BLOCK = NZ * SLAB
WHOLE = 384
REST = NB - WHOLE
TAIL = 2 * WHOLE
LANES = TAIL + 128
VMEM = 24 * 1024 * 1024

IN_VMEM = pl.BlockSpec(memory_space=pltpu.VMEM)
IN_SMEM = pl.BlockSpec(memory_space=pltpu.SMEM)
ANYWHERE = pl.BlockSpec(memory_space=pl.ANY)
PARAMS = pltpu.CompilerParams(vmem_limit_bytes=VMEM)


def band_route(dy, dx, dz):
    route = []
    for y in range(NY):
        for x in range(NX):
            for z in range(NZ):
                there = ((y + dy) % NY * NX + (x + dx) % NX) * NZ + (z + dz) % NZ
                route.append(((y * NX + x) * NZ + z, there))
    return route


def shift(block, dy, dx, dz):
    return lax.ppermute(block, "band", band_route(dy, dx, dz))


def swap_groups(block, bit):
    return lax.ppermute(block, "kgrp", [(k, k ^ bit) for k in range(4)])


def other_side(block):
    route = [(i, j) for i, j in band_route(0, 1, 0)]
    both = [((k ^ 2) * 64 + i, k * 64 + j) for k in range(4) for i, j in route]
    return lax.ppermute(block, ("kgrp", "band"), both)


def dot(a, b, a_axis, b_axis):
    dims = (((a_axis,), (b_axis,)), ((), ()))
    return lax.dot_general(a, b, dims, preferred_element_type=jnp.float32)


def near(array):
    return pltpu.with_memory_space_constraint(array, pltpu.VMEM)


def away(array):
    return pltpu.with_memory_space_constraint(array, pltpu.HBM)


def lay_body(orbit_ref, out_ref):
    gap = jnp.zeros((SLAB, 64 - REST), jnp.float32)
    real, imag = orbit_ref[0, 0], orbit_ref[0, 1]
    out_ref[:, :WHOLE] = real[:, :WHOLE]
    out_ref[:, WHOLE:TAIL] = imag[:, :WHOLE]
    last = [real[:, WHOLE:].astype(jnp.float32), gap, imag[:, WHOLE:].astype(jnp.float32), gap]
    out_ref[:, TAIL:] = jnp.concatenate(last, axis=1).astype(jnp.bfloat16)


def lay(orbitals):
    return pl.pallas_call(
        lay_body,
        out_shape=pltpu.VMEM((SLAB, LANES), jnp.bfloat16),
        in_specs=[IN_VMEM],
        out_specs=IN_VMEM,
        name="lay",
    )(orbitals)


def turned(rows):
    last = rows[:, TAIL:].astype(jnp.float32)
    lane = lax.broadcasted_iota(jnp.int32, last.shape, 1)
    last = pltpu.roll(last, 64, 1) * jnp.where(lane < 64, 1.0, -1.0)
    return jnp.concatenate(
        [rows[:, WHOLE:TAIL], -rows[:, :WHOLE], last.astype(rows.dtype)], axis=1
    )


def pack_body(odd_ref, own_ref, core_ref, far_ref, stored_ref, kernels_ref, out_ref, sem):
    odd = odd_ref[0] == 1
    own, core, far = stored_ref[own_ref[0]], stored_ref[core_ref[0]], stored_ref[far_ref[0]]
    shared = jnp.where(odd, own, core)
    single = jnp.where(odd, core, far)
    copies = []
    for i in range(GROUPS):
        at = pl.ds(i * BLOCK, BLOCK)
        half = kernels_ref.at[shared, odd_ref[0], :, at]
        copies.append(pltpu.make_async_copy(half, out_ref.at[i, 0], sem.at[0, i]))
        both = kernels_ref.at[single, :, :, at]
        copies.append(pltpu.make_async_copy(both, out_ref.at[i, pl.ds(1, 2)], sem.at[1, i]))
    for copy in copies:
        copy.start()
    for copy in copies:
        copy.wait()


def pack(odd, own, core, far, stored, kernels):
    return pl.pallas_call(
        pack_body,
        out_shape=jax.ShapeDtypeStruct((GROUPS, 3, SLAB, BLOCK), jnp.bfloat16),
        in_specs=[IN_SMEM] * 5 + [pl.BlockSpec(memory_space=pltpu.HBM)],
        out_specs=IN_VMEM,
        scratch_shapes=[pltpu.SemaphoreType.DMA((2, GROUPS))],
        compiler_params=PARAMS,
        name="pack",
    )(odd, own, core, far, stored, away(kernels))


def density_body(place_ref, slot_ref, *refs):
    four_ref, up_ref, over_here, over_side, down_ref = refs[:5]
    cols = refs[5 : 5 + NZ]
    own_ref, far_ref, row_ref, col_ref, other_rows, other_cols, sem = refs[5 + NZ :]

    def row_at(dy, side):
        return pl.ds(pl.multiple_of(place_ref[dy * NX + side] * SLAB, SLAB), SLAB)

    moves = []
    for i, piece in enumerate(cols):
        at = pl.ds(pl.multiple_of(slot_ref[i] * SLAB, SLAB), SLAB)
        moves.append((piece.at[0], col_ref.at[at, :]))
        moves.append((piece.at[1], other_cols.at[at, :]))
    for side, piece in enumerate((over_here, over_side)):
        moves.append((piece.at[0], row_ref.at[row_at(2, side), :]))
        moves.append((piece.at[1], other_rows.at[row_at(2, side), :]))
    copies = [pltpu.make_async_copy(*move, sem.at[i]) for i, move in enumerate(moves)]
    for copy in copies:
        copy.start()
    for dy, piece in ((0, four_ref), (1, up_ref), (3, down_ref)):
        for side in range(NX):
            row_ref[row_at(dy, side), :] = piece[2 * side]
            other_rows[row_at(dy, side), :] = piece[2 * side + 1]
    for copy in copies:
        copy.wait()
    for rows, columns, out in ((row_ref, col_ref, own_ref), (other_rows, other_cols, far_ref)):
        a, b = rows[...], columns[...]
        out[:, :BLOCK] = dot(a, b, 1, 1)
        out[:, BLOCK:] = dot(turned(a), b, 1, 1)


def density(place, slots, four, up, over, down, cols):
    product = pltpu.VMEM((BLOCK, 2 * BLOCK), jnp.float32)
    points = pltpu.VMEM((BLOCK, LANES), jnp.bfloat16)
    in_hbm = pl.BlockSpec(memory_space=pltpu.HBM)
    specs = [IN_VMEM] * 2 + [in_hbm] * 2 + [IN_VMEM] + [in_hbm] * NZ
    arrays = [near(four), near(up), *map(away, over), near(down), *map(away, cols)]
    return pl.pallas_call(
        density_body,
        out_shape=[product, product, points, points],
        in_specs=[IN_SMEM] * 2 + specs,
        out_specs=[IN_VMEM] * 4,
        scratch_shapes=[pltpu.VMEM((BLOCK, LANES), jnp.bfloat16)] * 2
        + [pltpu.SemaphoreType.DMA((2 * NX + 2 * NZ,))],
        compiler_params=PARAMS,
        name="density",
    )(place, slots, *arrays)


def mix_body(part, odd_ref, own_ref, far_ref, half_ref, kern_ref, m_ref):
    odd = odd_ref[0] == 1
    sign = jnp.where(odd, -1.0, 1.0).astype(jnp.float32)
    for step in range(GROUPS // 2):
        i = part * (GROUPS // 2) + step
        at, to = pl.ds(i * SLAB, SLAB), pl.ds(step * SLAB, SLAB)
        mine, other = kern_ref[i, 0], half_ref[i]
        k_re = jnp.where(odd, other, mine).astype(jnp.float32)
        k_im = jnp.where(odd, mine, other).astype(jnp.float32) * sign
        p_re, p_im = own_ref[at, :BLOCK], own_ref[at, BLOCK:]
        total_re = k_re * p_re - k_im * p_im
        total_im = k_re * p_im + k_im * p_re
        k_re = kern_ref[i, 1].astype(jnp.float32)
        k_im = kern_ref[i, 2].astype(jnp.float32) * -sign
        p_re, p_im = far_ref[at, :BLOCK], far_ref[at, BLOCK:]
        total_re += k_re * p_re - k_im * p_im
        total_im += k_re * p_im + k_im * p_re
        m_ref[to, :BLOCK] = total_re.astype(jnp.bfloat16)
        m_ref[to, BLOCK:] = total_im.astype(jnp.bfloat16)


def mix(part, odd, *arrays):
    return pl.pallas_call(
        functools.partial(mix_body, part),
        out_shape=pltpu.VMEM((BLOCK // 2, 2 * BLOCK), jnp.bfloat16),
        in_specs=[IN_SMEM] + [IN_VMEM] * 4,
        out_specs=IN_VMEM,
        compiler_params=PARAMS,
        name="mix",
    )(odd, *map(near, arrays))


def prepare_body(row_ref, col_ref, left_ref, right_ref):
    flipped = row_ref[...].T
    left_ref[pl.ds(0, WHOLE), :BLOCK] = flipped[:WHOLE]
    left_ref[pl.ds(WHOLE, REST), :BLOCK] = flipped[TAIL : TAIL + REST]
    left_ref[pl.ds(0, WHOLE), BLOCK:] = flipped[WHOLE:TAIL]
    left_ref[pl.ds(WHOLE, REST), BLOCK:] = flipped[TAIL + 64 : TAIL + 64 + REST]
    col = col_ref[...]
    right_ref[pl.ds(0, BLOCK), :] = col
    right_ref[pl.ds(BLOCK, BLOCK), :] = -turned(col)


def prepare(rows, cols):
    return pl.pallas_call(
        prepare_body,
        out_shape=[
            pltpu.VMEM((NB, 2 * BLOCK), jnp.bfloat16),
            pltpu.VMEM((2 * BLOCK, LANES), jnp.bfloat16),
        ],
        in_specs=[IN_VMEM] * 2,
        out_specs=[IN_VMEM] * 2,
        compiler_params=PARAMS,
        name="prepare",
    )(near(rows), near(cols))


def window_at(place):
    outer, half = place // (NZ // 2), place % (NZ // 2)
    return outer // 2 * NZ + 2 * half + outer % 2


def project_body(top_ref, low_ref, left_ref, right_ref, out_ref, x_ref, part_ref, sem):
    right = right_ref[...]
    y = jnp.concatenate([dot(m_ref[...], right, 1, 0) for m_ref in (top_ref, low_ref)], axis=0)
    high = y.astype(jnp.bfloat16)
    low = (y - high.astype(jnp.float32)).astype(jnp.bfloat16)
    high = jnp.concatenate([high, turned(high)], axis=0)
    low = jnp.concatenate([low, turned(low)], axis=0)
    x_ref[pl.ds(NB, 8), :] = jnp.zeros((8, LANES), jnp.float32)
    copies = []
    for part, (start, size) in enumerate(((0, 224), (224, 208))):
        at = pl.ds(start, size)
        x_ref[at, :] = -(dot(left_ref[at, :], high, 1, 0) + dot(left_ref[at, :], low, 1, 0))
        some = GROUPS * NZ // 4
        for pair in range(part * some, (part + 1) * some):
            starts = [27 * window_at(2 * pair + i) // 4 for i in range(2)]
            rows = [x_ref[pl.ds(first, 8), :] for first in starts]
            part_ref[pair] = jnp.concatenate(rows, axis=0).astype(jnp.bfloat16)
        chosen = pl.ds(part * some, some)
        copy = pltpu.make_async_copy(part_ref.at[chosen], out_ref.at[chosen], sem.at[part])
        copy.start()
        copies.append(copy)
    for copy in copies:
        copy.wait()


def project(m, left, right):
    windows = (GROUPS * NZ // 2, 16, LANES)
    return pl.pallas_call(
        project_body,
        out_shape=jax.ShapeDtypeStruct(windows, jnp.bfloat16),
        in_specs=[IN_VMEM] * 4,
        out_specs=pl.BlockSpec(memory_space=pltpu.HBM),
        scratch_shapes=[
            pltpu.VMEM((NB + 8, LANES), jnp.float32),
            pltpu.VMEM(windows, jnp.bfloat16),
            pltpu.SemaphoreType.DMA((2,)),
        ],
        compiler_params=PARAMS,
        name="project",
    )(*map(near, m), near(left), near(right))


def bundle_body(own_ref, far_ref, own_side, far_side, four_ref, both_ref):
    for i, ref in enumerate((own_ref, far_ref, own_side, far_side)):
        four_ref[i] = ref[...]
    both_ref[0] = own_ref[...]
    both_ref[1] = far_ref[...]


def bundle(*blocks):
    return pl.pallas_call(
        bundle_body,
        out_shape=[
            pltpu.VMEM((4, SLAB, LANES), jnp.bfloat16),
            pltpu.VMEM((2, SLAB, LANES), jnp.bfloat16),
        ],
        in_specs=[IN_VMEM] * 4,
        out_specs=[IN_VMEM] * 2,
        compiler_params=PARAMS,
        name="bundle",
    )(*map(near, blocks))


def reduce_windows(windows):
    quads = NZ // 2
    wide = [[g * NZ + 2 * j + i for g in range(GROUPS) for i in range(2)] for j in range(quads)]
    deep = [[g * NZ + 2 * j + i for j in range(quads)] for g in range(GROUPS) for i in range(2)]
    parts = windows.reshape(2 * GROUPS, quads, 8, LANES)
    parts = lax.all_to_all(parts, "band", 0, 0, axis_index_groups=wide)
    parts = jnp.sum(parts.astype(jnp.float32), axis=0)
    total = jnp.sum(lax.all_to_all(parts, "band", 0, 0, axis_index_groups=deep), axis=0)
    real = jnp.concatenate([total[:, :WHOLE], total[:, TAIL : TAIL + REST]], axis=1)
    imag = jnp.concatenate([total[:, WHOLE:TAIL], total[:, TAIL + 64 : TAIL + 64 + REST]], axis=1)
    return jnp.stack([real, imag])


def on_device(orbitals, kernels, pair_kdiff, stored_kernel_index):
    group = lax.axis_index("kgrp")
    band = lax.axis_index("band")
    y, x, z = band // (NX * NZ), band // NZ % NX, band % NZ
    odd = (group % 2).reshape(1)

    own = lay(orbitals)
    first = (
        swap_groups(pair_kdiff, 1),
        swap_groups(pair_kdiff, 2),
        swap_groups(own, 2),
        shift(own, 0, 1, 0),
        other_side(own),
    )
    diff_core, diff_far = first[:2]
    far, own_side, far_side = lax.optimization_barrier(first)[2:]

    over_yx = [[g * NZ + i for g in range(GROUPS)] for i in range(NZ)]
    sends = pack(odd, pair_kdiff, diff_core, diff_far, stored_kernel_index, kernels)

    four, both = bundle(own, far, own_side, far_side)
    steps = shift(four, 1, 0, 0), shift(four, -1, 0, 0), shift(both, 0, 0, 1), shift(both, 0, 0, -1)
    up, down, ahead, behind, sends = lax.optimization_barrier((*steps, sends))
    over = shift(up[:2], 1, 0, 0), shift(down[2:], -1, 0, 0)
    kern = lax.all_to_all(sends, "band", 0, 0, axis_index_groups=over_yx)
    cols = [both, ahead, behind]
    for _ in range(2):
        ahead, behind = shift(ahead, 0, 0, 1), shift(behind, 0, 0, -1)
        cols += [ahead, behind]
    cols.append(shift(ahead, 0, 0, 1))
    kern, over, cols = lax.optimization_barrier((kern, over, cols))
    half = swap_groups(kern[:, 0], 1)

    place = jnp.stack([(y - dy) % NY * NX + (x - dx) % NX for dy in range(NY) for dx in range(NX)])
    slots = jnp.stack([(z + i) % NZ for i in (0, -1, 1, -2, 2, -3, 3, -4)])
    p_own, p_far, rows, cols = density(place, slots, four, up, over, down, cols)
    m_own = [swap_groups(mix(part, odd, p_own, p_far, half, kern), 1) for part in range(2)]
    left, right = prepare(rows, cols)
    total = reduce_windows(project(m_own, left, right))
    flat = total.reshape(2, 8 * NB)
    flat = lax.dynamic_slice(flat, (0, band * 27 % 4 * 108), (2, 27 * 108))
    return flat[None]


def solution(mesh):
    return jax.shard_map(
        on_device,
        mesh=mesh,
        in_specs=(P("kgrp", None, "band", None), P(None, None, "band", None), P("kgrp"), P()),
        out_specs=P("kgrp", None, "band"),
        check_vma=False,
    )
```
